32 devices in a mesh: seq: 8 (over y, x, core), tp: 4 (over z).
Axes of the slice: x: 2, y: 2, z: 4, core: 2. Of those that a mesh axis runs over, the one named last changes fastest.
Arguments:
- tokens: bfloat16 [6144, 2048], P('seq', 'tp'), may hold values from -6 to 6
- mix_gain: bfloat16 [2048], P(('tp', 'seq')), may hold values from 0.5 to 1.5
- scan_branch: bfloat16 [2048, 2560], P('seq', 'tp'), may hold values from -0.125 to 0.125
- gate_branch: bfloat16 [2048, 2560], P('seq', 'tp'), may hold values from -0.125 to 0.125
- kernel_taps: bfloat16 [4, 2560], P(None, ('tp', 'seq')), may hold values from -3 to 3
- kernel_bias: bfloat16 [2560], P(('tp', 'seq')), may hold values from -1.796875 to 1.796875
- decay_gate: bfloat16 [16, 25600], P('tp', 'seq'), may hold values from -0.5 to 0.5
- decay_bias: bfloat16 [2560], P(('tp', 'seq')), may hold values from -3 to 3
- input_gate: bfloat16 [16, 25600], P('tp', 'seq'), may hold values from -0.5 to 0.5
- input_bias: bfloat16 [2560], P(('tp', 'seq')), may hold values from -3 to 3
- decay_logit: bfloat16 [2560], P(('tp', 'seq')), may hold values from 4 to 14
- mixer_out: bfloat16 [2560, 2048], P('tp', 'seq'), may hold values from -0.125 to 0.125
- feed_gain: bfloat16 [2048], P(('tp', 'seq')), may hold values from 0.5 to 1.5
- gate_weight: bfloat16 [2048, 6144], P('seq', 'tp'), may hold values from -0.125 to 0.125
- up_weight: bfloat16 [2048, 6144], P('seq', 'tp'), may hold values from -0.125 to 0.125
- down_weight: bfloat16 [6144, 2048], P('tp', 'seq'), may hold values from -0.078125 to 0.078125
- lengths: int32 [6], replicated, may hold values from 1 to 5822, as said below
- cotangent: bfloat16 [6144, 2048], P('seq', 'tp'), may hold values from -6 to 6
Outputs:
- block_out: float32 [6144, 2048], P('seq', 'tp')
- tokens_grad: float32 [6144, 2048], P('seq', 'tp')
- mix_gain_grad: float32 [2048], P(('tp', 'seq'))
- scan_branch_grad: float32 [2048, 2560], P('seq', 'tp')
- gate_branch_grad: float32 [2048, 2560], P('seq', 'tp')
- kernel_taps_grad: float32 [4, 2560], P(None, ('tp', 'seq'))
- kernel_bias_grad: float32 [2560], P(('tp', 'seq'))
- decay_gate_grad: float32 [16, 25600], P('tp', 'seq')
- decay_bias_grad: float32 [2560], P(('tp', 'seq'))
- input_gate_grad: float32 [16, 25600], P('tp', 'seq')
- input_bias_grad: float32 [2560], P(('tp', 'seq'))
- decay_logit_grad: float32 [2560], P(('tp', 'seq'))
- mixer_out_grad: float32 [2560, 2048], P('tp', 'seq')
- feed_gain_grad: float32 [2048], P(('tp', 'seq'))
- gate_weight_grad: float32 [2048, 6144], P('seq', 'tp')
- up_weight_grad: float32 [2048, 6144], P('seq', 'tp')
- down_weight_grad: float32 [6144, 2048], P('tp', 'seq')
- mean_decay: float32 [2560], P(('tp', 'seq'))
The draws below stay inside these ranges and needn't reach their ends.
Inputs may be any that keep to these rules, and one draw needn't show every extreme that they name: The lengths sum to 6144. One of them is long, of exactly the largest length; all others are at most 128 and together hold a fixed number of tokens, fewer than 768. Which one is long varies with the seed.
All inputs are finite; a program needn't handle non-finite values.
Results may differ from the reference program's by a relative error of at most 0.0098.
Values may be sent and summed in bfloat16 or wider, within the bound.
A program may use at most 256 MiB of HBM per device.

```python
import jax
import jax.numpy as jnp
from jax import lax

D = 2048
R = 2560
F = 6144
NB = 16
KW = 4
CD = 8
SEQS = 6
TOK_DEV = 768
BW = 160
TOKENS = 6144


def draw_lengths(key, part):
    key = jax.random.fold_in(key, 7)
    short_key, place_key = jax.random.split(key)
    short_most = TOK_DEV // SEQS
    pair_count = (SEQS - 1) // 2 + 1
    halves = jax.random.randint(short_key, (pair_count,), 1, short_most + 1, dtype=jnp.int32)
    halves = halves.at[0].set(1)
    longest_at = jax.random.randint(place_key, (), 0, SEQS, dtype=jnp.int32)
    ordinal = jnp.arange(SEQS, dtype=jnp.int32)
    rank = (ordinal - (ordinal > longest_at).astype(jnp.int32)).astype(jnp.int32)
    paired = halves[rank // 2]
    shorter = jnp.where(rank % 2 == 0, paired, short_most + 1 - paired)
    lone = ((SEQS - 1) % 2 == 1) & (rank == SEQS - 2)
    shorter = jnp.where(lone, (short_most + 1) // 2, shorter).astype(jnp.int32)
    fixed_sum = (SEQS - 1) // 2 * (short_most + 1) + (SEQS - 1) % 2 * ((short_most + 1) // 2)
    return jnp.where(ordinal == longest_at, TOKENS - fixed_sum, shorter).astype(jnp.int32)


def steps_of(own_key, extent, cuts, least, largest):
    gain = 1.0
    for dim, blocks in cuts:
        heights = jax.random.uniform(jax.random.fold_in(jax.random.fold_in(own_key, 6), dim), (blocks,), jnp.float32, least / len(cuts), largest / len(cuts))
        gain = gain * jnp.repeat(jnp.exp(heights), extent[dim] // blocks).reshape((-1,) + (1,) * (len(extent) - 1 - dim))
    return gain


def scatter_about(key, shape, spread, bound, cuts=(), kind=jnp.bfloat16):
    factor_of = steps_of(key, shape, cuts, -0.22, 0.18) if cuts else 1.0
    values = jax.random.normal(key, shape, jnp.float32) * spread * factor_of
    return jnp.minimum(jnp.maximum(values, -bound), bound).astype(kind)


def setup_inputs(seed: int = 0) -> dict:
    key_of = jax.random.split(jax.random.key(seed), 19)
    tokens = scatter_about(key_of[0], (TOKENS, D), 1.0, 6.0, ((0, 8), (1, 4)))
    mix_gain = jnp.clip(1.0 + 0.1 * jax.random.normal(key_of[1], (D,), jnp.float32), 0.5, 1.5).astype(jnp.bfloat16)
    scan_branch = scatter_about(key_of[2], (D, R), D ** -0.5, 0.125, ((0, 8), (1, 4)))
    gate_branch = scatter_about(key_of[3], (D, R), D ** -0.5, 0.125, ((0, 8), (1, 4)))
    kernel_taps = scatter_about(key_of[4], (KW, R), KW ** -0.5, 3.0, ((1, 32),))
    kernel_bias = scatter_about(key_of[5], (R,), 0.3, 1.796875, ((0, 32),))
    decay_gate = scatter_about(key_of[6], (NB, BW * BW), BW ** -0.5, 0.5, ((0, 4), (1, 8)))
    decay_bias = scatter_about(key_of[7], (R,), 0.5, 3.0, ((0, 32),))
    input_gate = scatter_about(key_of[8], (NB, BW * BW), BW ** -0.5, 0.5, ((0, 4), (1, 8)))
    input_bias = scatter_about(key_of[9], (R,), 0.5, 3.0, ((0, 32),))
    decay_logit = jnp.clip(4.0 + 10.0 * jax.random.uniform(key_of[10], (R,), jnp.float32) ** steps_of(key_of[10], (R,), ((0, 32),), -0.2, 0.2), 4.0, 14.0).astype(jnp.bfloat16)
    mixer_out = scatter_about(key_of[11], (R, D), R ** -0.5, 0.125, ((0, 4), (1, 8)))
    feed_gain = jnp.clip(1.0 + 0.1 * jax.random.normal(key_of[12], (D,), jnp.float32), 0.5, 1.5).astype(jnp.bfloat16)
    gate_weight = scatter_about(key_of[13], (D, F), D ** -0.5, 0.125, ((0, 8), (1, 4)))
    up_weight = scatter_about(key_of[14], (D, F), D ** -0.5, 0.125, ((0, 8), (1, 4)))
    down_weight = scatter_about(key_of[15], (F, D), F ** -0.5, 0.078125, ((0, 4), (1, 8)))
    lengths = draw_lengths(jax.random.fold_in(key_of[18], 71), 0)
    cotangent = scatter_about(key_of[17], (TOKENS, D), 1.0, 6.0, ((0, 8), (1, 4)))
    return {"tokens": tokens, "mix_gain": mix_gain, "scan_branch": scan_branch, "gate_branch": gate_branch, "kernel_taps": kernel_taps, "kernel_bias": kernel_bias, "decay_gate": decay_gate, "decay_bias": decay_bias, "input_gate": input_gate, "input_bias": input_bias, "decay_logit": decay_logit, "mixer_out": mixer_out, "feed_gain": feed_gain, "gate_weight": gate_weight, "up_weight": up_weight, "down_weight": down_weight, "lengths": lengths, "cotangent": cotangent}


EPSILON = 1e-06
FLOOR_VALUE = 0.001
HIGHEST = lax.Precision.HIGHEST

@jax.custom_vjp
def low(v):
    return lax.optimization_barrier(v.astype(jnp.bfloat16)).astype(jnp.float32)

@jax.custom_vjp
def low_back(v):
    return v

def low_keep(v):
    return (low(v), None)

def low_pass(kept, grad):
    return (grad,)

def back_keep(v):
    return (v, None)

def back_low(kept, grad):
    return (low(grad),)
low.defvjp(low_keep, low_pass)
low_back.defvjp(back_keep, back_low)

def matmul_high(left_side, right_side):
    return jnp.dot(left_side, right_side, precision=HIGHEST, preferred_element_type=jnp.float32)

def rms_scaled(values, gain_vector):
    mean_square = lax.optimization_barrier(jnp.mean(values * values, axis=1, keepdims=True))
    return values * lax.rsqrt(mean_square + EPSILON) * gain_vector

def smooth_gelu(values):
    return jax.nn.gelu(values, approximate=True)

def combine(earlier, later):
    return (earlier[0] * later[0], later[1] + later[0] * earlier[1])

def seq_offsets(lengths, first_index, row_total):
    ends_all = jnp.cumsum(lengths, dtype=jnp.int32).astype(jnp.int32)
    starts_all = (ends_all - lengths).astype(jnp.int32)
    position = (first_index + jnp.arange(row_total, dtype=jnp.int32)).astype(jnp.int32)
    begins = lax.optimization_barrier(jnp.max(jnp.where(starts_all[None, :] <= position[:, None], starts_all[None, :], 0), axis=1))
    return (position - begins).astype(jnp.int32)

def causal_conv(branch_rows, taps_matrix, taps_bias, offsets):
    result = taps_bias + taps_matrix[0] * branch_rows
    for lag_step in range(1, KW):
        earlier_rows = jnp.concatenate([jnp.zeros((lag_step, branch_rows.shape[1]), branch_rows.dtype), branch_rows[:-lag_step]], axis=0)
        result = result + jnp.where((offsets >= lag_step)[:, None], taps_matrix[lag_step] * earlier_rows, 0.0)
    return result

def gate_logits(conv_values, gate_matrix, bias_vector):
    blocked = conv_values.reshape(conv_values.shape[0], NB, BW)
    mixed_blocks = jnp.einsum('tnb,nbc->tnc', blocked, gate_matrix.reshape(NB, BW, BW), precision=HIGHEST)
    return mixed_blocks.reshape(conv_values.shape[0], R) + bias_vector

def recurrence_terms(decay_rows, input_rows, decay_param, conv_values, resets):
    recur_gate = jax.nn.sigmoid(decay_rows)
    input_open = jax.nn.sigmoid(input_rows)
    decay_now = jnp.exp(-CD * recur_gate * jax.nn.softplus(-decay_param))
    multiplier = jnp.where(resets[:, None], 1.0, jnp.sqrt(jnp.maximum(1.0 - decay_now * decay_now, FLOOR_VALUE)))
    kept_decay = jnp.where(resets[:, None], 0.0, decay_now)
    return (kept_decay, multiplier * input_open * conv_values, decay_now)

def reference(tokens, mix_gain, scan_branch, gate_branch, kernel_taps, kernel_bias, decay_gate, decay_bias, input_gate, input_bias, decay_logit, mixer_out, feed_gain, gate_weight, up_weight, down_weight, lengths, cotangent):
    offsets = seq_offsets(lengths, 0, TOKENS)
    resets = offsets == 0

    def forward(tokens_f, mix_f, scan_f, gatebr_f, taps_f, tapsb_f, decayw_f, decayb_f, inputw_f, inputb_f, logit_f, outw_f, feed_f, gatew_f, upw_f, downw_f):
        first_normed = low(rms_scaled(tokens_f, mix_f))
        scan_rows = low_back(matmul_high(first_normed, scan_f))
        gate_rows = low_back(matmul_high(first_normed, gatebr_f))
        conv_values = low(causal_conv(scan_rows, taps_f, tapsb_f, offsets))
        decay_rows = low_back(gate_logits(conv_values, decayw_f, decayb_f))
        input_rows = low_back(gate_logits(conv_values, inputw_f, inputb_f))
        kept_decay, driven, decay_now = recurrence_terms(decay_rows, input_rows, logit_f, conv_values, resets)
        scanned = lax.associative_scan(combine, (kept_decay, driven), axis=0)
        mixed = low(smooth_gelu(gate_rows) * scanned[1])
        resid = tokens_f + low_back(matmul_high(mixed, outw_f))
        second_normed = low(rms_scaled(resid, feed_f))
        gate_pre = low_back(matmul_high(second_normed, gatew_f))
        up_pre = low_back(matmul_high(second_normed, upw_f))
        hidden_mid = low(smooth_gelu(gate_pre) * up_pre)
        return (resid + matmul_high(hidden_mid, downw_f), lax.optimization_barrier(jnp.mean(decay_now, axis=0)))
    block_out, pullback, mean_decay = jax.vjp(forward, tokens.astype(jnp.float32), mix_gain.astype(jnp.float32), scan_branch.astype(jnp.float32), gate_branch.astype(jnp.float32), kernel_taps.astype(jnp.float32), kernel_bias.astype(jnp.float32), decay_gate.astype(jnp.float32), decay_bias.astype(jnp.float32), input_gate.astype(jnp.float32), input_bias.astype(jnp.float32), decay_logit.astype(jnp.float32), mixer_out.astype(jnp.float32), feed_gain.astype(jnp.float32), gate_weight.astype(jnp.float32), up_weight.astype(jnp.float32), down_weight.astype(jnp.float32), has_aux=True)
    gradients = pullback(cotangent.astype(jnp.float32))
    return (block_out, gradients[0], gradients[1], gradients[2], gradients[3], gradients[4], gradients[5], gradients[6], gradients[7], gradients[8], gradients[9], gradients[10], gradients[11], gradients[12], gradients[13], gradients[14], gradients[15], mean_decay)
```

```python
import functools

import jax
import jax.numpy as jnp
from jax import lax
from jax.experimental import pallas as pl
from jax.experimental.pallas import tpu as pltpu
from jax.sharding import PartitionSpec as P


D = 2048
KW = 4
CD = 8
BW = 160


EPSILON = 1e-06
FLOOR_VALUE = 0.001


def from_behind(value, axis, steps):
    count = lax.axis_size(axis)
    initial, last = (max(0, -steps), min(count, count - steps))
    return lax.ppermute(value, axis, [(source, source + steps) for source in range(initial, last)])


def entering(part, axis, combine, identity, reverse):
    count = lax.axis_size(axis)
    place = lax.axis_index(axis)
    ahead = count - 1 - place if reverse else place
    gathered = jax.tree.map(lambda a: lax.all_gather(a, axis), part)
    state = jax.tree.map(lambda a, e: jnp.zeros_like(a) + jnp.asarray(e, a.dtype), part, identity)

    def one(turn, state):
        source = count - 1 - turn if reverse else turn
        return combine(
            state, jax.tree.map(lambda a: lax.dynamic_index_in_dim(a, source, 0, False), gathered)
        )

    return lax.fori_loop(0, ahead, one, state)


def matmul(left_side, right_side):
    return jnp.dot(left_side, right_side, preferred_element_type=jnp.float32)


def matmul_tn(left_side, right_side):
    return lax.dot_general(
        left_side, right_side, (((0,), (0,)), ((), ())), preferred_element_type=jnp.float32
    )


def matmul_nt(left_side, right_side):
    return lax.dot_general(
        left_side, right_side, (((1,), (1,)), ((), ())), preferred_element_type=jnp.float32
    )


def smooth_gelu(values):
    return jax.nn.gelu(values, approximate=True)


def combine(earlier, later):
    return (earlier[0] * later[0], later[1] + later[0] * earlier[1])


def seq_offsets(lengths, first_index, row_total):
    ends_all = jnp.cumsum(lengths, dtype=jnp.int32)
    starts_all = ends_all - lengths
    position = first_index + jnp.arange(row_total, dtype=jnp.int32)
    begins = jnp.max(
        jnp.where(starts_all[None, :] <= position[:, None], starts_all[None, :], 0), axis=1
    )
    return position - begins


def recurrence_terms(decay_rows, input_rows, decay_param, conv_values, resets):
    recur_gate = jax.nn.sigmoid(decay_rows)
    input_open = jax.nn.sigmoid(input_rows)
    decay_now = jnp.exp(-CD * recur_gate * jax.nn.softplus(-decay_param))
    multiplier = jnp.where(
        resets[:, None], 1.0, jnp.sqrt(jnp.maximum(1.0 - decay_now * decay_now, FLOOR_VALUE))
    )
    kept_decay = jnp.where(resets[:, None], 0.0, decay_now)
    return (kept_decay, multiplier * input_open * conv_values, decay_now)


def row_scale(values):
    squares_sum = lax.psum(jnp.sum(values * values, axis=1), "tp")
    return lax.rsqrt(squares_sum / D + EPSILON)


def spread_rows(values):
    return lax.all_gather(values, "tp", axis=1, tiled=True)


def spread_grads(values):
    return lax.all_gather(values, "tp", axis=1, tiled=True)


def reduce_features(values):
    return lax.psum_scatter(values, "tp", scatter_dimension=1, tiled=True)


def norm_back(values, row_scales, gain_vector, upstream):
    weighted = upstream * gain_vector
    inner_sum = lax.psum(jnp.sum(weighted * values, axis=1), "tp")
    cubed = row_scales * row_scales * row_scales * inner_sum / D
    back_rows = row_scales[:, None] * weighted - values * cubed[:, None]
    return (back_rows, jnp.sum(upstream * values * row_scales[:, None], axis=0))


def block_mix(blocked, matrices):
    mixed_blocks = jnp.einsum("tnb,nbc->tnc", blocked, matrices, preferred_element_type=jnp.float32)
    return mixed_blocks.reshape(blocked.shape[0], -1)


def block_outer(blocked, gradients):
    shaped = gradients.reshape(blocked.shape)
    outer_sum = jnp.einsum("tnb,tnc->nbc", blocked, shaped, preferred_element_type=jnp.float32)
    return outer_sum.reshape(blocked.shape[1], -1)


def block_back(gradients, matrices):
    shaped = gradients.reshape(gradients.shape[0], matrices.shape[0], matrices.shape[1])
    backed = jnp.einsum("tnc,nbc->tnb", shaped, matrices, preferred_element_type=jnp.float32)
    return backed.reshape(gradients.shape[0], -1)


def shards_general(
    tokens,
    mix_gain,
    scan_branch,
    gate_branch,
    kernel_taps,
    kernel_bias,
    decay_gate,
    decay_bias,
    input_gate,
    input_bias,
    decay_logit,
    mixer_out,
    feed_gain,
    gate_weight,
    up_weight,
    down_weight,
    lengths,
    cotangent,
):
    row_count = tokens.shape[0]
    seq_devices = lax.axis_size("seq")
    shard_index = lax.axis_index("seq")
    offsets = seq_offsets(lengths, shard_index * row_count, row_count)
    resets = offsets == 0
    gathered = (
        lax.all_gather(mix_gain, "seq", axis=0, tiled=True),
        lax.all_gather(scan_branch, "seq", axis=0, tiled=True),
        lax.all_gather(gate_branch, "seq", axis=0, tiled=True),
        lax.all_gather(kernel_taps, "seq", axis=1, tiled=True),
        lax.all_gather(kernel_bias, "seq", axis=0, tiled=True),
        lax.all_gather(decay_gate, "seq", axis=1, tiled=True),
        lax.all_gather(decay_bias, "seq", axis=0, tiled=True),
        lax.all_gather(input_gate, "seq", axis=1, tiled=True),
        lax.all_gather(input_bias, "seq", axis=0, tiled=True),
        lax.all_gather(decay_logit, "seq", axis=0, tiled=True),
        lax.all_gather(mixer_out, "seq", axis=1, tiled=True),
        lax.all_gather(feed_gain, "seq", axis=0, tiled=True),
        lax.all_gather(gate_weight, "seq", axis=0, tiled=True),
        lax.all_gather(up_weight, "seq", axis=0, tiled=True),
        lax.all_gather(down_weight, "seq", axis=1, tiled=True),
    )
    mix_f = gathered[0].astype(jnp.float32)
    taps_f = gathered[3].astype(jnp.float32)
    taps_bias = gathered[4].astype(jnp.float32)
    feed_f = gathered[11].astype(jnp.float32)
    tokens_f = tokens.astype(jnp.float32)
    scale_first = row_scale(tokens_f)
    normed_first = spread_rows((tokens_f * scale_first[:, None] * mix_f).astype(jnp.bfloat16))
    scan_rows = matmul(normed_first, gathered[1])
    gate_rows = matmul(normed_first, gathered[2])
    gelu_rows, gelu_pull = jax.vjp(smooth_gelu, gate_rows)
    rim_rows = from_behind(scan_rows[row_count - (KW - 1) :], "seq", 1)
    padded_rows = jnp.concatenate([rim_rows, scan_rows], axis=0)
    conv_sum = taps_bias + taps_f[0] * scan_rows
    for lag_step in range(1, KW):
        lagged = padded_rows[KW - 1 - lag_step : KW - 1 - lag_step + row_count]
        conv_sum = conv_sum + jnp.where(
            (offsets >= lag_step)[:, None], taps_f[lag_step] * lagged, 0.0
        )
    conv_rows = conv_sum.astype(jnp.bfloat16)
    lanes = scan_rows.shape[1]
    groups = lanes // BW
    conv_blocks = conv_rows.reshape(row_count, groups, BW)
    decay_mats = gathered[5].reshape(groups, BW, BW)
    input_mats = gathered[7].reshape(groups, BW, BW)
    decay_rows = block_mix(conv_blocks, decay_mats) + gathered[6].astype(jnp.float32)
    input_rows = block_mix(conv_blocks, input_mats) + gathered[8].astype(jnp.float32)

    def local_terms(decay_in, input_in, logit_in, conv_in):
        kept_part, driven_part, decay_part = recurrence_terms(
            decay_in, input_in, logit_in, conv_in, resets
        )
        return ((kept_part, driven_part), decay_part)

    terms_out, terms_pull, decay_now = jax.vjp(
        local_terms,
        decay_rows,
        input_rows,
        gathered[9].astype(jnp.float32),
        conv_rows.astype(jnp.float32),
        has_aux=True,
    )
    kept_decay, driven = terms_out
    local_prod, local_state = lax.associative_scan(combine, (kept_decay, driven), axis=0)
    before = entering(
        (local_prod[row_count - 1], local_state[row_count - 1]),
        "seq",
        combine,
        (jnp.ones((lanes,), jnp.float32), jnp.zeros((lanes,), jnp.float32)),
        False,
    )
    state_in = before[1]
    hidden_state = local_state + local_prod * state_in[None, :]
    mixed = (gelu_rows * hidden_state).astype(jnp.bfloat16)
    resid = tokens_f + reduce_features(matmul(mixed, gathered[10]))
    scale_second = row_scale(resid)
    normed_second = spread_rows((resid * scale_second[:, None] * feed_f).astype(jnp.bfloat16))
    gate_pre = matmul(normed_second, gathered[12])
    up_pre = matmul(normed_second, gathered[13])
    gelu_mid, mid_pull = jax.vjp(smooth_gelu, gate_pre)
    hidden_mid = (gelu_mid * up_pre).astype(jnp.bfloat16)
    block_out = resid + reduce_features(matmul(hidden_mid, gathered[14]))
    cot_full = spread_grads(cotangent)
    down_grad = matmul_tn(hidden_mid, cot_full)
    grad_mid = matmul_nt(cot_full, gathered[14])
    grad_gate = mid_pull(grad_mid * up_pre)[0].astype(jnp.bfloat16)
    grad_up = (grad_mid * gelu_mid).astype(jnp.bfloat16)
    gate_grad = matmul_tn(normed_second, grad_gate)
    up_grad = matmul_tn(normed_second, grad_up)
    grad_second = reduce_features(
        matmul_nt(grad_gate, gathered[12]) + matmul_nt(grad_up, gathered[13])
    )
    back_second, feed_grad = norm_back(resid, scale_second, feed_f, grad_second)
    grad_resid = cotangent.astype(jnp.float32) + back_second
    grad_branch = spread_grads(grad_resid.astype(jnp.bfloat16))
    out_grad = matmul_tn(mixed, grad_branch)
    grad_mixed = matmul_nt(grad_branch, gathered[10])
    grad_hidden = grad_mixed * gelu_rows
    grad_gate_rows = gelu_pull(grad_mixed * hidden_state)[0].astype(jnp.bfloat16)
    next_decay = jnp.concatenate([kept_decay[1:], jnp.ones_like(kept_decay[:1])], axis=0)
    tail_prod, local_adjoint = lax.associative_scan(
        combine, (next_decay, grad_hidden), reverse=True, axis=0
    )
    after = entering(
        (local_prod[row_count - 1], kept_decay[0] * local_adjoint[0]),
        "seq",
        combine,
        (jnp.ones((lanes,), jnp.float32), jnp.zeros((lanes,), jnp.float32)),
        True,
    )
    adjoint_in = after[1]
    adjoint = local_adjoint + tail_prod * adjoint_in[None, :]
    prev_state = jnp.concatenate([state_in[None, :], hidden_state[:-1]], axis=0)
    grad_decay_rows, grad_input_rows, logit_grad, conv_direct = terms_pull(
        (adjoint * prev_state, adjoint)
    )
    decay_grad_low = grad_decay_rows.astype(jnp.bfloat16)
    input_grad_low = grad_input_rows.astype(jnp.bfloat16)
    decay_w_grad = block_outer(conv_blocks, decay_grad_low)
    input_w_grad = block_outer(conv_blocks, input_grad_low)
    decay_b_grad = jnp.sum(decay_grad_low.astype(jnp.float32), axis=0)
    input_b_grad = jnp.sum(input_grad_low.astype(jnp.float32), axis=0)
    grad_conv = (
        conv_direct
        + block_back(decay_grad_low, decay_mats)
        + block_back(input_grad_low, input_mats)
    )
    rim_back = from_behind(grad_conv[: KW - 1], "seq", -1)
    grad_extended = jnp.concatenate([grad_conv, rim_back], axis=0)
    ext_offsets = seq_offsets(lengths, shard_index * row_count, row_count + KW - 1)
    grad_scan = taps_f[0] * grad_conv
    tap_grads = [jnp.sum(grad_conv * scan_rows, axis=0)]
    for lag_step in range(1, KW):
        ahead = grad_extended[lag_step : lag_step + row_count]
        ahead_ok = (ext_offsets[lag_step : lag_step + row_count] >= lag_step)[:, None]
        grad_scan = grad_scan + jnp.where(ahead_ok, taps_f[lag_step] * ahead, 0.0)
        lagged = padded_rows[KW - 1 - lag_step : KW - 1 - lag_step + row_count]
        tap_grads.append(
            jnp.sum(jnp.where((offsets >= lag_step)[:, None], grad_conv * lagged, 0.0), axis=0)
        )
    taps_grad = jnp.stack(tap_grads, axis=0)
    taps_bias_grad = jnp.sum(grad_conv, axis=0)
    scan_grad_low = grad_scan.astype(jnp.bfloat16)
    scan_w_grad = matmul_tn(normed_first, scan_grad_low)
    gatebr_grad = matmul_tn(normed_first, grad_gate_rows)
    grad_first = reduce_features(
        matmul_nt(scan_grad_low, gathered[1]) + matmul_nt(grad_gate_rows, gathered[2])
    )
    back_first, mix_grad = norm_back(tokens_f, scale_first, mix_f, grad_first)
    tokens_grad = grad_resid + back_first
    decay_total = jnp.sum(decay_now, axis=0)
    summed = (
        lax.psum_scatter(mix_grad, "seq", scatter_dimension=0, tiled=True),
        lax.psum_scatter(scan_w_grad, "seq", scatter_dimension=0, tiled=True),
        lax.psum_scatter(gatebr_grad, "seq", scatter_dimension=0, tiled=True),
        lax.psum_scatter(taps_grad, "seq", scatter_dimension=1, tiled=True),
        lax.psum_scatter(taps_bias_grad, "seq", scatter_dimension=0, tiled=True),
        lax.psum_scatter(decay_w_grad, "seq", scatter_dimension=1, tiled=True),
        lax.psum_scatter(decay_b_grad, "seq", scatter_dimension=0, tiled=True),
        lax.psum_scatter(input_w_grad, "seq", scatter_dimension=1, tiled=True),
        lax.psum_scatter(input_b_grad, "seq", scatter_dimension=0, tiled=True),
        lax.psum_scatter(logit_grad, "seq", scatter_dimension=0, tiled=True),
        lax.psum_scatter(out_grad, "seq", scatter_dimension=1, tiled=True),
        lax.psum_scatter(feed_grad, "seq", scatter_dimension=0, tiled=True),
        lax.psum_scatter(gate_grad, "seq", scatter_dimension=0, tiled=True),
        lax.psum_scatter(up_grad, "seq", scatter_dimension=0, tiled=True),
        lax.psum_scatter(down_grad, "seq", scatter_dimension=1, tiled=True),
        lax.psum_scatter(decay_total, "seq", scatter_dimension=0, tiled=True),
    )
    mean_decay = summed[15] / (row_count * seq_devices)
    return (
        block_out,
        tokens_grad,
        summed[0],
        summed[1],
        summed[2],
        summed[3],
        summed[4],
        summed[5],
        summed[6],
        summed[7],
        summed[8],
        summed[9],
        summed[10],
        summed[11],
        summed[12],
        summed[13],
        summed[14],
        mean_decay,
    )


MESH = pl.DeviceIdType.MESH
F32 = jnp.float32
BF16 = jnp.bfloat16
LINE = 4
PLANE = 8
CHUNK = 128
ANY = pl.BlockSpec(memory_space=pl.ANY)
VM = pl.BlockSpec(memory_space=pltpu.VMEM)


def flip(place, bit):
    step = 1 << bit
    return place + step - 2 * step * lax.rem(place // step, 2)


def flip_all(place, bits):
    for bit in range(3):
        if bits & (1 << bit):
            place = flip(place, bit)
    return place


def meet(s, z):
    barrier = pltpu.get_barrier_semaphore()
    for bits in range(1, PLANE):
        pl.semaphore_signal(barrier, inc=1, device_id=(flip_all(s, bits), z), device_id_type=MESH)
    for step in range(1, LINE):
        pl.semaphore_signal(
            barrier, inc=1, device_id=(s, lax.rem(z + step, LINE)), device_id_type=MESH
        )
    pl.semaphore_wait(barrier, PLANE - 1 + LINE - 1)


def remote(src, dst, send, recv, target):
    return pltpu.make_async_remote_copy(
        src_ref=src,
        dst_ref=dst,
        send_sem=send,
        recv_sem=recv,
        device_id=target,
        device_id_type=MESH,
    )


class LineGather:
    def __init__(self, s, z, own_at, full_at, send, recv):
        self.s, self.z = s, z
        self.own_at, self.full_at = own_at, full_at
        self.send, self.recv = send, recv

    def copy(self, way, level, c):
        sign = 1 - 2 * way
        origin = self.z - sign * level
        src = self.own_at(c) if level == 0 else self.full_at(origin, c)
        return remote(
            src,
            self.full_at(origin, c),
            self.send.at[way, level, c],
            self.recv.at[way, level, c],
            (self.s, self.z + sign),
        )

    def arrival(self, way, level, c):
        sign = 1 - 2 * way
        part = self.full_at(self.z - sign * (level + 1), c)
        return remote(
            part,
            part,
            self.send.at[way, level, c],
            self.recv.at[way, level, c],
            (self.s, self.z + sign),
        )

    def sends(self, way, level):
        if way == 0:
            return (self.z >= level) & (self.z < LINE - 1)
        return (self.z <= LINE - 1 - level) & (self.z > 0)

    def gets(self, way, level):
        return self.z >= level + 1 if way == 0 else self.z <= LINE - 2 - level

    def start(self, c):
        for way in range(2):
            pl.when(self.sends(way, 0))(lambda way=way: self.copy(way, 0, c).start())

    def forward(self, level, c):
        for way in range(2):
            pl.when(self.gets(way, level - 1))(
                lambda way=way: self.arrival(way, level - 1, c).wait_recv()
            )
            if level < LINE - 1:
                pl.when(self.sends(way, level))(
                    lambda way=way: self.copy(way, level, c).start()
                )

    def drain(self, c):
        for way in range(2):
            for level in range(LINE - 1):
                pl.when(self.sends(way, level))(
                    lambda way=way, level=level: self.copy(way, level, c).wait_send()
                )


class PlaneGather:
    def __init__(self, s, z, own, block_at, half_at, send, recv, local):
        self.s, self.z, self.own = s, z, own
        self.block_at, self.half_at = block_at, half_at
        self.send, self.recv, self.local = send, recv, local
        self.near = (flip(s, 1), flip(s, 2))
        self.diag = flip(self.near[0], 2)
        self.twin = flip(s, 0)
        self.twin_near = (flip(self.near[0], 0), flip(self.near[1], 0))
        self.twin_diag = flip(self.diag, 0)

    def plan(self, i):
        block, half = self.block_at, self.half_at
        return (
            (self.own, block(self.s), self.near[0]),
            (self.own, block(self.s), self.near[1]),
            (half(self.near[1], 0), half(self.near[1], 0), self.near[0]),
            (half(self.near[0], 1), half(self.near[0], 1), self.near[1]),
            (self.own, block(self.s), self.twin),
            (block(self.near[0]), block(self.near[0]), self.twin),
            (block(self.near[1]), block(self.near[1]), self.twin),
            (half(self.diag, 0), half(self.diag, 0), self.twin),
            (half(self.diag, 1), half(self.diag, 1), self.twin),
        )[i]

    def landing(self, i):
        block, half = self.block_at, self.half_at
        return (
            block(self.near[0]),
            block(self.near[1]),
            half(self.diag, 0),
            half(self.diag, 1),
            block(self.twin),
            block(self.twin_near[0]),
            block(self.twin_near[1]),
            half(self.twin_diag, 0),
            half(self.twin_diag, 1),
        )[i]

    def copy(self, i):
        src, dst, target = self.plan(i)
        return remote(src, dst, self.send.at[i], self.recv.at[i], (target, self.z))

    def got(self, i):
        part = self.landing(i)
        remote(part, part, self.send.at[i], self.recv.at[i], (self.twin, self.z)).wait_recv()

    def keep(self):
        return pltpu.make_async_copy(self.own, self.block_at(self.s), self.local)

    def start(self):
        for i in (0, 1, 4):
            self.copy(i).start()
        self.keep().start()

    def turn(self):
        self.got(0)
        self.copy(3).start()
        self.copy(5).start()
        self.got(1)
        self.copy(2).start()
        self.copy(6).start()

    def last(self):
        self.got(2)
        self.copy(7).start()
        self.got(3)
        self.copy(8).start()

    def finish(self):
        for i in range(4, 9):
            self.got(i)
        for i in range(9):
            self.copy(i).wait_send()
        self.keep().wait()


class Spread:
    def __init__(self, s, z, slot_at, send, recv):
        self.s, self.z, self.slot_at, self.send, self.recv = s, z, slot_at, send, recv

    def copy(self, bits, origin):
        slot = self.slot_at(origin)
        return remote(
            slot,
            slot,
            self.send.at[bits - 1],
            self.recv.at[bits - 1],
            (flip_all(self.s, bits), self.z),
        )

    def start(self):
        for bits in range(1, PLANE):
            self.copy(bits, self.s).start()

    def finish(self):
        for bits in range(1, PLANE):
            self.copy(bits, flip_all(self.s, bits)).wait_recv()
        for bits in range(1, PLANE):
            self.copy(bits, self.s).wait_send()


def rows_of(ref, size, parts=2):
    def block(place):
        return ref.at[pl.ds(pl.multiple_of(place * size, size), size)]

    def half(place, h):
        part = size // parts
        return ref.at[pl.ds(pl.multiple_of(place * size + h * part, part), part)]

    return block, half


def columns_of(ref, size):
    height = ref.shape[0] // 2

    def block(place):
        return ref.at[:, pl.ds(pl.multiple_of(place * size, size), size)]

    def half(place, h):
        return ref.at[
            pl.ds(h * height, height), pl.ds(pl.multiple_of(place * size, size), size)
        ]

    return block, half


def chunk_rows(c):
    return pl.ds(pl.multiple_of(c * CHUNK, CHUNK), CHUNK)


def feature_columns(z, width):
    return pl.ds(pl.multiple_of(z * width, width), width)


def each_chunk(chunks, body):
    lax.fori_loop(0, chunks, lambda c, carry: (body(c), carry)[1], 0)


def gather_kernel(
    tok, pack, gains, scan, gate, mix, ffn,
    tok_all, pack_all, gains_all, scan_all, gate_all, mix_all, ffn_all,
    line_send, line_recv, gain_send, gain_recv, plane_send, plane_recv, small_send, small_recv, local,
):
    s, z = lax.axis_index("seq"), lax.axis_index("tp")
    chunks, width = tok.shape[0] // CHUNK, tok.shape[1]
    line = LineGather(
        s, z,
        lambda c: tok.at[chunk_rows(c)],
        lambda o, c: tok_all.at[chunk_rows(c), feature_columns(o, width)],
        line_send, line_recv,
    )
    gain_line = LineGather(
        s, z, lambda c: gains_all.at[z], lambda o, c: gains_all.at[o], gain_send, gain_recv
    )
    planes = []
    for i, (own, full, make) in enumerate(
        (
            (scan, scan_all, rows_of),
            (gate, gate_all, rows_of),
            (mix, mix_all, columns_of),
            (ffn, ffn_all, rows_of),
        )
    ):
        size = own.shape[1] if make is columns_of else own.shape[0]
        block, half = make(full, size)
        planes.append(
            PlaneGather(s, z, own, block, half, plane_send.at[i], plane_recv.at[i], local.at[i])
        )
    packs = Spread(s, z, lambda p: pack_all.at[p], small_send.at[0], small_recv.at[0])
    gain_plane = Spread(s, z, lambda p: gains_all.at[z, p], small_send.at[1], small_recv.at[1])
    keeps = [
        pltpu.make_async_copy(gains, gains_all.at[z, s], local.at[4]),
        pltpu.make_async_copy(pack, pack_all.at[s], local.at[5]),
        pltpu.make_async_copy(tok, tok_all.at[:, feature_columns(z, width)], local.at[6]),
    ]
    for keep in keeps:
        keep.start()
    meet(s, z)
    for keep in keeps[:2]:
        keep.wait()
    gain_plane.start()
    packs.start()
    for c in range(chunks):
        line.start(c)
    for plane in planes:
        plane.start()
    gain_plane.finish()
    packs.finish()
    gain_line.start(0)
    for c in range(chunks):
        line.forward(1, c)
    gain_line.forward(1, 0)
    planes[0].turn()
    for c in range(chunks):
        line.forward(2, c)
    gain_line.forward(2, 0)
    planes[1].turn()
    planes[0].last()
    planes[2].turn()
    planes[1].last()
    planes[3].turn()
    planes[2].last()
    for c in range(chunks):
        line.forward(3, c)
    gain_line.forward(3, 0)
    planes[3].last()
    for plane in planes:
        plane.finish()
    for c in range(chunks):
        line.drain(c)
    gain_line.drain(0)
    keeps[2].wait()


def dma(*shape):
    return pltpu.SemaphoreType.DMA(shape)


def struct(shape, kind):
    return jax.ShapeDtypeStruct(shape, kind)


def gather_first(tok, pack, gains, scan, gate, mix, ffn):
    rows, width = tok.shape
    chunks = rows // CHUNK
    return pl.pallas_call(
        gather_kernel,
        out_shape=(
            struct((rows, width * LINE), BF16),
            struct((PLANE,) + pack.shape, pack.dtype),
            struct((LINE, PLANE) + gains.shape, F32),
            struct((scan.shape[0] * PLANE, scan.shape[1]), BF16),
            struct((gate.shape[0] * PLANE, gate.shape[1]), BF16),
            struct((mix.shape[0], mix.shape[1] * PLANE), BF16),
            struct((ffn.shape[0] * PLANE, ffn.shape[1]), BF16),
        ),
        in_specs=[ANY] * 7,
        out_specs=[ANY] * 7,
        scratch_shapes=[
            dma(2, LINE - 1, chunks), dma(2, LINE - 1, chunks),
            dma(2, LINE - 1, 1), dma(2, LINE - 1, 1),
            dma(4, 9), dma(4, 9), dma(2, 7), dma(2, 7), dma(7),
        ],
        compiler_params=pltpu.CompilerParams(collective_id=0, has_side_effects=True),
        name="gather_first",
    )(tok, pack, gains, scan, gate, mix, ffn)


def sigmoid(values):
    return 0.5 * jnp.tanh(0.5 * values) + 0.5


ROOT = 0.7978845608028654


def gelu_of(values):
    return 0.5 * values * (1.0 + jnp.tanh(ROOT * (values + 0.044715 * values * values * values)))


def gelu_pair(values):
    squared = values * values
    bent = jnp.tanh(ROOT * values * (1.0 + 0.044715 * squared))
    half = 0.5 * (1.0 + bent)
    slope = half + 0.5 * values * (1.0 - bent * bent) * (ROOT * (1.0 + 3 * 0.044715 * squared))
    return values * half, slope


def dot(left_side, right_side):
    return jnp.dot(left_side, right_side, preferred_element_type=F32)


def dot_nt(left_side, right_side):
    return lax.dot_general(
        left_side, right_side, (((1,), (1,)), ((), ())), preferred_element_type=F32
    )


def dot_tn(left_side, right_side):
    return lax.dot_general(
        left_side, right_side, (((0,), (0,)), ((), ())), preferred_element_type=F32
    )


SUBS = 8


LANE = 128


def put(ref, at, values):
    for lane in range(ref.shape[0]):
        ref[lane, at, :] = values[:, lane * LANE : (lane + 1) * LANE]


def get(ref, at):
    return jnp.concatenate([ref[lane, at, :] for lane in range(ref.shape[0])], axis=1)


def strided(ref, step):
    at = pl.ds(step, SUBS, stride=ref.shape[1] // SUBS)
    return [ref[lane, at, :] for lane in range(ref.shape[0])]


def strided_put(ref, step, values):
    at = pl.ds(step, SUBS, stride=ref.shape[1] // SUBS)
    for lane in range(ref.shape[0]):
        ref[lane, at, :] = values[lane]


def lanes_of(values):
    return [values[:, i * LANE : (i + 1) * LANE] for i in range(values.shape[1] // LANE)]


def recur_kernel(
    tok_all, scan_w, gate_w, gates_w, par, gain, masks, cot, up, down,
    normed, scan_rows, gate_rows, conv, decay_rows, input_rows, hidden, mixed, state, decay_sum,
    cot_all, up_all, down_all,
    kept, driven, slots,
    line_send, line_recv, plane_send, plane_recv, small_send, small_recv, halo_send, halo_recv, local,
):
    s, z = lax.axis_index("seq"), lax.axis_index("tp")
    rows, features = tok_all.shape
    chunks, width, lanes = rows // CHUNK, cot.shape[1], gate_w.shape[1]
    line = LineGather(
        s, z,
        lambda c: cot.at[chunk_rows(c)],
        lambda o, c: cot_all.at[chunk_rows(c), feature_columns(o, width)],
        line_send, line_recv,
    )
    planes = [
        PlaneGather(
            s, z, up, *rows_of(up_all, up.shape[0]), plane_send.at[0], plane_recv.at[0], local.at[0]
        ),
        PlaneGather(
            s, z, down, *columns_of(down_all, down.shape[1]), plane_send.at[1], plane_recv.at[1],
            local.at[1],
        ),
    ]
    keep = pltpu.make_async_copy(cot, cot_all.at[:, feature_columns(z, width)], local.at[2])
    keep.start()
    meet(s, z)
    for c in range(chunks):
        line.start(c)
    for plane in planes:
        plane.start()

    def project(c):
        at = chunk_rows(c)
        x = tok_all[at, :].astype(F32)
        scale = lax.rsqrt(jnp.sum(x * x, axis=1, keepdims=True) / features + EPSILON)
        low = (x * scale * gain[0:1, :]).astype(BF16)
        normed[at, :] = low
        scan_rows[pl.ds(pl.multiple_of(c * CHUNK + 8, 8), CHUNK), :] = dot(low, scan_w[...])
        gate_rows[at, :] = dot(low, gate_w[...])

    each_chunk(chunks, project)
    halo = remote(
        scan_rows.at[pl.ds(rows, 8)], scan_rows.at[pl.ds(0, 8)], halo_send, halo_recv,
        (lax.rem(s + 1, PLANE), z),
    )
    first, final = s == 0, s == PLANE - 1
    pl.when(jnp.logical_not(final))(lambda: halo.start())

    @pl.when(first)
    def _():
        scan_rows[0:8, :] = jnp.zeros((8, lanes), F32)

    decay_sum[...] = jnp.zeros_like(decay_sum)
    pl.when(jnp.logical_not(first))(lambda: halo.wait_recv())

    def gates(c):
        at = chunk_rows(c)
        block = scan_rows[pl.ds(pl.multiple_of(c * CHUNK, 8), CHUNK + 8), :]
        mask = masks[at, :]
        total = par[4:5, :] + par[0:1, :] * block[8:, :]
        for lag in range(1, KW):
            total = total + mask[:, lag : lag + 1] * (
                par[lag : lag + 1, :] * block[8 - lag : 8 - lag + CHUNK, :]
            )
        low = total.astype(BF16)
        conv[at, :] = low
        rows_now = dot(low, gates_w[...])
        decays = rows_now[:, :lanes] + par[5:6, :]
        inputs = rows_now[:, lanes:] + par[6:7, :]
        decay_rows[at, :] = decays
        input_rows[at, :] = inputs
        decay = jnp.exp(-sigmoid(decays) * par[7:8, :])
        goes_on = mask[:, 0:1]
        multiplier = 1.0 + goes_on * (
            jnp.sqrt(jnp.maximum(1.0 - decay * decay, FLOOR_VALUE)) - 1.0
        )
        put(kept, at, goes_on * decay)
        put(driven, at, multiplier * sigmoid(inputs) * low.astype(F32))
        decay_sum[0:1, :] += jnp.sum(decay, axis=0, keepdims=True)
        line.forward(1, c)

    each_chunk(chunks, gates)
    count = rows // SUBS

    def total_of(step, carry):
        keeps, drives = strided(kept, step), strided(driven, step)
        return (
            [p * k for p, k in zip(carry[0], keeps)],
            [k * v + d for k, v, d in zip(keeps, carry[1], drives)],
        )

    groups = lanes // LANE
    product, value = lax.fori_loop(
        0,
        count,
        total_of,
        ([jnp.ones((SUBS, LANE), F32)] * groups, [jnp.zeros((SUBS, LANE), F32)] * groups),
        unroll=4,
    )
    product, value = jnp.concatenate(product, axis=1), jnp.concatenate(value, axis=1)
    whole = (jnp.ones((1, lanes), F32), jnp.zeros((1, lanes), F32))
    for sub in range(SUBS):
        here = product[sub : sub + 1, :]
        whole = (whole[0] * here, here * whole[1] + value[sub : sub + 1, :])
    slots[s, 0:1, :] = whole[0]
    slots[s, 1:2, :] = whole[1]
    spread = Spread(s, z, lambda p: slots.at[p], small_send, small_recv)
    spread.start()
    planes[0].turn()
    spread.finish()
    entry = jnp.zeros((1, lanes), F32)
    for place in range(PLANE - 1):
        entry = jnp.where(
            place < s, slots[place, 0:1, :] * entry + slots[place, 1:2, :], entry
        )
    state[...] = jnp.broadcast_to(entry, (8, lanes))
    entries = []
    for sub in range(SUBS):
        entries.append(entry)
        entry = product[sub : sub + 1, :] * entry + value[sub : sub + 1, :]

    def step_on(step, now):
        keeps, drives = strided(kept, step), strided(driven, step)
        now = [k * v + d for k, v, d in zip(keeps, now, drives)]
        strided_put(driven, step, now)
        return now

    lax.fori_loop(0, count, step_on, lanes_of(jnp.concatenate(entries, axis=0)), unroll=4)

    def mix(c):
        at = chunk_rows(c)
        now = get(driven, at)
        hidden[at, :] = now
        mixed[at, :] = (gelu_of(gate_rows[at, :]) * now).astype(BF16)
        line.forward(2, c)

    each_chunk(chunks, mix)
    planes[1].turn()
    planes[0].last()
    for c in range(chunks):
        line.forward(3, c)
    planes[1].last()
    for plane in planes:
        plane.finish()
    for c in range(chunks):
        line.drain(c)
    pl.when(jnp.logical_not(final))(lambda: halo.wait_send())
    keep.wait()


def recur_forward(tok_all, scan_w, gate_w, gates_w, par, gain, masks, cot, up, down):
    rows, features = tok_all.shape
    lanes = gate_w.shape[1]
    chunks = rows // CHUNK
    return pl.pallas_call(
        recur_kernel,
        out_shape=(
            struct((rows, features), BF16),
            struct((rows + 8, lanes), F32),
            struct((rows, lanes), F32),
            struct((rows, lanes), BF16),
            struct((rows, lanes), F32),
            struct((rows, lanes), F32),
            struct((rows, lanes), F32),
            struct((rows, lanes), BF16),
            struct((8, lanes), F32),
            struct((8, lanes), F32),
            struct((rows, features), BF16),
            struct((up.shape[0] * PLANE, up.shape[1]), BF16),
            struct((down.shape[0], down.shape[1] * PLANE), BF16),
        ),
        in_specs=[VM] * 7 + [ANY] * 3,
        out_specs=[VM] * 10 + [ANY] * 3,
        scratch_shapes=[
            pltpu.VMEM((lanes // LANE, rows, LANE), F32),
            pltpu.VMEM((lanes // LANE, rows, LANE), F32),
            pltpu.VMEM((PLANE, 8, lanes), F32),
            dma(2, LINE - 1, chunks), dma(2, LINE - 1, chunks),
            dma(2, 9), dma(2, 9), dma(7), dma(7),
            pltpu.SemaphoreType.DMA, pltpu.SemaphoreType.DMA, dma(3),
        ],
        compiler_params=pltpu.CompilerParams(
            collective_id=1, has_side_effects=True, vmem_limit_bytes=58 << 20
        ),
        name="recur_forward",
    )(tok_all, scan_w, gate_w, gates_w, par, gain, masks, cot, up, down)


def shards_fast(
    tokens, mix_gain, scan_branch, gate_branch, kernel_taps, kernel_bias, decay_gate, decay_bias,
    input_gate, input_bias, decay_logit, mixer_out, feed_gain, gate_weight, up_weight, down_weight,
    lengths, cotangent,
):
    row_count = tokens.shape[0]
    seq_devices = lax.axis_size("seq")
    shard_index = lax.axis_index("seq")
    ext_offsets = seq_offsets(lengths, shard_index * row_count, row_count + 8)
    lag_at = jnp.array([1, 1, 2, 3, 0, 0, 0, 0], jnp.int32)
    masks = (ext_offsets[:, None] >= lag_at[None, :]).astype(F32)
    lanes = scan_branch.shape[1]
    part = lanes // seq_devices
    groups = lanes // BW
    flat = jnp.concatenate(
        [
            kernel_taps.reshape(-1), kernel_bias, decay_bias, input_bias, decay_logit,
            decay_gate.reshape(-1), input_gate.reshape(-1),
        ]
    )
    pack_rows = -(-flat.shape[0] // (128 * 16)) * 16
    pack = jnp.pad(flat, (0, pack_rows * 128 - flat.shape[0])).reshape(pack_rows, 128)
    gains = jnp.pad(
        jnp.concatenate([mix_gain, feed_gain]).astype(F32)[None, :], ((0, 7), (0, 0))
    )
    tok_all, pack_all, gains_all, scan_w, gate_w, mix_w, ffn_gate = gather_first(
        tokens, pack, gains, scan_branch, gate_branch, mixer_out, gate_weight
    )
    pack_all = pack_all.reshape(seq_devices, -1)
    at = 0

    def take(rows):
        nonlocal at
        piece = pack_all[:, at : at + rows * part].reshape(seq_devices, rows, part)
        at += rows * part
        return piece.transpose(1, 0, 2).reshape(rows, lanes).astype(F32)

    taps_f = take(KW)
    biases = take(3)
    logit_f = take(1)
    gate_cut = groups * BW * BW // seq_devices
    mats = [
        pack_all[:, at + i * gate_cut : at + (i + 1) * gate_cut]
        .reshape(seq_devices, groups, BW // seq_devices, BW)
        .transpose(1, 0, 2, 3)
        .reshape(groups, BW, BW)
        for i in range(2)
    ]
    gates_w = jnp.concatenate(
        [
            jnp.concatenate(
                [jnp.pad(m[g], ((0, 0), (g * BW, lanes - (g + 1) * BW))) for g in range(groups)], 0
            )
            for m in mats
        ],
        1,
    )
    par = jnp.concatenate(
        [taps_f, biases, CD * jax.nn.softplus(-logit_f), jnp.zeros((8, lanes), F32)], 0
    )
    half = gains.shape[1] // 2
    gain_full = gains_all[:, :, 0, :].reshape(-1, 2, half).transpose(1, 0, 2).reshape(2, -1)
    gain_full = jnp.pad(gain_full, ((0, 6), (0, 0)))
    (
        normed_first, scan_pad, gate_rows, conv_rows, decay_rows, input_rows, hidden_state, mixed,
        state_rows, decay_sums, cot_full, up_w, down_w,
    ) = recur_forward(
        tok_all, scan_w, gate_w, gates_w, par, gain_full, masks, cotangent, up_weight, down_weight
    )

    offsets = ext_offsets[:row_count]
    resets = offsets == 0
    mix_f = lax.all_gather(mix_gain, "seq", axis=0, tiled=True).astype(F32)
    feed_f = lax.all_gather(feed_gain, "seq", axis=0, tiled=True).astype(F32)
    gathered=[None, scan_w, gate_w, None,None,None,biases[1],None,biases[2],logit_f[0],mix_w,None,ffn_gate,up_w,down_w]
    taps_bias=biases[0]
    normed_first_k=normed_first
    tokens_f = tokens.astype(jnp.float32)
    scale_first = row_scale(tokens_f)
    scan_rows = scan_pad[8:]
    gelu_rows, gelu_pull = jax.vjp(smooth_gelu, gate_rows)
    rim_rows = from_behind(scan_rows[row_count - (KW - 1) :], "seq", 1)
    padded_rows = jnp.concatenate([rim_rows, scan_rows], axis=0)
    conv_sum = taps_bias + taps_f[0] * scan_rows
    for lag_step in range(1, KW):
        lagged = padded_rows[KW - 1 - lag_step : KW - 1 - lag_step + row_count]
        conv_sum = conv_sum + jnp.where(
            (offsets >= lag_step)[:, None], taps_f[lag_step] * lagged, 0.0
        )
    lanes = scan_rows.shape[1]
    groups = lanes // BW
    conv_blocks = conv_rows.reshape(row_count, groups, BW)
    decay_mats = mats[0]
    input_mats = mats[1]
    decay_rows = block_mix(conv_blocks, decay_mats) + gathered[6].astype(jnp.float32)
    input_rows = block_mix(conv_blocks, input_mats) + gathered[8].astype(jnp.float32)

    def local_terms(decay_in, input_in, logit_in, conv_in):
        kept_part, driven_part, decay_part = recurrence_terms(
            decay_in, input_in, logit_in, conv_in, resets
        )
        return ((kept_part, driven_part), decay_part)

    terms_out, terms_pull, decay_now = jax.vjp(
        local_terms,
        decay_rows,
        input_rows,
        gathered[9].astype(jnp.float32),
        conv_rows.astype(jnp.float32),
        has_aux=True,
    )
    kept_decay, driven = terms_out
    local_prod, local_state = lax.associative_scan(combine, (kept_decay, driven), axis=0)
    before = entering(
        (local_prod[row_count - 1], local_state[row_count - 1]),
        "seq",
        combine,
        (jnp.ones((lanes,), jnp.float32), jnp.zeros((lanes,), jnp.float32)),
        False,
    )
    state_in = before[1]
    state_in=state_rows[0]
    resid = tokens_f + reduce_features(matmul(mixed, gathered[10]))
    scale_second = row_scale(resid)
    normed_second = spread_rows((resid * scale_second[:, None] * feed_f).astype(jnp.bfloat16))
    gate_pre = matmul(normed_second, gathered[12])
    up_pre = matmul(normed_second, gathered[13])
    gelu_mid, mid_pull = jax.vjp(smooth_gelu, gate_pre)
    hidden_mid = (gelu_mid * up_pre).astype(jnp.bfloat16)
    block_out = resid + reduce_features(matmul(hidden_mid, gathered[14]))
    down_grad = matmul_tn(hidden_mid, cot_full)
    grad_mid = matmul_nt(cot_full, gathered[14])
    grad_gate = mid_pull(grad_mid * up_pre)[0].astype(jnp.bfloat16)
    grad_up = (grad_mid * gelu_mid).astype(jnp.bfloat16)
    gate_grad = matmul_tn(normed_second, grad_gate)
    up_grad = matmul_tn(normed_second, grad_up)
    grad_second = reduce_features(
        matmul_nt(grad_gate, gathered[12]) + matmul_nt(grad_up, gathered[13])
    )
    back_second, feed_grad = norm_back(resid, scale_second, feed_f, grad_second)
    grad_resid = cotangent.astype(jnp.float32) + back_second
    grad_branch = spread_grads(grad_resid.astype(jnp.bfloat16))
    out_grad = matmul_tn(mixed, grad_branch)
    grad_mixed = matmul_nt(grad_branch, gathered[10])
    grad_hidden = grad_mixed * gelu_rows
    grad_gate_rows = gelu_pull(grad_mixed * hidden_state)[0].astype(jnp.bfloat16)
    next_decay = jnp.concatenate([kept_decay[1:], jnp.ones_like(kept_decay[:1])], axis=0)
    tail_prod, local_adjoint = lax.associative_scan(
        combine, (next_decay, grad_hidden), reverse=True, axis=0
    )
    after = entering(
        (local_prod[row_count - 1], kept_decay[0] * local_adjoint[0]),
        "seq",
        combine,
        (jnp.ones((lanes,), jnp.float32), jnp.zeros((lanes,), jnp.float32)),
        True,
    )
    adjoint_in = after[1]
    adjoint = local_adjoint + tail_prod * adjoint_in[None, :]
    prev_state = jnp.concatenate([state_in[None, :], hidden_state[:-1]], axis=0)
    grad_decay_rows, grad_input_rows, logit_grad, conv_direct = terms_pull(
        (adjoint * prev_state, adjoint)
    )
    decay_grad_low = grad_decay_rows.astype(jnp.bfloat16)
    input_grad_low = grad_input_rows.astype(jnp.bfloat16)
    decay_w_grad = block_outer(conv_blocks, decay_grad_low)
    input_w_grad = block_outer(conv_blocks, input_grad_low)
    decay_b_grad = jnp.sum(decay_grad_low.astype(jnp.float32), axis=0)
    input_b_grad = jnp.sum(input_grad_low.astype(jnp.float32), axis=0)
    grad_conv = (
        conv_direct
        + block_back(decay_grad_low, decay_mats)
        + block_back(input_grad_low, input_mats)
    )
    rim_back = from_behind(grad_conv[: KW - 1], "seq", -1)
    grad_extended = jnp.concatenate([grad_conv, rim_back], axis=0)
    ext_offsets = seq_offsets(lengths, shard_index * row_count, row_count + KW - 1)
    grad_scan = taps_f[0] * grad_conv
    tap_grads = [jnp.sum(grad_conv * scan_rows, axis=0)]
    for lag_step in range(1, KW):
        ahead = grad_extended[lag_step : lag_step + row_count]
        ahead_ok = (ext_offsets[lag_step : lag_step + row_count] >= lag_step)[:, None]
        grad_scan = grad_scan + jnp.where(ahead_ok, taps_f[lag_step] * ahead, 0.0)
        lagged = padded_rows[KW - 1 - lag_step : KW - 1 - lag_step + row_count]
        tap_grads.append(
            jnp.sum(jnp.where((offsets >= lag_step)[:, None], grad_conv * lagged, 0.0), axis=0)
        )
    taps_grad = jnp.stack(tap_grads, axis=0)
    taps_bias_grad = jnp.sum(grad_conv, axis=0)
    scan_grad_low = grad_scan.astype(jnp.bfloat16)
    scan_w_grad = matmul_tn(normed_first, scan_grad_low)
    gatebr_grad = matmul_tn(normed_first, grad_gate_rows)
    grad_first = reduce_features(
        matmul_nt(scan_grad_low, gathered[1]) + matmul_nt(grad_gate_rows, gathered[2])
    )
    back_first, mix_grad = norm_back(tokens_f, scale_first, mix_f, grad_first)
    tokens_grad = grad_resid + back_first
    decay_total = decay_sums[0]
    summed = (
        lax.psum_scatter(mix_grad, "seq", scatter_dimension=0, tiled=True),
        lax.psum_scatter(scan_w_grad, "seq", scatter_dimension=0, tiled=True),
        lax.psum_scatter(gatebr_grad, "seq", scatter_dimension=0, tiled=True),
        lax.psum_scatter(taps_grad, "seq", scatter_dimension=1, tiled=True),
        lax.psum_scatter(taps_bias_grad, "seq", scatter_dimension=0, tiled=True),
        lax.psum_scatter(decay_w_grad, "seq", scatter_dimension=1, tiled=True),
        lax.psum_scatter(decay_b_grad, "seq", scatter_dimension=0, tiled=True),
        lax.psum_scatter(input_w_grad, "seq", scatter_dimension=1, tiled=True),
        lax.psum_scatter(input_b_grad, "seq", scatter_dimension=0, tiled=True),
        lax.psum_scatter(logit_grad, "seq", scatter_dimension=0, tiled=True),
        lax.psum_scatter(out_grad, "seq", scatter_dimension=1, tiled=True),
        lax.psum_scatter(feed_grad, "seq", scatter_dimension=0, tiled=True),
        lax.psum_scatter(gate_grad, "seq", scatter_dimension=0, tiled=True),
        lax.psum_scatter(up_grad, "seq", scatter_dimension=0, tiled=True),
        lax.psum_scatter(down_grad, "seq", scatter_dimension=1, tiled=True),
        lax.psum_scatter(decay_total, "seq", scatter_dimension=0, tiled=True),
    )
    mean_decay = summed[15] / (row_count * seq_devices)
    return (
        block_out,
        tokens_grad,
        summed[0],
        summed[1],
        summed[2],
        summed[3],
        summed[4],
        summed[5],
        summed[6],
        summed[7],
        summed[8],
        summed[9],
        summed[10],
        summed[11],
        summed[12],
        summed[13],
        summed[14],
        mean_decay,
    )


def solution(mesh):
    placed = (
        P("seq", "tp"),
        P(("tp", "seq")),
        P("seq", "tp"),
        P("seq", "tp"),
        P(None, ("tp", "seq")),
        P(("tp", "seq")),
        P("tp", "seq"),
        P(("tp", "seq")),
        P("tp", "seq"),
        P(("tp", "seq")),
        P(("tp", "seq")),
        P("tp", "seq"),
        P(("tp", "seq")),
        P("seq", "tp"),
        P("seq", "tp"),
        P("tp", "seq"),
        P(),
        P("seq", "tp"),
    )
    return jax.shard_map(
        shards_fast if mesh.shape['seq']==8 else shards_general,
        mesh=mesh,
        in_specs=placed,
        out_specs=(
            P("seq", "tp"),
            P("seq", "tp"),
            P(("tp", "seq")),
            P("seq", "tp"),
            P("seq", "tp"),
            P(None, ("tp", "seq")),
            P(("tp", "seq")),
            P("tp", "seq"),
            P(("tp", "seq")),
            P("tp", "seq"),
            P(("tp", "seq")),
            P(("tp", "seq")),
            P("tp", "seq"),
            P(("tp", "seq")),
            P("seq", "tp"),
            P("seq", "tp"),
            P("tp", "seq"),
            P(("tp", "seq")),
        ),
        check_vma=False,
    )
```

```python
import functools

import jax
import jax.numpy as jnp
from jax import lax
from jax.experimental import pallas as pl
from jax.experimental.pallas import tpu as pltpu
from jax.sharding import PartitionSpec as P


D = 2048
KW = 4
CD = 8
BW = 160


EPSILON = 1e-06
FLOOR_VALUE = 0.001


def from_behind(value, axis, steps):
    count = lax.axis_size(axis)
    initial, last = (max(0, -steps), min(count, count - steps))
    return lax.ppermute(value, axis, [(source, source + steps) for source in range(initial, last)])


def entering(part, axis, combine, identity, reverse):
    count = lax.axis_size(axis)
    place = lax.axis_index(axis)
    ahead = count - 1 - place if reverse else place
    gathered = jax.tree.map(lambda a: lax.all_gather(a, axis), part)
    state = jax.tree.map(lambda a, e: jnp.zeros_like(a) + jnp.asarray(e, a.dtype), part, identity)

    def one(turn, state):
        source = count - 1 - turn if reverse else turn
        return combine(
            state, jax.tree.map(lambda a: lax.dynamic_index_in_dim(a, source, 0, False), gathered)
        )

    return lax.fori_loop(0, ahead, one, state)


def matmul(left_side, right_side):
    return jnp.dot(left_side, right_side, preferred_element_type=jnp.float32)


def matmul_tn(left_side, right_side):
    return lax.dot_general(
        left_side, right_side, (((0,), (0,)), ((), ())), preferred_element_type=jnp.float32
    )


def matmul_nt(left_side, right_side):
    return lax.dot_general(
        left_side, right_side, (((1,), (1,)), ((), ())), preferred_element_type=jnp.float32
    )


def smooth_gelu(values):
    return jax.nn.gelu(values, approximate=True)


def combine(earlier, later):
    return (earlier[0] * later[0], later[1] + later[0] * earlier[1])


def seq_offsets(lengths, first_index, row_total):
    ends_all = jnp.cumsum(lengths, dtype=jnp.int32)
    starts_all = ends_all - lengths
    position = first_index + jnp.arange(row_total, dtype=jnp.int32)
    begins = jnp.max(
        jnp.where(starts_all[None, :] <= position[:, None], starts_all[None, :], 0), axis=1
    )
    return position - begins


def recurrence_terms(decay_rows, input_rows, decay_param, conv_values, resets):
    recur_gate = jax.nn.sigmoid(decay_rows)
    input_open = jax.nn.sigmoid(input_rows)
    decay_now = jnp.exp(-CD * recur_gate * jax.nn.softplus(-decay_param))
    multiplier = jnp.where(
        resets[:, None], 1.0, jnp.sqrt(jnp.maximum(1.0 - decay_now * decay_now, FLOOR_VALUE))
    )
    kept_decay = jnp.where(resets[:, None], 0.0, decay_now)
    return (kept_decay, multiplier * input_open * conv_values, decay_now)


def row_scale(values):
    squares_sum = lax.psum(jnp.sum(values * values, axis=1), "tp")
    return lax.rsqrt(squares_sum / D + EPSILON)


def spread_rows(values):
    return lax.all_gather(values, "tp", axis=1, tiled=True)


def spread_grads(values):
    return lax.all_gather(values, "tp", axis=1, tiled=True)


def reduce_features(values):
    return lax.psum_scatter(values, "tp", scatter_dimension=1, tiled=True)


def norm_back(values, row_scales, gain_vector, upstream):
    weighted = upstream * gain_vector
    inner_sum = lax.psum(jnp.sum(weighted * values, axis=1), "tp")
    cubed = row_scales * row_scales * row_scales * inner_sum / D
    back_rows = row_scales[:, None] * weighted - values * cubed[:, None]
    return (back_rows, jnp.sum(upstream * values * row_scales[:, None], axis=0))


def block_mix(blocked, matrices):
    mixed_blocks = jnp.einsum("tnb,nbc->tnc", blocked, matrices, preferred_element_type=jnp.float32)
    return mixed_blocks.reshape(blocked.shape[0], -1)


def block_outer(blocked, gradients):
    shaped = gradients.reshape(blocked.shape)
    outer_sum = jnp.einsum("tnb,tnc->nbc", blocked, shaped, preferred_element_type=jnp.float32)
    return outer_sum.reshape(blocked.shape[1], -1)


def block_back(gradients, matrices):
    shaped = gradients.reshape(gradients.shape[0], matrices.shape[0], matrices.shape[1])
    backed = jnp.einsum("tnc,nbc->tnb", shaped, matrices, preferred_element_type=jnp.float32)
    return backed.reshape(gradients.shape[0], -1)


def shards_general(
    tokens,
    mix_gain,
    scan_branch,
    gate_branch,
    kernel_taps,
    kernel_bias,
    decay_gate,
    decay_bias,
    input_gate,
    input_bias,
    decay_logit,
    mixer_out,
    feed_gain,
    gate_weight,
    up_weight,
    down_weight,
    lengths,
    cotangent,
):
    row_count = tokens.shape[0]
    seq_devices = lax.axis_size("seq")
    shard_index = lax.axis_index("seq")
    offsets = seq_offsets(lengths, shard_index * row_count, row_count)
    resets = offsets == 0
    gathered = (
        lax.all_gather(mix_gain, "seq", axis=0, tiled=True),
        lax.all_gather(scan_branch, "seq", axis=0, tiled=True),
        lax.all_gather(gate_branch, "seq", axis=0, tiled=True),
        lax.all_gather(kernel_taps, "seq", axis=1, tiled=True),
        lax.all_gather(kernel_bias, "seq", axis=0, tiled=True),
        lax.all_gather(decay_gate, "seq", axis=1, tiled=True),
        lax.all_gather(decay_bias, "seq", axis=0, tiled=True),
        lax.all_gather(input_gate, "seq", axis=1, tiled=True),
        lax.all_gather(input_bias, "seq", axis=0, tiled=True),
        lax.all_gather(decay_logit, "seq", axis=0, tiled=True),
        lax.all_gather(mixer_out, "seq", axis=1, tiled=True),
        lax.all_gather(feed_gain, "seq", axis=0, tiled=True),
        lax.all_gather(gate_weight, "seq", axis=0, tiled=True),
        lax.all_gather(up_weight, "seq", axis=0, tiled=True),
        lax.all_gather(down_weight, "seq", axis=1, tiled=True),
    )
    mix_f = gathered[0].astype(jnp.float32)
    taps_f = gathered[3].astype(jnp.float32)
    taps_bias = gathered[4].astype(jnp.float32)
    feed_f = gathered[11].astype(jnp.float32)
    tokens_f = tokens.astype(jnp.float32)
    scale_first = row_scale(tokens_f)
    normed_first = spread_rows((tokens_f * scale_first[:, None] * mix_f).astype(jnp.bfloat16))
    scan_rows = matmul(normed_first, gathered[1])
    gate_rows = matmul(normed_first, gathered[2])
    gelu_rows, gelu_pull = jax.vjp(smooth_gelu, gate_rows)
    rim_rows = from_behind(scan_rows[row_count - (KW - 1) :], "seq", 1)
    padded_rows = jnp.concatenate([rim_rows, scan_rows], axis=0)
    conv_sum = taps_bias + taps_f[0] * scan_rows
    for lag_step in range(1, KW):
        lagged = padded_rows[KW - 1 - lag_step : KW - 1 - lag_step + row_count]
        conv_sum = conv_sum + jnp.where(
            (offsets >= lag_step)[:, None], taps_f[lag_step] * lagged, 0.0
        )
    conv_rows = conv_sum.astype(jnp.bfloat16)
    lanes = scan_rows.shape[1]
    groups = lanes // BW
    conv_blocks = conv_rows.reshape(row_count, groups, BW)
    decay_mats = gathered[5].reshape(groups, BW, BW)
    input_mats = gathered[7].reshape(groups, BW, BW)
    decay_rows = block_mix(conv_blocks, decay_mats) + gathered[6].astype(jnp.float32)
    input_rows = block_mix(conv_blocks, input_mats) + gathered[8].astype(jnp.float32)

    def local_terms(decay_in, input_in, logit_in, conv_in):
        kept_part, driven_part, decay_part = recurrence_terms(
            decay_in, input_in, logit_in, conv_in, resets
        )
        return ((kept_part, driven_part), decay_part)

    terms_out, terms_pull, decay_now = jax.vjp(
        local_terms,
        decay_rows,
        input_rows,
        gathered[9].astype(jnp.float32),
        conv_rows.astype(jnp.float32),
        has_aux=True,
    )
    kept_decay, driven = terms_out
    local_prod, local_state = lax.associative_scan(combine, (kept_decay, driven), axis=0)
    before = entering(
        (local_prod[row_count - 1], local_state[row_count - 1]),
        "seq",
        combine,
        (jnp.ones((lanes,), jnp.float32), jnp.zeros((lanes,), jnp.float32)),
        False,
    )
    state_in = before[1]
    hidden_state = local_state + local_prod * state_in[None, :]
    mixed = (gelu_rows * hidden_state).astype(jnp.bfloat16)
    resid = tokens_f + reduce_features(matmul(mixed, gathered[10]))
    scale_second = row_scale(resid)
    normed_second = spread_rows((resid * scale_second[:, None] * feed_f).astype(jnp.bfloat16))
    gate_pre = matmul(normed_second, gathered[12])
    up_pre = matmul(normed_second, gathered[13])
    gelu_mid, mid_pull = jax.vjp(smooth_gelu, gate_pre)
    hidden_mid = (gelu_mid * up_pre).astype(jnp.bfloat16)
    block_out = resid + reduce_features(matmul(hidden_mid, gathered[14]))
    cot_full = spread_grads(cotangent)
    down_grad = matmul_tn(hidden_mid, cot_full)
    grad_mid = matmul_nt(cot_full, gathered[14])
    grad_gate = mid_pull(grad_mid * up_pre)[0].astype(jnp.bfloat16)
    grad_up = (grad_mid * gelu_mid).astype(jnp.bfloat16)
    gate_grad = matmul_tn(normed_second, grad_gate)
    up_grad = matmul_tn(normed_second, grad_up)
    grad_second = reduce_features(
        matmul_nt(grad_gate, gathered[12]) + matmul_nt(grad_up, gathered[13])
    )
    back_second, feed_grad = norm_back(resid, scale_second, feed_f, grad_second)
    grad_resid = cotangent.astype(jnp.float32) + back_second
    grad_branch = spread_grads(grad_resid.astype(jnp.bfloat16))
    out_grad = matmul_tn(mixed, grad_branch)
    grad_mixed = matmul_nt(grad_branch, gathered[10])
    grad_hidden = grad_mixed * gelu_rows
    grad_gate_rows = gelu_pull(grad_mixed * hidden_state)[0].astype(jnp.bfloat16)
    next_decay = jnp.concatenate([kept_decay[1:], jnp.ones_like(kept_decay[:1])], axis=0)
    tail_prod, local_adjoint = lax.associative_scan(
        combine, (next_decay, grad_hidden), reverse=True, axis=0
    )
    after = entering(
        (local_prod[row_count - 1], kept_decay[0] * local_adjoint[0]),
        "seq",
        combine,
        (jnp.ones((lanes,), jnp.float32), jnp.zeros((lanes,), jnp.float32)),
        True,
    )
    adjoint_in = after[1]
    adjoint = local_adjoint + tail_prod * adjoint_in[None, :]
    prev_state = jnp.concatenate([state_in[None, :], hidden_state[:-1]], axis=0)
    grad_decay_rows, grad_input_rows, logit_grad, conv_direct = terms_pull(
        (adjoint * prev_state, adjoint)
    )
    decay_grad_low = grad_decay_rows.astype(jnp.bfloat16)
    input_grad_low = grad_input_rows.astype(jnp.bfloat16)
    decay_w_grad = block_outer(conv_blocks, decay_grad_low)
    input_w_grad = block_outer(conv_blocks, input_grad_low)
    decay_b_grad = jnp.sum(decay_grad_low.astype(jnp.float32), axis=0)
    input_b_grad = jnp.sum(input_grad_low.astype(jnp.float32), axis=0)
    grad_conv = (
        conv_direct
        + block_back(decay_grad_low, decay_mats)
        + block_back(input_grad_low, input_mats)
    )
    rim_back = from_behind(grad_conv[: KW - 1], "seq", -1)
    grad_extended = jnp.concatenate([grad_conv, rim_back], axis=0)
    ext_offsets = seq_offsets(lengths, shard_index * row_count, row_count + KW - 1)
    grad_scan = taps_f[0] * grad_conv
    tap_grads = [jnp.sum(grad_conv * scan_rows, axis=0)]
    for lag_step in range(1, KW):
        ahead = grad_extended[lag_step : lag_step + row_count]
        ahead_ok = (ext_offsets[lag_step : lag_step + row_count] >= lag_step)[:, None]
        grad_scan = grad_scan + jnp.where(ahead_ok, taps_f[lag_step] * ahead, 0.0)
        lagged = padded_rows[KW - 1 - lag_step : KW - 1 - lag_step + row_count]
        tap_grads.append(
            jnp.sum(jnp.where((offsets >= lag_step)[:, None], grad_conv * lagged, 0.0), axis=0)
        )
    taps_grad = jnp.stack(tap_grads, axis=0)
    taps_bias_grad = jnp.sum(grad_conv, axis=0)
    scan_grad_low = grad_scan.astype(jnp.bfloat16)
    scan_w_grad = matmul_tn(normed_first, scan_grad_low)
    gatebr_grad = matmul_tn(normed_first, grad_gate_rows)
    grad_first = reduce_features(
        matmul_nt(scan_grad_low, gathered[1]) + matmul_nt(grad_gate_rows, gathered[2])
    )
    back_first, mix_grad = norm_back(tokens_f, scale_first, mix_f, grad_first)
    tokens_grad = grad_resid + back_first
    decay_total = jnp.sum(decay_now, axis=0)
    summed = (
        lax.psum_scatter(mix_grad, "seq", scatter_dimension=0, tiled=True),
        lax.psum_scatter(scan_w_grad, "seq", scatter_dimension=0, tiled=True),
        lax.psum_scatter(gatebr_grad, "seq", scatter_dimension=0, tiled=True),
        lax.psum_scatter(taps_grad, "seq", scatter_dimension=1, tiled=True),
        lax.psum_scatter(taps_bias_grad, "seq", scatter_dimension=0, tiled=True),
        lax.psum_scatter(decay_w_grad, "seq", scatter_dimension=1, tiled=True),
        lax.psum_scatter(decay_b_grad, "seq", scatter_dimension=0, tiled=True),
        lax.psum_scatter(input_w_grad, "seq", scatter_dimension=1, tiled=True),
        lax.psum_scatter(input_b_grad, "seq", scatter_dimension=0, tiled=True),
        lax.psum_scatter(logit_grad, "seq", scatter_dimension=0, tiled=True),
        lax.psum_scatter(out_grad, "seq", scatter_dimension=1, tiled=True),
        lax.psum_scatter(feed_grad, "seq", scatter_dimension=0, tiled=True),
        lax.psum_scatter(gate_grad, "seq", scatter_dimension=0, tiled=True),
        lax.psum_scatter(up_grad, "seq", scatter_dimension=0, tiled=True),
        lax.psum_scatter(down_grad, "seq", scatter_dimension=1, tiled=True),
        lax.psum_scatter(decay_total, "seq", scatter_dimension=0, tiled=True),
    )
    mean_decay = summed[15] / (row_count * seq_devices)
    return (
        block_out,
        tokens_grad,
        summed[0],
        summed[1],
        summed[2],
        summed[3],
        summed[4],
        summed[5],
        summed[6],
        summed[7],
        summed[8],
        summed[9],
        summed[10],
        summed[11],
        summed[12],
        summed[13],
        summed[14],
        mean_decay,
    )


MESH = pl.DeviceIdType.MESH
F32 = jnp.float32
BF16 = jnp.bfloat16
LINE = 4
PLANE = 8
CHUNK = 128
ANY = pl.BlockSpec(memory_space=pl.ANY)
VM = pl.BlockSpec(memory_space=pltpu.VMEM)


def flip(place, bit):
    step = 1 << bit
    return place + step - 2 * step * lax.rem(place // step, 2)


def flip_all(place, bits):
    for bit in range(3):
        if bits & (1 << bit):
            place = flip(place, bit)
    return place


def meet(s, z):
    barrier = pltpu.get_barrier_semaphore()
    for bits in range(1, PLANE):
        pl.semaphore_signal(barrier, inc=1, device_id=(flip_all(s, bits), z), device_id_type=MESH)
    for step in range(1, LINE):
        pl.semaphore_signal(
            barrier, inc=1, device_id=(s, lax.rem(z + step, LINE)), device_id_type=MESH
        )
    pl.semaphore_wait(barrier, PLANE - 1 + LINE - 1)


def remote(src, dst, send, recv, target):
    return pltpu.make_async_remote_copy(
        src_ref=src,
        dst_ref=dst,
        send_sem=send,
        recv_sem=recv,
        device_id=target,
        device_id_type=MESH,
    )


class LineGather:
    def __init__(self, s, z, own_at, full_at, send, recv):
        self.s, self.z = s, z
        self.own_at, self.full_at = own_at, full_at
        self.send, self.recv = send, recv

    def copy(self, way, level, c):
        sign = 1 - 2 * way
        origin = self.z - sign * level
        src = self.own_at(c) if level == 0 else self.full_at(origin, c)
        return remote(
            src,
            self.full_at(origin, c),
            self.send.at[way, level, c],
            self.recv.at[way, level, c],
            (self.s, self.z + sign),
        )

    def arrival(self, way, level, c):
        sign = 1 - 2 * way
        part = self.full_at(self.z - sign * (level + 1), c)
        return remote(
            part,
            part,
            self.send.at[way, level, c],
            self.recv.at[way, level, c],
            (self.s, self.z + sign),
        )

    def sends(self, way, level):
        if way == 0:
            return (self.z >= level) & (self.z < LINE - 1)
        return (self.z <= LINE - 1 - level) & (self.z > 0)

    def gets(self, way, level):
        return self.z >= level + 1 if way == 0 else self.z <= LINE - 2 - level

    def start(self, c):
        for way in range(2):
            pl.when(self.sends(way, 0))(lambda way=way: self.copy(way, 0, c).start())

    def forward(self, level, c):
        for way in range(2):
            pl.when(self.gets(way, level - 1))(
                lambda way=way: self.arrival(way, level - 1, c).wait_recv()
            )
            if level < LINE - 1:
                pl.when(self.sends(way, level))(
                    lambda way=way: self.copy(way, level, c).start()
                )

    def drain(self, c):
        for way in range(2):
            for level in range(LINE - 1):
                pl.when(self.sends(way, level))(
                    lambda way=way, level=level: self.copy(way, level, c).wait_send()
                )


class PlaneGather:
    def __init__(self, s, z, own, block_at, half_at, send, recv, local):
        self.s, self.z, self.own = s, z, own
        self.block_at, self.half_at = block_at, half_at
        self.send, self.recv, self.local = send, recv, local
        self.near = (flip(s, 1), flip(s, 2))
        self.diag = flip(self.near[0], 2)
        self.twin = flip(s, 0)
        self.twin_near = (flip(self.near[0], 0), flip(self.near[1], 0))
        self.twin_diag = flip(self.diag, 0)

    def plan(self, i):
        block, half = self.block_at, self.half_at
        return (
            (self.own, block(self.s), self.near[0]),
            (self.own, block(self.s), self.near[1]),
            (half(self.near[1], 0), half(self.near[1], 0), self.near[0]),
            (half(self.near[0], 1), half(self.near[0], 1), self.near[1]),
            (self.own, block(self.s), self.twin),
            (block(self.near[0]), block(self.near[0]), self.twin),
            (block(self.near[1]), block(self.near[1]), self.twin),
            (half(self.diag, 0), half(self.diag, 0), self.twin),
            (half(self.diag, 1), half(self.diag, 1), self.twin),
        )[i]

    def landing(self, i):
        block, half = self.block_at, self.half_at
        return (
            block(self.near[0]),
            block(self.near[1]),
            half(self.diag, 0),
            half(self.diag, 1),
            block(self.twin),
            block(self.twin_near[0]),
            block(self.twin_near[1]),
            half(self.twin_diag, 0),
            half(self.twin_diag, 1),
        )[i]

    def copy(self, i):
        src, dst, target = self.plan(i)
        return remote(src, dst, self.send.at[i], self.recv.at[i], (target, self.z))

    def got(self, i):
        part = self.landing(i)
        remote(part, part, self.send.at[i], self.recv.at[i], (self.twin, self.z)).wait_recv()

    def keep(self):
        return pltpu.make_async_copy(self.own, self.block_at(self.s), self.local)

    def start(self):
        for i in (0, 1, 4):
            self.copy(i).start()
        self.keep().start()

    def turn(self):
        self.got(0)
        self.copy(3).start()
        self.copy(5).start()
        self.got(1)
        self.copy(2).start()
        self.copy(6).start()

    def last(self):
        self.got(2)
        self.copy(7).start()
        self.got(3)
        self.copy(8).start()

    def finish(self):
        for i in range(4, 9):
            self.got(i)
        for i in range(9):
            self.copy(i).wait_send()
        self.keep().wait()


class Spread:
    def __init__(self, s, z, slot_at, send, recv):
        self.s, self.z, self.slot_at, self.send, self.recv = s, z, slot_at, send, recv

    def copy(self, bits, origin):
        slot = self.slot_at(origin)
        return remote(
            slot,
            slot,
            self.send.at[bits - 1],
            self.recv.at[bits - 1],
            (flip_all(self.s, bits), self.z),
        )

    def start(self):
        for bits in range(1, PLANE):
            self.copy(bits, self.s).start()

    def finish(self):
        for bits in range(1, PLANE):
            self.copy(bits, flip_all(self.s, bits)).wait_recv()
        for bits in range(1, PLANE):
            self.copy(bits, self.s).wait_send()


def rows_of(ref, size, parts=2):
    def block(place):
        return ref.at[pl.ds(pl.multiple_of(place * size, size), size)]

    def half(place, h):
        part = size // parts
        return ref.at[pl.ds(pl.multiple_of(place * size + h * part, part), part)]

    return block, half


def columns_of(ref, size):
    height = ref.shape[0] // 2

    def block(place):
        return ref.at[:, pl.ds(pl.multiple_of(place * size, size), size)]

    def half(place, h):
        return ref.at[
            pl.ds(h * height, height), pl.ds(pl.multiple_of(place * size, size), size)
        ]

    return block, half


def chunk_rows(c):
    return pl.ds(pl.multiple_of(c * CHUNK, CHUNK), CHUNK)


def feature_columns(z, width):
    return pl.ds(pl.multiple_of(z * width, width), width)


def each_chunk(chunks, body):
    lax.fori_loop(0, chunks, lambda c, carry: (body(c), carry)[1], 0)


def gather_kernel(
    tok, pack, gains, scan, gate, mix, ffn,
    tok_all, pack_all, gains_all, scan_all, gate_all, mix_all, ffn_all,
    line_send, line_recv, gain_send, gain_recv, plane_send, plane_recv, small_send, small_recv, local,
):
    s, z = lax.axis_index("seq"), lax.axis_index("tp")
    chunks, width = tok.shape[0] // CHUNK, tok.shape[1]
    line = LineGather(
        s, z,
        lambda c: tok.at[chunk_rows(c)],
        lambda o, c: tok_all.at[chunk_rows(c), feature_columns(o, width)],
        line_send, line_recv,
    )
    gain_line = LineGather(
        s, z, lambda c: gains_all.at[z], lambda o, c: gains_all.at[o], gain_send, gain_recv
    )
    planes = []
    for i, (own, full, make) in enumerate(
        (
            (scan, scan_all, rows_of),
            (gate, gate_all, rows_of),
            (mix, mix_all, columns_of),
            (ffn, ffn_all, rows_of),
        )
    ):
        size = own.shape[1] if make is columns_of else own.shape[0]
        block, half = make(full, size)
        planes.append(
            PlaneGather(s, z, own, block, half, plane_send.at[i], plane_recv.at[i], local.at[i])
        )
    packs = Spread(s, z, lambda p: pack_all.at[p], small_send.at[0], small_recv.at[0])
    gain_plane = Spread(s, z, lambda p: gains_all.at[z, p], small_send.at[1], small_recv.at[1])
    keeps = [
        pltpu.make_async_copy(gains, gains_all.at[z, s], local.at[4]),
        pltpu.make_async_copy(pack, pack_all.at[s], local.at[5]),
        pltpu.make_async_copy(tok, tok_all.at[:, feature_columns(z, width)], local.at[6]),
    ]
    for keep in keeps:
        keep.start()
    meet(s, z)
    for keep in keeps[:2]:
        keep.wait()
    gain_plane.start()
    packs.start()
    for c in range(chunks):
        line.start(c)
    for plane in planes:
        plane.start()
    gain_plane.finish()
    packs.finish()
    gain_line.start(0)
    for c in range(chunks):
        line.forward(1, c)
    gain_line.forward(1, 0)
    planes[0].turn()
    for c in range(chunks):
        line.forward(2, c)
    gain_line.forward(2, 0)
    planes[1].turn()
    planes[0].last()
    planes[2].turn()
    planes[1].last()
    planes[3].turn()
    planes[2].last()
    for c in range(chunks):
        line.forward(3, c)
    gain_line.forward(3, 0)
    planes[3].last()
    for plane in planes:
        plane.finish()
    for c in range(chunks):
        line.drain(c)
    gain_line.drain(0)
    keeps[2].wait()


def dma(*shape):
    return pltpu.SemaphoreType.DMA(shape)


def struct(shape, kind):
    return jax.ShapeDtypeStruct(shape, kind)


def gather_first(tok, pack, gains, scan, gate, mix, ffn):
    rows, width = tok.shape
    chunks = rows // CHUNK
    return pl.pallas_call(
        gather_kernel,
        out_shape=(
            struct((rows, width * LINE), BF16),
            struct((PLANE,) + pack.shape, pack.dtype),
            struct((LINE, PLANE) + gains.shape, F32),
            struct((scan.shape[0] * PLANE, scan.shape[1]), BF16),
            struct((gate.shape[0] * PLANE, gate.shape[1]), BF16),
            struct((mix.shape[0], mix.shape[1] * PLANE), BF16),
            struct((ffn.shape[0] * PLANE, ffn.shape[1]), BF16),
        ),
        in_specs=[ANY] * 7,
        out_specs=[ANY] * 7,
        scratch_shapes=[
            dma(2, LINE - 1, chunks), dma(2, LINE - 1, chunks),
            dma(2, LINE - 1, 1), dma(2, LINE - 1, 1),
            dma(4, 9), dma(4, 9), dma(2, 7), dma(2, 7), dma(7),
        ],
        compiler_params=pltpu.CompilerParams(collective_id=0, has_side_effects=True),
        name="gather_first",
    )(tok, pack, gains, scan, gate, mix, ffn)


def sigmoid(values):
    return 0.5 * jnp.tanh(0.5 * values) + 0.5


ROOT = 0.7978845608028654


def gelu_of(values):
    return 0.5 * values * (1.0 + jnp.tanh(ROOT * (values + 0.044715 * values * values * values)))


def gelu_pair(values):
    squared = values * values
    bent = jnp.tanh(ROOT * values * (1.0 + 0.044715 * squared))
    half = 0.5 * (1.0 + bent)
    slope = half + 0.5 * values * (1.0 - bent * bent) * (ROOT * (1.0 + 3 * 0.044715 * squared))
    return values * half, slope


def dot(left_side, right_side):
    return jnp.dot(left_side, right_side, preferred_element_type=F32)


def dot_nt(left_side, right_side):
    return lax.dot_general(
        left_side, right_side, (((1,), (1,)), ((), ())), preferred_element_type=F32
    )


def dot_tn(left_side, right_side):
    return lax.dot_general(
        left_side, right_side, (((0,), (0,)), ((), ())), preferred_element_type=F32
    )


SUBS = 8


LANE = 128


def put(ref, at, values):
    for lane in range(ref.shape[0]):
        ref[lane, at, :] = values[:, lane * LANE : (lane + 1) * LANE]


def get(ref, at):
    return jnp.concatenate([ref[lane, at, :] for lane in range(ref.shape[0])], axis=1)


def strided(ref, step):
    at = pl.ds(step, SUBS, stride=ref.shape[1] // SUBS)
    return [ref[lane, at, :] for lane in range(ref.shape[0])]


def strided_put(ref, step, values):
    at = pl.ds(step, SUBS, stride=ref.shape[1] // SUBS)
    for lane in range(ref.shape[0]):
        ref[lane, at, :] = values[lane]


def lanes_of(values):
    return [values[:, i * LANE : (i + 1) * LANE] for i in range(values.shape[1] // LANE)]


def recur_kernel(
    tok_all, scan_w, gate_w, gates_w, par, gain, masks, cot, up, down,
    normed, scan_rows, gate_rows, conv, decay_rows, input_rows, hidden, mixed, scales, decay_sum,
    cot_all, up_all, down_all,
    kept, driven, slots,
    line_send, line_recv, plane_send, plane_recv, small_send, small_recv, halo_send, halo_recv, local,
):
    s, z = lax.axis_index("seq"), lax.axis_index("tp")
    rows, features = tok_all.shape
    chunks, width, lanes = rows // CHUNK, cot.shape[1], gate_w.shape[1]
    line = LineGather(
        s, z,
        lambda c: cot.at[chunk_rows(c)],
        lambda o, c: cot_all.at[chunk_rows(c), feature_columns(o, width)],
        line_send, line_recv,
    )
    planes = [
        PlaneGather(
            s, z, up, *rows_of(up_all, up.shape[0]), plane_send.at[0], plane_recv.at[0], local.at[0]
        ),
        PlaneGather(
            s, z, down, *columns_of(down_all, down.shape[1]), plane_send.at[1], plane_recv.at[1],
            local.at[1],
        ),
    ]
    keep = pltpu.make_async_copy(cot, cot_all.at[:, feature_columns(z, width)], local.at[2])
    keep.start()
    meet(s, z)
    for c in range(chunks):
        line.start(c)
    for plane in planes:
        plane.start()

    def project(c):
        at = chunk_rows(c)
        x = tok_all[at, :].astype(F32)
        scale = lax.rsqrt(jnp.sum(x * x, axis=1, keepdims=True) / features + EPSILON)
        scales[at, :] = jnp.broadcast_to(scale, (CHUNK, LANE))
        low = (x * scale * gain[0:1, :]).astype(BF16)
        normed[at, :] = low
        scan_rows[pl.ds(pl.multiple_of(c * CHUNK + 8, 8), CHUNK), :] = dot(low, scan_w[...])
        gate_rows[at, :] = dot(low, gate_w[...])

    each_chunk(chunks, project)
    halo = remote(
        scan_rows.at[pl.ds(rows, 8)], scan_rows.at[pl.ds(0, 8)], halo_send, halo_recv,
        (lax.rem(s + 1, PLANE), z),
    )
    first, final = s == 0, s == PLANE - 1
    pl.when(jnp.logical_not(final))(lambda: halo.start())

    @pl.when(first)
    def _():
        scan_rows[0:8, :] = jnp.zeros((8, lanes), F32)

    decay_sum[...] = jnp.zeros_like(decay_sum)
    pl.when(jnp.logical_not(first))(lambda: halo.wait_recv())

    def gates(c):
        at = chunk_rows(c)
        block = scan_rows[pl.ds(pl.multiple_of(c * CHUNK, 8), CHUNK + 8), :]
        mask = masks[at, :]
        total = par[4:5, :] + par[0:1, :] * block[8:, :]
        for lag in range(1, KW):
            total = total + mask[:, lag : lag + 1] * (
                par[lag : lag + 1, :] * block[8 - lag : 8 - lag + CHUNK, :]
            )
        low = total.astype(BF16)
        conv[at, :] = low
        rows_now = dot(low, gates_w[...])
        decays = rows_now[:, :lanes] + par[5:6, :]
        inputs = rows_now[:, lanes:] + par[6:7, :]
        decay_rows[at, :] = decays
        input_rows[at, :] = inputs
        decay = jnp.exp(-sigmoid(decays) * par[7:8, :])
        goes_on = mask[:, 0:1]
        multiplier = 1.0 + goes_on * (
            jnp.sqrt(jnp.maximum(1.0 - decay * decay, FLOOR_VALUE)) - 1.0
        )
        put(kept, at, goes_on * decay)
        put(driven, at, multiplier * sigmoid(inputs) * low.astype(F32))
        decay_sum[0:1, :] += jnp.sum(decay, axis=0, keepdims=True)
        line.forward(1, c)

    each_chunk(chunks, gates)
    count = rows // SUBS

    def total_of(step, carry):
        keeps, drives = strided(kept, step), strided(driven, step)
        return (
            [p * k for p, k in zip(carry[0], keeps)],
            [k * v + d for k, v, d in zip(keeps, carry[1], drives)],
        )

    groups = lanes // LANE
    product, value = lax.fori_loop(
        0,
        count,
        total_of,
        ([jnp.ones((SUBS, LANE), F32)] * groups, [jnp.zeros((SUBS, LANE), F32)] * groups),
        unroll=4,
    )
    product, value = jnp.concatenate(product, axis=1), jnp.concatenate(value, axis=1)
    whole = (jnp.ones((1, lanes), F32), jnp.zeros((1, lanes), F32))
    for sub in range(SUBS):
        here = product[sub : sub + 1, :]
        whole = (whole[0] * here, here * whole[1] + value[sub : sub + 1, :])
    slots[s, 0:1, :] = whole[0]
    slots[s, 1:2, :] = whole[1]
    spread = Spread(s, z, lambda p: slots.at[p], small_send, small_recv)
    spread.start()
    planes[0].turn()
    spread.finish()
    entry = jnp.zeros((1, lanes), F32)
    for place in range(PLANE - 1):
        entry = jnp.where(
            place < s, slots[place, 0:1, :] * entry + slots[place, 1:2, :], entry
        )
    hidden[0:8, :] = jnp.broadcast_to(entry, (8, lanes))
    entries = []
    for sub in range(SUBS):
        entries.append(entry)
        entry = product[sub : sub + 1, :] * entry + value[sub : sub + 1, :]

    def step_on(step, now):
        keeps, drives = strided(kept, step), strided(driven, step)
        now = [k * v + d for k, v, d in zip(keeps, now, drives)]
        strided_put(driven, step, now)
        return now

    lax.fori_loop(0, count, step_on, lanes_of(jnp.concatenate(entries, axis=0)), unroll=4)

    def mix(c):
        at = chunk_rows(c)
        now = get(driven, at)
        hidden[pl.ds(pl.multiple_of(c * CHUNK + 8, 8), CHUNK), :] = now
        mixed[at, :] = (gelu_of(gate_rows[at, :]) * now).astype(BF16)
        line.forward(2, c)

    each_chunk(chunks, mix)
    planes[1].turn()
    planes[0].last()
    for c in range(chunks):
        line.forward(3, c)
    planes[1].last()
    for plane in planes:
        plane.finish()
    for c in range(chunks):
        line.drain(c)
    pl.when(jnp.logical_not(final))(lambda: halo.wait_send())
    keep.wait()


def recur_forward(tok_all, scan_w, gate_w, gates_w, par, gain, masks, cot, up, down):
    rows, features = tok_all.shape
    lanes = gate_w.shape[1]
    chunks = rows // CHUNK
    return pl.pallas_call(
        recur_kernel,
        out_shape=(
            struct((rows, features), BF16),
            struct((rows + 8, lanes), F32),
            struct((rows, lanes), F32),
            struct((rows, lanes), BF16),
            struct((rows, lanes), F32),
            struct((rows, lanes), F32),
            struct((rows + 8, lanes), F32),
            struct((rows, lanes), BF16),
            struct((rows, LANE), F32),
            struct((8, lanes), F32),
            struct((rows, features), BF16),
            struct((up.shape[0] * PLANE, up.shape[1]), BF16),
            struct((down.shape[0], down.shape[1] * PLANE), BF16),
        ),
        in_specs=[VM] * 7 + [ANY] * 3,
        out_specs=[VM] * 10 + [ANY] * 3,
        scratch_shapes=[
            pltpu.VMEM((lanes // LANE, rows, LANE), F32),
            pltpu.VMEM((lanes // LANE, rows, LANE), F32),
            pltpu.VMEM((PLANE, 8, lanes), F32),
            dma(2, LINE - 1, chunks), dma(2, LINE - 1, chunks),
            dma(2, 9), dma(2, 9), dma(7), dma(7),
            pltpu.SemaphoreType.DMA, pltpu.SemaphoreType.DMA, dma(3),
        ],
        compiler_params=pltpu.CompilerParams(
            collective_id=1, has_side_effects=True, vmem_limit_bytes=58 << 20
        ),
        name="recur_forward",
    )(tok_all, scan_w, gate_w, gates_w, par, gain, masks, cot, up, down)


class LineReduce:
    def __init__(self, s, z, part, land, send, recv):
        self.s, self.z, self.part, self.land = s, z, part, land
        self.send, self.recv = send, recv

    def copy(self, way, me, o, c):
        target = me + 1 - 2 * way
        slot = LINE if way == 1 and o == target else o
        return remote(
            self.part.at[c, o],
            self.land.at[c, slot],
            self.send.at[o, c],
            self.recv.at[slot, c],
            (self.s, self.z + 1 - 2 * way),
        )

    def got(self, slot, c):
        part = self.land.at[c, slot]
        remote(part, part, self.send.at[0, c], self.recv.at[slot, c], (self.s, self.z)).wait_recv()

    def hop(self, level, c):
        for way in range(2):
            me = level if way == 0 else LINE - 1 - level
            order = range(LINE - 1, me - 1, -1) if way == 0 else range(me + 1)

            def work(way=way, me=me, order=order):
                for o in order:
                    slot = LINE if way == 1 and o == me else o
                    if level > 0:
                        self.got(slot, c)
                    if o != me:
                        if level > 0:
                            self.part[c, o] = (
                                self.part[c, o].astype(F32) + self.land[c, slot].astype(F32)
                            ).astype(BF16)
                        self.copy(way, me, o, c).start()

            pl.when(self.z == me)(work)

    def landed(self, c, into):
        @pl.when(self.z == 0)
        def _():
            into[...] = self.land[c, LINE].astype(F32)

        @pl.when(self.z > 0)
        def _():
            into[...] = self.land[c, self.z].astype(F32)

        @pl.when((self.z > 0) & (self.z < LINE - 1))
        def _():
            into[...] += self.land[c, LINE].astype(F32)

    def drain(self, c):
        for o in range(LINE):
            part = self.part.at[c, o]
            pl.when(self.z != o)(
                lambda part=part, o=o: remote(
                    part, part, self.send.at[o, c], self.recv.at[0, c], (self.s, self.z)
                ).wait_send()
            )


class LineSpread:
    def __init__(self, s, z, slot_at, send, recv):
        self.s, self.z, self.slot_at, self.send, self.recv = s, z, slot_at, send, recv

    def copy(self, step, origin, c):
        slot = self.slot_at(origin, c)
        target = (self.s, lax.rem(self.z + step, LINE))
        return remote(slot, slot, self.send.at[step - 1, c], self.recv.at[step - 1, c], target)

    def start(self, c):
        for step in range(1, LINE):
            self.copy(step, self.z, c).start()

    def finish(self, c):
        for step in range(1, LINE):
            self.copy(step, lax.rem(self.z + LINE - step, LINE), c).wait_recv()

    def drain(self, c):
        for step in range(1, LINE):
            self.copy(step, self.z, c).wait_send()


class Halves:
    def __init__(self, s, z, src, out, own, send, recv):
        self.s, self.z, self.src, self.out = s, z, src, out
        self.own, self.send, self.recv = own, send, recv

    def keep(self, c):
        at = chunk_rows(c)
        return pltpu.make_async_copy(self.src.at[at], self.out.at[0, at], self.own.at[c])

    def give(self, c):
        at = chunk_rows(c)
        return remote(
            self.src.at[at], self.out.at[1, at], self.send.at[c], self.recv.at[c],
            (flip(self.s, 0), self.z),
        )

    def start(self, c):
        self.keep(c).start()
        self.give(c).start()

    def drain(self, c):
        self.keep(c).wait()
        self.give(c).wait()


def as_row(column):
    return jnp.transpose(jnp.broadcast_to(column, (CHUNK, LANE)))[0:8, :]


def as_columns(row):
    return jnp.transpose(jnp.broadcast_to(row[0:1, :], (LANE, CHUNK)))


def in_range(c, chunks, body):
    pl.when((c >= 0) & (c < chunks))(lambda: body(c))


CUT = 768
AHEAD = 2
GROUP = 2 * CHUNK


def group_rows(g):
    return pl.ds(pl.multiple_of(g * GROUP, GROUP), GROUP)


def feed_kernel(
    mixed, mix_w, tok, gain, gate_w, up_w, down_w, cot,
    resid, scales, coefs, bo_part, gs_part, low_pair, cot_pair, mid_pair, gate_pair, up_pair,
    part, land, low, cots, mid, g_gate, g_up, bo_out, gs_out, gate_v, up_v, down_v,
    acc, bo_acc, gs_acc, inner, squares, inners,
    red_send, red_recv, line_send, line_recv, sq_send, sq_recv, in_send, in_recv,
    own_sem, give_send, give_recv, out_sem, load_sem,
):
    s, z = lax.axis_index("seq"), lax.axis_index("tp")
    rows, width = tok.shape
    chunks, features = rows // CHUNK, width * LINE
    loads = [
        pltpu.make_async_copy(src, dst, load_sem.at[i])
        for i, (src, dst) in enumerate(
            ((gate_w, gate_v), (up_w, up_v), (down_w, down_v), (cot, cots))
        )
    ]
    for load in loads:
        load.start()
    meet(s, z)
    red = LineReduce(s, z, part, land, red_send, red_recv)
    line = LineGather(
        s, z,
        lambda c: low.at[chunk_rows(c), feature_columns(z, width)],
        lambda o, c: low.at[chunk_rows(c), feature_columns(o, width)],
        line_send, line_recv,
    )
    square_spread = LineSpread(s, z, lambda o, c: squares.at[o, c], sq_send, sq_recv)
    inner_spread = LineSpread(s, z, lambda o, c: inners.at[o, c], in_send, in_recv)
    pairs = [
        Halves(s, z, src, out, own_sem.at[i], give_send.at[i], give_recv.at[i])
        for i, (src, out) in enumerate(
            ((low, low_pair), (cots, cot_pair), (mid, mid_pair), (g_gate, gate_pair), (g_up, up_pair))
        )
    ]

    def outs(c):
        return [
            pltpu.make_async_copy(bo_out.at[c], bo_part.at[c], out_sem.at[0, c]),
            pltpu.make_async_copy(gs_out.at[c], gs_part.at[c], out_sem.at[1, c]),
        ]

    def project(c):
        values = dot(mixed[chunk_rows(c), :], mix_w[...])
        for o in range(LINE):
            here = values[:, o * width : (o + 1) * width]
            part[c, o] = here.astype(BF16)

            @pl.when(z == o)
            def _(here=here):
                resid[chunk_rows(c), :] = here

        red.hop(0, c)

    for c in range(AHEAD):
        project(c)

    def reduced(c):
        at = chunk_rows(c)
        red.hop(3, c)
        red.landed(c, acc)
        values = tok[at, :].astype(F32) + (resid[at, :] + acc[...])
        resid[at, :] = values
        squares[z, c] = as_row(jnp.sum(values * values, axis=1, keepdims=True))
        square_spread.start(c)

    def scaled(c):
        at = chunk_rows(c)
        square_spread.finish(c)
        sums = squares[0, c] + squares[1, c] + squares[2, c] + squares[3, c]
        scale = lax.rsqrt(as_columns(sums) / features + EPSILON)
        scales[at, :] = scale
        low[at, feature_columns(z, width)] = (resid[at, :] * scale[:, 0:1] * gain[0:1, :]).astype(
            BF16
        )
        line.start(c)

    def forward(cut, g):
        at = group_rows(g)
        cols = slice(cut * CUT, (cut + 1) * CUT)
        x = low[at, :]
        gate_pre, up_pre = dot(x, gate_v[:, cols]), dot(x, up_v[:, cols])
        act, slope = gelu_pair(gate_pre)
        here = (act * up_pre).astype(BF16)
        mid[at, cols] = here
        grad = dot_nt(cots[at, :], down_v[cols, :])
        gate_grad = (grad * up_pre * slope).astype(BF16)
        up_grad = (grad * act).astype(BF16)
        g_gate[at, cols] = gate_grad
        g_up[at, cols] = up_grad
        products = jnp.sum(
            gate_grad.astype(F32) * gate_pre + up_grad.astype(F32) * up_pre, axis=1, keepdims=True
        )
        if cut == 0:
            inner[...] = products
        else:
            inner[...] += products

    def backward(cut, g):
        at = group_rows(g)
        cols = slice(cut * CUT, (cut + 1) * CUT)
        block = dot(mid[at, cols], down_v[cols, :])
        back = dot_nt(g_gate[at, cols], gate_v[:, cols]) + dot_nt(g_up[at, cols], up_v[:, cols])
        if cut == 0:
            bo_acc[...] = block
            gs_acc[...] = back
            return
        block = bo_acc[...] + block
        back = gs_acc[...] + back
        for k in range(GROUP // CHUNK):
            c = g * (GROUP // CHUNK) + k
            here = slice(k * CHUNK, (k + 1) * CHUNK)
            for o in range(LINE):
                bo_out[c, o] = block[here, o * width : (o + 1) * width].astype(BF16)
                gs_out[c, o] = back[here, o * width : (o + 1) * width].astype(BF16)
            inners[z, c] = as_row(inner[here, :])
            inner_spread.start(c)
            for pair in pairs:
                pair.start(c)
            for copy in outs(c):
                copy.start()

    def turn(t, carry):
        g, odd = (t - 4) // 2, lax.rem(t, 2) == 1
        ready = t >= 4
        pl.when(t == 3)(lambda: [load.wait() for load in loads] and None)
        in_range(t, chunks, lambda c: red.hop(1, c))
        in_range(t - 2, chunks, lambda c: line.forward(1, c))
        in_range(t - 3, chunks, lambda c: line.forward(3, c))
        pl.when(ready & jnp.logical_not(odd))(lambda: forward(0, g))
        pl.when(ready & odd)(lambda: forward(1, g))
        in_range(t - 1, chunks, reduced)
        in_range(t - 1, chunks, scaled)
        in_range(t - 2, chunks, lambda c: line.forward(2, c))
        pl.when(ready & jnp.logical_not(odd))(lambda: backward(0, g))
        in_range(t, chunks, lambda c: red.hop(2, c))
        in_range(t + AHEAD, chunks, project)
        pl.when(ready & odd)(lambda: backward(1, g))
        return carry

    lax.fori_loop(0, chunks + 4, turn, 0)

    def close(c):
        at = chunk_rows(c)
        inner_spread.finish(c)
        sums = inners[0, c] + inners[1, c] + inners[2, c] + inners[3, c]
        scale = scales[at, :]
        coefs[at, :] = scale * scale * as_columns(sums) / features
        red.drain(c)
        line.drain(c)
        square_spread.drain(c)
        inner_spread.drain(c)
        for pair in pairs:
            pair.drain(c)
        for copy in outs(c):
            copy.wait()

    each_chunk(chunks, close)


def vm(*shape, kind=BF16):
    return pltpu.VMEM(shape, kind)


def feed_forward(mixed, mix_w, tok, gain, gate_w, up_w, down_w, cot):
    rows, width = tok.shape
    features, hidden = width * LINE, gate_w.shape[1]
    chunks = rows // CHUNK
    blocks = struct((chunks, LINE, CHUNK, width), BF16)

    def pair(size):
        return struct((2, rows, size), BF16)

    return pl.pallas_call(
        feed_kernel,
        out_shape=(
            struct((rows, width), F32),
            struct((rows, LANE), F32),
            struct((rows, LANE), F32),
            blocks, blocks,
            pair(features), pair(features), pair(hidden), pair(hidden), pair(hidden),
        ),
        in_specs=[VM] * 4 + [ANY] * 4,
        out_specs=[VM] * 3 + [ANY] * 7,
        scratch_shapes=[
            vm(chunks, LINE, CHUNK, width), vm(chunks, LINE + 1, CHUNK, width),
            vm(rows, features), vm(rows, features),
            vm(rows, hidden), vm(rows, hidden), vm(rows, hidden),
            vm(chunks, LINE, CHUNK, width), vm(chunks, LINE, CHUNK, width),
            vm(features, hidden), vm(features, hidden), vm(hidden, features),
            vm(CHUNK, width, kind=F32), vm(GROUP, features, kind=F32),
            vm(GROUP, features, kind=F32), vm(GROUP, 1, kind=F32),
            vm(LINE, chunks, 8, LANE, kind=F32), vm(LINE, chunks, 8, LANE, kind=F32),
            dma(LINE, chunks), dma(LINE + 1, chunks),
            dma(2, LINE - 1, chunks), dma(2, LINE - 1, chunks),
            dma(LINE - 1, chunks), dma(LINE - 1, chunks),
            dma(LINE - 1, chunks), dma(LINE - 1, chunks),
            dma(5, chunks), dma(5, chunks), dma(5, chunks), dma(2, chunks), dma(4),
        ],
        compiler_params=pltpu.CompilerParams(
            collective_id=2, has_side_effects=True, vmem_limit_bytes=63 << 20
        ),
        name="feed_forward",
    )(mixed, mix_w, tok, gain, gate_w, up_w, down_w, cot)


class WeightGrads:
    def __init__(self, s, z, stage, land, own, send, recv, back):
        self.s, self.z = s, z
        self.stage, self.land, self.own = stage, land, own
        self.send, self.recv, self.back_sem = send, recv, back

    def owner(self, k):
        return flip_all(self.s, 2 * (k + 1)) if k < 3 else self.s

    def copy(self, k):
        return remote(
            self.stage.at[k], self.land.at[k], self.send.at[k], self.recv.at[k],
            (self.owner(k), self.z),
        )

    def block(self, k, left, right):
        size = self.own.shape[0]
        columns = feature_columns(self.owner(k), size)
        value = dot_tn(left[:, columns], right[...])
        if k == 3:
            self.own[...] = value
        else:
            self.stage[k] = value.astype(BF16)
            self.copy(k).start()

    def finish(self):
        backs = [
            pltpu.make_async_copy(self.land.at[k], self.stage.at[k], self.back_sem.at[k])
            for k in range(3)
        ]
        for k in range(3):
            self.copy(k).wait()
            backs[k].start()
        for back in backs:
            back.wait()
        self.own[...] += (
            self.stage[0].astype(F32) + self.stage[1].astype(F32) + self.stage[2].astype(F32)
        )


def back_kernel(
    resid, scales, coefs, cot, gain, gs_part, bo_part, low_pair, cot_pair, mid_pair, gate_pair, up_pair,
    grad, grad_all, out, gain_grad, gate_own, up_own, down_own, lands,
    part, land, part_bo, land_bo, low, acc, left, right, stages,
    red_send, red_recv, bo_send, bo_recv, line_send, line_recv, w_send, w_recv, w_back, load_sem, out_sem,
):
    s, z = lax.axis_index("seq"), lax.axis_index("tp")
    rows, width = cot.shape
    chunks = rows // CHUNK
    loads = [
        pltpu.make_async_copy(src, dst, load_sem.at[i])
        for i, (src, dst) in enumerate(
            (
                (gs_part, part), (bo_part, part_bo),
                (cot_pair, left.at[0]), (mid_pair, right.at[0]),
                (low_pair, left.at[1]), (gate_pair, right.at[1]),
            )
        )
    ]
    late = pltpu.make_async_copy(up_pair, right.at[0], load_sem.at[6])
    for load in loads:
        load.start()
    meet(s, z)
    red = LineReduce(s, z, part, land, red_send, red_recv)
    red_bo = LineReduce(s, z, part_bo, land_bo, bo_send, bo_recv)
    line = LineGather(
        s, z,
        lambda c: low.at[chunk_rows(c), feature_columns(z, width)],
        lambda o, c: low.at[chunk_rows(c), feature_columns(o, width)],
        line_send, line_recv,
    )
    weights = [
        WeightGrads(s, z, stages.at[i], lands.at[i], own, w_send.at[i], w_recv.at[i], w_back.at[i])
        for i, own in enumerate((down_own, gate_own, up_own))
    ]
    gain_grad[...] = jnp.zeros_like(gain_grad)
    loads[0].wait()
    for c in range(AHEAD):
        red.hop(0, c)
    for load in loads[1:]:
        load.wait()

    def reduced(c):
        at = chunk_rows(c)
        red.hop(3, c)
        red.landed(c, acc)
        up = acc[...] + part[c, z].astype(F32)
        scale, values = scales[at, 0:1], resid[at, :]
        gain_grad[0:1, :] += jnp.sum(up * values * scale, axis=0, keepdims=True)
        total = cot[at, :].astype(F32) + scale * gain[0:1, :] * up - values * coefs[at, 0:1]
        grad[at, :] = total
        low[at, feature_columns(z, width)] = total.astype(BF16)
        line.start(c)

    def result(c):
        at = chunk_rows(c)
        red_bo.hop(3, c)
        red_bo.landed(c, acc)
        out[at, :] = resid[at, :] + (acc[...] + part_bo[c, z].astype(F32))

    def keep(c):
        at = chunk_rows(c)
        return pltpu.make_async_copy(low.at[at], grad_all.at[at], out_sem.at[c])

    def arrived(c):
        line.forward(3, c)
        keep(c).start()

    def weigh(t):
        for k in range(4):
            pl.when(t == k)(lambda k=k: weights[0].block(k, left.at[0], right.at[0]))
            pl.when(t == 4 + k)(lambda k=k: weights[1].block(k, left.at[1], right.at[1]))
            pl.when(t == 8 + k)(lambda k=k: weights[2].block(k, left.at[1], right.at[0]))
        pl.when(t == 4)(lambda: late.start())
        pl.when(t == 7)(lambda: late.wait())

    def turn(t, carry):
        in_range(t, chunks, lambda c: red.hop(1, c))
        in_range(t - 2, chunks, lambda c: line.forward(1, c))
        in_range(t - 3, chunks, arrived)
        in_range(t - 5, chunks, lambda c: red_bo.hop(1, c))
        weigh(t)
        in_range(t - 1, chunks, reduced)
        in_range(t - 2, chunks, lambda c: line.forward(2, c))
        in_range(t - 6, chunks, result)
        in_range(t, chunks, lambda c: red.hop(2, c))
        in_range(t - 5, chunks, lambda c: red_bo.hop(2, c))
        in_range(t + AHEAD, chunks, lambda c: red.hop(0, c))
        in_range(t - 3, chunks, lambda c: red_bo.hop(0, c))
        return carry

    lax.fori_loop(0, chunks + 7, turn, 0)
    for weight in weights:
        weight.finish()

    def close(c):
        red.drain(c)
        red_bo.drain(c)
        line.drain(c)
        keep(c).wait()

    each_chunk(chunks, close)


def back_feed(resid, scales, coefs, cot, gain, gs_part, bo_part, pairs):
    rows, width = cot.shape
    features, hidden = width * LINE, pairs[2].shape[2]
    chunks, part = rows // CHUNK, features // PLANE
    blocks = vm(chunks, LINE, CHUNK, width)
    landing = vm(chunks, LINE + 1, CHUNK, width)
    return pl.pallas_call(
        back_kernel,
        out_shape=(
            struct((rows, width), F32),
            struct((rows, features), BF16),
            struct((rows, width), F32),
            struct((8, width), F32),
            struct((part, hidden), F32),
            struct((part, hidden), F32),
            struct((part, hidden), F32),
            struct((3, 3, part, hidden), BF16),
        ),
        in_specs=[VM] * 5 + [ANY] * 7,
        out_specs=[VM, ANY] + [VM] * 5 + [ANY],
        scratch_shapes=[
            blocks, landing, blocks, landing,
            vm(rows, features), vm(CHUNK, width, kind=F32),
            vm(2, 2 * rows, features), vm(2, 2 * rows, hidden), vm(3, 3, part, hidden),
            dma(LINE, chunks), dma(LINE + 1, chunks), dma(LINE, chunks), dma(LINE + 1, chunks),
            dma(2, LINE - 1, chunks), dma(2, LINE - 1, chunks),
            dma(3, 3), dma(3, 3), dma(3, 3), dma(7), dma(chunks),
        ],
        compiler_params=pltpu.CompilerParams(
            collective_id=3, has_side_effects=True, vmem_limit_bytes=63 << 20
        ),
        name="back_feed",
    )(
        resid, scales, coefs, cot, gain, gs_part, bo_part,
        *[pair.reshape(2 * rows, pair.shape[2]) for pair in pairs],
    )


def recur_back_kernel(
    low, mix_w, gate_rows, hidden, conv, decay_rows, input_rows, scan_rows, masks, par, gates_w, scales,
    normed_src, mixed_src, low_src,
    gates_grad, sums, coefs, normed_pair, mixed_pair, low_pair, scan_pair, gate_pair,
    kept, grads, spilled, both, conv_grad, scan_low, gate_low, slots, inners,
    small_send, small_recv, halo_send, halo_recv, in_send, in_recv,
    own_sem, give_send, give_recv, keep_sem, twin_send, twin_recv,
):
    s, z = lax.axis_index("seq"), lax.axis_index("tp")
    rows, features = low.shape
    lanes = gate_rows.shape[1]
    chunks = rows // CHUNK
    wholes = []
    for i, (src, out) in enumerate(
        ((normed_src, normed_pair), (mixed_src, mixed_pair), (low_src, low_pair))
    ):
        wholes.append(pltpu.make_async_copy(src, out.at[0], keep_sem.at[i]))
        wholes.append(
            remote(src, out.at[1], twin_send.at[i], twin_recv.at[i], (flip(s, 0), z))
        )
    pairs = [
        Halves(s, z, src, out, own_sem.at[i], give_send.at[i], give_recv.at[i])
        for i, (src, out) in enumerate(((scan_low, scan_pair), (gate_low, gate_pair)))
    ]
    inner_spread = LineSpread(s, z, lambda o, c: inners.at[o, c], in_send, in_recv)
    meet(s, z)
    for whole in wholes:
        whole.start()
    sums[...] = jnp.zeros_like(sums)

    def start(g):
        at = group_rows(g)
        grad = dot_nt(low[at, :], mix_w[...])
        for k in range(GROUP // CHUNK):
            c = g * (GROUP // CHUNK) + k
            here = chunk_rows(c)
            act, slope = gelu_pair(gate_rows[here, :])
            now = hidden[pl.ds(pl.multiple_of(c * CHUNK + 8, 8), CHUNK), :]
            part = grad[k * CHUNK : (k + 1) * CHUNK, :]
            gate_low[here, :] = (part * now * slope).astype(BF16)
            put(grads, here, part * act)
            decay = jnp.exp(-sigmoid(decay_rows[here, :]) * par[7:8, :])
            put(kept, here, masks[here, 0:1] * decay)

    lax.fori_loop(0, rows // GROUP, lambda g, carry: (start(g), carry)[1], 0)
    for c in range(chunks):
        pairs[1].start(c)
    count, groups = rows // SUBS, lanes // LANE

    def total_of(step, carry):
        keeps, adds = strided(kept, count - 1 - step), strided(grads, count - 1 - step)
        return (
            [p * k for p, k in zip(carry[0], keeps)],
            [k * (v + a) for k, v, a in zip(keeps, carry[1], adds)],
        )

    product, value = lax.fori_loop(
        0,
        count,
        total_of,
        ([jnp.ones((SUBS, LANE), F32)] * groups, [jnp.zeros((SUBS, LANE), F32)] * groups),
        unroll=4,
    )
    product, value = jnp.concatenate(product, axis=1), jnp.concatenate(value, axis=1)
    whole = (jnp.ones((1, lanes), F32), jnp.zeros((1, lanes), F32))
    for sub in range(SUBS - 1, -1, -1):
        here = product[sub : sub + 1, :]
        whole = (whole[0] * here, here * whole[1] + value[sub : sub + 1, :])
    slots[s, 0:1, :] = whole[0]
    slots[s, 1:2, :] = whole[1]
    spread = Spread(s, z, lambda p: slots.at[p], small_send, small_recv)
    spread.start()
    spread.finish()
    entry = jnp.zeros((1, lanes), F32)
    for place in range(PLANE - 1, 0, -1):
        entry = jnp.where(
            place > s, slots[place, 0:1, :] * entry + slots[place, 1:2, :], entry
        )
    entries = []
    for sub in range(SUBS - 1, -1, -1):
        entries.append(entry)
        entry = product[sub : sub + 1, :] * entry + value[sub : sub + 1, :]

    def step_back(step, now):
        keeps, adds = strided(kept, count - 1 - step), strided(grads, count - 1 - step)
        now = [v + a for v, a in zip(now, adds)]
        strided_put(grads, count - 1 - step, now)
        return [k * v for k, v in zip(keeps, now)]

    lax.fori_loop(
        0, count, step_back, lanes_of(jnp.concatenate(entries[::-1], axis=0)), unroll=4
    )

    def gates(c):
        at = chunk_rows(c)
        tall = pl.ds(pl.multiple_of(c * CHUNK, 8), CHUNK + 8)
        adjoint = get(grads, at)
        before = hidden[tall, :][7 : 7 + CHUNK, :]
        mask = masks[at, :]
        goes_on = mask[:, 0:1]
        opened = sigmoid(decay_rows[at, :])
        entered = sigmoid(input_rows[at, :])
        rate = par[7:8, :]
        decay = jnp.exp(-opened * rate)
        room = 1.0 - decay * decay
        root = jnp.sqrt(jnp.maximum(room, FLOOR_VALUE))
        multiplier = 1.0 + goes_on * (root - 1.0)
        conv_f = conv[at, :].astype(F32)
        direct = adjoint * multiplier
        grad_input = (direct * conv_f * (entered * (1.0 - entered))).astype(BF16)
        through = jnp.where(
            room > FLOOR_VALUE, 1.0, jnp.where(room == FLOOR_VALUE, 0.5, 0.0)
        )
        grad_decay = goes_on * (
            adjoint * before - adjoint * entered * conv_f * (through * decay / root)
        )
        scaled = grad_decay * decay * opened
        grad_rows = (-scaled * rate * (1.0 - opened)).astype(BF16)
        joined = jnp.concatenate([grad_rows, grad_input], axis=1)
        both[at, :] = joined
        grad_conv = direct * entered + dot_nt(joined, gates_w[...])
        conv_grad[at, :] = grad_conv
        block = scan_rows[tall, :]
        sums[0:1, :] += jnp.sum(grad_conv * block[8:, :], axis=0, keepdims=True)
        for lag in range(1, KW):
            sums[lag : lag + 1, :] += jnp.sum(
                mask[:, lag : lag + 1] * (grad_conv * block[8 - lag : 8 - lag + CHUNK, :]),
                axis=0,
                keepdims=True,
            )
        sums[4:5, :] += jnp.sum(grad_conv, axis=0, keepdims=True)
        sums[5:6, :] += jnp.sum(grad_rows.astype(F32), axis=0, keepdims=True)
        sums[6:7, :] += jnp.sum(grad_input.astype(F32), axis=0, keepdims=True)
        sums[7:8, :] += jnp.sum(scaled, axis=0, keepdims=True)

    each_chunk(chunks, gates)
    halo = remote(
        conv_grad.at[pl.ds(0, 8)], conv_grad.at[pl.ds(rows, 8)], halo_send, halo_recv,
        (lax.rem(s + PLANE - 1, PLANE), z),
    )
    first, final = s == 0, s == PLANE - 1
    pl.when(jnp.logical_not(first))(lambda: halo.start())
    gates_grad[...] = dot_tn(conv[...], both[...])
    sums[7:8, :] = sums[7:8, :] * par[8:9, :]

    @pl.when(final)
    def _():
        conv_grad[rows : rows + 8, :] = jnp.zeros((8, lanes), F32)

    pl.when(jnp.logical_not(final))(lambda: halo.wait_recv())

    def finish(c):
        at = chunk_rows(c)
        tall = pl.ds(pl.multiple_of(c * CHUNK, 8), CHUNK + 8)
        block, mask = conv_grad[tall, :], masks[tall, :]
        total = par[0:1, :] * block[:CHUNK, :]
        for lag in range(1, KW):
            total = total + mask[lag : lag + CHUNK, lag : lag + 1] * (
                par[lag : lag + 1, :] * block[lag : lag + CHUNK, :]
            )
        grad = total.astype(BF16)
        scan_low[at, :] = grad
        pairs[0].start(c)
        products = grad.astype(F32) * scan_rows[
            pl.ds(pl.multiple_of(c * CHUNK + 8, 8), CHUNK), :
        ] + gate_low[at, :].astype(F32) * gate_rows[at, :]
        inners[z, c] = as_row(jnp.sum(products, axis=1, keepdims=True))
        inner_spread.start(c)

    each_chunk(chunks, finish)

    def close(c):
        at = chunk_rows(c)
        inner_spread.finish(c)
        total = inners[0, c] + inners[1, c] + inners[2, c] + inners[3, c]
        scale = scales[at, :]
        coefs[at, :] = scale * scale * as_columns(total) / features
        inner_spread.drain(c)
        for pair in pairs:
            pair.drain(c)

    each_chunk(chunks, close)
    for whole in wholes:
        whole.wait()
    pl.when(jnp.logical_not(first))(lambda: halo.wait_send())


def recur_back(low, mix_w, gate_rows, hidden, conv, decay_rows, input_rows, scan_rows, masks, par,
               gates_w, scales, normed, mixed):
    rows, features = low.shape
    lanes = gate_rows.shape[1]
    chunks = rows // CHUNK

    def pair(size):
        return struct((2, rows, size), BF16)

    return pl.pallas_call(
        recur_back_kernel,
        out_shape=(
            struct((lanes, 2 * lanes), F32),
            struct((8, lanes), F32),
            struct((rows, LANE), F32),
            pair(features), pair(lanes), pair(features), pair(lanes), pair(lanes),
        ),
        in_specs=[VM] * 12 + [ANY] * 3,
        out_specs=[VM] * 3 + [ANY] * 5,
        scratch_shapes=[
            vm(lanes // LANE, rows, LANE, kind=F32), vm(lanes // LANE, rows, LANE, kind=F32),
            vm(8, LANE, kind=F32),
            vm(rows, 2 * lanes), vm(rows + 8, lanes, kind=F32), vm(rows, lanes), vm(rows, lanes),
            vm(PLANE, 8, lanes, kind=F32), vm(LINE, chunks, 8, LANE, kind=F32),
            dma(7), dma(7), pltpu.SemaphoreType.DMA, pltpu.SemaphoreType.DMA,
            dma(LINE - 1, chunks), dma(LINE - 1, chunks),
            dma(2, chunks), dma(2, chunks), dma(2, chunks), dma(3), dma(3), dma(3),
        ],
        compiler_params=pltpu.CompilerParams(
            collective_id=4, has_side_effects=True, vmem_limit_bytes=60 << 20
        ),
        name="recur_back",
    )(
        low, mix_w, gate_rows, hidden, conv, decay_rows, input_rows, scan_rows, masks, par, gates_w,
        scales, normed, mixed, low,
    )


def last_kernel(
    scan_w, gate_w, grad, tok, coefs, scales, gain, scan_low, gate_low, pack,
    normed_pair, mixed_pair, low_pair, scan_pair, gate_pair,
    tokens_grad, gain_grad, pack_sum, mix_own, scan_own, gate_own, lands,
    part, land, acc, left, right, stages, pack_land, gain_land,
    red_send, red_recv, w_send, w_recv, w_back, load_sem, pack_send, pack_recv, gain_send, gain_recv,
):
    s, z = lax.axis_index("seq"), lax.axis_index("tp")
    rows, width = tok.shape
    chunks = rows // CHUNK
    loads = [
        pltpu.make_async_copy(src, dst, load_sem.at[i])
        for i, (src, dst) in enumerate(
            (
                (low_pair, left.at[0]), (mixed_pair, right.at[0]), (normed_pair, left.at[1]),
                (scan_pair, right.at[1]), (gate_pair, right.at[2]),
            )
        )
    ]
    for load in loads:
        load.start()
    meet(s, z)
    packs = [
        remote(
            pack.at[flip_all(s, bits)], pack_land.at[s], pack_send.at[bits - 1],
            pack_recv.at[bits - 1], (flip_all(s, bits), z),
        )
        for bits in range(1, PLANE)
    ]
    for copy in packs:
        copy.start()
    red = LineReduce(s, z, part, land, red_send, red_recv)
    weights = [
        WeightGrads(s, z, stages.at[i], lands.at[i], own, w_send.at[i], w_recv.at[i], w_back.at[i])
        for i, own in enumerate((mix_own, scan_own, gate_own))
    ]
    gain_land[s] = jnp.zeros_like(gain_grad)

    def project(g):
        at = group_rows(g)
        values = dot_nt(scan_low[at, :], scan_w[...]) + dot_nt(gate_low[at, :], gate_w[...])
        for k in range(GROUP // CHUNK):
            c = g * (GROUP // CHUNK) + k
            here = slice(k * CHUNK, (k + 1) * CHUNK)
            for o in range(LINE):
                part[c, o] = values[here, o * width : (o + 1) * width].astype(BF16)
            red.hop(0, c)

    def reduced(c):
        at = chunk_rows(c)
        red.hop(3, c)
        red.landed(c, acc)
        up = acc[...] + part[c, z].astype(F32)
        scale, values = scales[at, 0:1], tok[at, :].astype(F32)
        gain_land[s, 0:1, :] += jnp.sum(up * values * scale, axis=0, keepdims=True)
        tokens_grad[at, :] = (
            grad[at, :] + scale * gain[0:1, :] * up - values * coefs[at, 0:1]
        )

    project(0)
    for load in loads:
        load.wait()

    def weigh(t):
        for k in range(4):
            pl.when(t == k)(lambda k=k: weights[1].block((k + 3) % 4, left.at[1], right.at[1]))
            pl.when(t == k)(lambda k=k: weights[2].block((k + 3) % 4, left.at[1], right.at[2]))
            pl.when(t == 4 + k // 2)(lambda k=k: weights[0].block(k, left.at[0], right.at[0]))

    def turn(t, carry):
        in_range(t, chunks, lambda c: red.hop(1, c))
        pl.when((lax.rem(t, 2) == 0) & (t < chunks - 2))(lambda: project(t // 2 + 1))
        weigh(t)
        in_range(t - 1, chunks, reduced)
        in_range(t, chunks, lambda c: red.hop(2, c))
        return carry

    lax.fori_loop(0, chunks + 1, turn, 0)
    gain_spread = Spread(s, z, lambda p: gain_land.at[p], gain_send, gain_recv)
    gain_spread.start()
    for bits in range(1, PLANE):
        other = pack_land.at[flip_all(s, bits)]
        remote(
            other, other, pack_send.at[bits - 1], pack_recv.at[bits - 1], (flip_all(s, bits), z)
        ).wait_recv()
    total = pack[s]
    for bits in range(1, PLANE):
        total = total + pack_land[flip_all(s, bits)]
    pack_sum[...] = total
    for weight in weights:
        weight.finish()
    gain_spread.finish()
    total = gain_land[0]
    for place in range(1, PLANE):
        total = total + gain_land[place]
    gain_grad[...] = total
    for copy in packs:
        copy.wait_send()
    each_chunk(chunks, red.drain)


def last_reduce(scan_w, gate_w, grad, tok, coefs, scales, gain, scan_low, gate_low, pack, pairs):
    rows, width = tok.shape
    features, lanes = width * LINE, scan_w.shape[1]
    chunks, part = rows // CHUNK, features // PLANE
    return pl.pallas_call(
        last_kernel,
        out_shape=(
            struct((rows, width), F32),
            struct((8, width), F32),
            struct(pack.shape[1:], F32),
            struct((part, lanes), F32),
            struct((part, lanes), F32),
            struct((part, lanes), F32),
            struct((3, 3, part, lanes), BF16),
        ),
        in_specs=[VM] * 10 + [ANY] * 5,
        out_specs=[VM] * 6 + [ANY],
        scratch_shapes=[
            vm(chunks, LINE, CHUNK, width), vm(chunks, LINE + 1, CHUNK, width),
            vm(CHUNK, width, kind=F32),
            vm(2, 2 * rows, features), vm(3, 2 * rows, lanes), vm(3, 3, part, lanes),
            vm(*pack.shape, kind=F32), vm(PLANE, 8, width, kind=F32),
            dma(LINE, chunks), dma(LINE + 1, chunks),
            dma(3, 3), dma(3, 3), dma(3, 3), dma(5), dma(7), dma(7), dma(7), dma(7),
        ],
        compiler_params=pltpu.CompilerParams(
            collective_id=5, has_side_effects=True, vmem_limit_bytes=63 << 20
        ),
        name="last_reduce",
    )(
        scan_w, gate_w, grad, tok, coefs, scales, gain, scan_low, gate_low, pack,
        *[pair.reshape(2 * rows, pair.shape[2]) for pair in pairs],
    )


def shards_fast(
    tokens, mix_gain, scan_branch, gate_branch, kernel_taps, kernel_bias, decay_gate, decay_bias,
    input_gate, input_bias, decay_logit, mixer_out, feed_gain, gate_weight, up_weight, down_weight,
    lengths, cotangent,
):
    row_count = tokens.shape[0]
    seq_devices = lax.axis_size("seq")
    shard_index = lax.axis_index("seq")
    ext_offsets = seq_offsets(lengths, shard_index * row_count, row_count + 8)
    lag_at = jnp.array([1, 1, 2, 3, 0, 0, 0, 0], jnp.int32)
    masks = (ext_offsets[:, None] >= lag_at[None, :]).astype(F32)
    lanes = scan_branch.shape[1]
    part = lanes // seq_devices
    groups = lanes // BW
    flat = jnp.concatenate(
        [
            kernel_taps.reshape(-1), kernel_bias, decay_bias, input_bias, decay_logit,
            decay_gate.reshape(-1), input_gate.reshape(-1),
        ]
    )
    pack_rows = -(-flat.shape[0] // (128 * 16)) * 16
    pack = jnp.pad(flat, (0, pack_rows * 128 - flat.shape[0])).reshape(pack_rows, 128)
    gains = jnp.pad(
        jnp.concatenate([mix_gain, feed_gain]).astype(F32)[None, :], ((0, 7), (0, 0))
    )
    tok_all, pack_all, gains_all, scan_w, gate_w, mix_w, ffn_gate = gather_first(
        tokens, pack, gains, scan_branch, gate_branch, mixer_out, gate_weight
    )
    pack_all = pack_all.reshape(seq_devices, -1)
    at = 0

    def take(rows):
        nonlocal at
        piece = pack_all[:, at : at + rows * part].reshape(seq_devices, rows, part)
        at += rows * part
        return piece.transpose(1, 0, 2).reshape(rows, lanes).astype(F32)

    taps_f = take(KW)
    biases = take(3)
    logit_f = take(1)
    gate_cut = groups * BW * BW // seq_devices
    mats = [
        pack_all[:, at + i * gate_cut : at + (i + 1) * gate_cut]
        .reshape(seq_devices, groups, BW // seq_devices, BW)
        .transpose(1, 0, 2, 3)
        .reshape(groups, BW, BW)
        for i in range(2)
    ]
    gates_w = jnp.concatenate(
        [
            jnp.concatenate(
                [jnp.pad(m[g], ((0, 0), (g * BW, lanes - (g + 1) * BW))) for g in range(groups)], 0
            )
            for m in mats
        ],
        1,
    )
    par = jnp.concatenate(
        [
            taps_f, biases, CD * jax.nn.softplus(-logit_f), CD * jax.nn.sigmoid(-logit_f),
            jnp.zeros((7, lanes), F32),
        ],
        0,
    )
    half = gains.shape[1] // 2
    gain_full = gains_all[:, :, 0, :].reshape(-1, 2, half).transpose(1, 0, 2).reshape(2, -1)
    gain_full = jnp.pad(gain_full, ((0, 6), (0, 0)))
    (
        normed_first, scan_pad, gate_rows, conv_rows, decay_rows, input_rows, hidden_state, mixed,
        scale_first_rows, decay_sums, cot_full, up_w, down_w,
    ) = recur_forward(
        tok_all, scan_w, gate_w, gates_w, par, gain_full, masks, cotangent, up_weight, down_weight
    )
    width = tokens.shape[1]
    own_feed = lax.dynamic_slice(
        gain_full[1:2], (0, lax.axis_index("tp") * width), (1, width)
    )
    feed_own = jnp.broadcast_to(own_feed, (8, width))
    (
        resid, scales, coefs, bo_part, gs_part,
        low_pair, cot_pair, mid_pair, gate_pair, up_pair,
    ) = feed_forward(
        mixed, mix_w, tokens, feed_own, ffn_gate, up_w, down_w, cot_full
    )
    grad_resid, grad_branch, block_out, feed_grads, gate_own, up_own, down_own, _ = back_feed(
        resid, scales, coefs, cotangent, feed_own, gs_part, bo_part,
        (low_pair, cot_pair, mid_pair, gate_pair, up_pair),
    )
    gates_grad, sums, first_coefs, normed_pair, mixed_pair, branch_pair, scan_pair, gaterow_pair = (
        recur_back(
            grad_branch, mix_w, gate_rows, hidden_state, conv_rows, decay_rows, input_rows, scan_pad,
            masks, par, gates_w, scale_first_rows, normed_first, mixed,
        )
    )

    def own_parts(rows):
        return rows.reshape(rows.shape[0], seq_devices, part).transpose(1, 0, 2)

    small = own_parts(jnp.concatenate([sums, decay_sums[0:1]], 0)).reshape(seq_devices, -1)
    tiles = [
        jnp.stack(
            [
                gates_grad[g * BW : (g + 1) * BW, i * lanes + g * BW : i * lanes + (g + 1) * BW]
                for g in range(groups)
            ]
        )
        .reshape(groups, seq_devices, -1)
        .transpose(1, 0, 2)
        .reshape(seq_devices, -1)
        for i in range(2)
    ]
    feed_part = feed_grads[0].reshape(seq_devices, -1)
    flat_grads = jnp.concatenate([*tiles, small, feed_part], 1)
    grad_rows = -(-flat_grads.shape[1] // (128 * 8)) * 8
    grad_pack = jnp.pad(flat_grads, ((0, 0), (0, grad_rows * 128 - flat_grads.shape[1])))
    own_mix = lax.dynamic_slice(gain_full[0:1], (0, lax.axis_index("tp") * width), (1, width))
    tokens_grad, mix_grads, pack_sum, mix_own, scan_own, gaterow_own, _ = last_reduce(
        scan_w, gate_w, grad_resid, tokens, first_coefs, scale_first_rows,
        jnp.broadcast_to(own_mix, (8, width)), scan_pair[0], gaterow_pair[0],
        grad_pack.reshape(seq_devices, grad_rows, 128),
        (normed_pair, mixed_pair, branch_pair, scan_pair, gaterow_pair),
    )
    pack_sum = pack_sum.reshape(-1)
    gate_size = groups * gate_cut // groups
    cut_at = 2 * gate_size
    small_sum = pack_sum[cut_at : cut_at + 9 * part].reshape(9, part)
    feed_sum = pack_sum[cut_at + 9 * part : cut_at + 9 * part + mix_gain.shape[0]]
    mix_sum = lax.dynamic_slice(
        mix_grads[0], (shard_index * mix_gain.shape[0],), (mix_gain.shape[0],)
    )
    return (
        block_out,
        tokens_grad,
        mix_sum,
        scan_own,
        gaterow_own,
        small_sum[0:KW],
        small_sum[KW],
        pack_sum[:gate_size].reshape(groups, -1),
        small_sum[KW + 1],
        pack_sum[gate_size : 2 * gate_size].reshape(groups, -1),
        small_sum[KW + 2],
        small_sum[KW + 3],
        mix_own.T,
        feed_sum,
        gate_own,
        up_own,
        down_own.T,
        small_sum[KW + 4] / (row_count * seq_devices),
    )


def solution(mesh):
    placed = (
        P("seq", "tp"),
        P(("tp", "seq")),
        P("seq", "tp"),
        P("seq", "tp"),
        P(None, ("tp", "seq")),
        P(("tp", "seq")),
        P("tp", "seq"),
        P(("tp", "seq")),
        P("tp", "seq"),
        P(("tp", "seq")),
        P(("tp", "seq")),
        P("tp", "seq"),
        P(("tp", "seq")),
        P("seq", "tp"),
        P("seq", "tp"),
        P("tp", "seq"),
        P(),
        P("seq", "tp"),
    )
    return jax.shard_map(
        shards_fast if (mesh.shape["seq"], mesh.shape["tp"]) == (PLANE, LINE) else shards_general,
        mesh=mesh,
        in_specs=placed,
        out_specs=(
            P("seq", "tp"),
            P("seq", "tp"),
            P(("tp", "seq")),
            P("seq", "tp"),
            P("seq", "tp"),
            P(None, ("tp", "seq")),
            P(("tp", "seq")),
            P("tp", "seq"),
            P(("tp", "seq")),
            P("tp", "seq"),
            P(("tp", "seq")),
            P(("tp", "seq")),
            P("tp", "seq"),
            P(("tp", "seq")),
            P("seq", "tp"),
            P("seq", "tp"),
            P("tp", "seq"),
            P(("tp", "seq")),
        ),
        check_vma=False,
    )
```

```python
import functools

import jax
import jax.numpy as jnp
import numpy as np
from jax import lax
from jax.experimental import pallas as pl
from jax.experimental.pallas import tpu as pltpu
from jax.sharding import PartitionSpec as P


D = 2048
KW = 4
CD = 8
BW = 160


EPSILON = 1e-06
FLOOR_VALUE = 0.001


def from_behind(value, axis, steps):
    count = lax.axis_size(axis)
    initial, last = (max(0, -steps), min(count, count - steps))
    return lax.ppermute(value, axis, [(source, source + steps) for source in range(initial, last)])


def entering(part, axis, combine, identity, reverse):
    count = lax.axis_size(axis)
    place = lax.axis_index(axis)
    ahead = count - 1 - place if reverse else place
    gathered = jax.tree.map(lambda a: lax.all_gather(a, axis), part)
    state = jax.tree.map(lambda a, e: jnp.zeros_like(a) + jnp.asarray(e, a.dtype), part, identity)

    def one(turn, state):
        source = count - 1 - turn if reverse else turn
        return combine(
            state, jax.tree.map(lambda a: lax.dynamic_index_in_dim(a, source, 0, False), gathered)
        )

    return lax.fori_loop(0, ahead, one, state)


def matmul(left_side, right_side):
    return jnp.dot(left_side, right_side, preferred_element_type=jnp.float32)


def matmul_tn(left_side, right_side):
    return lax.dot_general(
        left_side, right_side, (((0,), (0,)), ((), ())), preferred_element_type=jnp.float32
    )


def matmul_nt(left_side, right_side):
    return lax.dot_general(
        left_side, right_side, (((1,), (1,)), ((), ())), preferred_element_type=jnp.float32
    )


def smooth_gelu(values):
    return jax.nn.gelu(values, approximate=True)


def combine(earlier, later):
    return (earlier[0] * later[0], later[1] + later[0] * earlier[1])


def seq_offsets(lengths, first_index, row_total):
    ends_all = jnp.cumsum(lengths, dtype=jnp.int32)
    starts_all = ends_all - lengths
    position = first_index + jnp.arange(row_total, dtype=jnp.int32)
    begins = jnp.max(
        jnp.where(starts_all[None, :] <= position[:, None], starts_all[None, :], 0), axis=1
    )
    return position - begins


def recurrence_terms(decay_rows, input_rows, decay_param, conv_values, resets):
    recur_gate = jax.nn.sigmoid(decay_rows)
    input_open = jax.nn.sigmoid(input_rows)
    decay_now = jnp.exp(-CD * recur_gate * jax.nn.softplus(-decay_param))
    multiplier = jnp.where(
        resets[:, None], 1.0, jnp.sqrt(jnp.maximum(1.0 - decay_now * decay_now, FLOOR_VALUE))
    )
    kept_decay = jnp.where(resets[:, None], 0.0, decay_now)
    return (kept_decay, multiplier * input_open * conv_values, decay_now)


def row_scale(values):
    squares_sum = lax.psum(jnp.sum(values * values, axis=1), "tp")
    return lax.rsqrt(squares_sum / D + EPSILON)


def spread_rows(values):
    return lax.all_gather(values, "tp", axis=1, tiled=True)


def spread_grads(values):
    return lax.all_gather(values, "tp", axis=1, tiled=True)


def reduce_features(values):
    return lax.psum_scatter(values, "tp", scatter_dimension=1, tiled=True)


def norm_back(values, row_scales, gain_vector, upstream):
    weighted = upstream * gain_vector
    inner_sum = lax.psum(jnp.sum(weighted * values, axis=1), "tp")
    cubed = row_scales * row_scales * row_scales * inner_sum / D
    back_rows = row_scales[:, None] * weighted - values * cubed[:, None]
    return (back_rows, jnp.sum(upstream * values * row_scales[:, None], axis=0))


def block_mix(blocked, matrices):
    mixed_blocks = jnp.einsum("tnb,nbc->tnc", blocked, matrices, preferred_element_type=jnp.float32)
    return mixed_blocks.reshape(blocked.shape[0], -1)


def block_outer(blocked, gradients):
    shaped = gradients.reshape(blocked.shape)
    outer_sum = jnp.einsum("tnb,tnc->nbc", blocked, shaped, preferred_element_type=jnp.float32)
    return outer_sum.reshape(blocked.shape[1], -1)


def block_back(gradients, matrices):
    shaped = gradients.reshape(gradients.shape[0], matrices.shape[0], matrices.shape[1])
    backed = jnp.einsum("tnc,nbc->tnb", shaped, matrices, preferred_element_type=jnp.float32)
    return backed.reshape(gradients.shape[0], -1)


def shards_general(
    tokens,
    mix_gain,
    scan_branch,
    gate_branch,
    kernel_taps,
    kernel_bias,
    decay_gate,
    decay_bias,
    input_gate,
    input_bias,
    decay_logit,
    mixer_out,
    feed_gain,
    gate_weight,
    up_weight,
    down_weight,
    lengths,
    cotangent,
):
    row_count = tokens.shape[0]
    seq_devices = lax.axis_size("seq")
    shard_index = lax.axis_index("seq")
    offsets = seq_offsets(lengths, shard_index * row_count, row_count)
    resets = offsets == 0
    gathered = (
        lax.all_gather(mix_gain, "seq", axis=0, tiled=True),
        lax.all_gather(scan_branch, "seq", axis=0, tiled=True),
        lax.all_gather(gate_branch, "seq", axis=0, tiled=True),
        lax.all_gather(kernel_taps, "seq", axis=1, tiled=True),
        lax.all_gather(kernel_bias, "seq", axis=0, tiled=True),
        lax.all_gather(decay_gate, "seq", axis=1, tiled=True),
        lax.all_gather(decay_bias, "seq", axis=0, tiled=True),
        lax.all_gather(input_gate, "seq", axis=1, tiled=True),
        lax.all_gather(input_bias, "seq", axis=0, tiled=True),
        lax.all_gather(decay_logit, "seq", axis=0, tiled=True),
        lax.all_gather(mixer_out, "seq", axis=1, tiled=True),
        lax.all_gather(feed_gain, "seq", axis=0, tiled=True),
        lax.all_gather(gate_weight, "seq", axis=0, tiled=True),
        lax.all_gather(up_weight, "seq", axis=0, tiled=True),
        lax.all_gather(down_weight, "seq", axis=1, tiled=True),
    )
    mix_f = gathered[0].astype(jnp.float32)
    taps_f = gathered[3].astype(jnp.float32)
    taps_bias = gathered[4].astype(jnp.float32)
    feed_f = gathered[11].astype(jnp.float32)
    tokens_f = tokens.astype(jnp.float32)
    scale_first = row_scale(tokens_f)
    normed_first = spread_rows((tokens_f * scale_first[:, None] * mix_f).astype(jnp.bfloat16))
    scan_rows = matmul(normed_first, gathered[1])
    gate_rows = matmul(normed_first, gathered[2])
    gelu_rows, gelu_pull = jax.vjp(smooth_gelu, gate_rows)
    rim_rows = from_behind(scan_rows[row_count - (KW - 1) :], "seq", 1)
    padded_rows = jnp.concatenate([rim_rows, scan_rows], axis=0)
    conv_sum = taps_bias + taps_f[0] * scan_rows
    for lag_step in range(1, KW):
        lagged = padded_rows[KW - 1 - lag_step : KW - 1 - lag_step + row_count]
        conv_sum = conv_sum + jnp.where(
            (offsets >= lag_step)[:, None], taps_f[lag_step] * lagged, 0.0
        )
    conv_rows = conv_sum.astype(jnp.bfloat16)
    lanes = scan_rows.shape[1]
    groups = lanes // BW
    conv_blocks = conv_rows.reshape(row_count, groups, BW)
    decay_mats = gathered[5].reshape(groups, BW, BW)
    input_mats = gathered[7].reshape(groups, BW, BW)
    decay_rows = block_mix(conv_blocks, decay_mats) + gathered[6].astype(jnp.float32)
    input_rows = block_mix(conv_blocks, input_mats) + gathered[8].astype(jnp.float32)

    def local_terms(decay_in, input_in, logit_in, conv_in):
        kept_part, driven_part, decay_part = recurrence_terms(
            decay_in, input_in, logit_in, conv_in, resets
        )
        return ((kept_part, driven_part), decay_part)

    terms_out, terms_pull, decay_now = jax.vjp(
        local_terms,
        decay_rows,
        input_rows,
        gathered[9].astype(jnp.float32),
        conv_rows.astype(jnp.float32),
        has_aux=True,
    )
    kept_decay, driven = terms_out
    local_prod, local_state = lax.associative_scan(combine, (kept_decay, driven), axis=0)
    before = entering(
        (local_prod[row_count - 1], local_state[row_count - 1]),
        "seq",
        combine,
        (jnp.ones((lanes,), jnp.float32), jnp.zeros((lanes,), jnp.float32)),
        False,
    )
    state_in = before[1]
    hidden_state = local_state + local_prod * state_in[None, :]
    mixed = (gelu_rows * hidden_state).astype(jnp.bfloat16)
    resid = tokens_f + reduce_features(matmul(mixed, gathered[10]))
    scale_second = row_scale(resid)
    normed_second = spread_rows((resid * scale_second[:, None] * feed_f).astype(jnp.bfloat16))
    gate_pre = matmul(normed_second, gathered[12])
    up_pre = matmul(normed_second, gathered[13])
    gelu_mid, mid_pull = jax.vjp(smooth_gelu, gate_pre)
    hidden_mid = (gelu_mid * up_pre).astype(jnp.bfloat16)
    block_out = resid + reduce_features(matmul(hidden_mid, gathered[14]))
    cot_full = spread_grads(cotangent)
    down_grad = matmul_tn(hidden_mid, cot_full)
    grad_mid = matmul_nt(cot_full, gathered[14])
    grad_gate = mid_pull(grad_mid * up_pre)[0].astype(jnp.bfloat16)
    grad_up = (grad_mid * gelu_mid).astype(jnp.bfloat16)
    gate_grad = matmul_tn(normed_second, grad_gate)
    up_grad = matmul_tn(normed_second, grad_up)
    grad_second = reduce_features(
        matmul_nt(grad_gate, gathered[12]) + matmul_nt(grad_up, gathered[13])
    )
    back_second, feed_grad = norm_back(resid, scale_second, feed_f, grad_second)
    grad_resid = cotangent.astype(jnp.float32) + back_second
    grad_branch = spread_grads(grad_resid.astype(jnp.bfloat16))
    out_grad = matmul_tn(mixed, grad_branch)
    grad_mixed = matmul_nt(grad_branch, gathered[10])
    grad_hidden = grad_mixed * gelu_rows
    grad_gate_rows = gelu_pull(grad_mixed * hidden_state)[0].astype(jnp.bfloat16)
    next_decay = jnp.concatenate([kept_decay[1:], jnp.ones_like(kept_decay[:1])], axis=0)
    tail_prod, local_adjoint = lax.associative_scan(
        combine, (next_decay, grad_hidden), reverse=True, axis=0
    )
    after = entering(
        (local_prod[row_count - 1], kept_decay[0] * local_adjoint[0]),
        "seq",
        combine,
        (jnp.ones((lanes,), jnp.float32), jnp.zeros((lanes,), jnp.float32)),
        True,
    )
    adjoint_in = after[1]
    adjoint = local_adjoint + tail_prod * adjoint_in[None, :]
    prev_state = jnp.concatenate([state_in[None, :], hidden_state[:-1]], axis=0)
    grad_decay_rows, grad_input_rows, logit_grad, conv_direct = terms_pull(
        (adjoint * prev_state, adjoint)
    )
    decay_grad_low = grad_decay_rows.astype(jnp.bfloat16)
    input_grad_low = grad_input_rows.astype(jnp.bfloat16)
    decay_w_grad = block_outer(conv_blocks, decay_grad_low)
    input_w_grad = block_outer(conv_blocks, input_grad_low)
    decay_b_grad = jnp.sum(decay_grad_low.astype(jnp.float32), axis=0)
    input_b_grad = jnp.sum(input_grad_low.astype(jnp.float32), axis=0)
    grad_conv = (
        conv_direct
        + block_back(decay_grad_low, decay_mats)
        + block_back(input_grad_low, input_mats)
    )
    rim_back = from_behind(grad_conv[: KW - 1], "seq", -1)
    grad_extended = jnp.concatenate([grad_conv, rim_back], axis=0)
    ext_offsets = seq_offsets(lengths, shard_index * row_count, row_count + KW - 1)
    grad_scan = taps_f[0] * grad_conv
    tap_grads = [jnp.sum(grad_conv * scan_rows, axis=0)]
    for lag_step in range(1, KW):
        ahead = grad_extended[lag_step : lag_step + row_count]
        ahead_ok = (ext_offsets[lag_step : lag_step + row_count] >= lag_step)[:, None]
        grad_scan = grad_scan + jnp.where(ahead_ok, taps_f[lag_step] * ahead, 0.0)
        lagged = padded_rows[KW - 1 - lag_step : KW - 1 - lag_step + row_count]
        tap_grads.append(
            jnp.sum(jnp.where((offsets >= lag_step)[:, None], grad_conv * lagged, 0.0), axis=0)
        )
    taps_grad = jnp.stack(tap_grads, axis=0)
    taps_bias_grad = jnp.sum(grad_conv, axis=0)
    scan_grad_low = grad_scan.astype(jnp.bfloat16)
    scan_w_grad = matmul_tn(normed_first, scan_grad_low)
    gatebr_grad = matmul_tn(normed_first, grad_gate_rows)
    grad_first = reduce_features(
        matmul_nt(scan_grad_low, gathered[1]) + matmul_nt(grad_gate_rows, gathered[2])
    )
    back_first, mix_grad = norm_back(tokens_f, scale_first, mix_f, grad_first)
    tokens_grad = grad_resid + back_first
    decay_total = jnp.sum(decay_now, axis=0)
    summed = (
        lax.psum_scatter(mix_grad, "seq", scatter_dimension=0, tiled=True),
        lax.psum_scatter(scan_w_grad, "seq", scatter_dimension=0, tiled=True),
        lax.psum_scatter(gatebr_grad, "seq", scatter_dimension=0, tiled=True),
        lax.psum_scatter(taps_grad, "seq", scatter_dimension=1, tiled=True),
        lax.psum_scatter(taps_bias_grad, "seq", scatter_dimension=0, tiled=True),
        lax.psum_scatter(decay_w_grad, "seq", scatter_dimension=1, tiled=True),
        lax.psum_scatter(decay_b_grad, "seq", scatter_dimension=0, tiled=True),
        lax.psum_scatter(input_w_grad, "seq", scatter_dimension=1, tiled=True),
        lax.psum_scatter(input_b_grad, "seq", scatter_dimension=0, tiled=True),
        lax.psum_scatter(logit_grad, "seq", scatter_dimension=0, tiled=True),
        lax.psum_scatter(out_grad, "seq", scatter_dimension=1, tiled=True),
        lax.psum_scatter(feed_grad, "seq", scatter_dimension=0, tiled=True),
        lax.psum_scatter(gate_grad, "seq", scatter_dimension=0, tiled=True),
        lax.psum_scatter(up_grad, "seq", scatter_dimension=0, tiled=True),
        lax.psum_scatter(down_grad, "seq", scatter_dimension=1, tiled=True),
        lax.psum_scatter(decay_total, "seq", scatter_dimension=0, tiled=True),
    )
    mean_decay = summed[15] / (row_count * seq_devices)
    return (
        block_out,
        tokens_grad,
        summed[0],
        summed[1],
        summed[2],
        summed[3],
        summed[4],
        summed[5],
        summed[6],
        summed[7],
        summed[8],
        summed[9],
        summed[10],
        summed[11],
        summed[12],
        summed[13],
        summed[14],
        mean_decay,
    )


MESH = pl.DeviceIdType.MESH
F32 = jnp.float32
BF16 = jnp.bfloat16
LINE = 4
PLANE = 8
CHUNK = 128
ANY = pl.BlockSpec(memory_space=pl.ANY)
VM = pl.BlockSpec(memory_space=pltpu.VMEM)


def flip(place, bit):
    step = 1 << bit
    return place + step - 2 * step * lax.rem(place // step, 2)


def flip_all(place, bits):
    for bit in range(3):
        if bits & (1 << bit):
            place = flip(place, bit)
    return place


def meet(s, z):
    barrier = pltpu.get_barrier_semaphore()
    for bits in range(1, PLANE):
        pl.semaphore_signal(barrier, inc=1, device_id=(flip_all(s, bits), z), device_id_type=MESH)
    for step in range(1, LINE):
        pl.semaphore_signal(
            barrier, inc=1, device_id=(s, lax.rem(z + step, LINE)), device_id_type=MESH
        )
    pl.semaphore_wait(barrier, PLANE - 1 + LINE - 1)


def remote(src, dst, send, recv, target):
    return pltpu.make_async_remote_copy(
        src_ref=src,
        dst_ref=dst,
        send_sem=send,
        recv_sem=recv,
        device_id=target,
        device_id_type=MESH,
    )


class LineGather:
    def __init__(self, s, z, own_at, full_at, send, recv):
        self.s, self.z = s, z
        self.own_at, self.full_at = own_at, full_at
        self.send, self.recv = send, recv

    def copy(self, way, level, c):
        sign = 1 - 2 * way
        origin = self.z - sign * level
        src = self.own_at(c) if level == 0 else self.full_at(origin, c)
        return remote(
            src,
            self.full_at(origin, c),
            self.send.at[way, level, c],
            self.recv.at[way, level, c],
            (self.s, self.z + sign),
        )

    def arrival(self, way, level, c):
        sign = 1 - 2 * way
        part = self.full_at(self.z - sign * (level + 1), c)
        return remote(
            part,
            part,
            self.send.at[way, level, c],
            self.recv.at[way, level, c],
            (self.s, self.z + sign),
        )

    def sends(self, way, level):
        if way == 0:
            return (self.z >= level) & (self.z < LINE - 1)
        return (self.z <= LINE - 1 - level) & (self.z > 0)

    def gets(self, way, level):
        return self.z >= level + 1 if way == 0 else self.z <= LINE - 2 - level

    def start(self, c):
        for way in range(2):
            pl.when(self.sends(way, 0))(lambda way=way: self.copy(way, 0, c).start())

    def forward(self, level, c):
        for way in range(2):
            pl.when(self.gets(way, level - 1))(
                lambda way=way: self.arrival(way, level - 1, c).wait_recv()
            )
            if level < LINE - 1:
                pl.when(self.sends(way, level))(
                    lambda way=way: self.copy(way, level, c).start()
                )

    def drain(self, c):
        for way in range(2):
            for level in range(LINE - 1):
                pl.when(self.sends(way, level))(
                    lambda way=way, level=level: self.copy(way, level, c).wait_send()
                )


class PlaneGather:
    def __init__(self, s, z, own, block_at, half_at, send, recv, local):
        self.s, self.z, self.own = s, z, own
        self.block_at, self.half_at = block_at, half_at
        self.send, self.recv, self.local = send, recv, local
        self.near = (flip(s, 1), flip(s, 2))
        self.diag = flip(self.near[0], 2)
        self.twin = flip(s, 0)
        self.twin_near = (flip(self.near[0], 0), flip(self.near[1], 0))
        self.twin_diag = flip(self.diag, 0)

    def plan(self, i):
        block, half = self.block_at, self.half_at
        return (
            (self.own, block(self.s), self.near[0]),
            (self.own, block(self.s), self.near[1]),
            (half(self.near[1], 0), half(self.near[1], 0), self.near[0]),
            (half(self.near[0], 1), half(self.near[0], 1), self.near[1]),
            (self.own, block(self.s), self.twin),
            (block(self.near[0]), block(self.near[0]), self.twin),
            (block(self.near[1]), block(self.near[1]), self.twin),
            (half(self.diag, 0), half(self.diag, 0), self.twin),
            (half(self.diag, 1), half(self.diag, 1), self.twin),
        )[i]

    def landing(self, i):
        block, half = self.block_at, self.half_at
        return (
            block(self.near[0]),
            block(self.near[1]),
            half(self.diag, 0),
            half(self.diag, 1),
            block(self.twin),
            block(self.twin_near[0]),
            block(self.twin_near[1]),
            half(self.twin_diag, 0),
            half(self.twin_diag, 1),
        )[i]

    def copy(self, i):
        src, dst, target = self.plan(i)
        return remote(src, dst, self.send.at[i], self.recv.at[i], (target, self.z))

    def got(self, i):
        part = self.landing(i)
        remote(part, part, self.send.at[i], self.recv.at[i], (self.twin, self.z)).wait_recv()

    def keep(self):
        return pltpu.make_async_copy(self.own, self.block_at(self.s), self.local)

    def start(self):
        for i in (0, 1, 4):
            self.copy(i).start()
        self.keep().start()

    def turn(self):
        self.got(0)
        self.copy(3).start()
        self.copy(5).start()
        self.got(1)
        self.copy(2).start()
        self.copy(6).start()

    def last(self):
        self.got(2)
        self.copy(7).start()
        self.got(3)
        self.copy(8).start()

    def arrive(self):
        for i in range(4, 9):
            self.got(i)
        self.keep().wait()

    def drain(self):
        for i in range(9):
            self.copy(i).wait_send()


class Spread:
    def __init__(self, s, z, slot_at, send, recv):
        self.s, self.z, self.slot_at, self.send, self.recv = s, z, slot_at, send, recv

    def copy(self, bits, origin):
        slot = self.slot_at(origin)
        return remote(
            slot,
            slot,
            self.send.at[bits - 1],
            self.recv.at[bits - 1],
            (flip_all(self.s, bits), self.z),
        )

    def start(self):
        for bits in range(1, PLANE):
            self.copy(bits, self.s).start()

    def finish(self):
        for bits in range(1, PLANE):
            self.copy(bits, flip_all(self.s, bits)).wait_recv()
        for bits in range(1, PLANE):
            self.copy(bits, self.s).wait_send()


def rows_of(ref, size, parts=2):
    def block(place):
        return ref.at[pl.ds(pl.multiple_of(place * size, size), size)]

    def half(place, h):
        part = size // parts
        return ref.at[pl.ds(pl.multiple_of(place * size + h * part, part), part)]

    return block, half


def columns_of(ref, size):
    height = ref.shape[0] // 2

    def block(place):
        return ref.at[:, pl.ds(pl.multiple_of(place * size, size), size)]

    def half(place, h):
        return ref.at[
            pl.ds(h * height, height), pl.ds(pl.multiple_of(place * size, size), size)
        ]

    return block, half


def chunk_rows(c):
    return pl.ds(pl.multiple_of(c * CHUNK, CHUNK), CHUNK)


def feature_columns(z, width):
    return pl.ds(pl.multiple_of(z * width, width), width)


def each_chunk(chunks, body):
    lax.fori_loop(0, chunks, lambda c, carry: (body(c), carry)[1], 0)


def dma(*shape):
    return pltpu.SemaphoreType.DMA(shape)


def struct(shape, kind):
    return jax.ShapeDtypeStruct(shape, kind)


def vm(*shape, kind=BF16):
    return pltpu.VMEM(shape, kind)


def sigmoid(values):
    return 0.5 * jnp.tanh(0.5 * values) + 0.5


ROOT = 0.7978845608028654


def gelu_of(values):
    return 0.5 * values * (1.0 + jnp.tanh(ROOT * (values + 0.044715 * values * values * values)))


def gelu_pair(values):
    squared = values * values
    bent = jnp.tanh(ROOT * values * (1.0 + 0.044715 * squared))
    half = 0.5 * (1.0 + bent)
    slope = half + 0.5 * values * (1.0 - bent * bent) * (ROOT * (1.0 + 3 * 0.044715 * squared))
    return values * half, slope


def dot(left_side, right_side):
    return jnp.dot(left_side, right_side, preferred_element_type=F32)


def dot_nt(left_side, right_side):
    return lax.dot_general(
        left_side, right_side, (((1,), (1,)), ((), ())), preferred_element_type=F32
    )


def dot_tn(left_side, right_side):
    return lax.dot_general(
        left_side, right_side, (((0,), (0,)), ((), ())), preferred_element_type=F32
    )


SUBS = 8


LANE = 128


def put(ref, at, values):
    for lane in range(ref.shape[0]):
        ref[lane, at, :] = values[:, lane * LANE : (lane + 1) * LANE]


def get(ref, at):
    return jnp.concatenate([ref[lane, at, :] for lane in range(ref.shape[0])], axis=1)


def strided(ref, step):
    at = pl.ds(step, SUBS, stride=ref.shape[1] // SUBS)
    return [ref[lane, at, :] for lane in range(ref.shape[0])]


def strided_put(ref, step, values):
    at = pl.ds(step, SUBS, stride=ref.shape[1] // SUBS)
    for lane in range(ref.shape[0]):
        ref[lane, at, :] = values[lane]


def lanes_of(values):
    return [values[:, i * LANE : (i + 1) * LANE] for i in range(values.shape[1] // LANE)]


def first_kernel(
    tok, cot, small, gains, gate_blocks, scan, gate, mix, ffn, up, down, masks,
    row_order, tile, cells, lane_order,
    normed, scan_rows, gate_rows, conv, decay_rows, input_rows, hidden, mixed, scales, decay_sum,
    par, gates_w, gain_own, scan_w, gate_w, mix_all, ffn_all, up_all, down_all, cot_all,
    tok_all, small_all, gains_all, blocks_all, gain_full, kept, driven, slots,
    tok_send, tok_recv, cot_send, cot_recv, gain_send, gain_recv, plane_send, plane_recv,
    small_send, small_recv, carry_send, carry_recv, halo_send, halo_recv, local,
):
    s, z = lax.axis_index("seq"), lax.axis_index("tp")
    rows, width = tok.shape
    chunks, features, lanes = rows // CHUNK, width * LINE, gate.shape[1]
    part = gate_blocks.shape[0]

    def line_of(own, full, send, recv):
        return LineGather(
            s, z,
            lambda c: own.at[chunk_rows(c)],
            lambda o, c: full.at[chunk_rows(c), feature_columns(o, width)],
            send, recv,
        )

    toks = line_of(tok, tok_all, tok_send, tok_recv)
    cots = line_of(cot, cot_all, cot_send, cot_recv)
    gain_line = LineGather(
        s, z, lambda c: gains_all.at[z], lambda o, c: gains_all.at[o], gain_send, gain_recv
    )
    planes = []
    for i, (own, full, make) in enumerate(
        (
            (scan, scan_w, rows_of),
            (gate, gate_w, rows_of),
            (mix, mix_all, columns_of),
            (ffn, ffn_all, rows_of),
            (up, up_all, rows_of),
            (down, down_all, columns_of),
        )
    ):
        size = own.shape[1] if make is columns_of else own.shape[0]
        planes.append(
            PlaneGather(s, z, own, *make(full, size), plane_send.at[i], plane_recv.at[i], local.at[i])
        )
    spreads = [
        Spread(s, z, lambda p: gains_all.at[z, p], small_send.at[0], small_recv.at[0]),
        Spread(s, z, lambda p: small_all.at[p], small_send.at[1], small_recv.at[1]),
        Spread(
            s, z, lambda p: blocks_all.at[pl.ds(pl.multiple_of(p * part, 16), part)],
            small_send.at[2], small_recv.at[2],
        ),
    ]
    keep = pltpu.make_async_copy(cot, cot_all.at[:, feature_columns(z, width)], local.at[6])
    keep.start()
    tok_all[:, feature_columns(z, width)] = tok[...]
    gains_all[z, s] = gains[...]
    small_all[s] = small[...]
    blocks_all[pl.ds(pl.multiple_of(s * part, 16), part), :] = gate_blocks[...]
    meet(s, z)
    for spread in spreads:
        spread.start()
    for c in range(chunks):
        toks.start(c)
    for plane in planes[:2]:
        plane.start()
    for spread in spreads:
        spread.finish()
    gain_line.start(0)
    for c in range(chunks):
        toks.forward(1, c)
    gain_line.forward(1, 0)
    planes[2].start()
    planes[3].start()
    placed = dot(
        jnp.concatenate([small_all[p] for p in range(PLANE)], axis=1), lane_order[...]
    )
    par[...] = placed
    falling = jnp.exp(-placed[7:8, :])
    par[7:8, :] = CD * jnp.log1p(falling)
    par[8:9, :] = CD * falling / (1.0 + falling)
    half = blocks_all.shape[1] // 2
    for i in range(2):
        wide = dot(blocks_all[:, i * half : (i + 1) * half], tile[...]).astype(BF16)
        gates_w[:, i * lanes : (i + 1) * lanes] = dot(row_order[...], wide).astype(BF16) * cells[...]
    planes[0].turn()
    planes[1].turn()
    for c in range(chunks):
        toks.forward(2, c)
    gain_line.forward(2, 0)
    planes[0].last()
    planes[1].last()
    planes[4].start()
    gain_line.forward(3, 0)
    pick = lax.broadcasted_iota(jnp.int32, (LANE, LANE), 0)
    place = lax.broadcasted_iota(jnp.int32, (LANE, LANE), 1)
    cut = LANE // 2
    even = jnp.concatenate(
        [gains_all[o, p] for o in range(LINE) for p in range(0, PLANE, 2)], axis=0
    ).astype(BF16)
    odd = jnp.concatenate(
        [gains_all[o, p] for o in range(LINE) for p in range(1, PLANE, 2)], axis=0
    ).astype(BF16)
    for i in range(2):
        from_even = (pick == place + i * cut) & (place < cut)
        from_odd = (pick == place + (i - 1) * cut) & (place >= cut)
        spots = dot(even, from_even.astype(F32).astype(BF16)) + dot(
            odd, from_odd.astype(F32).astype(BF16)
        )
        for q in range(spots.shape[0] // 8):
            gain_full[i : i + 1, q * LANE : (q + 1) * LANE] = spots[8 * q : 8 * q + 1, :]
    gain_own[0:2, :] = gain_full[0:2, feature_columns(z, width)]
    planes[0].arrive()
    planes[1].arrive()

    def project(c):
        toks.forward(3, c)
        cots.start(c)
        at = chunk_rows(c)
        x = tok_all[at, :].astype(F32)
        scale = lax.rsqrt(jnp.sum(x * x, axis=1, keepdims=True) / features + EPSILON)
        scales[at, :] = jnp.broadcast_to(scale, (CHUNK, LANE))
        low = (x * scale * gain_full[0:1, :]).astype(BF16)
        normed[at, :] = low
        scan_rows[pl.ds(pl.multiple_of(c * CHUNK + 8, 8), CHUNK), :] = dot(low, scan_w[...])
        gate_rows[at, :] = dot(low, gate_w[...])

    each_chunk(chunks, project)
    halo = remote(
        scan_rows.at[pl.ds(rows, 8)], scan_rows.at[pl.ds(0, 8)], halo_send, halo_recv,
        (lax.rem(s + 1, PLANE), z),
    )
    first, final = s == 0, s == PLANE - 1
    pl.when(jnp.logical_not(final))(lambda: halo.start())

    @pl.when(first)
    def _():
        scan_rows[0:8, :] = jnp.zeros((8, lanes), F32)

    planes[2].turn()
    planes[3].turn()
    planes[5].start()
    decay_sum[...] = jnp.zeros_like(decay_sum)
    pl.when(jnp.logical_not(first))(lambda: halo.wait_recv())

    def gates(c):
        at = chunk_rows(c)
        block = scan_rows[pl.ds(pl.multiple_of(c * CHUNK, 8), CHUNK + 8), :]
        mask = masks[at, :]
        total = par[4:5, :] + par[0:1, :] * block[8:, :]
        for lag in range(1, KW):
            total = total + mask[:, lag : lag + 1] * (
                par[lag : lag + 1, :] * block[8 - lag : 8 - lag + CHUNK, :]
            )
        low = total.astype(BF16)
        conv[at, :] = low
        rows_now = dot(low, gates_w[...])
        decays = rows_now[:, :lanes] + par[5:6, :]
        inputs = rows_now[:, lanes:] + par[6:7, :]
        decay_rows[at, :] = decays
        input_rows[at, :] = inputs
        decay = jnp.exp(-sigmoid(decays) * par[7:8, :])
        goes_on = mask[:, 0:1]
        multiplier = 1.0 + goes_on * (
            jnp.sqrt(jnp.maximum(1.0 - decay * decay, FLOOR_VALUE)) - 1.0
        )
        put(kept, at, goes_on * decay)
        put(driven, at, multiplier * sigmoid(inputs) * low.astype(F32))
        decay_sum[0:1, :] += jnp.sum(decay, axis=0, keepdims=True)
        cots.forward(1, c)

    each_chunk(chunks, gates)
    planes[2].last()
    planes[3].last()
    planes[4].turn()
    count = rows // SUBS

    def total_of(step, carry):
        keeps, drives = strided(kept, step), strided(driven, step)
        return (
            [p * k for p, k in zip(carry[0], keeps)],
            [k * v + d for k, v, d in zip(keeps, carry[1], drives)],
        )

    groups = lanes // LANE
    product, value = lax.fori_loop(
        0,
        count,
        total_of,
        ([jnp.ones((SUBS, LANE), F32)] * groups, [jnp.zeros((SUBS, LANE), F32)] * groups),
        unroll=4,
    )
    product, value = jnp.concatenate(product, axis=1), jnp.concatenate(value, axis=1)
    whole = (jnp.ones((1, lanes), F32), jnp.zeros((1, lanes), F32))
    for sub in range(SUBS):
        here = product[sub : sub + 1, :]
        whole = (whole[0] * here, here * whole[1] + value[sub : sub + 1, :])
    slots[s, 0:1, :] = whole[0]
    slots[s, 1:2, :] = whole[1]
    spread = Spread(s, z, lambda p: slots.at[p], carry_send, carry_recv)
    spread.start()
    spread.finish()
    entry = jnp.zeros((1, lanes), F32)
    for place in range(PLANE - 1):
        entry = jnp.where(
            place < s, slots[place, 0:1, :] * entry + slots[place, 1:2, :], entry
        )
    hidden[0:8, :] = jnp.broadcast_to(entry, (8, lanes))
    entries = []
    for sub in range(SUBS):
        entries.append(entry)
        entry = product[sub : sub + 1, :] * entry + value[sub : sub + 1, :]

    def step_on(step, now):
        keeps, drives = strided(kept, step), strided(driven, step)
        now = [k * v + d for k, v, d in zip(keeps, now, drives)]
        strided_put(driven, step, now)
        return now

    lax.fori_loop(0, count, step_on, lanes_of(jnp.concatenate(entries, axis=0)), unroll=4)

    def mix(c):
        at = chunk_rows(c)
        now = get(driven, at)
        hidden[pl.ds(pl.multiple_of(c * CHUNK + 8, 8), CHUNK), :] = now
        mixed[at, :] = (gelu_of(gate_rows[at, :]) * now).astype(BF16)
        cots.forward(2, c)

    each_chunk(chunks, mix)
    planes[4].last()
    planes[5].turn()
    for c in range(chunks):
        cots.forward(3, c)
    planes[5].last()
    for plane in planes[2:]:
        plane.arrive()
    for plane in planes:
        plane.drain()
    for c in range(chunks):
        toks.drain(c)
        cots.drain(c)
    gain_line.drain(0)
    pl.when(jnp.logical_not(final))(lambda: halo.wait_send())
    keep.wait()


def first_half(tok, cot, small, gains, gate_blocks, scan, gate, mix, ffn, up, down, masks, consts):
    rows, width = tok.shape
    features, lanes = width * LINE, gate.shape[1]
    chunks = rows // CHUNK
    return pl.pallas_call(
        first_kernel,
        out_shape=(
            struct((rows, features), BF16),
            struct((rows + 8, lanes), F32),
            struct((rows, lanes), F32),
            struct((rows, lanes), BF16),
            struct((rows, lanes), F32),
            struct((rows, lanes), F32),
            struct((rows + 8, lanes), F32),
            struct((rows, lanes), BF16),
            struct((rows, LANE), F32),
            struct((8, lanes), F32),
            struct((16, lanes), F32),
            struct((lanes, 2 * lanes), BF16),
            struct((8, width), F32),
            struct((features, lanes), BF16),
            struct((features, lanes), BF16),
            struct((mix.shape[0], mix.shape[1] * PLANE), BF16),
            struct((ffn.shape[0] * PLANE, ffn.shape[1]), BF16),
            struct((up.shape[0] * PLANE, up.shape[1]), BF16),
            struct((down.shape[0], down.shape[1] * PLANE), BF16),
            struct((rows, features), BF16),
        ),
        in_specs=[VM] * 16,
        out_specs=[VM] * 15 + [ANY] * 5,
        scratch_shapes=[
            vm(rows, features),
            vm(PLANE, *small.shape), vm(LINE, PLANE, *gains.shape, kind=F32),
            vm(PLANE * gate_blocks.shape[0], gate_blocks.shape[1]), vm(8, features, kind=F32),
            vm(lanes // LANE, rows, LANE, kind=F32), vm(lanes // LANE, rows, LANE, kind=F32),
            vm(PLANE, 8, lanes, kind=F32),
            dma(2, LINE - 1, chunks), dma(2, LINE - 1, chunks),
            dma(2, LINE - 1, chunks), dma(2, LINE - 1, chunks),
            dma(2, LINE - 1, 1), dma(2, LINE - 1, 1),
            dma(6, 9), dma(6, 9), dma(3, 7), dma(3, 7), dma(7), dma(7),
            pltpu.SemaphoreType.DMA, pltpu.SemaphoreType.DMA, dma(7),
        ],
        compiler_params=pltpu.CompilerParams(
            collective_id=0, has_side_effects=True, vmem_limit_bytes=60 << 20
        ),
        name="first_half",
    )(tok, cot, small, gains, gate_blocks, scan, gate, mix, ffn, up, down, masks, *consts)


class LineReduce:
    def __init__(self, s, z, part, land, send, recv):
        self.s, self.z, self.part, self.land = s, z, part, land
        self.send, self.recv = send, recv

    def copy(self, way, me, o, c):
        target = me + 1 - 2 * way
        slot = LINE if way == 1 and o == target else o
        return remote(
            self.part.at[c, o],
            self.land.at[c, slot],
            self.send.at[o, c],
            self.recv.at[slot, c],
            (self.s, self.z + 1 - 2 * way),
        )

    def got(self, slot, c):
        part = self.land.at[c, slot]
        remote(part, part, self.send.at[0, c], self.recv.at[slot, c], (self.s, self.z)).wait_recv()

    def hop(self, level, c):
        for way in range(2):
            me = level if way == 0 else LINE - 1 - level
            order = range(LINE - 1, me - 1, -1) if way == 0 else range(me + 1)

            def work(way=way, me=me, order=order):
                for o in order:
                    slot = LINE if way == 1 and o == me else o
                    if level > 0:
                        self.got(slot, c)
                    if o != me:
                        if level > 0:
                            self.part[c, o] = (
                                self.part[c, o].astype(F32) + self.land[c, slot].astype(F32)
                            ).astype(BF16)
                        self.copy(way, me, o, c).start()

            pl.when(self.z == me)(work)

    def landed(self, c, into):
        @pl.when(self.z == 0)
        def _():
            into[...] = self.land[c, LINE].astype(F32)

        @pl.when(self.z > 0)
        def _():
            into[...] = self.land[c, self.z].astype(F32)

        @pl.when((self.z > 0) & (self.z < LINE - 1))
        def _():
            into[...] += self.land[c, LINE].astype(F32)

    def drain(self, c):
        for o in range(LINE):
            part = self.part.at[c, o]
            pl.when(self.z != o)(
                lambda part=part, o=o: remote(
                    part, part, self.send.at[o, c], self.recv.at[0, c], (self.s, self.z)
                ).wait_send()
            )


class LineSpread:
    def __init__(self, s, z, slot_at, send, recv):
        self.s, self.z, self.slot_at, self.send, self.recv = s, z, slot_at, send, recv

    def copy(self, step, origin, c):
        slot = self.slot_at(origin, c)
        target = (self.s, lax.rem(self.z + step, LINE))
        return remote(slot, slot, self.send.at[step - 1, c], self.recv.at[step - 1, c], target)

    def start(self, c):
        for step in range(1, LINE):
            self.copy(step, self.z, c).start()

    def finish(self, c):
        for step in range(1, LINE):
            self.copy(step, lax.rem(self.z + LINE - step, LINE), c).wait_recv()

    def drain(self, c):
        for step in range(1, LINE):
            self.copy(step, self.z, c).wait_send()


class Halves:
    def __init__(self, s, z, src, out, own, send, recv):
        self.s, self.z, self.src, self.out = s, z, src, out
        self.own, self.send, self.recv = own, send, recv

    def keep(self, c):
        at = chunk_rows(c)
        return pltpu.make_async_copy(self.src.at[at], self.out.at[0, at], self.own.at[c])

    def give(self, c):
        at = chunk_rows(c)
        return remote(
            self.src.at[at], self.out.at[1, at], self.send.at[c], self.recv.at[c],
            (flip(self.s, 0), self.z),
        )

    def start(self, c):
        self.keep(c).start()
        self.give(c).start()

    def drain(self, c):
        self.keep(c).wait()
        self.give(c).wait()


def as_row(column):
    return jnp.transpose(jnp.broadcast_to(column, (CHUNK, LANE)))[0:8, :]


def as_columns(row):
    return jnp.transpose(jnp.broadcast_to(row[0:1, :], (LANE, CHUNK)))


def in_range(c, chunks, body):
    pl.when((c >= 0) & (c < chunks))(lambda: body(c))


CUT = 768
AHEAD = 2
GROUP = 2 * CHUNK


def group_rows(g):
    return pl.ds(pl.multiple_of(g * GROUP, GROUP), GROUP)


def feed_kernel(
    mixed, mix_w, tok, gain, gate_w, up_w, down_w, cot,
    resid, scales, coefs, bo_part, gs_part, low_pair, cot_pair, mid_pair, gate_pair, up_pair,
    part, land, low, cots, mid, g_gate, g_up, bo_out, gs_out, gate_v, up_v, down_v,
    acc, bo_acc, gs_acc, inner, squares, inners,
    red_send, red_recv, line_send, line_recv, sq_send, sq_recv, in_send, in_recv,
    own_sem, give_send, give_recv, out_sem, load_sem,
):
    s, z = lax.axis_index("seq"), lax.axis_index("tp")
    rows, width = tok.shape
    chunks, features = rows // CHUNK, width * LINE
    loads = [
        pltpu.make_async_copy(src, dst, load_sem.at[i])
        for i, (src, dst) in enumerate(
            ((gate_w, gate_v), (up_w, up_v), (down_w, down_v), (cot, cots))
        )
    ]
    for load in loads:
        load.start()
    meet(s, z)
    red = LineReduce(s, z, part, land, red_send, red_recv)
    line = LineGather(
        s, z,
        lambda c: low.at[chunk_rows(c), feature_columns(z, width)],
        lambda o, c: low.at[chunk_rows(c), feature_columns(o, width)],
        line_send, line_recv,
    )
    square_spread = LineSpread(s, z, lambda o, c: squares.at[o, c], sq_send, sq_recv)
    inner_spread = LineSpread(s, z, lambda o, c: inners.at[o, c], in_send, in_recv)
    pairs = [
        Halves(s, z, src, out, own_sem.at[i], give_send.at[i], give_recv.at[i])
        for i, (src, out) in enumerate(
            ((low, low_pair), (cots, cot_pair), (mid, mid_pair), (g_gate, gate_pair), (g_up, up_pair))
        )
    ]

    def outs(c):
        return [
            pltpu.make_async_copy(bo_out.at[c], bo_part.at[c], out_sem.at[0, c]),
            pltpu.make_async_copy(gs_out.at[c], gs_part.at[c], out_sem.at[1, c]),
        ]

    def project(c):
        values = dot(mixed[chunk_rows(c), :], mix_w[...])
        for o in range(LINE):
            here = values[:, o * width : (o + 1) * width]
            part[c, o] = here.astype(BF16)

            @pl.when(z == o)
            def _(here=here):
                resid[chunk_rows(c), :] = here

        red.hop(0, c)

    for c in range(AHEAD):
        project(c)

    def reduced(c):
        at = chunk_rows(c)
        red.hop(3, c)
        red.landed(c, acc)
        values = tok[at, :].astype(F32) + (resid[at, :] + acc[...])
        resid[at, :] = values
        squares[z, c] = as_row(jnp.sum(values * values, axis=1, keepdims=True))
        square_spread.start(c)

    def scaled(c):
        at = chunk_rows(c)
        square_spread.finish(c)
        sums = squares[0, c] + squares[1, c] + squares[2, c] + squares[3, c]
        scale = lax.rsqrt(as_columns(sums) / features + EPSILON)
        scales[at, :] = scale
        low[at, feature_columns(z, width)] = (resid[at, :] * scale[:, 0:1] * gain[1:2, :]).astype(
            BF16
        )
        line.start(c)

    def forward(cut, g):
        at = group_rows(g)
        cols = slice(cut * CUT, (cut + 1) * CUT)
        x = low[at, :]
        gate_pre, up_pre = dot(x, gate_v[:, cols]), dot(x, up_v[:, cols])
        act, slope = gelu_pair(gate_pre)
        here = (act * up_pre).astype(BF16)
        mid[at, cols] = here
        grad = dot_nt(cots[at, :], down_v[cols, :])
        gate_grad = (grad * up_pre * slope).astype(BF16)
        up_grad = (grad * act).astype(BF16)
        g_gate[at, cols] = gate_grad
        g_up[at, cols] = up_grad
        products = jnp.sum(
            gate_grad.astype(F32) * gate_pre + up_grad.astype(F32) * up_pre, axis=1, keepdims=True
        )
        if cut == 0:
            inner[...] = products
        else:
            inner[...] += products

    def backward(cut, g):
        at = group_rows(g)
        cols = slice(cut * CUT, (cut + 1) * CUT)
        block = dot(mid[at, cols], down_v[cols, :])
        back = dot_nt(g_gate[at, cols], gate_v[:, cols]) + dot_nt(g_up[at, cols], up_v[:, cols])
        if cut == 0:
            bo_acc[...] = block
            gs_acc[...] = back
            return
        block = bo_acc[...] + block
        back = gs_acc[...] + back
        for k in range(GROUP // CHUNK):
            c = g * (GROUP // CHUNK) + k
            here = slice(k * CHUNK, (k + 1) * CHUNK)
            for o in range(LINE):
                bo_out[c, o] = block[here, o * width : (o + 1) * width].astype(BF16)
                gs_out[c, o] = back[here, o * width : (o + 1) * width].astype(BF16)
            inners[z, c] = as_row(inner[here, :])
            inner_spread.start(c)
            for pair in pairs:
                pair.start(c)
            for copy in outs(c):
                copy.start()

    def turn(t, carry):
        g, odd = (t - 4) // 2, lax.rem(t, 2) == 1
        ready = t >= 4
        pl.when(t == 3)(lambda: [load.wait() for load in loads] and None)
        in_range(t, chunks, lambda c: red.hop(1, c))
        in_range(t - 2, chunks, lambda c: line.forward(1, c))
        in_range(t - 3, chunks, lambda c: line.forward(3, c))
        pl.when(ready & jnp.logical_not(odd))(lambda: forward(0, g))
        pl.when(ready & odd)(lambda: forward(1, g))
        in_range(t - 1, chunks, reduced)
        in_range(t - 1, chunks, scaled)
        in_range(t - 2, chunks, lambda c: line.forward(2, c))
        pl.when(ready & jnp.logical_not(odd))(lambda: backward(0, g))
        in_range(t, chunks, lambda c: red.hop(2, c))
        in_range(t + AHEAD, chunks, project)
        pl.when(ready & odd)(lambda: backward(1, g))
        return carry

    lax.fori_loop(0, chunks + 4, turn, 0)

    def close(c):
        at = chunk_rows(c)
        inner_spread.finish(c)
        sums = inners[0, c] + inners[1, c] + inners[2, c] + inners[3, c]
        scale = scales[at, :]
        coefs[at, :] = scale * scale * as_columns(sums) / features
        red.drain(c)
        line.drain(c)
        square_spread.drain(c)
        inner_spread.drain(c)
        for pair in pairs:
            pair.drain(c)
        for copy in outs(c):
            copy.wait()

    each_chunk(chunks, close)


def feed_forward(mixed, mix_w, tok, gain, gate_w, up_w, down_w, cot):
    rows, width = tok.shape
    features, hidden = width * LINE, gate_w.shape[1]
    chunks = rows // CHUNK
    blocks = struct((chunks, LINE, CHUNK, width), BF16)

    def pair(size):
        return struct((2, rows, size), BF16)

    return pl.pallas_call(
        feed_kernel,
        out_shape=(
            struct((rows, width), F32),
            struct((rows, LANE), F32),
            struct((rows, LANE), F32),
            blocks, blocks,
            pair(features), pair(features), pair(hidden), pair(hidden), pair(hidden),
        ),
        in_specs=[VM] * 4 + [ANY] * 4,
        out_specs=[VM] * 3 + [ANY] * 7,
        scratch_shapes=[
            vm(chunks, LINE, CHUNK, width), vm(chunks, LINE + 1, CHUNK, width),
            vm(rows, features), vm(rows, features),
            vm(rows, hidden), vm(rows, hidden), vm(rows, hidden),
            vm(chunks, LINE, CHUNK, width), vm(chunks, LINE, CHUNK, width),
            vm(features, hidden), vm(features, hidden), vm(hidden, features),
            vm(CHUNK, width, kind=F32), vm(GROUP, features, kind=F32),
            vm(GROUP, features, kind=F32), vm(GROUP, 1, kind=F32),
            vm(LINE, chunks, 8, LANE, kind=F32), vm(LINE, chunks, 8, LANE, kind=F32),
            dma(LINE, chunks), dma(LINE + 1, chunks),
            dma(2, LINE - 1, chunks), dma(2, LINE - 1, chunks),
            dma(LINE - 1, chunks), dma(LINE - 1, chunks),
            dma(LINE - 1, chunks), dma(LINE - 1, chunks),
            dma(5, chunks), dma(5, chunks), dma(5, chunks), dma(2, chunks), dma(4),
        ],
        compiler_params=pltpu.CompilerParams(
            collective_id=2, has_side_effects=True, vmem_limit_bytes=63 << 20
        ),
        name="feed_forward",
    )(mixed, mix_w, tok, gain, gate_w, up_w, down_w, cot)


class WeightGrads:
    def __init__(self, s, z, stage, land, own, send, recv, back):
        self.s, self.z = s, z
        self.stage, self.land, self.own = stage, land, own
        self.send, self.recv, self.back_sem = send, recv, back

    def owner(self, k):
        return flip_all(self.s, 2 * (k + 1)) if k < 3 else self.s

    def copy(self, k):
        return remote(
            self.stage.at[k], self.land.at[k], self.send.at[k], self.recv.at[k],
            (self.owner(k), self.z),
        )

    def block(self, k, left, right):
        size = self.own.shape[0]
        columns = feature_columns(self.owner(k), size)
        value = dot_tn(left[:, columns], right[...])
        if k == 3:
            self.own[...] = value
        else:
            self.stage[k] = value.astype(BF16)
            self.copy(k).start()

    def finish(self):
        backs = [
            pltpu.make_async_copy(self.land.at[k], self.stage.at[k], self.back_sem.at[k])
            for k in range(3)
        ]
        for k in range(3):
            self.copy(k).wait()
            backs[k].start()
        for back in backs:
            back.wait()
        self.own[...] += (
            self.stage[0].astype(F32) + self.stage[1].astype(F32) + self.stage[2].astype(F32)
        )


def back_kernel(
    resid, scales, coefs, cot, gain, gs_part, bo_part, low_pair, cot_pair, mid_pair, gate_pair, up_pair,
    grad, grad_all, out, gain_grad, gate_own, up_own, down_own, lands,
    part, land, part_bo, land_bo, low, acc, left, right, stages,
    red_send, red_recv, bo_send, bo_recv, line_send, line_recv, w_send, w_recv, w_back, load_sem, out_sem,
):
    s, z = lax.axis_index("seq"), lax.axis_index("tp")
    rows, width = cot.shape
    chunks = rows // CHUNK
    loads = [
        pltpu.make_async_copy(src, dst, load_sem.at[i])
        for i, (src, dst) in enumerate(
            (
                (gs_part, part), (bo_part, part_bo),
                (cot_pair, left.at[0]), (mid_pair, right.at[0]),
                (low_pair, left.at[1]), (gate_pair, right.at[1]),
            )
        )
    ]
    late = pltpu.make_async_copy(up_pair, right.at[0], load_sem.at[6])
    for load in loads:
        load.start()
    meet(s, z)
    red = LineReduce(s, z, part, land, red_send, red_recv)
    red_bo = LineReduce(s, z, part_bo, land_bo, bo_send, bo_recv)
    line = LineGather(
        s, z,
        lambda c: low.at[chunk_rows(c), feature_columns(z, width)],
        lambda o, c: low.at[chunk_rows(c), feature_columns(o, width)],
        line_send, line_recv,
    )
    weights = [
        WeightGrads(s, z, stages.at[i], lands.at[i], own, w_send.at[i], w_recv.at[i], w_back.at[i])
        for i, own in enumerate((down_own, gate_own, up_own))
    ]
    gain_grad[...] = jnp.zeros_like(gain_grad)
    loads[0].wait()
    for c in range(AHEAD):
        red.hop(0, c)
    for load in loads[1:]:
        load.wait()

    def reduced(c):
        at = chunk_rows(c)
        red.hop(3, c)
        red.landed(c, acc)
        up = acc[...] + part[c, z].astype(F32)
        scale, values = scales[at, 0:1], resid[at, :]
        gain_grad[0:1, :] += jnp.sum(up * values * scale, axis=0, keepdims=True)
        total = cot[at, :].astype(F32) + scale * gain[1:2, :] * up - values * coefs[at, 0:1]
        grad[at, :] = total
        low[at, feature_columns(z, width)] = total.astype(BF16)
        line.start(c)

    def result(c):
        at = chunk_rows(c)
        red_bo.hop(3, c)
        red_bo.landed(c, acc)
        out[at, :] = resid[at, :] + (acc[...] + part_bo[c, z].astype(F32))

    def keep(c):
        at = chunk_rows(c)
        return pltpu.make_async_copy(low.at[at], grad_all.at[at], out_sem.at[c])

    def arrived(c):
        line.forward(3, c)
        keep(c).start()

    def weigh(t):
        for k in range(4):
            pl.when(t == k)(lambda k=k: weights[0].block(k, left.at[0], right.at[0]))
            pl.when(t == 4 + k)(lambda k=k: weights[1].block(k, left.at[1], right.at[1]))
            pl.when(t == 8 + k)(lambda k=k: weights[2].block(k, left.at[1], right.at[0]))
        pl.when(t == 4)(lambda: late.start())
        pl.when(t == 7)(lambda: late.wait())

    def turn(t, carry):
        in_range(t, chunks, lambda c: red.hop(1, c))
        in_range(t - 2, chunks, lambda c: line.forward(1, c))
        in_range(t - 3, chunks, arrived)
        in_range(t - 5, chunks, lambda c: red_bo.hop(1, c))
        weigh(t)
        in_range(t - 1, chunks, reduced)
        in_range(t - 2, chunks, lambda c: line.forward(2, c))
        in_range(t - 6, chunks, result)
        in_range(t, chunks, lambda c: red.hop(2, c))
        in_range(t - 5, chunks, lambda c: red_bo.hop(2, c))
        in_range(t + AHEAD, chunks, lambda c: red.hop(0, c))
        in_range(t - 3, chunks, lambda c: red_bo.hop(0, c))
        return carry

    lax.fori_loop(0, chunks + 7, turn, 0)
    for weight in weights:
        weight.finish()

    def close(c):
        red.drain(c)
        red_bo.drain(c)
        line.drain(c)
        keep(c).wait()

    each_chunk(chunks, close)


def back_feed(resid, scales, coefs, cot, gain, gs_part, bo_part, pairs):
    rows, width = cot.shape
    features, hidden = width * LINE, pairs[2].shape[2]
    chunks, part = rows // CHUNK, features // PLANE
    blocks = vm(chunks, LINE, CHUNK, width)
    landing = vm(chunks, LINE + 1, CHUNK, width)
    return pl.pallas_call(
        back_kernel,
        out_shape=(
            struct((rows, width), F32),
            struct((rows, features), BF16),
            struct((rows, width), F32),
            struct((8, width), F32),
            struct((part, hidden), F32),
            struct((part, hidden), F32),
            struct((part, hidden), F32),
            struct((3, 3, part, hidden), BF16),
        ),
        in_specs=[VM] * 5 + [ANY] * 7,
        out_specs=[VM, ANY] + [VM] * 5 + [ANY],
        scratch_shapes=[
            blocks, landing, blocks, landing,
            vm(rows, features), vm(CHUNK, width, kind=F32),
            vm(2, 2 * rows, features), vm(2, 2 * rows, hidden), vm(3, 3, part, hidden),
            dma(LINE, chunks), dma(LINE + 1, chunks), dma(LINE, chunks), dma(LINE + 1, chunks),
            dma(2, LINE - 1, chunks), dma(2, LINE - 1, chunks),
            dma(3, 3), dma(3, 3), dma(3, 3), dma(7), dma(chunks),
        ],
        compiler_params=pltpu.CompilerParams(
            collective_id=3, has_side_effects=True, vmem_limit_bytes=63 << 20
        ),
        name="back_feed",
    )(
        resid, scales, coefs, cot, gain, gs_part, bo_part,
        *[pair.reshape(2 * rows, pair.shape[2]) for pair in pairs],
    )


def recur_back_kernel(
    low, mix_w, gate_rows, hidden, conv, decay_rows, input_rows, scan_rows, masks, par, gates_w, scales,
    normed_src, mixed_src, low_src,
    gates_grad, sums, coefs, normed_twin, mixed_twin, low_twin, scan_pair, gate_pair,
    kept, grads, spilled, both, conv_grad, scan_low, gate_low, slots, inners,
    small_send, small_recv, halo_send, halo_recv, in_send, in_recv,
    own_sem, give_send, give_recv, twin_send, twin_recv,
):
    s, z = lax.axis_index("seq"), lax.axis_index("tp")
    rows, features = low.shape
    lanes = gate_rows.shape[1]
    chunks = rows // CHUNK
    wholes = [
        remote(src, out, twin_send.at[i], twin_recv.at[i], (flip(s, 0), z))
        for i, (src, out) in enumerate(
            ((normed_src, normed_twin), (mixed_src, mixed_twin), (low_src, low_twin))
        )
    ]
    pairs = [
        Halves(s, z, src, out, own_sem.at[i], give_send.at[i], give_recv.at[i])
        for i, (src, out) in enumerate(((scan_low, scan_pair), (gate_low, gate_pair)))
    ]
    inner_spread = LineSpread(s, z, lambda o, c: inners.at[o, c], in_send, in_recv)
    meet(s, z)
    for whole in wholes:
        whole.start()
    sums[...] = jnp.zeros_like(sums)

    def start(g):
        at = group_rows(g)
        grad = dot_nt(low[at, :], mix_w[...])
        for k in range(GROUP // CHUNK):
            c = g * (GROUP // CHUNK) + k
            here = chunk_rows(c)
            act, slope = gelu_pair(gate_rows[here, :])
            now = hidden[pl.ds(pl.multiple_of(c * CHUNK + 8, 8), CHUNK), :]
            part = grad[k * CHUNK : (k + 1) * CHUNK, :]
            gate_low[here, :] = (part * now * slope).astype(BF16)
            put(grads, here, part * act)
            decay = jnp.exp(-sigmoid(decay_rows[here, :]) * par[7:8, :])
            put(kept, here, masks[here, 0:1] * decay)

    lax.fori_loop(0, rows // GROUP, lambda g, carry: (start(g), carry)[1], 0)
    for c in range(chunks):
        pairs[1].start(c)
    count, groups = rows // SUBS, lanes // LANE

    def total_of(step, carry):
        keeps, adds = strided(kept, count - 1 - step), strided(grads, count - 1 - step)
        return (
            [p * k for p, k in zip(carry[0], keeps)],
            [k * (v + a) for k, v, a in zip(keeps, carry[1], adds)],
        )

    product, value = lax.fori_loop(
        0,
        count,
        total_of,
        ([jnp.ones((SUBS, LANE), F32)] * groups, [jnp.zeros((SUBS, LANE), F32)] * groups),
        unroll=4,
    )
    product, value = jnp.concatenate(product, axis=1), jnp.concatenate(value, axis=1)
    whole = (jnp.ones((1, lanes), F32), jnp.zeros((1, lanes), F32))
    for sub in range(SUBS - 1, -1, -1):
        here = product[sub : sub + 1, :]
        whole = (whole[0] * here, here * whole[1] + value[sub : sub + 1, :])
    slots[s, 0:1, :] = whole[0]
    slots[s, 1:2, :] = whole[1]
    spread = Spread(s, z, lambda p: slots.at[p], small_send, small_recv)
    spread.start()
    spread.finish()
    entry = jnp.zeros((1, lanes), F32)
    for place in range(PLANE - 1, 0, -1):
        entry = jnp.where(
            place > s, slots[place, 0:1, :] * entry + slots[place, 1:2, :], entry
        )
    entries = []
    for sub in range(SUBS - 1, -1, -1):
        entries.append(entry)
        entry = product[sub : sub + 1, :] * entry + value[sub : sub + 1, :]

    def step_back(step, now):
        keeps, adds = strided(kept, count - 1 - step), strided(grads, count - 1 - step)
        now = [v + a for v, a in zip(now, adds)]
        strided_put(grads, count - 1 - step, now)
        return [k * v for k, v in zip(keeps, now)]

    lax.fori_loop(
        0, count, step_back, lanes_of(jnp.concatenate(entries[::-1], axis=0)), unroll=4
    )

    def gates(c):
        at = chunk_rows(c)
        tall = pl.ds(pl.multiple_of(c * CHUNK, 8), CHUNK + 8)
        adjoint = get(grads, at)
        before = hidden[tall, :][7 : 7 + CHUNK, :]
        mask = masks[at, :]
        goes_on = mask[:, 0:1]
        opened = sigmoid(decay_rows[at, :])
        entered = sigmoid(input_rows[at, :])
        rate = par[7:8, :]
        decay = jnp.exp(-opened * rate)
        room = 1.0 - decay * decay
        root = jnp.sqrt(jnp.maximum(room, FLOOR_VALUE))
        multiplier = 1.0 + goes_on * (root - 1.0)
        conv_f = conv[at, :].astype(F32)
        direct = adjoint * multiplier
        grad_input = (direct * conv_f * (entered * (1.0 - entered))).astype(BF16)
        through = jnp.where(
            room > FLOOR_VALUE, 1.0, jnp.where(room == FLOOR_VALUE, 0.5, 0.0)
        )
        grad_decay = goes_on * (
            adjoint * before - adjoint * entered * conv_f * (through * decay / root)
        )
        scaled = grad_decay * decay * opened
        grad_rows = (-scaled * rate * (1.0 - opened)).astype(BF16)
        joined = jnp.concatenate([grad_rows, grad_input], axis=1)
        both[at, :] = joined
        grad_conv = direct * entered + dot_nt(joined, gates_w[...])
        conv_grad[at, :] = grad_conv
        block = scan_rows[tall, :]
        sums[0:1, :] += jnp.sum(grad_conv * block[8:, :], axis=0, keepdims=True)
        for lag in range(1, KW):
            sums[lag : lag + 1, :] += jnp.sum(
                mask[:, lag : lag + 1] * (grad_conv * block[8 - lag : 8 - lag + CHUNK, :]),
                axis=0,
                keepdims=True,
            )
        sums[4:5, :] += jnp.sum(grad_conv, axis=0, keepdims=True)
        sums[5:6, :] += jnp.sum(grad_rows.astype(F32), axis=0, keepdims=True)
        sums[6:7, :] += jnp.sum(grad_input.astype(F32), axis=0, keepdims=True)
        sums[7:8, :] += jnp.sum(scaled, axis=0, keepdims=True)

    each_chunk(chunks, gates)
    halo = remote(
        conv_grad.at[pl.ds(0, 8)], conv_grad.at[pl.ds(rows, 8)], halo_send, halo_recv,
        (lax.rem(s + PLANE - 1, PLANE), z),
    )
    first, final = s == 0, s == PLANE - 1
    pl.when(jnp.logical_not(first))(lambda: halo.start())
    gates_grad[...] = dot_tn(conv[...], both[...])
    sums[7:8, :] = sums[7:8, :] * par[8:9, :]

    @pl.when(final)
    def _():
        conv_grad[rows : rows + 8, :] = jnp.zeros((8, lanes), F32)

    pl.when(jnp.logical_not(final))(lambda: halo.wait_recv())

    def finish(c):
        at = chunk_rows(c)
        tall = pl.ds(pl.multiple_of(c * CHUNK, 8), CHUNK + 8)
        block, mask = conv_grad[tall, :], masks[tall, :]
        total = par[0:1, :] * block[:CHUNK, :]
        for lag in range(1, KW):
            total = total + mask[lag : lag + CHUNK, lag : lag + 1] * (
                par[lag : lag + 1, :] * block[lag : lag + CHUNK, :]
            )
        grad = total.astype(BF16)
        scan_low[at, :] = grad
        pairs[0].start(c)
        products = grad.astype(F32) * scan_rows[
            pl.ds(pl.multiple_of(c * CHUNK + 8, 8), CHUNK), :
        ] + gate_low[at, :].astype(F32) * gate_rows[at, :]
        inners[z, c] = as_row(jnp.sum(products, axis=1, keepdims=True))
        inner_spread.start(c)

    each_chunk(chunks, finish)

    def close(c):
        at = chunk_rows(c)
        inner_spread.finish(c)
        total = inners[0, c] + inners[1, c] + inners[2, c] + inners[3, c]
        scale = scales[at, :]
        coefs[at, :] = scale * scale * as_columns(total) / features
        inner_spread.drain(c)
        for pair in pairs:
            pair.drain(c)

    each_chunk(chunks, close)
    for whole in wholes:
        whole.wait()
    pl.when(jnp.logical_not(first))(lambda: halo.wait_send())


def recur_back(low, mix_w, gate_rows, hidden, conv, decay_rows, input_rows, scan_rows, masks, par,
               gates_w, scales, normed, mixed):
    rows, features = low.shape
    lanes = gate_rows.shape[1]
    chunks = rows // CHUNK

    def pair(size):
        return struct((2, rows, size), BF16)

    return pl.pallas_call(
        recur_back_kernel,
        out_shape=(
            struct((lanes, 2 * lanes), F32),
            struct((8, lanes), F32),
            struct((rows, LANE), F32),
            struct((rows, features), BF16), struct((rows, lanes), BF16), struct((rows, features), BF16),
            pair(lanes), pair(lanes),
        ),
        in_specs=[VM] * 12 + [ANY] * 3,
        out_specs=[VM] * 3 + [ANY] * 5,
        scratch_shapes=[
            vm(lanes // LANE, rows, LANE, kind=F32), vm(lanes // LANE, rows, LANE, kind=F32),
            vm(8, LANE, kind=F32),
            vm(rows, 2 * lanes), vm(rows + 8, lanes, kind=F32), vm(rows, lanes), vm(rows, lanes),
            vm(PLANE, 8, lanes, kind=F32), vm(LINE, chunks, 8, LANE, kind=F32),
            dma(7), dma(7), pltpu.SemaphoreType.DMA, pltpu.SemaphoreType.DMA,
            dma(LINE - 1, chunks), dma(LINE - 1, chunks),
            dma(2, chunks), dma(2, chunks), dma(2, chunks), dma(3), dma(3),
        ],
        compiler_params=pltpu.CompilerParams(
            collective_id=4, has_side_effects=True, vmem_limit_bytes=60 << 20
        ),
        name="recur_back",
    )(
        low, mix_w, gate_rows, hidden, conv, decay_rows, input_rows, scan_rows, masks, par, gates_w,
        scales, normed, mixed, low,
    )


def last_kernel(
    scan_w, gate_w, grad, tok, coefs, scales, gain, scan_low, gate_low, pack,
    normed, normed_twin, mixed, mixed_twin, low, low_twin, scan_pair, gate_pair,
    tokens_grad, gain_grad, pack_sum, mix_own, scan_own, gate_own, lands,
    part, land, acc, left, right, stages, pack_land, gain_land,
    red_send, red_recv, w_send, w_recv, w_back, load_sem, pack_send, pack_recv, gain_send, gain_recv,
):
    s, z = lax.axis_index("seq"), lax.axis_index("tp")
    rows, width = tok.shape
    chunks = rows // CHUNK
    loads = [
        pltpu.make_async_copy(src, dst, load_sem.at[i])
        for i, (src, dst) in enumerate(
            (
                (low, left.at[0, :rows]), (low_twin, left.at[0, rows:]),
                (mixed, right.at[0, :rows]), (mixed_twin, right.at[0, rows:]),
                (normed, left.at[1, :rows]), (normed_twin, left.at[1, rows:]),
                (scan_pair, right.at[1]), (gate_pair, right.at[2]),
            )
        )
    ]
    for load in loads:
        load.start()
    meet(s, z)
    packs = [
        remote(
            pack.at[flip_all(s, bits)], pack_land.at[s], pack_send.at[bits - 1],
            pack_recv.at[bits - 1], (flip_all(s, bits), z),
        )
        for bits in range(1, PLANE)
    ]
    for copy in packs:
        copy.start()
    red = LineReduce(s, z, part, land, red_send, red_recv)
    weights = [
        WeightGrads(s, z, stages.at[i], lands.at[i], own, w_send.at[i], w_recv.at[i], w_back.at[i])
        for i, own in enumerate((mix_own, scan_own, gate_own))
    ]
    gain_land[s] = jnp.zeros_like(gain_grad)

    def project(g):
        at = group_rows(g)
        values = dot_nt(scan_low[at, :], scan_w[...]) + dot_nt(gate_low[at, :], gate_w[...])
        for k in range(GROUP // CHUNK):
            c = g * (GROUP // CHUNK) + k
            here = slice(k * CHUNK, (k + 1) * CHUNK)
            for o in range(LINE):
                part[c, o] = values[here, o * width : (o + 1) * width].astype(BF16)
            red.hop(0, c)

    def reduced(c):
        at = chunk_rows(c)
        red.hop(3, c)
        red.landed(c, acc)
        up = acc[...] + part[c, z].astype(F32)
        scale, values = scales[at, 0:1], tok[at, :].astype(F32)
        gain_land[s, 0:1, :] += jnp.sum(up * values * scale, axis=0, keepdims=True)
        tokens_grad[at, :] = (
            grad[at, :] + scale * gain[0:1, :] * up - values * coefs[at, 0:1]
        )

    project(0)
    for load in loads:
        load.wait()

    def weigh(t):
        for k in range(4):
            pl.when(t == k)(lambda k=k: weights[1].block((k + 3) % 4, left.at[1], right.at[1]))
            pl.when(t == k)(lambda k=k: weights[2].block((k + 3) % 4, left.at[1], right.at[2]))
            pl.when(t == 4 + k // 2)(lambda k=k: weights[0].block(k, left.at[0], right.at[0]))

    def turn(t, carry):
        in_range(t, chunks, lambda c: red.hop(1, c))
        pl.when((lax.rem(t, 2) == 0) & (t < chunks - 2))(lambda: project(t // 2 + 1))
        weigh(t)
        in_range(t - 1, chunks, reduced)
        in_range(t, chunks, lambda c: red.hop(2, c))
        return carry

    lax.fori_loop(0, chunks + 1, turn, 0)
    gain_spread = Spread(s, z, lambda p: gain_land.at[p], gain_send, gain_recv)
    gain_spread.start()
    for bits in range(1, PLANE):
        other = pack_land.at[flip_all(s, bits)]
        remote(
            other, other, pack_send.at[bits - 1], pack_recv.at[bits - 1], (flip_all(s, bits), z)
        ).wait_recv()
    total = pack[s]
    for bits in range(1, PLANE):
        total = total + pack_land[flip_all(s, bits)]
    pack_sum[...] = total
    for weight in weights:
        weight.finish()
    gain_spread.finish()
    total = gain_land[0]
    for place in range(1, PLANE):
        total = total + gain_land[place]
    gain_grad[...] = total
    for copy in packs:
        copy.wait_send()
    each_chunk(chunks, red.drain)


def last_reduce(scan_w, gate_w, grad, tok, coefs, scales, gain, scan_low, gate_low, pack, pairs):
    rows, width = tok.shape
    features, lanes = width * LINE, scan_w.shape[1]
    chunks, part = rows // CHUNK, features // PLANE
    return pl.pallas_call(
        last_kernel,
        out_shape=(
            struct((rows, width), F32),
            struct((8, width), F32),
            struct(pack.shape[1:], F32),
            struct((part, lanes), F32),
            struct((part, lanes), F32),
            struct((part, lanes), F32),
            struct((3, 3, part, lanes), BF16),
        ),
        in_specs=[VM] * 10 + [ANY] * 8,
        out_specs=[VM] * 6 + [ANY],
        scratch_shapes=[
            vm(chunks, LINE, CHUNK, width), vm(chunks, LINE + 1, CHUNK, width),
            vm(CHUNK, width, kind=F32),
            vm(2, 2 * rows, features), vm(3, 2 * rows, lanes), vm(3, 3, part, lanes),
            vm(*pack.shape, kind=F32), vm(PLANE, 8, width, kind=F32),
            dma(LINE, chunks), dma(LINE + 1, chunks),
            dma(3, 3), dma(3, 3), dma(3, 3), dma(8), dma(7), dma(7), dma(7), dma(7),
        ],
        compiler_params=pltpu.CompilerParams(
            collective_id=5, has_side_effects=True, vmem_limit_bytes=63 << 20
        ),
        name="last_reduce",
    )(
        scan_w, gate_w, grad, tok, coefs, scales, gain, scan_low, gate_low, pack,
        *pairs[:6],
        *[pair.reshape(2 * rows, pair.shape[2]) for pair in pairs[6:]],
    )


def placements(lanes, groups, seq_devices):
    cut, part = BW // seq_devices, lanes // seq_devices
    rows = np.arange(lanes)
    source = (rows % BW) // cut * part + rows // BW * cut + rows % cut
    row_order = (source[:, None] == rows[None, :]).astype(np.float32)
    tile = (np.arange(2 * LANE)[:, None] == rows[None, :] % BW).astype(np.float32)
    cells = (rows[:, None] // BW == rows[None, :] // BW).astype(np.float32)
    spots = np.arange(seq_devices * LANE)
    lane_order = (
        (rows[None, :] // part == spots[:, None] // LANE)
        & (rows[None, :] % part == spots[:, None] % LANE)
    ).astype(np.float32)
    return tuple(jnp.asarray(m, BF16) for m in (row_order, tile, cells, lane_order))


def shards_fast(
    tokens, mix_gain, scan_branch, gate_branch, kernel_taps, kernel_bias, decay_gate, decay_bias,
    input_gate, input_bias, decay_logit, mixer_out, feed_gain, gate_weight, up_weight, down_weight,
    lengths, cotangent,
):
    row_count, width = tokens.shape
    seq_devices = lax.axis_size("seq")
    shard_index = lax.axis_index("seq")
    ext_offsets = seq_offsets(lengths, shard_index * row_count, row_count + 8)
    lag_at = jnp.array([1, 1, 2, 3, 0, 0, 0, 0], jnp.int32)
    masks = (ext_offsets[:, None] >= lag_at[None, :]).astype(F32)
    lanes = scan_branch.shape[1]
    part = lanes // seq_devices
    groups = lanes // BW
    consts = placements(lanes, groups, seq_devices)
    small = jnp.concatenate(
        [
            kernel_taps, kernel_bias[None], decay_bias[None], input_bias[None], decay_logit[None],
            jnp.zeros((8, part), BF16),
        ]
    )
    small = jnp.pad(small, ((0, 0), (0, LANE - part)))
    gains = jnp.pad(
        jnp.concatenate([mix_gain, feed_gain]).astype(F32)[None, :], ((0, 7), (0, 0))
    )
    pad = ((0, 0), (0, 2 * LANE - BW))
    gate_blocks = jnp.concatenate(
        [jnp.pad(m.reshape(part, BW), pad) for m in (decay_gate, input_gate)], 1
    )
    (
        normed_first, scan_pad, gate_rows, conv_rows, decay_rows, input_rows, hidden_state, mixed,
        scale_first_rows, decay_sums, par, gates_w, gain_own, scan_w, gate_w, mix_w, ffn_gate, up_w, down_w, cot_full,
    ) = first_half(
        tokens, cotangent, small, gains, gate_blocks, scan_branch, gate_branch, mixer_out, gate_weight,
        up_weight, down_weight, masks, consts,
    )
    resid, scales, coefs, bo_part, gs_part, low_pair, cot_pair, mid_pair, gate_pair, up_pair = (
        feed_forward(mixed, mix_w, tokens, gain_own, ffn_gate, up_w, down_w, cot_full)
    )
    grad_resid, grad_branch, block_out, feed_grads, gate_own, up_own, down_own, _ = back_feed(
        resid, scales, coefs, cotangent, gain_own, gs_part, bo_part,
        (low_pair, cot_pair, mid_pair, gate_pair, up_pair),
    )
    gates_grad, sums, first_coefs, normed_twin, mixed_twin, branch_twin, scan_pair, gaterow_pair = (
        recur_back(
            grad_branch, mix_w, gate_rows, hidden_state, conv_rows, decay_rows, input_rows, scan_pad,
            masks, par, gates_w, scale_first_rows, normed_first, mixed,
        )
    )

    def own_parts(rows):
        return rows.reshape(rows.shape[0], seq_devices, part).transpose(1, 0, 2)

    small = own_parts(jnp.concatenate([sums, decay_sums[0:1]], 0)).reshape(seq_devices, -1)
    tiles = [
        jnp.stack(
            [
                gates_grad[g * BW : (g + 1) * BW, i * lanes + g * BW : i * lanes + (g + 1) * BW]
                for g in range(groups)
            ]
        )
        .reshape(groups, seq_devices, -1)
        .transpose(1, 0, 2)
        .reshape(seq_devices, -1)
        for i in range(2)
    ]
    feed_part = feed_grads[0].reshape(seq_devices, -1)
    flat_grads = jnp.concatenate([*tiles, small, feed_part], 1)
    grad_rows = -(-flat_grads.shape[1] // (128 * 8)) * 8
    grad_pack = jnp.pad(flat_grads, ((0, 0), (0, grad_rows * 128 - flat_grads.shape[1])))
    tokens_grad, mix_grads, pack_sum, mix_own, scan_own, gaterow_own, _ = last_reduce(
        scan_w, gate_w, grad_resid, tokens, first_coefs, scale_first_rows,
        gain_own, scan_pair[0], gaterow_pair[0],
        grad_pack.reshape(seq_devices, grad_rows, 128),
        (
            normed_first, normed_twin, mixed, mixed_twin, grad_branch, branch_twin, scan_pair,
            gaterow_pair,
        ),
    )
    pack_sum = pack_sum.reshape(-1)
    gate_size = part * BW
    cut_at = 2 * gate_size
    small_sum = pack_sum[cut_at : cut_at + 9 * part].reshape(9, part)
    feed_sum = pack_sum[cut_at + 9 * part : cut_at + 9 * part + mix_gain.shape[0]]
    mix_sum = lax.dynamic_slice(
        mix_grads[0], (shard_index * mix_gain.shape[0],), (mix_gain.shape[0],)
    )
    return (
        block_out,
        tokens_grad,
        mix_sum,
        scan_own,
        gaterow_own,
        small_sum[0:KW],
        small_sum[KW],
        pack_sum[:gate_size].reshape(groups, -1),
        small_sum[KW + 1],
        pack_sum[gate_size : 2 * gate_size].reshape(groups, -1),
        small_sum[KW + 2],
        small_sum[KW + 3],
        mix_own.T,
        feed_sum,
        gate_own,
        up_own,
        down_own.T,
        small_sum[KW + 4] / (row_count * seq_devices),
    )


def solution(mesh):
    placed = (
        P("seq", "tp"),
        P(("tp", "seq")),
        P("seq", "tp"),
        P("seq", "tp"),
        P(None, ("tp", "seq")),
        P(("tp", "seq")),
        P("tp", "seq"),
        P(("tp", "seq")),
        P("tp", "seq"),
        P(("tp", "seq")),
        P(("tp", "seq")),
        P("tp", "seq"),
        P(("tp", "seq")),
        P("seq", "tp"),
        P("seq", "tp"),
        P("tp", "seq"),
        P(),
        P("seq", "tp"),
    )
    return jax.shard_map(
        shards_fast if (mesh.shape["seq"], mesh.shape["tp"]) == (PLANE, LINE) else shards_general,
        mesh=mesh,
        in_specs=placed,
        out_specs=(
            P("seq", "tp"),
            P("seq", "tp"),
            P(("tp", "seq")),
            P("seq", "tp"),
            P("seq", "tp"),
            P(None, ("tp", "seq")),
            P(("tp", "seq")),
            P("tp", "seq"),
            P(("tp", "seq")),
            P("tp", "seq"),
            P(("tp", "seq")),
            P(("tp", "seq")),
            P("tp", "seq"),
            P(("tp", "seq")),
            P("seq", "tp"),
            P("seq", "tp"),
            P("tp", "seq"),
            P(("tp", "seq")),
        ),
        check_vma=False,
    )
```

```python
import functools

import jax
import jax.numpy as jnp
import numpy as np
from jax import lax
from jax.experimental import pallas as pl
from jax.experimental.pallas import tpu as pltpu
from jax.sharding import PartitionSpec as P


D = 2048
KW = 4
CD = 8
BW = 160


EPSILON = 1e-06
FLOOR_VALUE = 0.001


def from_behind(value, axis, steps):
    count = lax.axis_size(axis)
    initial, last = (max(0, -steps), min(count, count - steps))
    return lax.ppermute(value, axis, [(source, source + steps) for source in range(initial, last)])


def entering(part, axis, combine, identity, reverse):
    count = lax.axis_size(axis)
    place = lax.axis_index(axis)
    ahead = count - 1 - place if reverse else place
    gathered = jax.tree.map(lambda a: lax.all_gather(a, axis), part)
    state = jax.tree.map(lambda a, e: jnp.zeros_like(a) + jnp.asarray(e, a.dtype), part, identity)

    def one(turn, state):
        source = count - 1 - turn if reverse else turn
        return combine(
            state, jax.tree.map(lambda a: lax.dynamic_index_in_dim(a, source, 0, False), gathered)
        )

    return lax.fori_loop(0, ahead, one, state)


def matmul(left_side, right_side):
    return jnp.dot(left_side, right_side, preferred_element_type=jnp.float32)


def matmul_tn(left_side, right_side):
    return lax.dot_general(
        left_side, right_side, (((0,), (0,)), ((), ())), preferred_element_type=jnp.float32
    )


def matmul_nt(left_side, right_side):
    return lax.dot_general(
        left_side, right_side, (((1,), (1,)), ((), ())), preferred_element_type=jnp.float32
    )


def smooth_gelu(values):
    return jax.nn.gelu(values, approximate=True)


def combine(earlier, later):
    return (earlier[0] * later[0], later[1] + later[0] * earlier[1])


def seq_offsets(lengths, first_index, row_total):
    ends_all = jnp.cumsum(lengths, dtype=jnp.int32)
    starts_all = ends_all - lengths
    position = first_index + jnp.arange(row_total, dtype=jnp.int32)
    begins = jnp.max(
        jnp.where(starts_all[None, :] <= position[:, None], starts_all[None, :], 0), axis=1
    )
    return position - begins


def recurrence_terms(decay_rows, input_rows, decay_param, conv_values, resets):
    recur_gate = jax.nn.sigmoid(decay_rows)
    input_open = jax.nn.sigmoid(input_rows)
    decay_now = jnp.exp(-CD * recur_gate * jax.nn.softplus(-decay_param))
    multiplier = jnp.where(
        resets[:, None], 1.0, jnp.sqrt(jnp.maximum(1.0 - decay_now * decay_now, FLOOR_VALUE))
    )
    kept_decay = jnp.where(resets[:, None], 0.0, decay_now)
    return (kept_decay, multiplier * input_open * conv_values, decay_now)


def row_scale(values):
    squares_sum = lax.psum(jnp.sum(values * values, axis=1), "tp")
    return lax.rsqrt(squares_sum / D + EPSILON)


def spread_rows(values):
    return lax.all_gather(values, "tp", axis=1, tiled=True)


def spread_grads(values):
    return lax.all_gather(values, "tp", axis=1, tiled=True)


def reduce_features(values):
    return lax.psum_scatter(values, "tp", scatter_dimension=1, tiled=True)


def norm_back(values, row_scales, gain_vector, upstream):
    weighted = upstream * gain_vector
    inner_sum = lax.psum(jnp.sum(weighted * values, axis=1), "tp")
    cubed = row_scales * row_scales * row_scales * inner_sum / D
    back_rows = row_scales[:, None] * weighted - values * cubed[:, None]
    return (back_rows, jnp.sum(upstream * values * row_scales[:, None], axis=0))


def block_mix(blocked, matrices):
    mixed_blocks = jnp.einsum("tnb,nbc->tnc", blocked, matrices, preferred_element_type=jnp.float32)
    return mixed_blocks.reshape(blocked.shape[0], -1)


def block_outer(blocked, gradients):
    shaped = gradients.reshape(blocked.shape)
    outer_sum = jnp.einsum("tnb,tnc->nbc", blocked, shaped, preferred_element_type=jnp.float32)
    return outer_sum.reshape(blocked.shape[1], -1)


def block_back(gradients, matrices):
    shaped = gradients.reshape(gradients.shape[0], matrices.shape[0], matrices.shape[1])
    backed = jnp.einsum("tnc,nbc->tnb", shaped, matrices, preferred_element_type=jnp.float32)
    return backed.reshape(gradients.shape[0], -1)


def shards_general(
    tokens,
    mix_gain,
    scan_branch,
    gate_branch,
    kernel_taps,
    kernel_bias,
    decay_gate,
    decay_bias,
    input_gate,
    input_bias,
    decay_logit,
    mixer_out,
    feed_gain,
    gate_weight,
    up_weight,
    down_weight,
    lengths,
    cotangent,
):
    row_count = tokens.shape[0]
    seq_devices = lax.axis_size("seq")
    shard_index = lax.axis_index("seq")
    offsets = seq_offsets(lengths, shard_index * row_count, row_count)
    resets = offsets == 0
    gathered = (
        lax.all_gather(mix_gain, "seq", axis=0, tiled=True),
        lax.all_gather(scan_branch, "seq", axis=0, tiled=True),
        lax.all_gather(gate_branch, "seq", axis=0, tiled=True),
        lax.all_gather(kernel_taps, "seq", axis=1, tiled=True),
        lax.all_gather(kernel_bias, "seq", axis=0, tiled=True),
        lax.all_gather(decay_gate, "seq", axis=1, tiled=True),
        lax.all_gather(decay_bias, "seq", axis=0, tiled=True),
        lax.all_gather(input_gate, "seq", axis=1, tiled=True),
        lax.all_gather(input_bias, "seq", axis=0, tiled=True),
        lax.all_gather(decay_logit, "seq", axis=0, tiled=True),
        lax.all_gather(mixer_out, "seq", axis=1, tiled=True),
        lax.all_gather(feed_gain, "seq", axis=0, tiled=True),
        lax.all_gather(gate_weight, "seq", axis=0, tiled=True),
        lax.all_gather(up_weight, "seq", axis=0, tiled=True),
        lax.all_gather(down_weight, "seq", axis=1, tiled=True),
    )
    mix_f = gathered[0].astype(jnp.float32)
    taps_f = gathered[3].astype(jnp.float32)
    taps_bias = gathered[4].astype(jnp.float32)
    feed_f = gathered[11].astype(jnp.float32)
    tokens_f = tokens.astype(jnp.float32)
    scale_first = row_scale(tokens_f)
    normed_first = spread_rows((tokens_f * scale_first[:, None] * mix_f).astype(jnp.bfloat16))
    scan_rows = matmul(normed_first, gathered[1])
    gate_rows = matmul(normed_first, gathered[2])
    gelu_rows, gelu_pull = jax.vjp(smooth_gelu, gate_rows)
    rim_rows = from_behind(scan_rows[row_count - (KW - 1) :], "seq", 1)
    padded_rows = jnp.concatenate([rim_rows, scan_rows], axis=0)
    conv_sum = taps_bias + taps_f[0] * scan_rows
    for lag_step in range(1, KW):
        lagged = padded_rows[KW - 1 - lag_step : KW - 1 - lag_step + row_count]
        conv_sum = conv_sum + jnp.where(
            (offsets >= lag_step)[:, None], taps_f[lag_step] * lagged, 0.0
        )
    conv_rows = conv_sum.astype(jnp.bfloat16)
    lanes = scan_rows.shape[1]
    groups = lanes // BW
    conv_blocks = conv_rows.reshape(row_count, groups, BW)
    decay_mats = gathered[5].reshape(groups, BW, BW)
    input_mats = gathered[7].reshape(groups, BW, BW)
    decay_rows = block_mix(conv_blocks, decay_mats) + gathered[6].astype(jnp.float32)
    input_rows = block_mix(conv_blocks, input_mats) + gathered[8].astype(jnp.float32)

    def local_terms(decay_in, input_in, logit_in, conv_in):
        kept_part, driven_part, decay_part = recurrence_terms(
            decay_in, input_in, logit_in, conv_in, resets
        )
        return ((kept_part, driven_part), decay_part)

    terms_out, terms_pull, decay_now = jax.vjp(
        local_terms,
        decay_rows,
        input_rows,
        gathered[9].astype(jnp.float32),
        conv_rows.astype(jnp.float32),
        has_aux=True,
    )
    kept_decay, driven = terms_out
    local_prod, local_state = lax.associative_scan(combine, (kept_decay, driven), axis=0)
    before = entering(
        (local_prod[row_count - 1], local_state[row_count - 1]),
        "seq",
        combine,
        (jnp.ones((lanes,), jnp.float32), jnp.zeros((lanes,), jnp.float32)),
        False,
    )
    state_in = before[1]
    hidden_state = local_state + local_prod * state_in[None, :]
    mixed = (gelu_rows * hidden_state).astype(jnp.bfloat16)
    resid = tokens_f + reduce_features(matmul(mixed, gathered[10]))
    scale_second = row_scale(resid)
    normed_second = spread_rows((resid * scale_second[:, None] * feed_f).astype(jnp.bfloat16))
    gate_pre = matmul(normed_second, gathered[12])
    up_pre = matmul(normed_second, gathered[13])
    gelu_mid, mid_pull = jax.vjp(smooth_gelu, gate_pre)
    hidden_mid = (gelu_mid * up_pre).astype(jnp.bfloat16)
    block_out = resid + reduce_features(matmul(hidden_mid, gathered[14]))
    cot_full = spread_grads(cotangent)
    down_grad = matmul_tn(hidden_mid, cot_full)
    grad_mid = matmul_nt(cot_full, gathered[14])
    grad_gate = mid_pull(grad_mid * up_pre)[0].astype(jnp.bfloat16)
    grad_up = (grad_mid * gelu_mid).astype(jnp.bfloat16)
    gate_grad = matmul_tn(normed_second, grad_gate)
    up_grad = matmul_tn(normed_second, grad_up)
    grad_second = reduce_features(
        matmul_nt(grad_gate, gathered[12]) + matmul_nt(grad_up, gathered[13])
    )
    back_second, feed_grad = norm_back(resid, scale_second, feed_f, grad_second)
    grad_resid = cotangent.astype(jnp.float32) + back_second
    grad_branch = spread_grads(grad_resid.astype(jnp.bfloat16))
    out_grad = matmul_tn(mixed, grad_branch)
    grad_mixed = matmul_nt(grad_branch, gathered[10])
    grad_hidden = grad_mixed * gelu_rows
    grad_gate_rows = gelu_pull(grad_mixed * hidden_state)[0].astype(jnp.bfloat16)
    next_decay = jnp.concatenate([kept_decay[1:], jnp.ones_like(kept_decay[:1])], axis=0)
    tail_prod, local_adjoint = lax.associative_scan(
        combine, (next_decay, grad_hidden), reverse=True, axis=0
    )
    after = entering(
        (local_prod[row_count - 1], kept_decay[0] * local_adjoint[0]),
        "seq",
        combine,
        (jnp.ones((lanes,), jnp.float32), jnp.zeros((lanes,), jnp.float32)),
        True,
    )
    adjoint_in = after[1]
    adjoint = local_adjoint + tail_prod * adjoint_in[None, :]
    prev_state = jnp.concatenate([state_in[None, :], hidden_state[:-1]], axis=0)
    grad_decay_rows, grad_input_rows, logit_grad, conv_direct = terms_pull(
        (adjoint * prev_state, adjoint)
    )
    decay_grad_low = grad_decay_rows.astype(jnp.bfloat16)
    input_grad_low = grad_input_rows.astype(jnp.bfloat16)
    decay_w_grad = block_outer(conv_blocks, decay_grad_low)
    input_w_grad = block_outer(conv_blocks, input_grad_low)
    decay_b_grad = jnp.sum(decay_grad_low.astype(jnp.float32), axis=0)
    input_b_grad = jnp.sum(input_grad_low.astype(jnp.float32), axis=0)
    grad_conv = (
        conv_direct
        + block_back(decay_grad_low, decay_mats)
        + block_back(input_grad_low, input_mats)
    )
    rim_back = from_behind(grad_conv[: KW - 1], "seq", -1)
    grad_extended = jnp.concatenate([grad_conv, rim_back], axis=0)
    ext_offsets = seq_offsets(lengths, shard_index * row_count, row_count + KW - 1)
    grad_scan = taps_f[0] * grad_conv
    tap_grads = [jnp.sum(grad_conv * scan_rows, axis=0)]
    for lag_step in range(1, KW):
        ahead = grad_extended[lag_step : lag_step + row_count]
        ahead_ok = (ext_offsets[lag_step : lag_step + row_count] >= lag_step)[:, None]
        grad_scan = grad_scan + jnp.where(ahead_ok, taps_f[lag_step] * ahead, 0.0)
        lagged = padded_rows[KW - 1 - lag_step : KW - 1 - lag_step + row_count]
        tap_grads.append(
            jnp.sum(jnp.where((offsets >= lag_step)[:, None], grad_conv * lagged, 0.0), axis=0)
        )
    taps_grad = jnp.stack(tap_grads, axis=0)
    taps_bias_grad = jnp.sum(grad_conv, axis=0)
    scan_grad_low = grad_scan.astype(jnp.bfloat16)
    scan_w_grad = matmul_tn(normed_first, scan_grad_low)
    gatebr_grad = matmul_tn(normed_first, grad_gate_rows)
    grad_first = reduce_features(
        matmul_nt(scan_grad_low, gathered[1]) + matmul_nt(grad_gate_rows, gathered[2])
    )
    back_first, mix_grad = norm_back(tokens_f, scale_first, mix_f, grad_first)
    tokens_grad = grad_resid + back_first
    decay_total = jnp.sum(decay_now, axis=0)
    summed = (
        lax.psum_scatter(mix_grad, "seq", scatter_dimension=0, tiled=True),
        lax.psum_scatter(scan_w_grad, "seq", scatter_dimension=0, tiled=True),
        lax.psum_scatter(gatebr_grad, "seq", scatter_dimension=0, tiled=True),
        lax.psum_scatter(taps_grad, "seq", scatter_dimension=1, tiled=True),
        lax.psum_scatter(taps_bias_grad, "seq", scatter_dimension=0, tiled=True),
        lax.psum_scatter(decay_w_grad, "seq", scatter_dimension=1, tiled=True),
        lax.psum_scatter(decay_b_grad, "seq", scatter_dimension=0, tiled=True),
        lax.psum_scatter(input_w_grad, "seq", scatter_dimension=1, tiled=True),
        lax.psum_scatter(input_b_grad, "seq", scatter_dimension=0, tiled=True),
        lax.psum_scatter(logit_grad, "seq", scatter_dimension=0, tiled=True),
        lax.psum_scatter(out_grad, "seq", scatter_dimension=1, tiled=True),
        lax.psum_scatter(feed_grad, "seq", scatter_dimension=0, tiled=True),
        lax.psum_scatter(gate_grad, "seq", scatter_dimension=0, tiled=True),
        lax.psum_scatter(up_grad, "seq", scatter_dimension=0, tiled=True),
        lax.psum_scatter(down_grad, "seq", scatter_dimension=1, tiled=True),
        lax.psum_scatter(decay_total, "seq", scatter_dimension=0, tiled=True),
    )
    mean_decay = summed[15] / (row_count * seq_devices)
    return (
        block_out,
        tokens_grad,
        summed[0],
        summed[1],
        summed[2],
        summed[3],
        summed[4],
        summed[5],
        summed[6],
        summed[7],
        summed[8],
        summed[9],
        summed[10],
        summed[11],
        summed[12],
        summed[13],
        summed[14],
        mean_decay,
    )


MESH = pl.DeviceIdType.MESH
F32 = jnp.float32
BF16 = jnp.bfloat16
LINE = 4
PLANE = 8
CHUNK = 128
ANY = pl.BlockSpec(memory_space=pl.ANY)
VM = pl.BlockSpec(memory_space=pltpu.VMEM)


def flip(place, bit):
    step = 1 << bit
    return place + step - 2 * step * lax.rem(place // step, 2)


def flip_all(place, bits):
    for bit in range(3):
        if bits & (1 << bit):
            place = flip(place, bit)
    return place


def meet(s, z):
    barrier = pltpu.get_barrier_semaphore()
    for bits in range(1, PLANE):
        pl.semaphore_signal(barrier, inc=1, device_id=(flip_all(s, bits), z), device_id_type=MESH)
    for step in range(1, LINE):
        pl.semaphore_signal(
            barrier, inc=1, device_id=(s, lax.rem(z + step, LINE)), device_id_type=MESH
        )
    pl.semaphore_wait(barrier, PLANE - 1 + LINE - 1)


def remote(src, dst, send, recv, target):
    return pltpu.make_async_remote_copy(
        src_ref=src,
        dst_ref=dst,
        send_sem=send,
        recv_sem=recv,
        device_id=target,
        device_id_type=MESH,
    )


class LineGather:
    def __init__(self, s, z, own_at, full_at, send, recv):
        self.s, self.z = s, z
        self.own_at, self.full_at = own_at, full_at
        self.send, self.recv = send, recv

    def copy(self, way, level, c):
        sign = 1 - 2 * way
        origin = self.z - sign * level
        src = self.own_at(c) if level == 0 else self.full_at(origin, c)
        return remote(
            src,
            self.full_at(origin, c),
            self.send.at[way, level, c],
            self.recv.at[way, level, c],
            (self.s, self.z + sign),
        )

    def arrival(self, way, level, c):
        sign = 1 - 2 * way
        part = self.full_at(self.z - sign * (level + 1), c)
        return remote(
            part,
            part,
            self.send.at[way, level, c],
            self.recv.at[way, level, c],
            (self.s, self.z + sign),
        )

    def sends(self, way, level):
        if way == 0:
            return (self.z >= level) & (self.z < LINE - 1)
        return (self.z <= LINE - 1 - level) & (self.z > 0)

    def gets(self, way, level):
        return self.z >= level + 1 if way == 0 else self.z <= LINE - 2 - level

    def start(self, c):
        for way in range(2):
            pl.when(self.sends(way, 0))(lambda way=way: self.copy(way, 0, c).start())

    def forward(self, level, c):
        for way in range(2):
            pl.when(self.gets(way, level - 1))(
                lambda way=way: self.arrival(way, level - 1, c).wait_recv()
            )
            if level < LINE - 1:
                pl.when(self.sends(way, level))(
                    lambda way=way: self.copy(way, level, c).start()
                )

    def drain(self, c):
        for way in range(2):
            for level in range(LINE - 1):
                pl.when(self.sends(way, level))(
                    lambda way=way, level=level: self.copy(way, level, c).wait_send()
                )


class PlaneGather:
    def __init__(self, s, z, own, block_at, half_at, send, recv, local):
        self.s, self.z, self.own = s, z, own
        self.block_at, self.half_at = block_at, half_at
        self.send, self.recv, self.local = send, recv, local
        self.near = (flip(s, 1), flip(s, 2))
        self.diag = flip(self.near[0], 2)
        self.twin = flip(s, 0)
        self.twin_near = (flip(self.near[0], 0), flip(self.near[1], 0))
        self.twin_diag = flip(self.diag, 0)

    def plan(self, i):
        block, half = self.block_at, self.half_at
        return (
            (self.own, block(self.s), self.near[0]),
            (self.own, block(self.s), self.near[1]),
            (half(self.near[1], 0), half(self.near[1], 0), self.near[0]),
            (half(self.near[0], 1), half(self.near[0], 1), self.near[1]),
            (self.own, block(self.s), self.twin),
            (block(self.near[0]), block(self.near[0]), self.twin),
            (block(self.near[1]), block(self.near[1]), self.twin),
            (half(self.diag, 0), half(self.diag, 0), self.twin),
            (half(self.diag, 1), half(self.diag, 1), self.twin),
        )[i]

    def landing(self, i):
        block, half = self.block_at, self.half_at
        return (
            block(self.near[0]),
            block(self.near[1]),
            half(self.diag, 0),
            half(self.diag, 1),
            block(self.twin),
            block(self.twin_near[0]),
            block(self.twin_near[1]),
            half(self.twin_diag, 0),
            half(self.twin_diag, 1),
        )[i]

    def copy(self, i):
        src, dst, target = self.plan(i)
        return remote(src, dst, self.send.at[i], self.recv.at[i], (target, self.z))

    def got(self, i):
        part = self.landing(i)
        remote(part, part, self.send.at[i], self.recv.at[i], (self.twin, self.z)).wait_recv()

    def keep(self):
        return pltpu.make_async_copy(self.own, self.block_at(self.s), self.local)

    def start(self):
        for i in (0, 1, 4):
            self.copy(i).start()
        self.keep().start()

    def turn(self):
        self.got(0)
        self.copy(3).start()
        self.copy(5).start()
        self.got(1)
        self.copy(2).start()
        self.copy(6).start()

    def last(self):
        self.got(2)
        self.copy(7).start()
        self.got(3)
        self.copy(8).start()

    def arrive(self):
        for i in range(4, 9):
            self.got(i)
        self.keep().wait()

    def drain(self):
        for i in range(9):
            self.copy(i).wait_send()


class Spread:
    def __init__(self, s, z, slot_at, send, recv):
        self.s, self.z, self.slot_at, self.send, self.recv = s, z, slot_at, send, recv

    def copy(self, bits, origin):
        slot = self.slot_at(origin)
        return remote(
            slot,
            slot,
            self.send.at[bits - 1],
            self.recv.at[bits - 1],
            (flip_all(self.s, bits), self.z),
        )

    def start(self):
        for bits in range(1, PLANE):
            self.copy(bits, self.s).start()

    def finish(self):
        for bits in range(1, PLANE):
            self.copy(bits, flip_all(self.s, bits)).wait_recv()
        for bits in range(1, PLANE):
            self.copy(bits, self.s).wait_send()


def rows_of(ref, size, parts=2):
    def block(place):
        return ref.at[pl.ds(pl.multiple_of(place * size, size), size)]

    def half(place, h):
        part = size // parts
        return ref.at[pl.ds(pl.multiple_of(place * size + h * part, part), part)]

    return block, half


def columns_of(ref, size):
    height = ref.shape[0] // 2

    def block(place):
        return ref.at[:, pl.ds(pl.multiple_of(place * size, size), size)]

    def half(place, h):
        return ref.at[
            pl.ds(h * height, height), pl.ds(pl.multiple_of(place * size, size), size)
        ]

    return block, half


def chunk_rows(c):
    return pl.ds(pl.multiple_of(c * CHUNK, CHUNK), CHUNK)


def feature_columns(z, width):
    return pl.ds(pl.multiple_of(z * width, width), width)


def each_chunk(chunks, body):
    lax.fori_loop(0, chunks, lambda c, carry: (body(c), carry)[1], 0)


def dma(*shape):
    return pltpu.SemaphoreType.DMA(shape)


def struct(shape, kind):
    return jax.ShapeDtypeStruct(shape, kind)


def vm(*shape, kind=BF16):
    return pltpu.VMEM(shape, kind)


def sigmoid(values):
    return 0.5 * jnp.tanh(0.5 * values) + 0.5


ROOT = 0.7978845608028654


def gelu_of(values):
    return 0.5 * values * (1.0 + jnp.tanh(ROOT * (values + 0.044715 * values * values * values)))


def gelu_pair(values):
    squared = values * values
    bent = jnp.tanh(ROOT * values * (1.0 + 0.044715 * squared))
    half = 0.5 * (1.0 + bent)
    slope = half + 0.5 * values * (1.0 - bent * bent) * (ROOT * (1.0 + 3 * 0.044715 * squared))
    return values * half, slope


def dot(left_side, right_side):
    return jnp.dot(left_side, right_side, preferred_element_type=F32)


def dot_nt(left_side, right_side):
    return lax.dot_general(
        left_side, right_side, (((1,), (1,)), ((), ())), preferred_element_type=F32
    )


def dot_tn(left_side, right_side):
    return lax.dot_general(
        left_side, right_side, (((0,), (0,)), ((), ())), preferred_element_type=F32
    )


SUBS = 8


LANE = 128


def put(ref, at, values):
    for lane in range(ref.shape[0]):
        ref[lane, at, :] = values[:, lane * LANE : (lane + 1) * LANE]


def get(ref, at):
    return jnp.concatenate([ref[lane, at, :] for lane in range(ref.shape[0])], axis=1)


def strided(ref, step):
    at = pl.ds(step, SUBS, stride=ref.shape[1] // SUBS)
    return [ref[lane, at, :] for lane in range(ref.shape[0])]


def strided_put(ref, step, values):
    at = pl.ds(step, SUBS, stride=ref.shape[1] // SUBS)
    for lane in range(ref.shape[0]):
        ref[lane, at, :] = values[lane]


def lanes_of(values):
    return [values[:, i * LANE : (i + 1) * LANE] for i in range(values.shape[1] // LANE)]


def first_kernel(
    tok, cot, small, gains, gate_blocks, scan, gate, mix, ffn, masks,
    row_order, tile, cells, lane_order,
    normed_out, scan_rows_out, gate_rows_out, conv_out, decay_rows_out, input_rows_out, hidden_out,
    mixed_out, scan_w_out, gate_w_out, gates_w_out,
    scales, decay_sum, par, gain_own, mix_all, ffn_all, cot_all,
    normed, scan_rows, gate_rows, conv, decay_rows, input_rows, hidden, mixed, scan_w, gate_w, gates_w,
    tok_all, small_all, gains_all, blocks_all, gain_full, kept, driven, slots,
    tok_send, tok_recv, cot_send, cot_recv, gain_send, gain_recv, plane_send, plane_recv,
    small_send, small_recv, carry_send, carry_recv, halo_send, halo_recv, local, out_sem,
):
    s, z = lax.axis_index("seq"), lax.axis_index("tp")
    rows, width = tok.shape
    chunks, features, lanes = rows // CHUNK, width * LINE, gate.shape[1]
    part = gate_blocks.shape[0]

    def line_of(own, full, send, recv):
        return LineGather(
            s, z,
            lambda c: own.at[chunk_rows(c)],
            lambda o, c: full.at[chunk_rows(c), feature_columns(o, width)],
            send, recv,
        )

    toks = line_of(tok, tok_all, tok_send, tok_recv)
    cots = line_of(cot, cot_all, cot_send, cot_recv)
    gain_line = LineGather(
        s, z, lambda c: gains_all.at[z], lambda o, c: gains_all.at[o], gain_send, gain_recv
    )
    planes = []
    for i, (own, full, make) in enumerate(
        (
            (scan, scan_w, rows_of),
            (gate, gate_w, rows_of),
            (mix, mix_all, columns_of),
            (ffn, ffn_all, rows_of),
        )
    ):
        size = own.shape[1] if make is columns_of else own.shape[0]
        planes.append(
            PlaneGather(s, z, own, *make(full, size), plane_send.at[i], plane_recv.at[i], local.at[i])
        )
    spreads = [
        Spread(s, z, lambda p: gains_all.at[z, p], small_send.at[0], small_recv.at[0]),
        Spread(s, z, lambda p: small_all.at[p], small_send.at[1], small_recv.at[1]),
        Spread(
            s, z, lambda p: blocks_all.at[pl.ds(pl.multiple_of(p * part, 16), part)],
            small_send.at[2], small_recv.at[2],
        ),
    ]
    keep = pltpu.make_async_copy(cot, cot_all.at[:, feature_columns(z, width)], local.at[6])
    keep.start()
    outs = {
        name: pltpu.make_async_copy(src, dst, out_sem.at[i])
        for i, (name, src, dst) in enumerate(
            (
                ("normed", normed, normed_out), ("scan_rows", scan_rows, scan_rows_out),
                ("gate_rows", gate_rows, gate_rows_out), ("conv", conv, conv_out),
                ("decay_rows", decay_rows, decay_rows_out), ("input_rows", input_rows, input_rows_out),
                ("hidden", hidden, hidden_out), ("mixed", mixed, mixed_out),
                ("scan_w", scan_w, scan_w_out), ("gate_w", gate_w, gate_w_out),
                ("gates_w", gates_w, gates_w_out),
            )
        )
    }
    tok_all[:, feature_columns(z, width)] = tok[...]
    gains_all[z, s] = gains[...]
    small_all[s] = small[...]
    blocks_all[pl.ds(pl.multiple_of(s * part, 16), part), :] = gate_blocks[...]
    meet(s, z)
    for spread in spreads:
        spread.start()
    for c in range(chunks):
        toks.start(c)
    for plane in planes[:2]:
        plane.start()
    for spread in spreads:
        spread.finish()
    gain_line.start(0)
    for c in range(chunks):
        toks.forward(1, c)
    gain_line.forward(1, 0)
    planes[2].start()
    planes[3].start()
    placed = dot(
        jnp.concatenate([small_all[p] for p in range(PLANE)], axis=1), lane_order[...]
    )
    par[...] = placed
    falling = jnp.exp(-placed[7:8, :])
    par[7:8, :] = CD * jnp.log1p(falling)
    par[8:9, :] = CD * falling / (1.0 + falling)
    half = blocks_all.shape[1] // 2
    for i in range(2):
        wide = dot(blocks_all[:, i * half : (i + 1) * half], tile[...]).astype(BF16)
        gates_w[:, i * lanes : (i + 1) * lanes] = dot(row_order[...], wide).astype(BF16) * cells[...]
    planes[0].turn()
    planes[1].turn()
    for c in range(chunks):
        toks.forward(2, c)
    gain_line.forward(2, 0)
    planes[0].last()
    planes[1].last()
    gain_line.forward(3, 0)
    for c in range(chunks):
        cots.start(c)
    pick = lax.broadcasted_iota(jnp.int32, (LANE, LANE), 0)
    place = lax.broadcasted_iota(jnp.int32, (LANE, LANE), 1)
    cut = LANE // 2
    even = jnp.concatenate(
        [gains_all[o, p] for o in range(LINE) for p in range(0, PLANE, 2)], axis=0
    ).astype(BF16)
    odd = jnp.concatenate(
        [gains_all[o, p] for o in range(LINE) for p in range(1, PLANE, 2)], axis=0
    ).astype(BF16)
    for i in range(2):
        from_even = (pick == place + i * cut) & (place < cut)
        from_odd = (pick == place + (i - 1) * cut) & (place >= cut)
        spots = dot(even, from_even.astype(F32).astype(BF16)) + dot(
            odd, from_odd.astype(F32).astype(BF16)
        )
        for q in range(spots.shape[0] // 8):
            gain_full[i : i + 1, q * LANE : (q + 1) * LANE] = spots[8 * q : 8 * q + 1, :]
    gain_own[0:2, :] = gain_full[0:2, feature_columns(z, width)]
    planes[0].arrive()
    planes[1].arrive()
    for name in ("scan_w", "gate_w", "gates_w"):
        outs[name].start()

    def project(c):
        toks.forward(3, c)
        at = chunk_rows(c)
        x = tok_all[at, :].astype(F32)
        scale = lax.rsqrt(jnp.sum(x * x, axis=1, keepdims=True) / features + EPSILON)
        scales[at, :] = jnp.broadcast_to(scale, (CHUNK, LANE))
        low = (x * scale * gain_full[0:1, :]).astype(BF16)
        normed[at, :] = low
        scan_rows[pl.ds(pl.multiple_of(c * CHUNK + 8, 8), CHUNK), :] = dot(low, scan_w[...])
        gate_rows[at, :] = dot(low, gate_w[...])

    each_chunk(chunks, project)
    halo = remote(
        scan_rows.at[pl.ds(rows, 8)], scan_rows.at[pl.ds(0, 8)], halo_send, halo_recv,
        (lax.rem(s + 1, PLANE), z),
    )
    first, final = s == 0, s == PLANE - 1
    pl.when(jnp.logical_not(final))(lambda: halo.start())

    @pl.when(first)
    def _():
        scan_rows[0:8, :] = jnp.zeros((8, lanes), F32)

    planes[2].turn()
    planes[3].turn()
    decay_sum[...] = jnp.zeros_like(decay_sum)
    pl.when(jnp.logical_not(first))(lambda: halo.wait_recv())
    for name in ("normed", "scan_rows", "gate_rows"):
        outs[name].start()

    def gates(c):
        at = chunk_rows(c)
        block = scan_rows[pl.ds(pl.multiple_of(c * CHUNK, 8), CHUNK + 8), :]
        mask = masks[at, :]
        total = par[4:5, :] + par[0:1, :] * block[8:, :]
        for lag in range(1, KW):
            total = total + mask[:, lag : lag + 1] * (
                par[lag : lag + 1, :] * block[8 - lag : 8 - lag + CHUNK, :]
            )
        low = total.astype(BF16)
        conv[at, :] = low
        rows_now = dot(low, gates_w[...])
        decays = rows_now[:, :lanes] + par[5:6, :]
        inputs = rows_now[:, lanes:] + par[6:7, :]
        decay_rows[at, :] = decays
        input_rows[at, :] = inputs
        decay = jnp.exp(-sigmoid(decays) * par[7:8, :])
        goes_on = mask[:, 0:1]
        multiplier = 1.0 + goes_on * (
            jnp.sqrt(jnp.maximum(1.0 - decay * decay, FLOOR_VALUE)) - 1.0
        )
        put(kept, at, goes_on * decay)
        put(driven, at, multiplier * sigmoid(inputs) * low.astype(F32))
        decay_sum[0:1, :] += jnp.sum(decay, axis=0, keepdims=True)
        cots.forward(1, c)

    each_chunk(chunks, gates)
    for name in ("conv", "decay_rows", "input_rows"):
        outs[name].start()
    planes[2].last()
    planes[3].last()
    count = rows // SUBS

    def total_of(step, carry):
        keeps, drives = strided(kept, step), strided(driven, step)
        return (
            [p * k for p, k in zip(carry[0], keeps)],
            [k * v + d for k, v, d in zip(keeps, carry[1], drives)],
        )

    groups = lanes // LANE
    product, value = lax.fori_loop(
        0,
        count,
        total_of,
        ([jnp.ones((SUBS, LANE), F32)] * groups, [jnp.zeros((SUBS, LANE), F32)] * groups),
        unroll=4,
    )
    product, value = jnp.concatenate(product, axis=1), jnp.concatenate(value, axis=1)
    whole = (jnp.ones((1, lanes), F32), jnp.zeros((1, lanes), F32))
    for sub in range(SUBS):
        here = product[sub : sub + 1, :]
        whole = (whole[0] * here, here * whole[1] + value[sub : sub + 1, :])
    slots[s, 0:1, :] = whole[0]
    slots[s, 1:2, :] = whole[1]
    spread = Spread(s, z, lambda p: slots.at[p], carry_send, carry_recv)
    spread.start()
    spread.finish()
    entry = jnp.zeros((1, lanes), F32)
    for place in range(PLANE - 1):
        entry = jnp.where(
            place < s, slots[place, 0:1, :] * entry + slots[place, 1:2, :], entry
        )
    hidden[0:8, :] = jnp.broadcast_to(entry, (8, lanes))
    entries = []
    for sub in range(SUBS):
        entries.append(entry)
        entry = product[sub : sub + 1, :] * entry + value[sub : sub + 1, :]

    def step_on(step, now):
        keeps, drives = strided(kept, step), strided(driven, step)
        now = [k * v + d for k, v, d in zip(keeps, now, drives)]
        strided_put(driven, step, now)
        return now

    lax.fori_loop(0, count, step_on, lanes_of(jnp.concatenate(entries, axis=0)), unroll=4)

    def mix(c):
        at = chunk_rows(c)
        now = get(driven, at)
        hidden[pl.ds(pl.multiple_of(c * CHUNK + 8, 8), CHUNK), :] = now
        mixed[at, :] = (gelu_of(gate_rows[at, :]) * now).astype(BF16)
        cots.forward(2, c)

    each_chunk(chunks, mix)
    for name in ("hidden", "mixed"):
        outs[name].start()
    for c in range(chunks):
        cots.forward(3, c)
    for plane in planes[2:]:
        plane.arrive()
    for plane in planes:
        plane.drain()
    for c in range(chunks):
        toks.drain(c)
        cots.drain(c)
    gain_line.drain(0)
    pl.when(jnp.logical_not(final))(lambda: halo.wait_send())
    keep.wait()
    for copy in outs.values():
        copy.wait()


def first_half(tok, cot, small, gains, gate_blocks, scan, gate, mix, ffn, masks, consts):
    rows, width = tok.shape
    features, lanes = width * LINE, gate.shape[1]
    chunks = rows // CHUNK
    return pl.pallas_call(
        first_kernel,
        out_shape=(
            struct((rows, features), BF16),
            struct((rows + 8, lanes), F32),
            struct((rows, lanes), F32),
            struct((rows, lanes), BF16),
            struct((rows, lanes), F32),
            struct((rows, lanes), F32),
            struct((rows + 8, lanes), F32),
            struct((rows, lanes), BF16),
            struct((features, lanes), BF16),
            struct((features, lanes), BF16),
            struct((lanes, 2 * lanes), BF16),
            struct((rows, LANE), F32),
            struct((8, lanes), F32),
            struct((16, lanes), F32),
            struct((8, width), F32),
            struct((mix.shape[0], mix.shape[1] * PLANE), BF16),
            struct((ffn.shape[0] * PLANE, ffn.shape[1]), BF16),
            struct((rows, features), BF16),
        ),
        in_specs=[VM] * 14,
        out_specs=[ANY] * 11 + [VM] * 4 + [ANY] * 3,
        scratch_shapes=[
            vm(rows, features), vm(rows + 8, lanes, kind=F32), vm(rows, lanes, kind=F32),
            vm(rows, lanes), vm(rows, lanes, kind=F32), vm(rows, lanes, kind=F32),
            vm(rows + 8, lanes, kind=F32), vm(rows, lanes), vm(features, lanes), vm(features, lanes),
            vm(lanes, 2 * lanes), vm(rows, features),
            vm(PLANE, *small.shape), vm(LINE, PLANE, *gains.shape, kind=F32),
            vm(PLANE * gate_blocks.shape[0], gate_blocks.shape[1]), vm(8, features, kind=F32),
            vm(lanes // LANE, rows, LANE, kind=F32), vm(lanes // LANE, rows, LANE, kind=F32),
            vm(PLANE, 8, lanes, kind=F32),
            dma(2, LINE - 1, chunks), dma(2, LINE - 1, chunks),
            dma(2, LINE - 1, chunks), dma(2, LINE - 1, chunks),
            dma(2, LINE - 1, 1), dma(2, LINE - 1, 1),
            dma(4, 9), dma(4, 9), dma(3, 7), dma(3, 7), dma(7), dma(7),
            pltpu.SemaphoreType.DMA, pltpu.SemaphoreType.DMA, dma(7), dma(11),
        ],
        compiler_params=pltpu.CompilerParams(
            collective_id=0, has_side_effects=True, vmem_limit_bytes=60 << 20
        ),
        name="first_half",
    )(tok, cot, small, gains, gate_blocks, scan, gate, mix, ffn, masks, *consts)


class WeightGrads:
    def __init__(self, s, z, stage, land, own, send, recv, back):
        self.s, self.z = s, z
        self.stage, self.land, self.own = stage, land, own
        self.send, self.recv, self.back_sem = send, recv, back

    def owner(self, k):
        return flip_all(self.s, 2 * (k + 1)) if k < 3 else self.s

    def stage_of(self, k):
        size = self.own.shape[0]
        return self.stage.at[pl.ds(k * size, size)]

    def copy(self, k):
        return remote(
            self.stage_of(k), self.land.at[k], self.send.at[k], self.recv.at[k],
            (self.owner(k), self.z),
        )

    def block(self, k, left, right):
        size = self.own.shape[0]
        columns = feature_columns(self.owner(k), size)
        value = dot_tn(left[:, columns], right[...])
        if k == 3:
            self.own[...] = value
        else:
            self.stage_of(k)[...] = value.astype(BF16)
            self.copy(k).start()

    def finish(self):
        backs = [
            pltpu.make_async_copy(self.land.at[k], self.stage_of(k), self.back_sem.at[k])
            for k in range(3)
        ]
        for k in range(3):
            self.copy(k).wait()
            backs[k].start()
        for back in backs:
            back.wait()
        self.own[...] += (
            self.stage_of(0)[...].astype(F32)
            + self.stage_of(1)[...].astype(F32)
            + self.stage_of(2)[...].astype(F32)
        )


class LineReduce:
    def __init__(self, s, z, part, land, send, recv):
        self.s, self.z, self.part, self.land = s, z, part, land
        self.send, self.recv = send, recv

    def copy(self, o, target, slot, c):
        return remote(
            self.part.at[c, o],
            self.land.at[c, slot],
            self.send.at[o, c],
            self.recv.at[slot, c],
            (self.s, self.z + target),
        )

    def got(self, slot, c):
        part = self.land.at[c, slot]
        remote(part, part, self.send.at[0, c], self.recv.at[slot, c], (self.s, self.z)).wait_recv()

    def start(self, c):
        end = LINE - 1
        pl.when(self.z == 0)(lambda: self.copy(end, 1, LINE, c).start())
        pl.when(self.z == end)(lambda: self.copy(0, -1, LINE, c).start())
        pl.when(self.z == 0)(lambda: self.copy(2, 2, 1, c).start())
        pl.when(self.z == end)(lambda: self.copy(1, -2, 3, c).start())
        for me in range(LINE):

            def work(me=me):
                if me < end:
                    self.copy(me + 1, 1, 0, c).start()
                if me > 0:
                    self.copy(me - 1, -1, 2, c).start()

            pl.when(self.z == me)(work)

    def forward(self, c):
        end = LINE - 1
        for me, o, step, slot in ((1, end, 2, 1), (2, 0, -2, 3)):

            def work(o=o, step=step, slot=slot):
                self.got(LINE, c)
                self.part[c, o] = (
                    self.part[c, o].astype(F32) + self.land[c, LINE].astype(F32)
                ).astype(BF16)
                self.copy(o, step, slot, c).start()

            pl.when(self.z == me)(work)

    def total(self, c, into):
        slots = ((2, 3), (0, 2, 3), (0, 1, 2), (0, 1))
        for me in range(LINE):

            def work(me=me):
                for slot in slots[me]:
                    self.got(slot, c)
                value = self.land[c, slots[me][0]].astype(F32)
                for slot in slots[me][1:]:
                    value = value + self.land[c, slot].astype(F32)
                into[...] = value

            pl.when(self.z == me)(work)

    def drain(self, c):
        for o in range(LINE):
            part = self.part.at[c, o]
            pl.when(self.z != o)(
                lambda part=part, o=o: remote(
                    part, part, self.send.at[o, c], self.recv.at[0, c], (self.s, self.z)
                ).wait_send()
            )


class LineSpread:
    def __init__(self, s, z, slot_at, send, recv):
        self.s, self.z, self.slot_at, self.send, self.recv = s, z, slot_at, send, recv

    def copy(self, step, origin, c):
        slot = self.slot_at(origin, c)
        target = (self.s, lax.rem(self.z + step, LINE))
        return remote(slot, slot, self.send.at[step - 1, c], self.recv.at[step - 1, c], target)

    def start(self, c):
        for step in range(1, LINE):
            self.copy(step, self.z, c).start()

    def finish(self, c):
        for step in range(1, LINE):
            self.copy(step, lax.rem(self.z + LINE - step, LINE), c).wait_recv()

    def drain(self, c):
        for step in range(1, LINE):
            self.copy(step, self.z, c).wait_send()


class Halves:
    def __init__(self, s, z, src, out, own, send, recv):
        self.s, self.z, self.src, self.out = s, z, src, out
        self.own, self.send, self.recv = own, send, recv

    def keep(self, c):
        at = chunk_rows(c)
        return pltpu.make_async_copy(self.src.at[at], self.out.at[0, at], self.own.at[c])

    def give(self, c):
        at = chunk_rows(c)
        return remote(
            self.src.at[at], self.out.at[1, at], self.send.at[c], self.recv.at[c],
            (flip(self.s, 0), self.z),
        )

    def start(self, c):
        self.keep(c).start()
        self.give(c).start()

    def drain(self, c):
        self.keep(c).wait()
        self.give(c).wait()


def as_row(column):
    return jnp.transpose(jnp.broadcast_to(column, (CHUNK, LANE)))[0:8, :]


def as_columns(row):
    return jnp.transpose(jnp.broadcast_to(row[0:1, :], (LANE, CHUNK)))


def in_range(c, chunks, body):
    pl.when((c >= 0) & (c < chunks))(lambda: body(c))


CUT = 768
AHEAD = 2
GROUP = 2 * CHUNK


def group_rows(g):
    return pl.ds(pl.multiple_of(g * GROUP, GROUP), GROUP)


def feed_kernel(
    mixed, mix_w, tok, cot, gain, up, down, gate_w, cot_all,
    resid, grad, gain_grad, down_own, ffn_own, lands, grad_all, bo_part, low_pair, cot_pair, mid_pair, gate_pair, up_pair,
    part, land, low, low_grad, cots, mid, g_gate, g_up, bo_out, gate_v, up_v, down_v,
    acc, inner, scales, squares, inners,
    red_send, red_recv, gs_send, gs_recv, line_send, line_recv, grad_send, grad_recv,
    sq_send, sq_recv, in_send, in_recv, plane_send, plane_recv, local,
    own_sem, give_send, give_recv, out_sem, load_sem, w_send, w_recv, w_back,
):
    s, z = lax.axis_index("seq"), lax.axis_index("tp")
    rows, width = tok.shape
    chunks, features = rows // CHUNK, width * LINE
    loads = [
        pltpu.make_async_copy(gate_w, gate_v, load_sem.at[0]),
        pltpu.make_async_copy(cot_all, cots, load_sem.at[1]),
    ]
    for load in loads:
        load.start()
    meet(s, z)
    red = LineReduce(s, z, part, land, red_send, red_recv)
    red_gs = LineReduce(s, z, part, land, gs_send, gs_recv)

    def line_of(full, send, recv):
        return LineGather(
            s, z,
            lambda c: full.at[chunk_rows(c), feature_columns(z, width)],
            lambda o, c: full.at[chunk_rows(c), feature_columns(o, width)],
            send, recv,
        )

    line = line_of(low, line_send, line_recv)
    grads = line_of(low_grad, grad_send, grad_recv)
    planes = [
        PlaneGather(
            s, z, up, *rows_of(up_v, up.shape[0]), plane_send.at[0], plane_recv.at[0], local.at[0]
        ),
        PlaneGather(
            s, z, down, *columns_of(down_v, down.shape[1]), plane_send.at[1], plane_recv.at[1],
            local.at[1],
        ),
    ]
    square_spread = LineSpread(s, z, lambda o, c: squares.at[o, c], sq_send, sq_recv)
    inner_spread = LineSpread(s, z, lambda o, c: inners.at[o, c], in_send, in_recv)
    pairs = [
        Halves(s, z, src, out, own_sem.at[i], give_send.at[i], give_recv.at[i])
        for i, (src, out) in enumerate(
            ((low, low_pair), (cots, cot_pair), (mid, mid_pair), (g_gate, gate_pair), (g_up, up_pair))
        )
    ]
    gain_grad[...] = jnp.zeros_like(gain_grad)

    def bo_copy(c):
        return pltpu.make_async_copy(bo_out.at[c], bo_part.at[c], out_sem.at[0, c])

    def grad_copy(c):
        at = chunk_rows(c)
        return pltpu.make_async_copy(low_grad.at[at], grad_all.at[at], out_sem.at[1, c])

    def project(c):
        values = dot(mixed[chunk_rows(c), :], mix_w[...])
        for o in range(LINE):
            here = values[:, o * width : (o + 1) * width]
            part[c, o] = here.astype(BF16)

            @pl.when(z == o)
            def _(here=here):
                resid[chunk_rows(c), :] = here

        red.start(c)

    for c in range(AHEAD):
        project(c)
    for plane in planes:
        plane.start()

    def reduced(c):
        at = chunk_rows(c)
        red.total(c, acc)
        values = tok[at, :].astype(F32) + (resid[at, :] + acc[...])
        resid[at, :] = values
        squares[z, c] = as_row(jnp.sum(values * values, axis=1, keepdims=True))
        square_spread.start(c)

    def scaled(c):
        at = chunk_rows(c)
        square_spread.finish(c)
        sums = squares[0, c] + squares[1, c] + squares[2, c] + squares[3, c]
        scale = lax.rsqrt(as_columns(sums) / features + EPSILON)
        scales[at, :] = scale
        low[at, feature_columns(z, width)] = (resid[at, :] * scale[:, 0:1] * gain[1:2, :]).astype(
            BF16
        )
        line.start(c)

    def forward(cut, g):
        at = group_rows(g)
        cols = slice(cut * CUT, (cut + 1) * CUT)
        x = low[at, :]
        gate_pre, up_pre = dot(x, gate_v[:, cols]), dot(x, up_v[:, cols])
        act, slope = gelu_pair(gate_pre)
        here = (act * up_pre).astype(BF16)
        mid[at, cols] = here
        back = dot_nt(cots[at, :], down_v[cols, :])
        gate_grad = (back * up_pre * slope).astype(BF16)
        up_grad = (back * act).astype(BF16)
        g_gate[at, cols] = gate_grad
        g_up[at, cols] = up_grad
        products = jnp.sum(
            gate_grad.astype(F32) * gate_pre + up_grad.astype(F32) * up_pre, axis=1, keepdims=True
        )
        if cut == 0:
            inner[...] = products
        else:
            inner[...] += products

    def backward(g):
        at = group_rows(g)
        back = dot_nt(g_gate[at, :], gate_v[...]) + dot_nt(g_up[at, :], up_v[...])
        for k in range(GROUP // CHUNK):
            c = g * (GROUP // CHUNK) + k
            here = slice(k * CHUNK, (k + 1) * CHUNK)
            red.drain(c)
            for o in range(LINE):
                part[c, o] = back[here, o * width : (o + 1) * width].astype(BF16)
            red_gs.start(c)
            inners[z, c] = as_row(inner[here, :])
            inner_spread.start(c)
        block = dot(mid[at, :], down_v[...])
        for k in range(GROUP // CHUNK):
            c = g * (GROUP // CHUNK) + k
            here = slice(k * CHUNK, (k + 1) * CHUNK)
            for o in range(LINE):
                bo_out[c, o] = block[here, o * width : (o + 1) * width].astype(BF16)
            for pair in pairs:
                pair.start(c)
            bo_copy(c).start()

    def turned(c):
        at = chunk_rows(c)
        red_gs.total(c, acc)
        inner_spread.finish(c)
        sums = inners[0, c] + inners[1, c] + inners[2, c] + inners[3, c]
        scale = scales[at, :]
        coef = scale * scale * as_columns(sums) / features
        above = acc[...] + part[c, z].astype(F32)
        scale, values = scale[:, 0:1], resid[at, :]
        gain_grad[0:1, :] += jnp.sum(above * values * scale, axis=0, keepdims=True)
        total = cot[at, :].astype(F32) + scale * gain[1:2, :] * above - values * coef[:, 0:1]
        grad[at, :] = total
        low_grad[at, feature_columns(z, width)] = total.astype(BF16)
        grads.start(c)

    def twice(start, body):
        def both(t):
            pl.when((t >= start) & (lax.rem(t - start, 2) == 0) & (t < start + chunks))(
                lambda: (body(t - start), body(t - start + 1)) and None
            )

        return both

    def whole(c):
        grads.forward(3, c)
        grad_copy(c).start()

    left, rights = down_v, (gate_v, up_v)

    def fill(i, src, dst):
        return [
            pltpu.make_async_copy(
                src.at[half], dst.at[pl.ds(half * rows, rows)], load_sem.at[2 + 2 * i + half]
            )
            for half in range(2)
        ]

    fills = [
        fill(0, cot_pair, left), fill(1, mid_pair, rights[0]),
        fill(2, low_pair, left), fill(3, gate_pair, rights[1]),
    ]
    weights = [
        WeightGrads(s, z, stage, lands.at[i], own, w_send.at[i], w_recv.at[i], w_back.at[i])
        for i, (stage, own) in enumerate(((mid, down_own), (g_gate, ffn_own)))
    ]

    def ready_pairs(c):
        for pair in pairs:
            pair.drain(c)

    def weigh(step):
        @pl.when(step == 0)
        def _():
            each_chunk(chunks, ready_pairs)
            for plane in planes:
                plane.drain()
            for i in (0, 1, 3):
                for copy in fills[i]:
                    copy.start()
            for i in (0, 1):
                for copy in fills[i]:
                    copy.wait()
            for k in range(4):
                weights[0].block(k, left, rights[0].at[pl.ds(0, 2 * rows)])
            for copy in fills[2]:
                copy.start()

        @pl.when(step == 1)
        def _():
            for i in (2, 3):
                for copy in fills[i]:
                    copy.wait()
            for k in range(4):
                weights[1].block(k, left, rights[1].at[pl.ds(0, 2 * rows)])

    gs_one = twice(6, lambda c: red_gs.forward(c))
    gs_three = twice(7, turned)
    to_one = twice(8, lambda c: grads.forward(1, c))
    to_two = twice(9, lambda c: grads.forward(2, c))
    to_three = twice(10, whole)

    def turn(t, carry):
        g, odd = (t - 4) // 2, lax.rem(t, 2) == 1
        ready = (t >= 4) & (t < chunks + 4)

        @pl.when(t == 2)
        def _():
            for plane in planes:
                plane.turn()

        @pl.when(t == 4)
        def _():
            for plane in planes:
                plane.last()
            for plane in planes:
                plane.arrive()
            for load in loads:
                load.wait()

        in_range(t, chunks, lambda c: red.forward(c))
        gs_one(t)
        in_range(t - 2, chunks, lambda c: line.forward(1, c))
        in_range(t - 3, chunks, lambda c: line.forward(3, c))
        to_one(t)
        to_three(t)
        pl.when(ready & jnp.logical_not(odd))(lambda: forward(0, g))
        gs_three(t)
        in_range(t - 1, chunks, reduced)
        in_range(t - 1, chunks, scaled)
        in_range(t - 2, chunks, lambda c: line.forward(2, c))
        to_two(t)
        pl.when(ready & jnp.logical_not(odd))(lambda: forward(1, g))
        weigh(t - chunks - 4)
        in_range(t + AHEAD, chunks, project)
        pl.when(ready & odd)(lambda: backward(g))
        return carry

    lax.fori_loop(0, chunks + 9, turn, 0)

    def close(c):
        red_gs.drain(c)
        line.drain(c)
        grads.drain(c)
        square_spread.drain(c)
        inner_spread.drain(c)
        bo_copy(c).wait()
        grad_copy(c).wait()

    each_chunk(chunks, close)
    for weight in weights:
        weight.finish()


def feed_both(mixed, mix_w, tok, cot, gain, up, down, gate_w, cot_all):
    rows, width = tok.shape
    features, hidden = width * LINE, gate_w.shape[1]
    chunks = rows // CHUNK

    def pair(size):
        return struct((2, rows, size), BF16)

    return pl.pallas_call(
        feed_kernel,
        out_shape=(
            struct((rows, width), F32),
            struct((rows, width), F32),
            struct((8, width), F32),
            struct((features // PLANE, hidden), F32),
            struct((features // PLANE, hidden), F32),
            struct((2, 3, features // PLANE, hidden), BF16),
            struct((rows, features), BF16),
            struct((chunks, LINE, CHUNK, width), BF16),
            pair(features), pair(features), pair(hidden), pair(hidden), pair(hidden),
        ),
        in_specs=[VM] * 7 + [ANY] * 2,
        out_specs=[VM] * 5 + [ANY] * 8,
        scratch_shapes=[
            vm(chunks, LINE, CHUNK, width), vm(chunks, LINE + 1, CHUNK, width),
            vm(rows, features), vm(rows, features), vm(rows, features),
            vm(rows, hidden), vm(rows, hidden), vm(rows, hidden),
            vm(chunks, LINE, CHUNK, width),
            vm(features, hidden), vm(features, hidden), vm(hidden, features),
            vm(CHUNK, width, kind=F32), vm(GROUP, 1, kind=F32), vm(rows, LANE, kind=F32),
            vm(LINE, chunks, 8, LANE, kind=F32), vm(LINE, chunks, 8, LANE, kind=F32),
            dma(LINE, chunks), dma(LINE + 1, chunks), dma(LINE, chunks), dma(LINE + 1, chunks),
            dma(2, LINE - 1, chunks), dma(2, LINE - 1, chunks),
            dma(2, LINE - 1, chunks), dma(2, LINE - 1, chunks),
            dma(LINE - 1, chunks), dma(LINE - 1, chunks),
            dma(LINE - 1, chunks), dma(LINE - 1, chunks),
            dma(2, 9), dma(2, 9), dma(2),
            dma(5, chunks), dma(5, chunks), dma(5, chunks), dma(2, chunks), dma(10),
            dma(2, 3), dma(2, 3), dma(2, 3),
        ],
        compiler_params=pltpu.CompilerParams(
            collective_id=2, has_side_effects=True, vmem_limit_bytes=64 << 20
        ),
        name="feed_both",
    )(mixed, mix_w, tok, cot, gain, up, down, gate_w, cot_all)


def recur_back_kernel(
    low, mix_w, gate_rows, hidden, conv, decay_rows, input_rows, scan_rows, masks, par, gates_w, scales,
    resid, normed_src, mixed_src, low_src, bo_part, feed_pair, feed_up_pair,
    gates_grad, sums, coefs, out, up_own,
    normed_twin, mixed_twin, low_twin, scan_pair, gate_pair, lands,
    kept, grads, both, conv_grad, scan_low, gate_low, slots, inners,
    part, land, acc, left, right, stages,
    small_send, small_recv, halo_send, halo_recv, in_send, in_recv,
    own_sem, give_send, give_recv, twin_send, twin_recv,
    bo_send, bo_recv, w_send, w_recv, w_back, load_sem,
):
    s, z = lax.axis_index("seq"), lax.axis_index("tp")
    rows, features = low.shape
    lanes = gate_rows.shape[1]
    chunks = rows // CHUNK
    wholes = [
        remote(src, out, twin_send.at[i], twin_recv.at[i], (flip(s, 0), z))
        for i, (src, out) in enumerate(
            ((normed_src, normed_twin), (mixed_src, mixed_twin), (low_src, low_twin))
        )
    ]
    pairs = [
        Halves(s, z, src, out, own_sem.at[i], give_send.at[i], give_recv.at[i])
        for i, (src, out) in enumerate(((scan_low, scan_pair), (gate_low, gate_pair)))
    ]
    inner_spread = LineSpread(s, z, lambda o, c: inners.at[o, c], in_send, in_recv)
    loads = [
        pltpu.make_async_copy(src, dst, load_sem.at[i])
        for i, (src, dst) in enumerate(
            (
                (bo_part, part), (feed_pair, left), (feed_up_pair, right),
            )
        )
    ]
    for load in loads:
        load.start()
    meet(s, z)
    for whole in wholes:
        whole.start()
    sums[...] = jnp.zeros_like(sums)
    red = LineReduce(s, z, part, land, bo_send, bo_recv)
    weight = WeightGrads(s, z, stages, lands, up_own, w_send, w_recv, w_back)
    loads[0].wait()
    for c in range(chunks):
        red.start(c)

    def result(c):
        at = chunk_rows(c)
        red.total(c, acc)
        out[at, :] = resid[at, :] + (acc[...] + part[c, z].astype(F32))

    def sum_on(t):
        in_range(t, chunks, lambda c: red.forward(c))
        in_range(t - 2, chunks, result)

    def start(g):
        at = group_rows(g)
        grad = dot_nt(low[at, :], mix_w[...])
        for k in range(GROUP // CHUNK):
            c = g * (GROUP // CHUNK) + k
            here = chunk_rows(c)
            act, slope = gelu_pair(gate_rows[here, :])
            now = hidden[pl.ds(pl.multiple_of(c * CHUNK + 8, 8), CHUNK), :]
            part = grad[k * CHUNK : (k + 1) * CHUNK, :]
            gate_low[here, :] = (part * now * slope).astype(BF16)
            put(grads, here, part * act)
            decay = jnp.exp(-sigmoid(decay_rows[here, :]) * par[7:8, :])
            put(kept, here, masks[here, 0:1] * decay)

    lax.fori_loop(0, rows // GROUP, lambda g, carry: (start(g), carry)[1], 0)
    for c in range(chunks):
        pairs[1].start(c)
    count, groups = rows // SUBS, lanes // LANE

    def total_of(step, carry):
        keeps, adds = strided(kept, count - 1 - step), strided(grads, count - 1 - step)
        return (
            [p * k for p, k in zip(carry[0], keeps)],
            [k * (v + a) for k, v, a in zip(keeps, carry[1], adds)],
        )

    product, value = lax.fori_loop(
        0,
        count,
        total_of,
        ([jnp.ones((SUBS, LANE), F32)] * groups, [jnp.zeros((SUBS, LANE), F32)] * groups),
        unroll=4,
    )
    product, value = jnp.concatenate(product, axis=1), jnp.concatenate(value, axis=1)
    whole = (jnp.ones((1, lanes), F32), jnp.zeros((1, lanes), F32))
    for sub in range(SUBS - 1, -1, -1):
        here = product[sub : sub + 1, :]
        whole = (whole[0] * here, here * whole[1] + value[sub : sub + 1, :])
    slots[s, 0:1, :] = whole[0]
    slots[s, 1:2, :] = whole[1]
    spread = Spread(s, z, lambda p: slots.at[p], small_send, small_recv)
    spread.start()
    spread.finish()
    entry = jnp.zeros((1, lanes), F32)
    for place in range(PLANE - 1, 0, -1):
        entry = jnp.where(
            place > s, slots[place, 0:1, :] * entry + slots[place, 1:2, :], entry
        )
    entries = []
    for sub in range(SUBS - 1, -1, -1):
        entries.append(entry)
        entry = product[sub : sub + 1, :] * entry + value[sub : sub + 1, :]

    def step_back(step, now):
        keeps, adds = strided(kept, count - 1 - step), strided(grads, count - 1 - step)
        now = [v + a for v, a in zip(now, adds)]
        strided_put(grads, count - 1 - step, now)
        return [k * v for k, v in zip(keeps, now)]

    lax.fori_loop(
        0, count, step_back, lanes_of(jnp.concatenate(entries[::-1], axis=0)), unroll=4
    )

    def gates(c):
        at = chunk_rows(c)
        tall = pl.ds(pl.multiple_of(c * CHUNK, 8), CHUNK + 8)
        adjoint = get(grads, at)
        before = hidden[tall, :][7 : 7 + CHUNK, :]
        mask = masks[at, :]
        goes_on = mask[:, 0:1]
        opened = sigmoid(decay_rows[at, :])
        entered = sigmoid(input_rows[at, :])
        rate = par[7:8, :]
        decay = jnp.exp(-opened * rate)
        room = 1.0 - decay * decay
        root = jnp.sqrt(jnp.maximum(room, FLOOR_VALUE))
        multiplier = 1.0 + goes_on * (root - 1.0)
        conv_f = conv[at, :].astype(F32)
        direct = adjoint * multiplier
        grad_input = (direct * conv_f * (entered * (1.0 - entered))).astype(BF16)
        through = jnp.where(
            room > FLOOR_VALUE, 1.0, jnp.where(room == FLOOR_VALUE, 0.5, 0.0)
        )
        grad_decay = goes_on * (
            adjoint * before - adjoint * entered * conv_f * (through * decay / root)
        )
        scaled = grad_decay * decay * opened
        grad_rows = (-scaled * rate * (1.0 - opened)).astype(BF16)
        joined = jnp.concatenate([grad_rows, grad_input], axis=1)
        both[at, :] = joined
        grad_conv = direct * entered + dot_nt(joined, gates_w[...])
        conv_grad[at, :] = grad_conv
        block = scan_rows[tall, :]
        sums[0:1, :] += jnp.sum(grad_conv * block[8:, :], axis=0, keepdims=True)
        for lag in range(1, KW):
            sums[lag : lag + 1, :] += jnp.sum(
                mask[:, lag : lag + 1] * (grad_conv * block[8 - lag : 8 - lag + CHUNK, :]),
                axis=0,
                keepdims=True,
            )
        sums[4:5, :] += jnp.sum(grad_conv, axis=0, keepdims=True)
        sums[5:6, :] += jnp.sum(grad_rows.astype(F32), axis=0, keepdims=True)
        sums[6:7, :] += jnp.sum(grad_input.astype(F32), axis=0, keepdims=True)
        sums[7:8, :] += jnp.sum(scaled, axis=0, keepdims=True)
        for k in range(4):
            pl.when(c == k)(lambda k=k: weight.block(k, left, right))
        sum_on(c)

    for load in loads[1:3]:
        load.wait()
    each_chunk(chunks, gates)
    halo = remote(
        conv_grad.at[pl.ds(0, 8)], conv_grad.at[pl.ds(rows, 8)], halo_send, halo_recv,
        (lax.rem(s + PLANE - 1, PLANE), z),
    )
    first, final = s == 0, s == PLANE - 1
    pl.when(jnp.logical_not(first))(lambda: halo.start())
    gates_grad[...] = dot_tn(conv[...], both[...])
    sums[7:8, :] = sums[7:8, :] * par[8:9, :]

    @pl.when(final)
    def _():
        conv_grad[rows : rows + 8, :] = jnp.zeros((8, lanes), F32)

    pl.when(jnp.logical_not(final))(lambda: halo.wait_recv())

    def finish(c):
        at = chunk_rows(c)
        tall = pl.ds(pl.multiple_of(c * CHUNK, 8), CHUNK + 8)
        block, mask = conv_grad[tall, :], masks[tall, :]
        total = par[0:1, :] * block[:CHUNK, :]
        for lag in range(1, KW):
            total = total + mask[lag : lag + CHUNK, lag : lag + 1] * (
                par[lag : lag + 1, :] * block[lag : lag + CHUNK, :]
            )
        grad = total.astype(BF16)
        scan_low[at, :] = grad
        pairs[0].start(c)
        products = grad.astype(F32) * scan_rows[
            pl.ds(pl.multiple_of(c * CHUNK + 8, 8), CHUNK), :
        ] + gate_low[at, :].astype(F32) * gate_rows[at, :]
        inners[z, c] = as_row(jnp.sum(products, axis=1, keepdims=True))
        inner_spread.start(c)
        sum_on(c + chunks)

    each_chunk(chunks, finish)
    weight.finish()

    def close(c):
        at = chunk_rows(c)
        inner_spread.finish(c)
        total = inners[0, c] + inners[1, c] + inners[2, c] + inners[3, c]
        scale = scales[at, :]
        coefs[at, :] = scale * scale * as_columns(total) / features
        inner_spread.drain(c)
        red.drain(c)
        for pair in pairs:
            pair.drain(c)

    each_chunk(chunks, close)
    for whole in wholes:
        whole.wait()
    pl.when(jnp.logical_not(first))(lambda: halo.wait_send())


def recur_back(low, mix_w, gate_rows, hidden, conv, decay_rows, input_rows, scan_rows, masks, par,
               gates_w, scales, resid, normed, mixed, bo_part, pairs):
    rows, features = low.shape
    lanes, width = gate_rows.shape[1], resid.shape[1]
    chunks, hidden_size, part = rows // CHUNK, pairs[1].shape[2], features // PLANE

    def pair(size):
        return struct((2, rows, size), BF16)

    return pl.pallas_call(
        recur_back_kernel,
        out_shape=(
            struct((lanes, 2 * lanes), F32),
            struct((8, lanes), F32),
            struct((rows, LANE), F32),
            struct((rows, width), F32),
            struct((part, hidden_size), F32),
            struct((rows, features), BF16), struct((rows, lanes), BF16), struct((rows, features), BF16),
            pair(lanes), pair(lanes),
            struct((3, part, hidden_size), BF16),
        ),
        in_specs=[VM] * 13 + [ANY] * 6,
        out_specs=[VM] * 5 + [ANY] * 6,
        scratch_shapes=[
            vm(lanes // LANE, rows, LANE, kind=F32), vm(lanes // LANE, rows, LANE, kind=F32),
            vm(rows, 2 * lanes), vm(rows + 8, lanes, kind=F32), vm(rows, lanes), vm(rows, lanes),
            vm(PLANE, 8, lanes, kind=F32), vm(LINE, chunks, 8, LANE, kind=F32),
            vm(chunks, LINE, CHUNK, width), vm(chunks, LINE + 1, CHUNK, width),
            vm(CHUNK, width, kind=F32),
            vm(2 * rows, features), vm(2 * rows, hidden_size), vm(3 * part, hidden_size),
            dma(7), dma(7), pltpu.SemaphoreType.DMA, pltpu.SemaphoreType.DMA,
            dma(LINE - 1, chunks), dma(LINE - 1, chunks),
            dma(2, chunks), dma(2, chunks), dma(2, chunks), dma(3), dma(3),
            dma(LINE, chunks), dma(LINE + 1, chunks), dma(3), dma(3), dma(3), dma(3),
        ],
        compiler_params=pltpu.CompilerParams(
            collective_id=4, has_side_effects=True, vmem_limit_bytes=64 << 20
        ),
        name="recur_back",
    )(
        low, mix_w, gate_rows, hidden, conv, decay_rows, input_rows, scan_rows, masks, par, gates_w,
        scales, resid, normed, mixed, low, bo_part,
        *[pair.reshape(2 * rows, pair.shape[2]) for pair in pairs],
    )


def last_kernel(
    scan_w, gate_w, grad, tok, coefs, scales, gain, scan_low, gate_low, pack,
    normed, normed_twin, mixed, mixed_twin, low, low_twin, scan_pair, gate_pair,
    tokens_grad, gain_grad, pack_sum, mix_own, scan_own, gate_own, lands,
    part, land, acc, left, right, stages, pack_land, gain_land,
    red_send, red_recv, w_send, w_recv, w_back, load_sem, pack_send, pack_recv, gain_send, gain_recv,
):
    s, z = lax.axis_index("seq"), lax.axis_index("tp")
    rows, width = tok.shape
    chunks = rows // CHUNK
    loads = [
        pltpu.make_async_copy(src, dst, load_sem.at[i])
        for i, (src, dst) in enumerate(
            (
                (low, left.at[0, :rows]), (low_twin, left.at[0, rows:]),
                (mixed, right.at[0, :rows]), (mixed_twin, right.at[0, rows:]),
                (normed, left.at[1, :rows]), (normed_twin, left.at[1, rows:]),
                (scan_pair, right.at[1]), (gate_pair, right.at[2]),
            )
        )
    ]
    for load in loads:
        load.start()
    meet(s, z)
    packs = [
        remote(
            pack.at[flip_all(s, bits)], pack_land.at[s], pack_send.at[bits - 1],
            pack_recv.at[bits - 1], (flip_all(s, bits), z),
        )
        for bits in range(1, PLANE)
    ]
    for copy in packs:
        copy.start()
    red = LineReduce(s, z, part, land, red_send, red_recv)
    weights = [
        WeightGrads(s, z, stages.at[i], lands.at[i], own, w_send.at[i], w_recv.at[i], w_back.at[i])
        for i, own in enumerate((mix_own, scan_own, gate_own))
    ]
    gain_land[s] = jnp.zeros_like(gain_grad)

    def project(g):
        at = group_rows(g)
        values = dot_nt(scan_low[at, :], scan_w[...]) + dot_nt(gate_low[at, :], gate_w[...])
        for k in range(GROUP // CHUNK):
            c = g * (GROUP // CHUNK) + k
            here = slice(k * CHUNK, (k + 1) * CHUNK)
            for o in range(LINE):
                part[c, o] = values[here, o * width : (o + 1) * width].astype(BF16)
            red.start(c)

    def reduced(c):
        at = chunk_rows(c)
        red.total(c, acc)
        up = acc[...] + part[c, z].astype(F32)
        scale, values = scales[at, 0:1], tok[at, :].astype(F32)
        gain_land[s, 0:1, :] += jnp.sum(up * values * scale, axis=0, keepdims=True)
        tokens_grad[at, :] = (
            grad[at, :] + scale * gain[0:1, :] * up - values * coefs[at, 0:1]
        )

    project(0)
    for load in loads:
        load.wait()

    def weigh(t):
        for k in range(4):
            pl.when(t == k)(lambda k=k: weights[1].block(k, left.at[1], right.at[1]))
            pl.when(t == k)(lambda k=k: weights[2].block(k, left.at[1], right.at[2]))
            pl.when(t == 4 + k // 2)(lambda k=k: weights[0].block(k, left.at[0], right.at[0]))

    def turn(t, carry):
        in_range(t, chunks, lambda c: red.forward(c))
        pl.when((lax.rem(t, 2) == 0) & (t < chunks - 2))(lambda: project(t // 2 + 1))
        weigh(t)
        in_range(t - 1, chunks, reduced)
        return carry

    lax.fori_loop(0, chunks + 1, turn, 0)
    gain_spread = Spread(s, z, lambda p: gain_land.at[p], gain_send, gain_recv)
    gain_spread.start()
    for bits in range(1, PLANE):
        other = pack_land.at[flip_all(s, bits)]
        remote(
            other, other, pack_send.at[bits - 1], pack_recv.at[bits - 1], (flip_all(s, bits), z)
        ).wait_recv()
    total = pack[s]
    for bits in range(1, PLANE):
        total = total + pack_land[flip_all(s, bits)]
    pack_sum[...] = total
    for weight in weights:
        weight.finish()
    gain_spread.finish()
    total = gain_land[0]
    for place in range(1, PLANE):
        total = total + gain_land[place]
    gain_grad[...] = total
    for copy in packs:
        copy.wait_send()
    each_chunk(chunks, red.drain)


def last_reduce(scan_w, gate_w, grad, tok, coefs, scales, gain, scan_low, gate_low, pack, pairs):
    rows, width = tok.shape
    features, lanes = width * LINE, scan_w.shape[1]
    chunks, part = rows // CHUNK, features // PLANE
    return pl.pallas_call(
        last_kernel,
        out_shape=(
            struct((rows, width), F32),
            struct((8, width), F32),
            struct(pack.shape[1:], F32),
            struct((part, lanes), F32),
            struct((part, lanes), F32),
            struct((part, lanes), F32),
            struct((3, 3, part, lanes), BF16),
        ),
        in_specs=[VM] * 10 + [ANY] * 8,
        out_specs=[VM] * 6 + [ANY],
        scratch_shapes=[
            vm(chunks, LINE, CHUNK, width), vm(chunks, LINE + 1, CHUNK, width),
            vm(CHUNK, width, kind=F32),
            vm(2, 2 * rows, features), vm(3, 2 * rows, lanes),
            vm(3, 3 * part, lanes),
            vm(*pack.shape, kind=F32), vm(PLANE, 8, width, kind=F32),
            dma(LINE, chunks), dma(LINE + 1, chunks),
            dma(3, 3), dma(3, 3), dma(3, 3), dma(8), dma(7), dma(7), dma(7), dma(7),
        ],
        compiler_params=pltpu.CompilerParams(
            collective_id=5, has_side_effects=True, vmem_limit_bytes=63 << 20
        ),
        name="last_reduce",
    )(
        scan_w, gate_w, grad, tok, coefs, scales, gain, scan_low, gate_low, pack,
        *pairs[:6],
        *[pair.reshape(2 * rows, pair.shape[2]) for pair in pairs[6:]],
    )


def placements(lanes, groups, seq_devices):
    cut, part = BW // seq_devices, lanes // seq_devices
    rows = np.arange(lanes)
    source = (rows % BW) // cut * part + rows // BW * cut + rows % cut
    row_order = (source[:, None] == rows[None, :]).astype(np.float32)
    tile = (np.arange(2 * LANE)[:, None] == rows[None, :] % BW).astype(np.float32)
    cells = (rows[:, None] // BW == rows[None, :] // BW).astype(np.float32)
    spots = np.arange(seq_devices * LANE)
    lane_order = (
        (rows[None, :] // part == spots[:, None] // LANE)
        & (rows[None, :] % part == spots[:, None] % LANE)
    ).astype(np.float32)
    return tuple(jnp.asarray(m, BF16) for m in (row_order, tile, cells, lane_order))


def shards_fast(
    tokens, mix_gain, scan_branch, gate_branch, kernel_taps, kernel_bias, decay_gate, decay_bias,
    input_gate, input_bias, decay_logit, mixer_out, feed_gain, gate_weight, up_weight, down_weight,
    lengths, cotangent,
):
    row_count, width = tokens.shape
    seq_devices = lax.axis_size("seq")
    shard_index = lax.axis_index("seq")
    ext_offsets = seq_offsets(lengths, shard_index * row_count, row_count + 8)
    lag_at = jnp.array([1, 1, 2, 3, 0, 0, 0, 0], jnp.int32)
    masks = (ext_offsets[:, None] >= lag_at[None, :]).astype(F32)
    lanes = scan_branch.shape[1]
    part = lanes // seq_devices
    groups = lanes // BW
    consts = placements(lanes, groups, seq_devices)
    small = jnp.concatenate(
        [
            kernel_taps, kernel_bias[None], decay_bias[None], input_bias[None], decay_logit[None],
            jnp.zeros((8, part), BF16),
        ]
    )
    small = jnp.pad(small, ((0, 0), (0, LANE - part)))
    gains = jnp.pad(
        jnp.concatenate([mix_gain, feed_gain]).astype(F32)[None, :], ((0, 7), (0, 0))
    )
    pad = ((0, 0), (0, 2 * LANE - BW))
    gate_blocks = jnp.concatenate(
        [jnp.pad(m.reshape(part, BW), pad) for m in (decay_gate, input_gate)], 1
    )
    (
        normed_first, scan_pad, gate_rows, conv_rows, decay_rows, input_rows, hidden_state, mixed,
        scan_w, gate_w, gates_w, scale_first_rows, decay_sums, par, gain_own, mix_w, ffn_gate, cot_full,
    ) = first_half(
        tokens, cotangent, small, gains, gate_blocks, scan_branch, gate_branch, mixer_out, gate_weight,
        masks, consts,
    )
    (
        resid, grad_resid, feed_grads, down_own, gate_own, _, grad_branch, bo_part,
        low_pair, cot_pair, mid_pair, gate_pair, up_pair,
    ) = feed_both(
        mixed, mix_w, tokens, cotangent, gain_own, up_weight, down_weight, ffn_gate, cot_full
    )
    (
        gates_grad, sums, first_coefs, block_out, up_own,
        normed_twin, mixed_twin, branch_twin, scan_pair, gaterow_pair, _,
    ) = recur_back(
        grad_branch, mix_w, gate_rows, hidden_state, conv_rows, decay_rows, input_rows, scan_pad,
        masks, par, gates_w, scale_first_rows, resid, normed_first, mixed, bo_part,
        (low_pair, up_pair),
    )

    def own_parts(rows):
        return rows.reshape(rows.shape[0], seq_devices, part).transpose(1, 0, 2)

    small = own_parts(jnp.concatenate([sums, decay_sums[0:1]], 0)).reshape(seq_devices, -1)
    tiles = [
        jnp.stack(
            [
                gates_grad[g * BW : (g + 1) * BW, i * lanes + g * BW : i * lanes + (g + 1) * BW]
                for g in range(groups)
            ]
        )
        .reshape(groups, seq_devices, -1)
        .transpose(1, 0, 2)
        .reshape(seq_devices, -1)
        for i in range(2)
    ]
    feed_part = feed_grads[0].reshape(seq_devices, -1)
    flat_grads = jnp.concatenate([*tiles, small, feed_part], 1)
    grad_rows = -(-flat_grads.shape[1] // (128 * 8)) * 8
    grad_pack = jnp.pad(flat_grads, ((0, 0), (0, grad_rows * 128 - flat_grads.shape[1])))
    tokens_grad, mix_grads, pack_sum, mix_own, scan_own, gaterow_own, _ = last_reduce(
        scan_w, gate_w, grad_resid, tokens, first_coefs, scale_first_rows,
        gain_own, scan_pair[0], gaterow_pair[0],
        grad_pack.reshape(seq_devices, grad_rows, 128),
        (
            normed_first, normed_twin, mixed, mixed_twin, grad_branch, branch_twin, scan_pair,
            gaterow_pair,
        ),
    )
    pack_sum = pack_sum.reshape(-1)
    gate_size = part * BW
    cut_at = 2 * gate_size
    small_sum = pack_sum[cut_at : cut_at + 9 * part].reshape(9, part)
    feed_sum = pack_sum[cut_at + 9 * part : cut_at + 9 * part + mix_gain.shape[0]]
    mix_sum = lax.dynamic_slice(
        mix_grads[0], (shard_index * mix_gain.shape[0],), (mix_gain.shape[0],)
    )
    return (
        block_out,
        tokens_grad,
        mix_sum,
        scan_own,
        gaterow_own,
        small_sum[0:KW],
        small_sum[KW],
        pack_sum[:gate_size].reshape(groups, -1),
        small_sum[KW + 1],
        pack_sum[gate_size : 2 * gate_size].reshape(groups, -1),
        small_sum[KW + 2],
        small_sum[KW + 3],
        mix_own.T,
        feed_sum,
        gate_own,
        up_own,
        down_own.T,
        small_sum[KW + 4] / (row_count * seq_devices),
    )


def solution(mesh):
    placed = (
        P("seq", "tp"),
        P(("tp", "seq")),
        P("seq", "tp"),
        P("seq", "tp"),
        P(None, ("tp", "seq")),
        P(("tp", "seq")),
        P("tp", "seq"),
        P(("tp", "seq")),
        P("tp", "seq"),
        P(("tp", "seq")),
        P(("tp", "seq")),
        P("tp", "seq"),
        P(("tp", "seq")),
        P("seq", "tp"),
        P("seq", "tp"),
        P("tp", "seq"),
        P(),
        P("seq", "tp"),
    )
    return jax.shard_map(
        shards_fast if (mesh.shape["seq"], mesh.shape["tp"]) == (PLANE, LINE) else shards_general,
        mesh=mesh,
        in_specs=placed,
        out_specs=(
            P("seq", "tp"),
            P("seq", "tp"),
            P(("tp", "seq")),
            P("seq", "tp"),
            P("seq", "tp"),
            P(None, ("tp", "seq")),
            P(("tp", "seq")),
            P("tp", "seq"),
            P(("tp", "seq")),
            P("tp", "seq"),
            P(("tp", "seq")),
            P(("tp", "seq")),
            P("tp", "seq"),
            P(("tp", "seq")),
            P("seq", "tp"),
            P("seq", "tp"),
            P("tp", "seq"),
            P(("tp", "seq")),
        ),
        check_vma=False,
    )
```

```python
import functools

import jax
import jax.numpy as jnp
import numpy as np
from jax import lax
from jax.experimental import pallas as pl
from jax.experimental.pallas import tpu as pltpu
from jax.sharding import PartitionSpec as P


D = 2048
KW = 4
CD = 8
BW = 160


EPSILON = 1e-06
FLOOR_VALUE = 0.001


def from_behind(value, axis, steps):
    count = lax.axis_size(axis)
    initial, last = (max(0, -steps), min(count, count - steps))
    return lax.ppermute(value, axis, [(source, source + steps) for source in range(initial, last)])


def entering(part, axis, combine, identity, reverse):
    count = lax.axis_size(axis)
    place = lax.axis_index(axis)
    ahead = count - 1 - place if reverse else place
    gathered = jax.tree.map(lambda a: lax.all_gather(a, axis), part)
    state = jax.tree.map(lambda a, e: jnp.zeros_like(a) + jnp.asarray(e, a.dtype), part, identity)

    def one(turn, state):
        source = count - 1 - turn if reverse else turn
        return combine(
            state, jax.tree.map(lambda a: lax.dynamic_index_in_dim(a, source, 0, False), gathered)
        )

    return lax.fori_loop(0, ahead, one, state)


def matmul(left_side, right_side):
    return jnp.dot(left_side, right_side, preferred_element_type=jnp.float32)


def matmul_tn(left_side, right_side):
    return lax.dot_general(
        left_side, right_side, (((0,), (0,)), ((), ())), preferred_element_type=jnp.float32
    )


def matmul_nt(left_side, right_side):
    return lax.dot_general(
        left_side, right_side, (((1,), (1,)), ((), ())), preferred_element_type=jnp.float32
    )


def smooth_gelu(values):
    return jax.nn.gelu(values, approximate=True)


def combine(earlier, later):
    return (earlier[0] * later[0], later[1] + later[0] * earlier[1])


def seq_offsets(lengths, first_index, row_total):
    ends_all = jnp.cumsum(lengths, dtype=jnp.int32)
    starts_all = ends_all - lengths
    position = first_index + jnp.arange(row_total, dtype=jnp.int32)
    begins = jnp.max(
        jnp.where(starts_all[None, :] <= position[:, None], starts_all[None, :], 0), axis=1
    )
    return position - begins


def recurrence_terms(decay_rows, input_rows, decay_param, conv_values, resets):
    recur_gate = jax.nn.sigmoid(decay_rows)
    input_open = jax.nn.sigmoid(input_rows)
    decay_now = jnp.exp(-CD * recur_gate * jax.nn.softplus(-decay_param))
    multiplier = jnp.where(
        resets[:, None], 1.0, jnp.sqrt(jnp.maximum(1.0 - decay_now * decay_now, FLOOR_VALUE))
    )
    kept_decay = jnp.where(resets[:, None], 0.0, decay_now)
    return (kept_decay, multiplier * input_open * conv_values, decay_now)


def row_scale(values):
    squares_sum = lax.psum(jnp.sum(values * values, axis=1), "tp")
    return lax.rsqrt(squares_sum / D + EPSILON)


def spread_rows(values):
    return lax.all_gather(values, "tp", axis=1, tiled=True)


def spread_grads(values):
    return lax.all_gather(values, "tp", axis=1, tiled=True)


def reduce_features(values):
    return lax.psum_scatter(values, "tp", scatter_dimension=1, tiled=True)


def norm_back(values, row_scales, gain_vector, upstream):
    weighted = upstream * gain_vector
    inner_sum = lax.psum(jnp.sum(weighted * values, axis=1), "tp")
    cubed = row_scales * row_scales * row_scales * inner_sum / D
    back_rows = row_scales[:, None] * weighted - values * cubed[:, None]
    return (back_rows, jnp.sum(upstream * values * row_scales[:, None], axis=0))


def block_mix(blocked, matrices):
    mixed_blocks = jnp.einsum("tnb,nbc->tnc", blocked, matrices, preferred_element_type=jnp.float32)
    return mixed_blocks.reshape(blocked.shape[0], -1)


def block_outer(blocked, gradients):
    shaped = gradients.reshape(blocked.shape)
    outer_sum = jnp.einsum("tnb,tnc->nbc", blocked, shaped, preferred_element_type=jnp.float32)
    return outer_sum.reshape(blocked.shape[1], -1)


def block_back(gradients, matrices):
    shaped = gradients.reshape(gradients.shape[0], matrices.shape[0], matrices.shape[1])
    backed = jnp.einsum("tnc,nbc->tnb", shaped, matrices, preferred_element_type=jnp.float32)
    return backed.reshape(gradients.shape[0], -1)


def shards_general(
    tokens,
    mix_gain,
    scan_branch,
    gate_branch,
    kernel_taps,
    kernel_bias,
    decay_gate,
    decay_bias,
    input_gate,
    input_bias,
    decay_logit,
    mixer_out,
    feed_gain,
    gate_weight,
    up_weight,
    down_weight,
    lengths,
    cotangent,
):
    row_count = tokens.shape[0]
    seq_devices = lax.axis_size("seq")
    shard_index = lax.axis_index("seq")
    offsets = seq_offsets(lengths, shard_index * row_count, row_count)
    resets = offsets == 0
    gathered = (
        lax.all_gather(mix_gain, "seq", axis=0, tiled=True),
        lax.all_gather(scan_branch, "seq", axis=0, tiled=True),
        lax.all_gather(gate_branch, "seq", axis=0, tiled=True),
        lax.all_gather(kernel_taps, "seq", axis=1, tiled=True),
        lax.all_gather(kernel_bias, "seq", axis=0, tiled=True),
        lax.all_gather(decay_gate, "seq", axis=1, tiled=True),
        lax.all_gather(decay_bias, "seq", axis=0, tiled=True),
        lax.all_gather(input_gate, "seq", axis=1, tiled=True),
        lax.all_gather(input_bias, "seq", axis=0, tiled=True),
        lax.all_gather(decay_logit, "seq", axis=0, tiled=True),
        lax.all_gather(mixer_out, "seq", axis=1, tiled=True),
        lax.all_gather(feed_gain, "seq", axis=0, tiled=True),
        lax.all_gather(gate_weight, "seq", axis=0, tiled=True),
        lax.all_gather(up_weight, "seq", axis=0, tiled=True),
        lax.all_gather(down_weight, "seq", axis=1, tiled=True),
    )
    mix_f = gathered[0].astype(jnp.float32)
    taps_f = gathered[3].astype(jnp.float32)
    taps_bias = gathered[4].astype(jnp.float32)
    feed_f = gathered[11].astype(jnp.float32)
    tokens_f = tokens.astype(jnp.float32)
    scale_first = row_scale(tokens_f)
    normed_first = spread_rows((tokens_f * scale_first[:, None] * mix_f).astype(jnp.bfloat16))
    scan_rows = matmul(normed_first, gathered[1])
    gate_rows = matmul(normed_first, gathered[2])
    gelu_rows, gelu_pull = jax.vjp(smooth_gelu, gate_rows)
    rim_rows = from_behind(scan_rows[row_count - (KW - 1) :], "seq", 1)
    padded_rows = jnp.concatenate([rim_rows, scan_rows], axis=0)
    conv_sum = taps_bias + taps_f[0] * scan_rows
    for lag_step in range(1, KW):
        lagged = padded_rows[KW - 1 - lag_step : KW - 1 - lag_step + row_count]
        conv_sum = conv_sum + jnp.where(
            (offsets >= lag_step)[:, None], taps_f[lag_step] * lagged, 0.0
        )
    conv_rows = conv_sum.astype(jnp.bfloat16)
    lanes = scan_rows.shape[1]
    groups = lanes // BW
    conv_blocks = conv_rows.reshape(row_count, groups, BW)
    decay_mats = gathered[5].reshape(groups, BW, BW)
    input_mats = gathered[7].reshape(groups, BW, BW)
    decay_rows = block_mix(conv_blocks, decay_mats) + gathered[6].astype(jnp.float32)
    input_rows = block_mix(conv_blocks, input_mats) + gathered[8].astype(jnp.float32)

    def local_terms(decay_in, input_in, logit_in, conv_in):
        kept_part, driven_part, decay_part = recurrence_terms(
            decay_in, input_in, logit_in, conv_in, resets
        )
        return ((kept_part, driven_part), decay_part)

    terms_out, terms_pull, decay_now = jax.vjp(
        local_terms,
        decay_rows,
        input_rows,
        gathered[9].astype(jnp.float32),
        conv_rows.astype(jnp.float32),
        has_aux=True,
    )
    kept_decay, driven = terms_out
    local_prod, local_state = lax.associative_scan(combine, (kept_decay, driven), axis=0)
    before = entering(
        (local_prod[row_count - 1], local_state[row_count - 1]),
        "seq",
        combine,
        (jnp.ones((lanes,), jnp.float32), jnp.zeros((lanes,), jnp.float32)),
        False,
    )
    state_in = before[1]
    hidden_state = local_state + local_prod * state_in[None, :]
    mixed = (gelu_rows * hidden_state).astype(jnp.bfloat16)
    resid = tokens_f + reduce_features(matmul(mixed, gathered[10]))
    scale_second = row_scale(resid)
    normed_second = spread_rows((resid * scale_second[:, None] * feed_f).astype(jnp.bfloat16))
    gate_pre = matmul(normed_second, gathered[12])
    up_pre = matmul(normed_second, gathered[13])
    gelu_mid, mid_pull = jax.vjp(smooth_gelu, gate_pre)
    hidden_mid = (gelu_mid * up_pre).astype(jnp.bfloat16)
    block_out = resid + reduce_features(matmul(hidden_mid, gathered[14]))
    cot_full = spread_grads(cotangent)
    down_grad = matmul_tn(hidden_mid, cot_full)
    grad_mid = matmul_nt(cot_full, gathered[14])
    grad_gate = mid_pull(grad_mid * up_pre)[0].astype(jnp.bfloat16)
    grad_up = (grad_mid * gelu_mid).astype(jnp.bfloat16)
    gate_grad = matmul_tn(normed_second, grad_gate)
    up_grad = matmul_tn(normed_second, grad_up)
    grad_second = reduce_features(
        matmul_nt(grad_gate, gathered[12]) + matmul_nt(grad_up, gathered[13])
    )
    back_second, feed_grad = norm_back(resid, scale_second, feed_f, grad_second)
    grad_resid = cotangent.astype(jnp.float32) + back_second
    grad_branch = spread_grads(grad_resid.astype(jnp.bfloat16))
    out_grad = matmul_tn(mixed, grad_branch)
    grad_mixed = matmul_nt(grad_branch, gathered[10])
    grad_hidden = grad_mixed * gelu_rows
    grad_gate_rows = gelu_pull(grad_mixed * hidden_state)[0].astype(jnp.bfloat16)
    next_decay = jnp.concatenate([kept_decay[1:], jnp.ones_like(kept_decay[:1])], axis=0)
    tail_prod, local_adjoint = lax.associative_scan(
        combine, (next_decay, grad_hidden), reverse=True, axis=0
    )
    after = entering(
        (local_prod[row_count - 1], kept_decay[0] * local_adjoint[0]),
        "seq",
        combine,
        (jnp.ones((lanes,), jnp.float32), jnp.zeros((lanes,), jnp.float32)),
        True,
    )
    adjoint_in = after[1]
    adjoint = local_adjoint + tail_prod * adjoint_in[None, :]
    prev_state = jnp.concatenate([state_in[None, :], hidden_state[:-1]], axis=0)
    grad_decay_rows, grad_input_rows, logit_grad, conv_direct = terms_pull(
        (adjoint * prev_state, adjoint)
    )
    decay_grad_low = grad_decay_rows.astype(jnp.bfloat16)
    input_grad_low = grad_input_rows.astype(jnp.bfloat16)
    decay_w_grad = block_outer(conv_blocks, decay_grad_low)
    input_w_grad = block_outer(conv_blocks, input_grad_low)
    decay_b_grad = jnp.sum(decay_grad_low.astype(jnp.float32), axis=0)
    input_b_grad = jnp.sum(input_grad_low.astype(jnp.float32), axis=0)
    grad_conv = (
        conv_direct
        + block_back(decay_grad_low, decay_mats)
        + block_back(input_grad_low, input_mats)
    )
    rim_back = from_behind(grad_conv[: KW - 1], "seq", -1)
    grad_extended = jnp.concatenate([grad_conv, rim_back], axis=0)
    ext_offsets = seq_offsets(lengths, shard_index * row_count, row_count + KW - 1)
    grad_scan = taps_f[0] * grad_conv
    tap_grads = [jnp.sum(grad_conv * scan_rows, axis=0)]
    for lag_step in range(1, KW):
        ahead = grad_extended[lag_step : lag_step + row_count]
        ahead_ok = (ext_offsets[lag_step : lag_step + row_count] >= lag_step)[:, None]
        grad_scan = grad_scan + jnp.where(ahead_ok, taps_f[lag_step] * ahead, 0.0)
        lagged = padded_rows[KW - 1 - lag_step : KW - 1 - lag_step + row_count]
        tap_grads.append(
            jnp.sum(jnp.where((offsets >= lag_step)[:, None], grad_conv * lagged, 0.0), axis=0)
        )
    taps_grad = jnp.stack(tap_grads, axis=0)
    taps_bias_grad = jnp.sum(grad_conv, axis=0)
    scan_grad_low = grad_scan.astype(jnp.bfloat16)
    scan_w_grad = matmul_tn(normed_first, scan_grad_low)
    gatebr_grad = matmul_tn(normed_first, grad_gate_rows)
    grad_first = reduce_features(
        matmul_nt(scan_grad_low, gathered[1]) + matmul_nt(grad_gate_rows, gathered[2])
    )
    back_first, mix_grad = norm_back(tokens_f, scale_first, mix_f, grad_first)
    tokens_grad = grad_resid + back_first
    decay_total = jnp.sum(decay_now, axis=0)
    summed = (
        lax.psum_scatter(mix_grad, "seq", scatter_dimension=0, tiled=True),
        lax.psum_scatter(scan_w_grad, "seq", scatter_dimension=0, tiled=True),
        lax.psum_scatter(gatebr_grad, "seq", scatter_dimension=0, tiled=True),
        lax.psum_scatter(taps_grad, "seq", scatter_dimension=1, tiled=True),
        lax.psum_scatter(taps_bias_grad, "seq", scatter_dimension=0, tiled=True),
        lax.psum_scatter(decay_w_grad, "seq", scatter_dimension=1, tiled=True),
        lax.psum_scatter(decay_b_grad, "seq", scatter_dimension=0, tiled=True),
        lax.psum_scatter(input_w_grad, "seq", scatter_dimension=1, tiled=True),
        lax.psum_scatter(input_b_grad, "seq", scatter_dimension=0, tiled=True),
        lax.psum_scatter(logit_grad, "seq", scatter_dimension=0, tiled=True),
        lax.psum_scatter(out_grad, "seq", scatter_dimension=1, tiled=True),
        lax.psum_scatter(feed_grad, "seq", scatter_dimension=0, tiled=True),
        lax.psum_scatter(gate_grad, "seq", scatter_dimension=0, tiled=True),
        lax.psum_scatter(up_grad, "seq", scatter_dimension=0, tiled=True),
        lax.psum_scatter(down_grad, "seq", scatter_dimension=1, tiled=True),
        lax.psum_scatter(decay_total, "seq", scatter_dimension=0, tiled=True),
    )
    mean_decay = summed[15] / (row_count * seq_devices)
    return (
        block_out,
        tokens_grad,
        summed[0],
        summed[1],
        summed[2],
        summed[3],
        summed[4],
        summed[5],
        summed[6],
        summed[7],
        summed[8],
        summed[9],
        summed[10],
        summed[11],
        summed[12],
        summed[13],
        summed[14],
        mean_decay,
    )


MESH = pl.DeviceIdType.MESH
F32 = jnp.float32
BF16 = jnp.bfloat16
LINE = 4
PLANE = 8
CHUNK = 128
ANY = pl.BlockSpec(memory_space=pl.ANY)
VM = pl.BlockSpec(memory_space=pltpu.VMEM)


def flip(place, bit):
    step = 1 << bit
    return place + step - 2 * step * lax.rem(place // step, 2)


def flip_all(place, bits):
    for bit in range(3):
        if bits & (1 << bit):
            place = flip(place, bit)
    return place


def meet(s, z):
    barrier = pltpu.get_barrier_semaphore()
    for bits in range(1, PLANE):
        pl.semaphore_signal(barrier, inc=1, device_id=(flip_all(s, bits), z), device_id_type=MESH)
    for step in range(1, LINE):
        pl.semaphore_signal(
            barrier, inc=1, device_id=(s, lax.rem(z + step, LINE)), device_id_type=MESH
        )
    pl.semaphore_wait(barrier, PLANE - 1 + LINE - 1)


def remote(src, dst, send, recv, target):
    return pltpu.make_async_remote_copy(
        src_ref=src,
        dst_ref=dst,
        send_sem=send,
        recv_sem=recv,
        device_id=target,
        device_id_type=MESH,
    )


class LineGather:
    def __init__(self, s, z, own_at, full_at, send, recv):
        self.s, self.z = s, z
        self.own_at, self.full_at = own_at, full_at
        self.send, self.recv = send, recv

    def copy(self, way, level, c):
        sign = 1 - 2 * way
        origin = self.z - sign * level
        src = self.own_at(c) if level == 0 else self.full_at(origin, c)
        return remote(
            src,
            self.full_at(origin, c),
            self.send.at[way, level, c],
            self.recv.at[way, level, c],
            (self.s, self.z + sign),
        )

    def arrival(self, way, level, c):
        sign = 1 - 2 * way
        part = self.full_at(self.z - sign * (level + 1), c)
        return remote(
            part,
            part,
            self.send.at[way, level, c],
            self.recv.at[way, level, c],
            (self.s, self.z + sign),
        )

    def sends(self, way, level):
        if way == 0:
            return (self.z >= level) & (self.z < LINE - 1)
        return (self.z <= LINE - 1 - level) & (self.z > 0)

    def gets(self, way, level):
        return self.z >= level + 1 if way == 0 else self.z <= LINE - 2 - level

    def start(self, c):
        for way in range(2):
            pl.when(self.sends(way, 0))(lambda way=way: self.copy(way, 0, c).start())

    def forward(self, level, c):
        for way in range(2):
            pl.when(self.gets(way, level - 1))(
                lambda way=way: self.arrival(way, level - 1, c).wait_recv()
            )
            if level < LINE - 1:
                pl.when(self.sends(way, level))(
                    lambda way=way: self.copy(way, level, c).start()
                )

    def drain(self, c):
        for way in range(2):
            for level in range(LINE - 1):
                pl.when(self.sends(way, level))(
                    lambda way=way, level=level: self.copy(way, level, c).wait_send()
                )


class PlaneGather:
    def __init__(self, s, z, own, block_at, half_at, send, recv, local):
        self.s, self.z, self.own = s, z, own
        self.block_at, self.half_at = block_at, half_at
        self.send, self.recv, self.local = send, recv, local
        self.near = (flip(s, 1), flip(s, 2))
        self.diag = flip(self.near[0], 2)
        self.twin = flip(s, 0)
        self.twin_near = (flip(self.near[0], 0), flip(self.near[1], 0))
        self.twin_diag = flip(self.diag, 0)

    def plan(self, i):
        block, half = self.block_at, self.half_at
        return (
            (self.own, block(self.s), self.near[0]),
            (self.own, block(self.s), self.near[1]),
            (half(self.near[1], 0), half(self.near[1], 0), self.near[0]),
            (half(self.near[0], 1), half(self.near[0], 1), self.near[1]),
            (self.own, block(self.s), self.twin),
            (block(self.near[0]), block(self.near[0]), self.twin),
            (block(self.near[1]), block(self.near[1]), self.twin),
            (half(self.diag, 0), half(self.diag, 0), self.twin),
            (half(self.diag, 1), half(self.diag, 1), self.twin),
        )[i]

    def landing(self, i):
        block, half = self.block_at, self.half_at
        return (
            block(self.near[0]),
            block(self.near[1]),
            half(self.diag, 0),
            half(self.diag, 1),
            block(self.twin),
            block(self.twin_near[0]),
            block(self.twin_near[1]),
            half(self.twin_diag, 0),
            half(self.twin_diag, 1),
        )[i]

    def copy(self, i):
        src, dst, target = self.plan(i)
        return remote(src, dst, self.send.at[i], self.recv.at[i], (target, self.z))

    def got(self, i):
        part = self.landing(i)
        remote(part, part, self.send.at[i], self.recv.at[i], (self.twin, self.z)).wait_recv()

    def keep(self):
        return pltpu.make_async_copy(self.own, self.block_at(self.s), self.local)

    def start(self):
        for i in (0, 1, 4):
            self.copy(i).start()
        self.keep().start()

    def turn(self):
        self.got(0)
        self.copy(3).start()
        self.copy(5).start()
        self.got(1)
        self.copy(2).start()
        self.copy(6).start()

    def last(self):
        self.got(2)
        self.copy(7).start()
        self.got(3)
        self.copy(8).start()

    def arrive(self):
        for i in range(4, 9):
            self.got(i)
        self.keep().wait()

    def drain(self):
        for i in range(9):
            self.copy(i).wait_send()


class Spread:
    def __init__(self, s, z, slot_at, send, recv):
        self.s, self.z, self.slot_at, self.send, self.recv = s, z, slot_at, send, recv

    def copy(self, bits, origin):
        slot = self.slot_at(origin)
        return remote(
            slot,
            slot,
            self.send.at[bits - 1],
            self.recv.at[bits - 1],
            (flip_all(self.s, bits), self.z),
        )

    def start(self):
        for bits in range(1, PLANE):
            self.copy(bits, self.s).start()

    def finish(self):
        for bits in range(1, PLANE):
            self.copy(bits, flip_all(self.s, bits)).wait_recv()
        for bits in range(1, PLANE):
            self.copy(bits, self.s).wait_send()


def rows_of(ref, size, parts=2):
    def block(place):
        return ref.at[pl.ds(pl.multiple_of(place * size, size), size)]

    def half(place, h):
        part = size // parts
        return ref.at[pl.ds(pl.multiple_of(place * size + h * part, part), part)]

    return block, half


def columns_of(ref, size):
    height = ref.shape[0] // 2

    def block(place):
        return ref.at[:, pl.ds(pl.multiple_of(place * size, size), size)]

    def half(place, h):
        return ref.at[
            pl.ds(h * height, height), pl.ds(pl.multiple_of(place * size, size), size)
        ]

    return block, half


def chunk_rows(c):
    return pl.ds(pl.multiple_of(c * CHUNK, CHUNK), CHUNK)


def feature_columns(z, width):
    return pl.ds(pl.multiple_of(z * width, width), width)


def each_chunk(chunks, body):
    lax.fori_loop(0, chunks, lambda c, carry: (body(c), carry)[1], 0)


def dma(*shape):
    return pltpu.SemaphoreType.DMA(shape)


def struct(shape, kind):
    return jax.ShapeDtypeStruct(shape, kind)


def vm(*shape, kind=BF16):
    return pltpu.VMEM(shape, kind)


def sigmoid(values):
    return 0.5 * jnp.tanh(0.5 * values) + 0.5


ROOT = 0.7978845608028654


def gelu_of(values):
    return 0.5 * values * (1.0 + jnp.tanh(ROOT * (values + 0.044715 * values * values * values)))


def gelu_pair(values):
    squared = values * values
    bent = jnp.tanh(ROOT * values * (1.0 + 0.044715 * squared))
    half = 0.5 * (1.0 + bent)
    slope = half + 0.5 * values * (1.0 - bent * bent) * (ROOT * (1.0 + 3 * 0.044715 * squared))
    return values * half, slope


def dot(left_side, right_side):
    return jnp.dot(left_side, right_side, preferred_element_type=F32)


def dot_nt(left_side, right_side):
    return lax.dot_general(
        left_side, right_side, (((1,), (1,)), ((), ())), preferred_element_type=F32
    )


def dot_tn(left_side, right_side):
    return lax.dot_general(
        left_side, right_side, (((0,), (0,)), ((), ())), preferred_element_type=F32
    )


SUBS = 8


LANE = 128


def put(ref, at, values):
    for lane in range(ref.shape[0]):
        ref[lane, at, :] = values[:, lane * LANE : (lane + 1) * LANE]


def get(ref, at):
    return jnp.concatenate([ref[lane, at, :] for lane in range(ref.shape[0])], axis=1)


def strided(ref, step):
    at = pl.ds(step, SUBS, stride=ref.shape[1] // SUBS)
    return [ref[lane, at, :] for lane in range(ref.shape[0])]


def strided_put(ref, step, values):
    at = pl.ds(step, SUBS, stride=ref.shape[1] // SUBS)
    for lane in range(ref.shape[0]):
        ref[lane, at, :] = values[lane]


def lanes_of(values):
    return [values[:, i * LANE : (i + 1) * LANE] for i in range(values.shape[1] // LANE)]


def first_kernel(
    tok, cot, small, gains, gate_blocks, scan, gate, mix, ffn, masks,
    row_order, tile, cells, lane_order,
    normed_out, scan_rows_out, gate_rows_out, conv_out, decay_rows_out, input_rows_out, hidden_out,
    mixed_out, scan_w_out, gate_w_out, gates_w_out,
    scales, decay_sum, par, gain_own, mix_all, ffn_all, cot_all,
    normed, scan_rows, gate_rows, conv, decay_rows, input_rows, hidden, mixed, scan_w, gate_w, gates_w,
    tok_all, small_all, gains_all, blocks_all, gain_full, kept, driven, slots,
    tok_send, tok_recv, cot_send, cot_recv, gain_send, gain_recv, plane_send, plane_recv,
    small_send, small_recv, carry_send, carry_recv, halo_send, halo_recv, local, out_sem,
):
    s, z = lax.axis_index("seq"), lax.axis_index("tp")
    rows, width = tok.shape
    chunks, features, lanes = rows // CHUNK, width * LINE, gate.shape[1]
    part = gate_blocks.shape[0]

    def line_of(own, full, send, recv):
        return LineGather(
            s, z,
            lambda c: own.at[chunk_rows(c)],
            lambda o, c: full.at[chunk_rows(c), feature_columns(o, width)],
            send, recv,
        )

    toks = line_of(tok, tok_all, tok_send, tok_recv)
    cots = line_of(cot, cot_all, cot_send, cot_recv)
    gain_line = LineGather(
        s, z, lambda c: gains_all.at[z], lambda o, c: gains_all.at[o], gain_send, gain_recv
    )
    planes = []
    for i, (own, full, make) in enumerate(
        (
            (scan, scan_w, rows_of),
            (gate, gate_w, rows_of),
            (mix, mix_all, columns_of),
            (ffn, ffn_all, rows_of),
        )
    ):
        size = own.shape[1] if make is columns_of else own.shape[0]
        planes.append(
            PlaneGather(s, z, own, *make(full, size), plane_send.at[i], plane_recv.at[i], local.at[i])
        )
    spreads = [
        Spread(s, z, lambda p: gains_all.at[z, p], small_send.at[0], small_recv.at[0]),
        Spread(s, z, lambda p: small_all.at[p], small_send.at[1], small_recv.at[1]),
        Spread(
            s, z, lambda p: blocks_all.at[pl.ds(pl.multiple_of(p * part, 16), part)],
            small_send.at[2], small_recv.at[2],
        ),
    ]
    keep = pltpu.make_async_copy(cot, cot_all.at[:, feature_columns(z, width)], local.at[6])
    keep.start()
    outs = {
        name: pltpu.make_async_copy(src, dst, out_sem.at[i])
        for i, (name, src, dst) in enumerate(
            (
                ("normed", normed, normed_out), ("scan_rows", scan_rows, scan_rows_out),
                ("gate_rows", gate_rows, gate_rows_out), ("conv", conv, conv_out),
                ("decay_rows", decay_rows, decay_rows_out), ("input_rows", input_rows, input_rows_out),
                ("hidden", hidden, hidden_out), ("mixed", mixed, mixed_out),
                ("scan_w", scan_w, scan_w_out), ("gate_w", gate_w, gate_w_out),
                ("gates_w", gates_w, gates_w_out),
            )
        )
    }
    tok_all[:, feature_columns(z, width)] = tok[...]
    gains_all[z, s] = gains[...]
    small_all[s] = small[...]
    blocks_all[pl.ds(pl.multiple_of(s * part, 16), part), :] = gate_blocks[...]
    meet(s, z)
    for spread in spreads:
        spread.start()
    for c in range(chunks):
        toks.start(c)
    for plane in planes[:2]:
        plane.start()
    for spread in spreads:
        spread.finish()
    gain_line.start(0)
    for c in range(chunks):
        toks.forward(1, c)
    gain_line.forward(1, 0)
    planes[2].start()
    planes[3].start()
    placed = dot(
        jnp.concatenate([small_all[p] for p in range(PLANE)], axis=1), lane_order[...]
    )
    par[...] = placed
    falling = jnp.exp(-placed[7:8, :])
    par[7:8, :] = CD * jnp.log1p(falling)
    par[8:9, :] = CD * falling / (1.0 + falling)
    half = blocks_all.shape[1] // 2
    for i in range(2):
        wide = dot(blocks_all[:, i * half : (i + 1) * half], tile[...]).astype(BF16)
        gates_w[:, i * lanes : (i + 1) * lanes] = dot(row_order[...], wide).astype(BF16) * cells[...]
    planes[0].turn()
    planes[1].turn()
    for c in range(chunks):
        toks.forward(2, c)
    gain_line.forward(2, 0)
    planes[0].last()
    planes[1].last()
    gain_line.forward(3, 0)
    for c in range(chunks):
        cots.start(c)
    pick = lax.broadcasted_iota(jnp.int32, (LANE, LANE), 0)
    place = lax.broadcasted_iota(jnp.int32, (LANE, LANE), 1)
    cut = LANE // 2
    even = jnp.concatenate(
        [gains_all[o, p] for o in range(LINE) for p in range(0, PLANE, 2)], axis=0
    ).astype(BF16)
    odd = jnp.concatenate(
        [gains_all[o, p] for o in range(LINE) for p in range(1, PLANE, 2)], axis=0
    ).astype(BF16)
    for i in range(2):
        from_even = (pick == place + i * cut) & (place < cut)
        from_odd = (pick == place + (i - 1) * cut) & (place >= cut)
        spots = dot(even, from_even.astype(F32).astype(BF16)) + dot(
            odd, from_odd.astype(F32).astype(BF16)
        )
        for q in range(spots.shape[0] // 8):
            gain_full[i : i + 1, q * LANE : (q + 1) * LANE] = spots[8 * q : 8 * q + 1, :]
    gain_own[0:2, :] = gain_full[0:2, feature_columns(z, width)]
    planes[0].arrive()
    planes[1].arrive()
    for name in ("scan_w", "gate_w", "gates_w"):
        outs[name].start()

    def project(c):
        toks.forward(3, c)
        at = chunk_rows(c)
        x = tok_all[at, :].astype(F32)
        scale = lax.rsqrt(jnp.sum(x * x, axis=1, keepdims=True) / features + EPSILON)
        scales[at, :] = jnp.broadcast_to(scale, (CHUNK, LANE))
        low = (x * scale * gain_full[0:1, :]).astype(BF16)
        normed[at, :] = low
        scan_rows[pl.ds(pl.multiple_of(c * CHUNK + 8, 8), CHUNK), :] = dot(low, scan_w[...])
        gate_rows[at, :] = dot(low, gate_w[...])

    each_chunk(chunks, project)
    halo = remote(
        scan_rows.at[pl.ds(rows, 8)], scan_rows.at[pl.ds(0, 8)], halo_send, halo_recv,
        (lax.rem(s + 1, PLANE), z),
    )
    first, final = s == 0, s == PLANE - 1
    pl.when(jnp.logical_not(final))(lambda: halo.start())

    @pl.when(first)
    def _():
        scan_rows[0:8, :] = jnp.zeros((8, lanes), F32)

    planes[2].turn()
    planes[3].turn()
    decay_sum[...] = jnp.zeros_like(decay_sum)
    pl.when(jnp.logical_not(first))(lambda: halo.wait_recv())
    for name in ("normed", "scan_rows", "gate_rows"):
        outs[name].start()

    def gates(c):
        at = chunk_rows(c)
        block = scan_rows[pl.ds(pl.multiple_of(c * CHUNK, 8), CHUNK + 8), :]
        mask = masks[at, :]
        total = par[4:5, :] + par[0:1, :] * block[8:, :]
        for lag in range(1, KW):
            total = total + mask[:, lag : lag + 1] * (
                par[lag : lag + 1, :] * block[8 - lag : 8 - lag + CHUNK, :]
            )
        low = total.astype(BF16)
        conv[at, :] = low
        rows_now = dot(low, gates_w[...])
        decays = rows_now[:, :lanes] + par[5:6, :]
        inputs = rows_now[:, lanes:] + par[6:7, :]
        decay_rows[at, :] = decays
        input_rows[at, :] = inputs
        decay = jnp.exp(-sigmoid(decays) * par[7:8, :])
        goes_on = mask[:, 0:1]
        multiplier = 1.0 + goes_on * (
            jnp.sqrt(jnp.maximum(1.0 - decay * decay, FLOOR_VALUE)) - 1.0
        )
        put(kept, at, goes_on * decay)
        put(driven, at, multiplier * sigmoid(inputs) * low.astype(F32))
        decay_sum[0:1, :] += jnp.sum(decay, axis=0, keepdims=True)
        cots.forward(1, c)

    each_chunk(chunks, gates)
    for name in ("conv", "decay_rows", "input_rows"):
        outs[name].start()
    planes[2].last()
    planes[3].last()
    count = rows // SUBS

    def total_of(step, carry):
        keeps, drives = strided(kept, step), strided(driven, step)
        return (
            [p * k for p, k in zip(carry[0], keeps)],
            [k * v + d for k, v, d in zip(keeps, carry[1], drives)],
        )

    groups = lanes // LANE
    product, value = lax.fori_loop(
        0,
        count,
        total_of,
        ([jnp.ones((SUBS, LANE), F32)] * groups, [jnp.zeros((SUBS, LANE), F32)] * groups),
        unroll=4,
    )
    product, value = jnp.concatenate(product, axis=1), jnp.concatenate(value, axis=1)
    whole = (jnp.ones((1, lanes), F32), jnp.zeros((1, lanes), F32))
    for sub in range(SUBS):
        here = product[sub : sub + 1, :]
        whole = (whole[0] * here, here * whole[1] + value[sub : sub + 1, :])
    slots[s, 0:1, :] = whole[0]
    slots[s, 1:2, :] = whole[1]
    spread = Spread(s, z, lambda p: slots.at[p], carry_send, carry_recv)
    spread.start()
    spread.finish()
    entry = jnp.zeros((1, lanes), F32)
    for place in range(PLANE - 1):
        entry = jnp.where(
            place < s, slots[place, 0:1, :] * entry + slots[place, 1:2, :], entry
        )
    hidden[0:8, :] = jnp.broadcast_to(entry, (8, lanes))
    entries = []
    for sub in range(SUBS):
        entries.append(entry)
        entry = product[sub : sub + 1, :] * entry + value[sub : sub + 1, :]

    def step_on(step, now):
        keeps, drives = strided(kept, step), strided(driven, step)
        now = [k * v + d for k, v, d in zip(keeps, now, drives)]
        strided_put(driven, step, now)
        return now

    lax.fori_loop(0, count, step_on, lanes_of(jnp.concatenate(entries, axis=0)), unroll=4)

    def mix(c):
        at = chunk_rows(c)
        now = get(driven, at)
        hidden[pl.ds(pl.multiple_of(c * CHUNK + 8, 8), CHUNK), :] = now
        mixed[at, :] = (gelu_of(gate_rows[at, :]) * now).astype(BF16)
        cots.forward(2, c)

    each_chunk(chunks, mix)
    for name in ("hidden", "mixed"):
        outs[name].start()
    for c in range(chunks):
        cots.forward(3, c)
    for plane in planes[2:]:
        plane.arrive()
    for plane in planes:
        plane.drain()
    for c in range(chunks):
        toks.drain(c)
        cots.drain(c)
    gain_line.drain(0)
    pl.when(jnp.logical_not(final))(lambda: halo.wait_send())
    keep.wait()
    for copy in outs.values():
        copy.wait()


def first_half(tok, cot, small, gains, gate_blocks, scan, gate, mix, ffn, masks, consts):
    rows, width = tok.shape
    features, lanes = width * LINE, gate.shape[1]
    chunks = rows // CHUNK
    return pl.pallas_call(
        first_kernel,
        out_shape=(
            struct((rows, features), BF16),
            struct((rows + 8, lanes), F32),
            struct((rows, lanes), F32),
            struct((rows, lanes), BF16),
            struct((rows, lanes), F32),
            struct((rows, lanes), F32),
            struct((rows + 8, lanes), F32),
            struct((rows, lanes), BF16),
            struct((features, lanes), BF16),
            struct((features, lanes), BF16),
            struct((lanes, 2 * lanes), BF16),
            struct((rows, LANE), F32),
            struct((8, lanes), F32),
            struct((16, lanes), F32),
            struct((8, width), F32),
            struct((mix.shape[0], mix.shape[1] * PLANE), BF16),
            struct((ffn.shape[0] * PLANE, ffn.shape[1]), BF16),
            struct((rows, features), BF16),
        ),
        in_specs=[VM] * 14,
        out_specs=[ANY] * 11 + [VM] * 4 + [ANY] * 3,
        scratch_shapes=[
            vm(rows, features), vm(rows + 8, lanes, kind=F32), vm(rows, lanes, kind=F32),
            vm(rows, lanes), vm(rows, lanes, kind=F32), vm(rows, lanes, kind=F32),
            vm(rows + 8, lanes, kind=F32), vm(rows, lanes), vm(features, lanes), vm(features, lanes),
            vm(lanes, 2 * lanes), vm(rows, features),
            vm(PLANE, *small.shape), vm(LINE, PLANE, *gains.shape, kind=F32),
            vm(PLANE * gate_blocks.shape[0], gate_blocks.shape[1]), vm(8, features, kind=F32),
            vm(lanes // LANE, rows, LANE, kind=F32), vm(lanes // LANE, rows, LANE, kind=F32),
            vm(PLANE, 8, lanes, kind=F32),
            dma(2, LINE - 1, chunks), dma(2, LINE - 1, chunks),
            dma(2, LINE - 1, chunks), dma(2, LINE - 1, chunks),
            dma(2, LINE - 1, 1), dma(2, LINE - 1, 1),
            dma(4, 9), dma(4, 9), dma(3, 7), dma(3, 7), dma(7), dma(7),
            pltpu.SemaphoreType.DMA, pltpu.SemaphoreType.DMA, dma(7), dma(11),
        ],
        compiler_params=pltpu.CompilerParams(
            collective_id=0, has_side_effects=True, vmem_limit_bytes=60 << 20
        ),
        name="first_half",
    )(tok, cot, small, gains, gate_blocks, scan, gate, mix, ffn, masks, *consts)


class WeightGrads:
    def __init__(self, s, z, stage, land, adds, add_land, own, send, recv, load):
        self.s, self.z = s, z
        self.stage, self.land, self.adds, self.add_land = stage, land, adds, add_land
        self.own, self.send, self.recv, self.load = own, send, recv, load
        self.size = own.shape[0]
        self.near = (flip(s, 1), flip(s, 2))

    def stage_of(self, k):
        return self.stage.at[pl.ds(k * self.size, self.size)]

    def copy(self, k):
        half = self.size // 2
        if k < 2:
            src, dst = self.stage_of(k), self.land.at[k]
        else:
            src = self.stage.at[pl.ds(2 * self.size + (k - 2) * half, half)]
            dst = self.add_land.at[pl.ds((k - 2) * half, half)]
        return remote(src, dst, self.send.at[k], self.recv.at[k], (self.near[k % 2], self.z))

    def product(self, owner, left, right):
        return dot_tn(left[:, feature_columns(owner, self.size)], right[...])

    def across(self, left, right):
        self.stage_of(2)[...] = self.product(flip(self.near[0], 2), left, right).astype(BF16)
        self.copy(2).start()
        self.copy(3).start()

    def beside(self, k, left, right):
        half = self.size // 2
        value = self.product(self.near[k], left, right)
        mine, other = (pl.ds(half, half), slice(half, None)), slice(0, half)
        if k == 1:
            mine, other = (pl.ds(0, half), slice(0, half)), slice(half, None)
        self.copy(3 - k).wait_recv()
        back = pltpu.make_async_copy(
            self.add_land.at[mine[0]], self.adds.at[mine[0]], self.load.at[2 + k]
        )
        back.start()
        self.stage_of(k)[other, :] = value[other].astype(BF16)
        back.wait()
        self.stage_of(k)[mine[1], :] = (value[mine[1]] + self.adds[mine[0], :].astype(F32)).astype(BF16)
        self.copy(k).start()

    def mine(self, left, right):
        self.own[...] = self.product(self.s, left, right)

    def finish(self):
        backs = []
        for k in range(2):
            self.copy(k).wait()
            self.copy(2 + k).wait_send()
            backs.append(
                pltpu.make_async_copy(self.land.at[k], self.stage_of(k), self.load.at[k])
            )
            backs[k].start()
        for back in backs:
            back.wait()
        self.own[...] += self.stage_of(0)[...].astype(F32) + self.stage_of(1)[...].astype(F32)


class LineReduce:
    def __init__(self, s, z, part, land, send, recv):
        self.s, self.z, self.part, self.land = s, z, part, land
        self.send, self.recv = send, recv

    def copy(self, o, target, slot, c):
        return remote(
            self.part.at[c, o],
            self.land.at[c, slot],
            self.send.at[o, c],
            self.recv.at[slot, c],
            (self.s, self.z + target),
        )

    def got(self, slot, c):
        part = self.land.at[c, slot]
        remote(part, part, self.send.at[0, c], self.recv.at[slot, c], (self.s, self.z)).wait_recv()

    def start(self, c):
        end = LINE - 1
        pl.when(self.z == 0)(lambda: self.copy(end, 1, LINE, c).start())
        pl.when(self.z == end)(lambda: self.copy(0, -1, LINE, c).start())
        pl.when(self.z == 0)(lambda: self.copy(2, 2, 1, c).start())
        pl.when(self.z == end)(lambda: self.copy(1, -2, 3, c).start())
        for me in range(LINE):

            def work(me=me):
                if me < end:
                    self.copy(me + 1, 1, 0, c).start()
                if me > 0:
                    self.copy(me - 1, -1, 2, c).start()

            pl.when(self.z == me)(work)

    def forward(self, c):
        end = LINE - 1
        for me, o, step, slot in ((1, end, 2, 1), (2, 0, -2, 3)):

            def work(o=o, step=step, slot=slot):
                self.got(LINE, c)
                self.part[c, o] = (
                    self.part[c, o].astype(F32) + self.land[c, LINE].astype(F32)
                ).astype(BF16)
                self.copy(o, step, slot, c).start()

            pl.when(self.z == me)(work)

    def total(self, c, into, more=False):
        slots = ((2, 3), (0, 2, 3), (0, 1, 2), (0, 1))
        for me in range(LINE):

            def work(me=me):
                for slot in slots[me]:
                    self.got(slot, c)
                value = self.land[c, slots[me][0]].astype(F32)
                for slot in slots[me][1:]:
                    value = value + self.land[c, slot].astype(F32)
                into[...] = into[...] + value if more else value

            pl.when(self.z == me)(work)

    def drain(self, c):
        for o in range(LINE):
            part = self.part.at[c, o]
            pl.when(self.z != o)(
                lambda part=part, o=o: remote(
                    part, part, self.send.at[o, c], self.recv.at[0, c], (self.s, self.z)
                ).wait_send()
            )


class LineSpread:
    def __init__(self, s, z, slot_at, send, recv):
        self.s, self.z, self.slot_at, self.send, self.recv = s, z, slot_at, send, recv

    def copy(self, step, origin, c):
        slot = self.slot_at(origin, c)
        target = (self.s, lax.rem(self.z + step, LINE))
        return remote(slot, slot, self.send.at[step - 1, c], self.recv.at[step - 1, c], target)

    def start(self, c):
        for step in range(1, LINE):
            self.copy(step, self.z, c).start()

    def finish(self, c):
        for step in range(1, LINE):
            self.copy(step, lax.rem(self.z + LINE - step, LINE), c).wait_recv()

    def drain(self, c):
        for step in range(1, LINE):
            self.copy(step, self.z, c).wait_send()


class Halves:
    def __init__(self, s, z, src, out, own, send, recv):
        self.s, self.z, self.src, self.out = s, z, src, out
        self.own, self.send, self.recv = own, send, recv

    def keep(self, c):
        at = chunk_rows(c)
        return pltpu.make_async_copy(self.src.at[at], self.out.at[0, at], self.own.at[c])

    def give(self, c):
        at = chunk_rows(c)
        return remote(
            self.src.at[at], self.out.at[1, at], self.send.at[c], self.recv.at[c],
            (flip(self.s, 0), self.z),
        )

    def start(self, c):
        self.keep(c).start()
        self.give(c).start()

    def drain(self, c):
        self.keep(c).wait()
        self.give(c).wait()


def as_row(column):
    return jnp.transpose(jnp.broadcast_to(column, (CHUNK, LANE)))[0:8, :]


def as_columns(row):
    return jnp.transpose(jnp.broadcast_to(row[0:1, :], (LANE, CHUNK)))


def in_range(c, chunks, body):
    pl.when((c >= 0) & (c < chunks))(lambda: body(c))


CUT = 768
AHEAD = 2
THIRDS = 3
GROUP = 2 * CHUNK


def group_rows(g):
    return pl.ds(pl.multiple_of(g * GROUP, GROUP), GROUP)


def feed_kernel(
    mixed, mix_w, tok, cot, gain, up, down, gate_w, cot_all,
    resid, grad, gain_grad, down_own, lands, adds, grad_all, bo_part, low_pair, cot_pair, mid_pair, gate_pair, up_pair,
    part, land, low, low_grad, cots, mid, g_gate, g_up, bo_out, gate_v, up_v, down_v,
    acc, inner, scales, squares, inners,
    red_send, red_recv, gs_send, gs_recv, line_send, line_recv, grad_send, grad_recv,
    sq_send, sq_recv, in_send, in_recv, plane_send, plane_recv, local,
    own_sem, give_send, give_recv, out_sem, load_sem, w_send, w_recv, w_load,
):
    s, z = lax.axis_index("seq"), lax.axis_index("tp")
    rows, width = tok.shape
    chunks, features = rows // CHUNK, width * LINE
    loads = [
        pltpu.make_async_copy(gate_w, gate_v, load_sem.at[0]),
        pltpu.make_async_copy(cot_all, cots, load_sem.at[1]),
    ]
    for load in loads:
        load.start()
    meet(s, z)
    red = LineReduce(s, z, part, land, red_send, red_recv)
    red_gs = LineReduce(s, z, part, land, gs_send, gs_recv)

    def line_of(full, send, recv):
        return LineGather(
            s, z,
            lambda c: full.at[chunk_rows(c), feature_columns(z, width)],
            lambda o, c: full.at[chunk_rows(c), feature_columns(o, width)],
            send, recv,
        )

    line = line_of(low, line_send, line_recv)
    grads = line_of(low_grad, grad_send, grad_recv)
    planes = [
        PlaneGather(
            s, z, up, *rows_of(up_v, up.shape[0]), plane_send.at[0], plane_recv.at[0], local.at[0]
        ),
        PlaneGather(
            s, z, down, *columns_of(down_v, down.shape[1]), plane_send.at[1], plane_recv.at[1],
            local.at[1],
        ),
    ]
    square_spread = LineSpread(s, z, lambda o, c: squares.at[o, c], sq_send, sq_recv)
    inner_spread = LineSpread(s, z, lambda o, c: inners.at[o, c], in_send, in_recv)
    pairs = [
        Halves(s, z, src, out, own_sem.at[i], give_send.at[i], give_recv.at[i])
        for i, (src, out) in enumerate(
            ((low, low_pair), (cots, cot_pair), (mid, mid_pair), (g_gate, gate_pair), (g_up, up_pair))
        )
    ]
    gain_grad[...] = jnp.zeros_like(gain_grad)

    def bo_copy(c):
        return pltpu.make_async_copy(bo_out.at[c], bo_part.at[c], out_sem.at[0, c])

    def grad_copy(c):
        at = chunk_rows(c)
        return pltpu.make_async_copy(low_grad.at[at], grad_all.at[at], out_sem.at[1, c])

    def project(c):
        values = dot(mixed[chunk_rows(c), :], mix_w[...])
        for o in range(LINE):
            here = values[:, o * width : (o + 1) * width]
            part[c, o] = here.astype(BF16)

            @pl.when(z == o)
            def _(here=here):
                resid[chunk_rows(c), :] = here

        red.start(c)

    for c in range(AHEAD):
        project(c)
    for plane in planes:
        plane.start()

    def reduced(c):
        at = chunk_rows(c)
        red.total(c, acc)
        values = tok[at, :].astype(F32) + (resid[at, :] + acc[...])
        resid[at, :] = values
        squares[z, c] = as_row(jnp.sum(values * values, axis=1, keepdims=True))
        square_spread.start(c)

    def scaled(c):
        at = chunk_rows(c)
        square_spread.finish(c)
        sums = squares[0, c] + squares[1, c] + squares[2, c] + squares[3, c]
        scale = lax.rsqrt(as_columns(sums) / features + EPSILON)
        scales[at, :] = scale
        low[at, feature_columns(z, width)] = (resid[at, :] * scale[:, 0:1] * gain[1:2, :]).astype(
            BF16
        )
        line.start(c)

    def forward(cut, g):
        at = group_rows(g)
        cols = slice(cut * CUT, (cut + 1) * CUT)
        x = low[at, :]
        gate_pre, up_pre = dot(x, gate_v[:, cols]), dot(x, up_v[:, cols])
        act, slope = gelu_pair(gate_pre)
        here = (act * up_pre).astype(BF16)
        mid[at, cols] = here
        back = dot_nt(cots[at, :], down_v[cols, :])
        gate_grad = (back * up_pre * slope).astype(BF16)
        up_grad = (back * act).astype(BF16)
        g_gate[at, cols] = gate_grad
        g_up[at, cols] = up_grad
        products = jnp.sum(
            gate_grad.astype(F32) * gate_pre + up_grad.astype(F32) * up_pre, axis=1, keepdims=True
        )
        if cut == 0:
            inner[...] = products
        else:
            inner[...] += products

    def backward(g):
        at = group_rows(g)
        back = dot_nt(g_gate[at, :], gate_v[...]) + dot_nt(g_up[at, :], up_v[...])
        for k in range(GROUP // CHUNK):
            c = g * (GROUP // CHUNK) + k
            here = slice(k * CHUNK, (k + 1) * CHUNK)
            red.drain(c)
            for o in range(LINE):
                part[c, o] = back[here, o * width : (o + 1) * width].astype(BF16)
            red_gs.start(c)
            inners[z, c] = as_row(inner[here, :])
            inner_spread.start(c)
        block = dot(mid[at, :], down_v[...])
        for k in range(GROUP // CHUNK):
            c = g * (GROUP // CHUNK) + k
            here = slice(k * CHUNK, (k + 1) * CHUNK)
            for o in range(LINE):
                bo_out[c, o] = block[here, o * width : (o + 1) * width].astype(BF16)
            for pair in pairs:
                pair.start(c)
            bo_copy(c).start()

    def turned(c):
        at = chunk_rows(c)
        red_gs.total(c, acc)
        inner_spread.finish(c)
        sums = inners[0, c] + inners[1, c] + inners[2, c] + inners[3, c]
        scale = scales[at, :]
        coef = scale * scale * as_columns(sums) / features
        above = acc[...] + part[c, z].astype(F32)
        scale, values = scale[:, 0:1], resid[at, :]
        gain_grad[0:1, :] += jnp.sum(above * values * scale, axis=0, keepdims=True)
        total = cot[at, :].astype(F32) + scale * gain[1:2, :] * above - values * coef[:, 0:1]
        grad[at, :] = total
        low_grad[at, feature_columns(z, width)] = total.astype(BF16)
        grads.start(c)

    def twice(start, body):
        def both(t):
            pl.when((t >= start) & (lax.rem(t - start, 2) == 0) & (t < start + chunks))(
                lambda: (body(t - start), body(t - start + 1)) and None
            )

        return both

    def whole(c):
        grads.forward(3, c)
        grad_copy(c).start()

    left, right = down_v, gate_v.at[pl.ds(0, 2 * rows)]
    fills = [
        pltpu.make_async_copy(
            src.at[half], dst.at[pl.ds(half * rows, rows)], load_sem.at[2 + 2 * i + half]
        )
        for i, (src, dst) in enumerate(((cot_pair, left), (mid_pair, right)))
        for half in range(2)
    ]
    weight = WeightGrads(
        s, z, mid, lands, g_up.at[pl.ds(0, features // PLANE)], adds, down_own, w_send, w_recv, w_load
    )

    def ready_pairs(c):
        for pair in pairs:
            pair.drain(c)

    def weigh_one():
        each_chunk(chunks, ready_pairs)
        for plane in planes:
            plane.drain()
        for copy in fills:
            copy.start()
        for copy in fills:
            copy.wait()
        weight.across(left, right)
        weight.mine(left, right)

    def weigh_two():
        weight.beside(0, left, right)
        weight.beside(1, left, right)

    gs_one = twice(6, lambda c: red_gs.forward(c))
    gs_three = twice(7, turned)
    to_one = twice(8, lambda c: grads.forward(1, c))
    to_two = twice(9, lambda c: grads.forward(2, c))
    to_three = twice(10, whole)

    def turn(t, carry):
        g, odd = (t - 4) // 2, lax.rem(t, 2) == 1
        ready = (t >= 4) & (t < chunks + 4)

        @pl.when(t == 2)
        def _():
            for plane in planes:
                plane.turn()

        @pl.when(t == 4)
        def _():
            for plane in planes:
                plane.last()
            for plane in planes:
                plane.arrive()
            for load in loads:
                load.wait()

        in_range(t, chunks, lambda c: red.forward(c))
        gs_one(t)
        in_range(t - 2, chunks, lambda c: line.forward(1, c))
        in_range(t - 3, chunks, lambda c: line.forward(3, c))
        to_one(t)
        to_three(t)
        pl.when(ready & jnp.logical_not(odd))(lambda: forward(0, g))
        gs_three(t)
        in_range(t - 1, chunks, reduced)
        in_range(t - 1, chunks, scaled)
        in_range(t - 2, chunks, lambda c: line.forward(2, c))
        to_two(t)
        pl.when(ready & jnp.logical_not(odd))(lambda: forward(1, g))
        pl.when(t == chunks + 4)(weigh_one)
        in_range(t + AHEAD, chunks, project)
        pl.when(ready & odd)(lambda: backward(g))
        pl.when(t == chunks + 5)(weigh_two)
        return carry

    lax.fori_loop(0, chunks + 9, turn, 0)

    def close(c):
        red_gs.drain(c)
        line.drain(c)
        grads.drain(c)
        square_spread.drain(c)
        inner_spread.drain(c)
        bo_copy(c).wait()
        grad_copy(c).wait()

    each_chunk(chunks, close)
    weight.finish()


def feed_both(mixed, mix_w, tok, cot, gain, up, down, gate_w, cot_all):
    rows, width = tok.shape
    features, hidden = width * LINE, gate_w.shape[1]
    chunks = rows // CHUNK

    def pair(size):
        return struct((2, rows, size), BF16)

    return pl.pallas_call(
        feed_kernel,
        out_shape=(
            struct((rows, width), F32),
            struct((rows, width), F32),
            struct((8, width), F32),
            struct((features // PLANE, hidden), F32),
            struct((2, features // PLANE, hidden), BF16),
            struct((features // PLANE, hidden), BF16),
            struct((rows, features), BF16),
            struct((chunks, LINE, CHUNK, width), BF16),
            pair(features), pair(features), pair(hidden), pair(hidden), pair(hidden),
        ),
        in_specs=[VM] * 7 + [ANY] * 2,
        out_specs=[VM] * 4 + [ANY] * 9,
        scratch_shapes=[
            vm(chunks, LINE, CHUNK, width), vm(chunks, LINE + 1, CHUNK, width),
            vm(rows, features), vm(rows, features), vm(rows, features),
            vm(rows, hidden), vm(rows, hidden), vm(rows, hidden),
            vm(chunks, LINE, CHUNK, width),
            vm(features, hidden), vm(features, hidden), vm(hidden, features),
            vm(CHUNK, width, kind=F32), vm(GROUP, 1, kind=F32), vm(rows, LANE, kind=F32),
            vm(LINE, chunks, 8, LANE, kind=F32), vm(LINE, chunks, 8, LANE, kind=F32),
            dma(LINE, chunks), dma(LINE + 1, chunks), dma(LINE, chunks), dma(LINE + 1, chunks),
            dma(2, LINE - 1, chunks), dma(2, LINE - 1, chunks),
            dma(2, LINE - 1, chunks), dma(2, LINE - 1, chunks),
            dma(LINE - 1, chunks), dma(LINE - 1, chunks),
            dma(LINE - 1, chunks), dma(LINE - 1, chunks),
            dma(2, 9), dma(2, 9), dma(2),
            dma(5, chunks), dma(5, chunks), dma(5, chunks), dma(2, chunks), dma(10),
            dma(4), dma(4), dma(4),
        ],
        compiler_params=pltpu.CompilerParams(
            collective_id=2, has_side_effects=True, vmem_limit_bytes=64 << 20
        ),
        name="feed_both",
    )(mixed, mix_w, tok, cot, gain, up, down, gate_w, cot_all)


def recur_back_kernel(
    masks, par, gates_w,
    low_src, mix_w_src, gate_rows_src, hidden_src, decay_rows_src, conv_src, input_rows_src, scan_rows_src,
    scales, resid, normed_src, mixed_src, bo_part, feed_pair, feed_up_pair, feed_gate_pair,
    gates_grad, sums, coefs, out, up_own, third_own,
    normed_twin, mixed_twin, low_twin, scan_pair, gate_pair, lands, third_lands, adds, third_adds,
    kept, grads, both, conv_grad, gate_low, slots, inners,
    low, mix_w, gate_rows, hidden, decay_rows, conv, input_rows, scan_rows,
    part, land, left, right, right_third, stages, stages_third, add_v, third_add_v,
    small_send, small_recv, halo_send, halo_recv, in_send, in_recv,
    own_sem, give_send, give_recv, twin_send, twin_recv,
    bo_send, bo_recv, w_send, w_recv, w_load, load_sem,
):
    s, z = lax.axis_index("seq"), lax.axis_index("tp")
    rows, features = low.shape
    lanes = gate_rows.shape[1]
    chunks = rows // CHUNK
    wholes = [
        remote(src, out, twin_send.at[i], twin_recv.at[i], (flip(s, 0), z))
        for i, (src, out) in enumerate(
            ((normed_src, normed_twin), (mixed_src, mixed_twin), (low_src, low_twin))
        )
    ]
    pairs = [
        Halves(s, z, src, out, own_sem.at[i], give_send.at[i], give_recv.at[i])
        for i, (src, out) in enumerate(
            ((both.at[:, pl.ds(0, lanes)], scan_pair), (gate_low, gate_pair))
        )
    ]
    inner_spread = LineSpread(s, z, lambda o, c: inners.at[o, c], in_send, in_recv)
    third = right_third.shape[1]
    loads = [
        pltpu.make_async_copy(src, dst, load_sem.at[i])
        for i, (src, dst) in enumerate(
            (
                (bo_part, part), (feed_pair, left), (feed_up_pair, right),
                (feed_gate_pair.at[:, pl.ds(0, third)], right_third),
                (low_src, low), (mix_w_src, mix_w), (gate_rows_src, gate_rows),
                (hidden_src, hidden), (decay_rows_src, decay_rows), (conv_src, conv),
                (input_rows_src, input_rows), (scan_rows_src, scan_rows), (resid, out),
                (scales, coefs),
            )
        )
    ]
    for load in loads[:1] + loads[4:] + loads[1:4]:
        load.start()
    meet(s, z)
    for whole in wholes:
        whole.start()
    sums[...] = jnp.zeros_like(sums)
    red = LineReduce(s, z, part, land, bo_send, bo_recv)
    weights = [
        WeightGrads(s, z, *refs, w_send.at[i], w_recv.at[i], w_load.at[i])
        for i, refs in enumerate(
            (
                (stages, lands, add_v, adds, up_own),
                (stages_third, third_lands, third_add_v, third_adds, third_own),
            )
        )
    ]
    loads[0].wait()
    for c in range(chunks):
        red.start(c)

    def result(c):
        at = chunk_rows(c)
        red.total(c, out.at[at], True)
        out[at, :] += part[c, z].astype(F32)

    def sum_on(t):
        in_range(t, chunks, lambda c: red.forward(c))
        in_range(t - 2, chunks, result)

    for load in loads[4:9]:
        load.wait()

    def start(g):
        at = group_rows(g)
        grad = dot_nt(low[at, :], mix_w[...])
        for k in range(GROUP // CHUNK):
            c = g * (GROUP // CHUNK) + k
            here = chunk_rows(c)
            act, slope = gelu_pair(gate_rows[here, :])
            now = hidden[pl.ds(pl.multiple_of(c * CHUNK + 8, 8), CHUNK), :]
            part = grad[k * CHUNK : (k + 1) * CHUNK, :]
            gate_low[here, :] = (part * now * slope).astype(BF16)
            put(grads, here, part * act)
            decay = jnp.exp(-sigmoid(decay_rows[here, :]) * par[7:8, :])
            put(kept, here, masks[here, 0:1] * decay)

    lax.fori_loop(0, rows // GROUP, lambda g, carry: (start(g), carry)[1], 0)
    for c in range(chunks):
        pairs[1].start(c)
    count, groups = rows // SUBS, lanes // LANE

    def total_of(step, carry):
        keeps, adds = strided(kept, count - 1 - step), strided(grads, count - 1 - step)
        return (
            [p * k for p, k in zip(carry[0], keeps)],
            [k * (v + a) for k, v, a in zip(keeps, carry[1], adds)],
        )

    product, value = lax.fori_loop(
        0,
        count,
        total_of,
        ([jnp.ones((SUBS, LANE), F32)] * groups, [jnp.zeros((SUBS, LANE), F32)] * groups),
        unroll=4,
    )
    product, value = jnp.concatenate(product, axis=1), jnp.concatenate(value, axis=1)
    whole = (jnp.ones((1, lanes), F32), jnp.zeros((1, lanes), F32))
    for sub in range(SUBS - 1, -1, -1):
        here = product[sub : sub + 1, :]
        whole = (whole[0] * here, here * whole[1] + value[sub : sub + 1, :])
    slots[s, 0:1, :] = whole[0]
    slots[s, 1:2, :] = whole[1]
    spread = Spread(s, z, lambda p: slots.at[p], small_send, small_recv)
    spread.start()
    for load in loads[1:4]:
        load.wait()
    weights[0].across(left, right)
    weights[1].across(left, right_third)
    spread.finish()
    entry = jnp.zeros((1, lanes), F32)
    for place in range(PLANE - 1, 0, -1):
        entry = jnp.where(
            place > s, slots[place, 0:1, :] * entry + slots[place, 1:2, :], entry
        )
    entries = []
    for sub in range(SUBS - 1, -1, -1):
        entries.append(entry)
        entry = product[sub : sub + 1, :] * entry + value[sub : sub + 1, :]

    def step_back(step, now):
        keeps, adds = strided(kept, count - 1 - step), strided(grads, count - 1 - step)
        now = [v + a for v, a in zip(now, adds)]
        strided_put(grads, count - 1 - step, now)
        return [k * v for k, v in zip(keeps, now)]

    lax.fori_loop(
        0, count, step_back, lanes_of(jnp.concatenate(entries[::-1], axis=0)), unroll=4
    )

    def gates(c):
        at = chunk_rows(c)
        tall = pl.ds(pl.multiple_of(c * CHUNK, 8), CHUNK + 8)
        adjoint = get(grads, at)
        before = hidden[tall, :][7 : 7 + CHUNK, :]
        mask = masks[at, :]
        goes_on = mask[:, 0:1]
        opened = sigmoid(decay_rows[at, :])
        entered = sigmoid(input_rows[at, :])
        rate = par[7:8, :]
        decay = jnp.exp(-opened * rate)
        room = 1.0 - decay * decay
        root = jnp.sqrt(jnp.maximum(room, FLOOR_VALUE))
        multiplier = 1.0 + goes_on * (root - 1.0)
        conv_f = conv[at, :].astype(F32)
        direct = adjoint * multiplier
        grad_input = (direct * conv_f * (entered * (1.0 - entered))).astype(BF16)
        through = jnp.where(
            room > FLOOR_VALUE, 1.0, jnp.where(room == FLOOR_VALUE, 0.5, 0.0)
        )
        grad_decay = goes_on * (
            adjoint * before - adjoint * entered * conv_f * (through * decay / root)
        )
        scaled = grad_decay * decay * opened
        grad_rows = (-scaled * rate * (1.0 - opened)).astype(BF16)
        joined = jnp.concatenate([grad_rows, grad_input], axis=1)
        both[at, :] = joined
        grad_conv = direct * entered + dot_nt(joined, gates_w[...])
        conv_grad[at, :] = grad_conv
        block = scan_rows[tall, :]
        sums[0:1, :] += jnp.sum(grad_conv * block[8:, :], axis=0, keepdims=True)
        for lag in range(1, KW):
            sums[lag : lag + 1, :] += jnp.sum(
                mask[:, lag : lag + 1] * (grad_conv * block[8 - lag : 8 - lag + CHUNK, :]),
                axis=0,
                keepdims=True,
            )
        sums[4:5, :] += jnp.sum(grad_conv, axis=0, keepdims=True)
        sums[5:6, :] += jnp.sum(grad_rows.astype(F32), axis=0, keepdims=True)
        sums[6:7, :] += jnp.sum(grad_input.astype(F32), axis=0, keepdims=True)
        sums[7:8, :] += jnp.sum(scaled, axis=0, keepdims=True)
        pl.when(c == 0)(lambda: weights[0].beside(0, left, right))
        pl.when(c == 1)(lambda: weights[0].beside(1, left, right))
        pl.when(c == 2)(lambda: weights[1].beside(0, left, right_third))
        pl.when(c == 3)(lambda: weights[1].beside(1, left, right_third))
        pl.when(c == 4)(lambda: weights[0].mine(left, right))
        pl.when(c == 5)(lambda: weights[1].mine(left, right_third))
        sum_on(c)

    for load in loads[9:]:
        load.wait()
    each_chunk(chunks, gates)
    halo = remote(
        conv_grad.at[pl.ds(0, 8)], conv_grad.at[pl.ds(rows, 8)], halo_send, halo_recv,
        (lax.rem(s + PLANE - 1, PLANE), z),
    )
    first, final = s == 0, s == PLANE - 1
    pl.when(jnp.logical_not(first))(lambda: halo.start())
    gates_grad[...] = dot_tn(conv[...], both[...])
    sums[7:8, :] = sums[7:8, :] * par[8:9, :]

    @pl.when(final)
    def _():
        conv_grad[rows : rows + 8, :] = jnp.zeros((8, lanes), F32)

    pl.when(jnp.logical_not(final))(lambda: halo.wait_recv())

    def finish(c):
        at = chunk_rows(c)
        tall = pl.ds(pl.multiple_of(c * CHUNK, 8), CHUNK + 8)
        block, mask = conv_grad[tall, :], masks[tall, :]
        total = par[0:1, :] * block[:CHUNK, :]
        for lag in range(1, KW):
            total = total + mask[lag : lag + CHUNK, lag : lag + 1] * (
                par[lag : lag + 1, :] * block[lag : lag + CHUNK, :]
            )
        grad = total.astype(BF16)
        both[at, 0:lanes] = grad
        pairs[0].start(c)
        products = grad.astype(F32) * scan_rows[
            pl.ds(pl.multiple_of(c * CHUNK + 8, 8), CHUNK), :
        ] + gate_low[at, :].astype(F32) * gate_rows[at, :]
        inners[z, c] = as_row(jnp.sum(products, axis=1, keepdims=True))
        inner_spread.start(c)
        sum_on(c + chunks)

    each_chunk(chunks, finish)
    for weight in weights:
        weight.finish()

    def close(c):
        at = chunk_rows(c)
        inner_spread.finish(c)
        total = inners[0, c] + inners[1, c] + inners[2, c] + inners[3, c]
        scale = coefs[at, :]
        coefs[at, :] = scale * scale * as_columns(total) / features
        inner_spread.drain(c)
        red.drain(c)
        for pair in pairs:
            pair.drain(c)

    each_chunk(chunks, close)
    for whole in wholes:
        whole.wait()
    pl.when(jnp.logical_not(first))(lambda: halo.wait_send())


def recur_back(low, mix_w, gate_rows, hidden, conv, decay_rows, input_rows, scan_rows, masks, par,
               gates_w, scales, resid, normed, mixed, bo_part, pairs):
    rows, features = low.shape
    lanes, width = gate_rows.shape[1], resid.shape[1]
    chunks, hidden_size, part = rows // CHUNK, pairs[1].shape[2], features // PLANE
    two = hidden_size // THIRDS * (THIRDS - 1)

    def pair(size):
        return struct((2, rows, size), BF16)

    return pl.pallas_call(
        recur_back_kernel,
        out_shape=(
            struct((lanes, 2 * lanes), F32),
            struct((8, lanes), F32),
            struct((rows, LANE), F32),
            struct((rows, width), F32),
            struct((part, hidden_size), F32),
            struct((part, two), F32),
            struct((rows, features), BF16), struct((rows, lanes), BF16), struct((rows, features), BF16),
            pair(lanes), pair(lanes),
            struct((2, part, hidden_size), BF16),
            struct((2, part, two), BF16),
            struct((part, hidden_size), BF16),
            struct((part, two), BF16),
        ),
        in_specs=[VM] * 3 + [ANY] * 16,
        out_specs=[VM] * 6 + [ANY] * 9,
        scratch_shapes=[
            vm(lanes // LANE, rows, LANE, kind=F32), vm(lanes // LANE, rows, LANE, kind=F32),
            vm(rows, 2 * lanes), vm(rows + 8, lanes, kind=F32), vm(rows, lanes),
            vm(PLANE, 8, lanes, kind=F32), vm(LINE, chunks, 8, LANE, kind=F32),
            vm(rows, features), vm(lanes, features), vm(rows, lanes, kind=F32),
            vm(rows + 8, lanes, kind=F32), vm(rows, lanes, kind=F32), vm(rows, lanes),
            vm(rows, lanes, kind=F32), vm(rows + 8, lanes, kind=F32),
            vm(chunks, LINE, CHUNK, width), vm(chunks, LINE + 1, CHUNK, width),
            vm(2 * rows, features), vm(2 * rows, hidden_size), vm(2 * rows, two),
            vm(3 * part, hidden_size), vm(3 * part, two),
            vm(part, hidden_size), vm(part, two),
            dma(7), dma(7), pltpu.SemaphoreType.DMA, pltpu.SemaphoreType.DMA,
            dma(LINE - 1, chunks), dma(LINE - 1, chunks),
            dma(2, chunks), dma(2, chunks), dma(2, chunks), dma(3), dma(3),
            dma(LINE, chunks), dma(LINE + 1, chunks), dma(2, 4), dma(2, 4), dma(2, 4), dma(14),
        ],
        compiler_params=pltpu.CompilerParams(
            collective_id=4, has_side_effects=True, vmem_limit_bytes=64 << 20
        ),
        name="recur_back",
    )(
        masks, par, gates_w, low, mix_w, gate_rows, hidden, decay_rows, conv, input_rows, scan_rows,
        scales, resid, normed, mixed, bo_part,
        *[pair.reshape(2 * rows, pair.shape[2]) for pair in pairs],
    )


def last_kernel(
    scan_w, gate_w, grad, tok, coefs, scales, gain, pack,
    normed, normed_twin, mixed, mixed_twin, low, low_twin, scan_pair, gate_pair,
    feed_pair, feed_gate_pair,
    tokens_grad, gain_grad, pack_sum, mix_own, scan_own, gate_own, third_own, lands, third_lands, adds, third_adds,
    part, land, acc, left, right, right_third, stages, stages_third, add_v, third_add_v, pack_land, gain_land,
    red_send, red_recv, w_send, w_recv, w_load, load_sem, pack_send, pack_recv, gain_send, gain_recv,
):
    s, z = lax.axis_index("seq"), lax.axis_index("tp")
    rows, width = tok.shape
    chunks = rows // CHUNK
    third = right_third.shape[1]
    loads = [
        pltpu.make_async_copy(src, dst, load_sem.at[i])
        for i, (src, dst) in enumerate(
            (
                (scan_pair, right.at[1]), (gate_pair, right.at[2]),
                (normed, left.at[1, :rows]), (normed_twin, left.at[1, rows:]),
                (mixed, right.at[0, :rows]), (mixed_twin, right.at[0, rows:]),
                (low, left.at[0, :rows]), (low_twin, left.at[0, rows:]), (feed_pair, left.at[2]),
                (feed_gate_pair.at[:, pl.ds(2 * third, third)], right_third),
            )
        )
    ]
    for load in loads:
        load.start()
    meet(s, z)
    packs = [
        remote(
            pack.at[flip_all(s, bits)], pack_land.at[s], pack_send.at[bits - 1],
            pack_recv.at[bits - 1], (flip_all(s, bits), z),
        )
        for bits in range(1, PLANE)
    ]
    for copy in packs:
        copy.start()
    red = LineReduce(s, z, part, land, red_send, red_recv)
    weights = [
        WeightGrads(
            s, z, stages.at[i], lands.at[i], add_v.at[i], adds.at[i], own,
            w_send.at[i], w_recv.at[i], w_load.at[i],
        )
        for i, own in enumerate((mix_own, scan_own, gate_own))
    ]
    weights.append(
        WeightGrads(
            s, z, stages_third, third_lands, third_add_v, third_adds, third_own,
            w_send.at[3], w_recv.at[3], w_load.at[3],
        )
    )
    gain_land[s] = jnp.zeros_like(gain_grad)

    def project(g):
        at = group_rows(g)
        values = dot_nt(right[1, at, :], scan_w[...]) + dot_nt(right[2, at, :], gate_w[...])
        for k in range(GROUP // CHUNK):
            c = g * (GROUP // CHUNK) + k
            here = slice(k * CHUNK, (k + 1) * CHUNK)
            for o in range(LINE):
                part[c, o] = values[here, o * width : (o + 1) * width].astype(BF16)
            red.start(c)

    def reduced(c):
        at = chunk_rows(c)
        red.total(c, acc)
        up = acc[...] + part[c, z].astype(F32)
        scale, values = scales[at, 0:1], tok[at, :].astype(F32)
        gain_land[s, 0:1, :] += jnp.sum(up * values * scale, axis=0, keepdims=True)
        tokens_grad[at, :] = (
            grad[at, :] + scale * gain[0:1, :] * up - values * coefs[at, 0:1]
        )

    for load in loads[:2]:
        load.wait()
    project(0)

    for g in range(1, chunks * CHUNK // GROUP):
        project(g)
    for load in loads[2:]:
        load.wait()
    factors = (
        (left.at[0], right.at[0]), (left.at[1], right.at[1]), (left.at[1], right.at[2]),
        (left.at[2], right_third),
    )
    for weight, pair in zip(weights[::-1], factors[::-1]):
        weight.across(*pair)
    for weight, pair in zip(weights[::-1], factors[::-1]):
        weight.beside(0, *pair)
        weight.beside(1, *pair)

    def weigh(t):
        for i in range(4):
            pl.when(t == i)(lambda i=i: weights[i].mine(*factors[i]))

    def turn(t, carry):
        in_range(t, chunks, lambda c: red.forward(c))
        weigh(t)
        in_range(t - 1, chunks, reduced)
        return carry

    lax.fori_loop(0, chunks + 1, turn, 0)
    gain_spread = Spread(s, z, lambda p: gain_land.at[p], gain_send, gain_recv)
    gain_spread.start()
    for bits in range(1, PLANE):
        other = pack_land.at[flip_all(s, bits)]
        remote(
            other, other, pack_send.at[bits - 1], pack_recv.at[bits - 1], (flip_all(s, bits), z)
        ).wait_recv()
    total = pack[s]
    for bits in range(1, PLANE):
        total = total + pack_land[flip_all(s, bits)]
    pack_sum[...] = total
    for weight in weights:
        weight.finish()
    gain_spread.finish()
    total = gain_land[0]
    for place in range(1, PLANE):
        total = total + gain_land[place]
    gain_grad[...] = total
    for copy in packs:
        copy.wait_send()
    each_chunk(chunks, red.drain)


def last_reduce(scan_w, gate_w, grad, tok, coefs, scales, gain, pack, pairs):
    rows, width = tok.shape
    features, lanes = width * LINE, scan_w.shape[1]
    chunks, part = rows // CHUNK, features // PLANE
    return pl.pallas_call(
        last_kernel,
        out_shape=(
            struct((rows, width), F32),
            struct((8, width), F32),
            struct(pack.shape[1:], F32),
            struct((part, lanes), F32),
            struct((part, lanes), F32),
            struct((part, lanes), F32),
            struct((part, pairs[9].shape[2] // THIRDS), F32),
            struct((3, 2, part, lanes), BF16),
            struct((2, part, pairs[9].shape[2] // THIRDS), BF16),
            struct((3, part, lanes), BF16),
            struct((part, pairs[9].shape[2] // THIRDS), BF16),
        ),
        in_specs=[VM] * 8 + [ANY] * 10,
        out_specs=[VM] * 7 + [ANY] * 4,
        scratch_shapes=[
            vm(chunks, LINE, CHUNK, width), vm(chunks, LINE + 1, CHUNK, width),
            vm(CHUNK, width, kind=F32),
            vm(3, 2 * rows, features), vm(3, 2 * rows, lanes), vm(2 * rows, pairs[9].shape[2] // THIRDS),
            vm(3, 3 * part, lanes), vm(3 * part, pairs[9].shape[2] // THIRDS),
            vm(3, part, lanes), vm(part, pairs[9].shape[2] // THIRDS),
            vm(*pack.shape, kind=F32), vm(PLANE, 8, width, kind=F32),
            dma(LINE, chunks), dma(LINE + 1, chunks),
            dma(4, 4), dma(4, 4), dma(4, 4), dma(10), dma(7), dma(7), dma(7), dma(7),
        ],
        compiler_params=pltpu.CompilerParams(
            collective_id=5, has_side_effects=True, vmem_limit_bytes=63 << 20
        ),
        name="last_reduce",
    )(
        scan_w, gate_w, grad, tok, coefs, scales, gain, pack,
        *pairs[:6],
        *[pair.reshape(2 * rows, pair.shape[2]) for pair in pairs[6:]],
    )


def placements(lanes, groups, seq_devices):
    cut, part = BW // seq_devices, lanes // seq_devices
    rows = np.arange(lanes)
    source = (rows % BW) // cut * part + rows // BW * cut + rows % cut
    row_order = (source[:, None] == rows[None, :]).astype(np.float32)
    tile = (np.arange(2 * LANE)[:, None] == rows[None, :] % BW).astype(np.float32)
    cells = (rows[:, None] // BW == rows[None, :] // BW).astype(np.float32)
    spots = np.arange(seq_devices * LANE)
    lane_order = (
        (rows[None, :] // part == spots[:, None] // LANE)
        & (rows[None, :] % part == spots[:, None] % LANE)
    ).astype(np.float32)
    return tuple(jnp.asarray(m, BF16) for m in (row_order, tile, cells, lane_order))


def shards_fast(
    tokens, mix_gain, scan_branch, gate_branch, kernel_taps, kernel_bias, decay_gate, decay_bias,
    input_gate, input_bias, decay_logit, mixer_out, feed_gain, gate_weight, up_weight, down_weight,
    lengths, cotangent,
):
    row_count, width = tokens.shape
    seq_devices = lax.axis_size("seq")
    shard_index = lax.axis_index("seq")
    ext_offsets = seq_offsets(lengths, shard_index * row_count, row_count + 8)
    lag_at = jnp.array([1, 1, 2, 3, 0, 0, 0, 0], jnp.int32)
    masks = (ext_offsets[:, None] >= lag_at[None, :]).astype(F32)
    lanes = scan_branch.shape[1]
    part = lanes // seq_devices
    groups = lanes // BW
    consts = placements(lanes, groups, seq_devices)
    small = jnp.concatenate(
        [
            kernel_taps, kernel_bias[None], decay_bias[None], input_bias[None], decay_logit[None],
            jnp.zeros((8, part), BF16),
        ]
    )
    small = jnp.pad(small, ((0, 0), (0, LANE - part)))
    gains = jnp.pad(
        jnp.concatenate([mix_gain, feed_gain]).astype(F32)[None, :], ((0, 7), (0, 0))
    )
    pad = ((0, 0), (0, 2 * LANE - BW))
    gate_blocks = jnp.concatenate(
        [jnp.pad(m.reshape(part, BW), pad) for m in (decay_gate, input_gate)], 1
    )
    (
        normed_first, scan_pad, gate_rows, conv_rows, decay_rows, input_rows, hidden_state, mixed,
        scan_w, gate_w, gates_w, scale_first_rows, decay_sums, par, gain_own, mix_w, ffn_gate, cot_full,
    ) = first_half(
        tokens, cotangent, small, gains, gate_blocks, scan_branch, gate_branch, mixer_out, gate_weight,
        masks, consts,
    )
    (
        resid, grad_resid, feed_grads, down_own, _, _, grad_branch, bo_part,
        low_pair, cot_pair, mid_pair, gate_pair, up_pair,
    ) = feed_both(
        mixed, mix_w, tokens, cotangent, gain_own, up_weight, down_weight, ffn_gate, cot_full
    )
    (
        gates_grad, sums, first_coefs, block_out, up_own, third_b,
        normed_twin, mixed_twin, branch_twin, scan_pair, gaterow_pair, *_,
    ) = recur_back(
        grad_branch, mix_w, gate_rows, hidden_state, conv_rows, decay_rows, input_rows, scan_pad,
        masks, par, gates_w, scale_first_rows, resid, normed_first, mixed, bo_part,
        (low_pair, up_pair, gate_pair),
    )

    def own_parts(rows):
        return rows.reshape(rows.shape[0], seq_devices, part).transpose(1, 0, 2)

    small = own_parts(jnp.concatenate([sums, decay_sums[0:1]], 0)).reshape(seq_devices, -1)
    tiles = [
        jnp.stack(
            [
                gates_grad[g * BW : (g + 1) * BW, i * lanes + g * BW : i * lanes + (g + 1) * BW]
                for g in range(groups)
            ]
        )
        .reshape(groups, seq_devices, -1)
        .transpose(1, 0, 2)
        .reshape(seq_devices, -1)
        for i in range(2)
    ]
    feed_part = feed_grads[0].reshape(seq_devices, -1)
    flat_grads = jnp.concatenate([*tiles, small, feed_part], 1)
    grad_rows = -(-flat_grads.shape[1] // (128 * 8)) * 8
    grad_pack = jnp.pad(flat_grads, ((0, 0), (0, grad_rows * 128 - flat_grads.shape[1])))
    tokens_grad, mix_grads, pack_sum, mix_own, scan_own, gaterow_own, third_c, *_ = last_reduce(
        scan_w, gate_w, grad_resid, tokens, first_coefs, scale_first_rows,
        gain_own,
        grad_pack.reshape(seq_devices, grad_rows, 128),
        (
            normed_first, normed_twin, mixed, mixed_twin, grad_branch, branch_twin, scan_pair,
            gaterow_pair, low_pair, gate_pair,
        ),
    )
    pack_sum = pack_sum.reshape(-1)
    gate_size = part * BW
    cut_at = 2 * gate_size
    small_sum = pack_sum[cut_at : cut_at + 9 * part].reshape(9, part)
    feed_sum = pack_sum[cut_at + 9 * part : cut_at + 9 * part + mix_gain.shape[0]]
    mix_sum = lax.dynamic_slice(
        mix_grads[0], (shard_index * mix_gain.shape[0],), (mix_gain.shape[0],)
    )
    return (
        block_out,
        tokens_grad,
        mix_sum,
        scan_own,
        gaterow_own,
        small_sum[0:KW],
        small_sum[KW],
        pack_sum[:gate_size].reshape(groups, -1),
        small_sum[KW + 1],
        pack_sum[gate_size : 2 * gate_size].reshape(groups, -1),
        small_sum[KW + 2],
        small_sum[KW + 3],
        mix_own.T,
        feed_sum,
        jnp.concatenate([third_b, third_c], axis=1),
        up_own,
        down_own.T,
        small_sum[KW + 4] / (row_count * seq_devices),
    )


def solution(mesh):
    placed = (
        P("seq", "tp"),
        P(("tp", "seq")),
        P("seq", "tp"),
        P("seq", "tp"),
        P(None, ("tp", "seq")),
        P(("tp", "seq")),
        P("tp", "seq"),
        P(("tp", "seq")),
        P("tp", "seq"),
        P(("tp", "seq")),
        P(("tp", "seq")),
        P("tp", "seq"),
        P(("tp", "seq")),
        P("seq", "tp"),
        P("seq", "tp"),
        P("tp", "seq"),
        P(),
        P("seq", "tp"),
    )
    return jax.shard_map(
        shards_fast if (mesh.shape["seq"], mesh.shape["tp"]) == (PLANE, LINE) else shards_general,
        mesh=mesh,
        in_specs=placed,
        out_specs=(
            P("seq", "tp"),
            P("seq", "tp"),
            P(("tp", "seq")),
            P("seq", "tp"),
            P("seq", "tp"),
            P(None, ("tp", "seq")),
            P(("tp", "seq")),
            P("tp", "seq"),
            P(("tp", "seq")),
            P("tp", "seq"),
            P(("tp", "seq")),
            P(("tp", "seq")),
            P("tp", "seq"),
            P(("tp", "seq")),
            P("seq", "tp"),
            P("seq", "tp"),
            P("tp", "seq"),
            P(("tp", "seq")),
        ),
        check_vma=False,
    )
```

```python
import functools

import jax
import jax.numpy as jnp
import numpy as np
from jax import lax
from jax.experimental import pallas as pl
from jax.experimental.pallas import tpu as pltpu
from jax.sharding import PartitionSpec as P


D = 2048
KW = 4
CD = 8
BW = 160


EPSILON = 1e-06
FLOOR_VALUE = 0.001


def from_behind(value, axis, steps):
    count = lax.axis_size(axis)
    initial, last = (max(0, -steps), min(count, count - steps))
    return lax.ppermute(value, axis, [(source, source + steps) for source in range(initial, last)])


def entering(part, axis, combine, identity, reverse):
    count = lax.axis_size(axis)
    place = lax.axis_index(axis)
    ahead = count - 1 - place if reverse else place
    gathered = jax.tree.map(lambda a: lax.all_gather(a, axis), part)
    state = jax.tree.map(lambda a, e: jnp.zeros_like(a) + jnp.asarray(e, a.dtype), part, identity)

    def one(turn, state):
        source = count - 1 - turn if reverse else turn
        return combine(
            state, jax.tree.map(lambda a: lax.dynamic_index_in_dim(a, source, 0, False), gathered)
        )

    return lax.fori_loop(0, ahead, one, state)


def matmul(left_side, right_side):
    return jnp.dot(left_side, right_side, preferred_element_type=jnp.float32)


def matmul_tn(left_side, right_side):
    return lax.dot_general(
        left_side, right_side, (((0,), (0,)), ((), ())), preferred_element_type=jnp.float32
    )


def matmul_nt(left_side, right_side):
    return lax.dot_general(
        left_side, right_side, (((1,), (1,)), ((), ())), preferred_element_type=jnp.float32
    )


def smooth_gelu(values):
    return jax.nn.gelu(values, approximate=True)


def combine(earlier, later):
    return (earlier[0] * later[0], later[1] + later[0] * earlier[1])


def seq_offsets(lengths, first_index, row_total):
    ends_all = jnp.cumsum(lengths, dtype=jnp.int32)
    starts_all = ends_all - lengths
    position = first_index + jnp.arange(row_total, dtype=jnp.int32)
    begins = jnp.max(
        jnp.where(starts_all[None, :] <= position[:, None], starts_all[None, :], 0), axis=1
    )
    return position - begins


def recurrence_terms(decay_rows, input_rows, decay_param, conv_values, resets):
    recur_gate = jax.nn.sigmoid(decay_rows)
    input_open = jax.nn.sigmoid(input_rows)
    decay_now = jnp.exp(-CD * recur_gate * jax.nn.softplus(-decay_param))
    multiplier = jnp.where(
        resets[:, None], 1.0, jnp.sqrt(jnp.maximum(1.0 - decay_now * decay_now, FLOOR_VALUE))
    )
    kept_decay = jnp.where(resets[:, None], 0.0, decay_now)
    return (kept_decay, multiplier * input_open * conv_values, decay_now)


def row_scale(values):
    squares_sum = lax.psum(jnp.sum(values * values, axis=1), "tp")
    return lax.rsqrt(squares_sum / D + EPSILON)


def spread_rows(values):
    return lax.all_gather(values, "tp", axis=1, tiled=True)


def spread_grads(values):
    return lax.all_gather(values, "tp", axis=1, tiled=True)


def reduce_features(values):
    return lax.psum_scatter(values, "tp", scatter_dimension=1, tiled=True)


def norm_back(values, row_scales, gain_vector, upstream):
    weighted = upstream * gain_vector
    inner_sum = lax.psum(jnp.sum(weighted * values, axis=1), "tp")
    cubed = row_scales * row_scales * row_scales * inner_sum / D
    back_rows = row_scales[:, None] * weighted - values * cubed[:, None]
    return (back_rows, jnp.sum(upstream * values * row_scales[:, None], axis=0))


def block_mix(blocked, matrices):
    mixed_blocks = jnp.einsum("tnb,nbc->tnc", blocked, matrices, preferred_element_type=jnp.float32)
    return mixed_blocks.reshape(blocked.shape[0], -1)


def block_outer(blocked, gradients):
    shaped = gradients.reshape(blocked.shape)
    outer_sum = jnp.einsum("tnb,tnc->nbc", blocked, shaped, preferred_element_type=jnp.float32)
    return outer_sum.reshape(blocked.shape[1], -1)


def block_back(gradients, matrices):
    shaped = gradients.reshape(gradients.shape[0], matrices.shape[0], matrices.shape[1])
    backed = jnp.einsum("tnc,nbc->tnb", shaped, matrices, preferred_element_type=jnp.float32)
    return backed.reshape(gradients.shape[0], -1)


def shards_general(
    tokens,
    mix_gain,
    scan_branch,
    gate_branch,
    kernel_taps,
    kernel_bias,
    decay_gate,
    decay_bias,
    input_gate,
    input_bias,
    decay_logit,
    mixer_out,
    feed_gain,
    gate_weight,
    up_weight,
    down_weight,
    lengths,
    cotangent,
):
    row_count = tokens.shape[0]
    seq_devices = lax.axis_size("seq")
    shard_index = lax.axis_index("seq")
    offsets = seq_offsets(lengths, shard_index * row_count, row_count)
    resets = offsets == 0
    gathered = (
        lax.all_gather(mix_gain, "seq", axis=0, tiled=True),
        lax.all_gather(scan_branch, "seq", axis=0, tiled=True),
        lax.all_gather(gate_branch, "seq", axis=0, tiled=True),
        lax.all_gather(kernel_taps, "seq", axis=1, tiled=True),
        lax.all_gather(kernel_bias, "seq", axis=0, tiled=True),
        lax.all_gather(decay_gate, "seq", axis=1, tiled=True),
        lax.all_gather(decay_bias, "seq", axis=0, tiled=True),
        lax.all_gather(input_gate, "seq", axis=1, tiled=True),
        lax.all_gather(input_bias, "seq", axis=0, tiled=True),
        lax.all_gather(decay_logit, "seq", axis=0, tiled=True),
        lax.all_gather(mixer_out, "seq", axis=1, tiled=True),
        lax.all_gather(feed_gain, "seq", axis=0, tiled=True),
        lax.all_gather(gate_weight, "seq", axis=0, tiled=True),
        lax.all_gather(up_weight, "seq", axis=0, tiled=True),
        lax.all_gather(down_weight, "seq", axis=1, tiled=True),
    )
    mix_f = gathered[0].astype(jnp.float32)
    taps_f = gathered[3].astype(jnp.float32)
    taps_bias = gathered[4].astype(jnp.float32)
    feed_f = gathered[11].astype(jnp.float32)
    tokens_f = tokens.astype(jnp.float32)
    scale_first = row_scale(tokens_f)
    normed_first = spread_rows((tokens_f * scale_first[:, None] * mix_f).astype(jnp.bfloat16))
    scan_rows = matmul(normed_first, gathered[1])
    gate_rows = matmul(normed_first, gathered[2])
    gelu_rows, gelu_pull = jax.vjp(smooth_gelu, gate_rows)
    rim_rows = from_behind(scan_rows[row_count - (KW - 1) :], "seq", 1)
    padded_rows = jnp.concatenate([rim_rows, scan_rows], axis=0)
    conv_sum = taps_bias + taps_f[0] * scan_rows
    for lag_step in range(1, KW):
        lagged = padded_rows[KW - 1 - lag_step : KW - 1 - lag_step + row_count]
        conv_sum = conv_sum + jnp.where(
            (offsets >= lag_step)[:, None], taps_f[lag_step] * lagged, 0.0
        )
    conv_rows = conv_sum.astype(jnp.bfloat16)
    lanes = scan_rows.shape[1]
    groups = lanes // BW
    conv_blocks = conv_rows.reshape(row_count, groups, BW)
    decay_mats = gathered[5].reshape(groups, BW, BW)
    input_mats = gathered[7].reshape(groups, BW, BW)
    decay_rows = block_mix(conv_blocks, decay_mats) + gathered[6].astype(jnp.float32)
    input_rows = block_mix(conv_blocks, input_mats) + gathered[8].astype(jnp.float32)

    def local_terms(decay_in, input_in, logit_in, conv_in):
        kept_part, driven_part, decay_part = recurrence_terms(
            decay_in, input_in, logit_in, conv_in, resets
        )
        return ((kept_part, driven_part), decay_part)

    terms_out, terms_pull, decay_now = jax.vjp(
        local_terms,
        decay_rows,
        input_rows,
        gathered[9].astype(jnp.float32),
        conv_rows.astype(jnp.float32),
        has_aux=True,
    )
    kept_decay, driven = terms_out
    local_prod, local_state = lax.associative_scan(combine, (kept_decay, driven), axis=0)
    before = entering(
        (local_prod[row_count - 1], local_state[row_count - 1]),
        "seq",
        combine,
        (jnp.ones((lanes,), jnp.float32), jnp.zeros((lanes,), jnp.float32)),
        False,
    )
    state_in = before[1]
    hidden_state = local_state + local_prod * state_in[None, :]
    mixed = (gelu_rows * hidden_state).astype(jnp.bfloat16)
    resid = tokens_f + reduce_features(matmul(mixed, gathered[10]))
    scale_second = row_scale(resid)
    normed_second = spread_rows((resid * scale_second[:, None] * feed_f).astype(jnp.bfloat16))
    gate_pre = matmul(normed_second, gathered[12])
    up_pre = matmul(normed_second, gathered[13])
    gelu_mid, mid_pull = jax.vjp(smooth_gelu, gate_pre)
    hidden_mid = (gelu_mid * up_pre).astype(jnp.bfloat16)
    block_out = resid + reduce_features(matmul(hidden_mid, gathered[14]))
    cot_full = spread_grads(cotangent)
    down_grad = matmul_tn(hidden_mid, cot_full)
    grad_mid = matmul_nt(cot_full, gathered[14])
    grad_gate = mid_pull(grad_mid * up_pre)[0].astype(jnp.bfloat16)
    grad_up = (grad_mid * gelu_mid).astype(jnp.bfloat16)
    gate_grad = matmul_tn(normed_second, grad_gate)
    up_grad = matmul_tn(normed_second, grad_up)
    grad_second = reduce_features(
        matmul_nt(grad_gate, gathered[12]) + matmul_nt(grad_up, gathered[13])
    )
    back_second, feed_grad = norm_back(resid, scale_second, feed_f, grad_second)
    grad_resid = cotangent.astype(jnp.float32) + back_second
    grad_branch = spread_grads(grad_resid.astype(jnp.bfloat16))
    out_grad = matmul_tn(mixed, grad_branch)
    grad_mixed = matmul_nt(grad_branch, gathered[10])
    grad_hidden = grad_mixed * gelu_rows
    grad_gate_rows = gelu_pull(grad_mixed * hidden_state)[0].astype(jnp.bfloat16)
    next_decay = jnp.concatenate([kept_decay[1:], jnp.ones_like(kept_decay[:1])], axis=0)
    tail_prod, local_adjoint = lax.associative_scan(
        combine, (next_decay, grad_hidden), reverse=True, axis=0
    )
    after = entering(
        (local_prod[row_count - 1], kept_decay[0] * local_adjoint[0]),
        "seq",
        combine,
        (jnp.ones((lanes,), jnp.float32), jnp.zeros((lanes,), jnp.float32)),
        True,
    )
    adjoint_in = after[1]
    adjoint = local_adjoint + tail_prod * adjoint_in[None, :]
    prev_state = jnp.concatenate([state_in[None, :], hidden_state[:-1]], axis=0)
    grad_decay_rows, grad_input_rows, logit_grad, conv_direct = terms_pull(
        (adjoint * prev_state, adjoint)
    )
    decay_grad_low = grad_decay_rows.astype(jnp.bfloat16)
    input_grad_low = grad_input_rows.astype(jnp.bfloat16)
    decay_w_grad = block_outer(conv_blocks, decay_grad_low)
    input_w_grad = block_outer(conv_blocks, input_grad_low)
    decay_b_grad = jnp.sum(decay_grad_low.astype(jnp.float32), axis=0)
    input_b_grad = jnp.sum(input_grad_low.astype(jnp.float32), axis=0)
    grad_conv = (
        conv_direct
        + block_back(decay_grad_low, decay_mats)
        + block_back(input_grad_low, input_mats)
    )
    rim_back = from_behind(grad_conv[: KW - 1], "seq", -1)
    grad_extended = jnp.concatenate([grad_conv, rim_back], axis=0)
    ext_offsets = seq_offsets(lengths, shard_index * row_count, row_count + KW - 1)
    grad_scan = taps_f[0] * grad_conv
    tap_grads = [jnp.sum(grad_conv * scan_rows, axis=0)]
    for lag_step in range(1, KW):
        ahead = grad_extended[lag_step : lag_step + row_count]
        ahead_ok = (ext_offsets[lag_step : lag_step + row_count] >= lag_step)[:, None]
        grad_scan = grad_scan + jnp.where(ahead_ok, taps_f[lag_step] * ahead, 0.0)
        lagged = padded_rows[KW - 1 - lag_step : KW - 1 - lag_step + row_count]
        tap_grads.append(
            jnp.sum(jnp.where((offsets >= lag_step)[:, None], grad_conv * lagged, 0.0), axis=0)
        )
    taps_grad = jnp.stack(tap_grads, axis=0)
    taps_bias_grad = jnp.sum(grad_conv, axis=0)
    scan_grad_low = grad_scan.astype(jnp.bfloat16)
    scan_w_grad = matmul_tn(normed_first, scan_grad_low)
    gatebr_grad = matmul_tn(normed_first, grad_gate_rows)
    grad_first = reduce_features(
        matmul_nt(scan_grad_low, gathered[1]) + matmul_nt(grad_gate_rows, gathered[2])
    )
    back_first, mix_grad = norm_back(tokens_f, scale_first, mix_f, grad_first)
    tokens_grad = grad_resid + back_first
    decay_total = jnp.sum(decay_now, axis=0)
    summed = (
        lax.psum_scatter(mix_grad, "seq", scatter_dimension=0, tiled=True),
        lax.psum_scatter(scan_w_grad, "seq", scatter_dimension=0, tiled=True),
        lax.psum_scatter(gatebr_grad, "seq", scatter_dimension=0, tiled=True),
        lax.psum_scatter(taps_grad, "seq", scatter_dimension=1, tiled=True),
        lax.psum_scatter(taps_bias_grad, "seq", scatter_dimension=0, tiled=True),
        lax.psum_scatter(decay_w_grad, "seq", scatter_dimension=1, tiled=True),
        lax.psum_scatter(decay_b_grad, "seq", scatter_dimension=0, tiled=True),
        lax.psum_scatter(input_w_grad, "seq", scatter_dimension=1, tiled=True),
        lax.psum_scatter(input_b_grad, "seq", scatter_dimension=0, tiled=True),
        lax.psum_scatter(logit_grad, "seq", scatter_dimension=0, tiled=True),
        lax.psum_scatter(out_grad, "seq", scatter_dimension=1, tiled=True),
        lax.psum_scatter(feed_grad, "seq", scatter_dimension=0, tiled=True),
        lax.psum_scatter(gate_grad, "seq", scatter_dimension=0, tiled=True),
        lax.psum_scatter(up_grad, "seq", scatter_dimension=0, tiled=True),
        lax.psum_scatter(down_grad, "seq", scatter_dimension=1, tiled=True),
        lax.psum_scatter(decay_total, "seq", scatter_dimension=0, tiled=True),
    )
    mean_decay = summed[15] / (row_count * seq_devices)
    return (
        block_out,
        tokens_grad,
        summed[0],
        summed[1],
        summed[2],
        summed[3],
        summed[4],
        summed[5],
        summed[6],
        summed[7],
        summed[8],
        summed[9],
        summed[10],
        summed[11],
        summed[12],
        summed[13],
        summed[14],
        mean_decay,
    )


MESH = pl.DeviceIdType.MESH
F32 = jnp.float32
BF16 = jnp.bfloat16
LINE = 4
PLANE = 8
CHUNK = 128
ANY = pl.BlockSpec(memory_space=pl.ANY)
VM = pl.BlockSpec(memory_space=pltpu.VMEM)


def flip(place, bit):
    step = 1 << bit
    return place + step - 2 * step * lax.rem(place // step, 2)


def flip_all(place, bits):
    for bit in range(3):
        if bits & (1 << bit):
            place = flip(place, bit)
    return place


def meet(s, z):
    barrier = pltpu.get_barrier_semaphore()
    for bits in range(1, PLANE):
        pl.semaphore_signal(barrier, inc=1, device_id=(flip_all(s, bits), z), device_id_type=MESH)
    for step in range(1, LINE):
        pl.semaphore_signal(
            barrier, inc=1, device_id=(s, lax.rem(z + step, LINE)), device_id_type=MESH
        )
    pl.semaphore_wait(barrier, PLANE - 1 + LINE - 1)


def remote(src, dst, send, recv, target):
    return pltpu.make_async_remote_copy(
        src_ref=src,
        dst_ref=dst,
        send_sem=send,
        recv_sem=recv,
        device_id=target,
        device_id_type=MESH,
    )


class LineGather:
    def __init__(self, s, z, own_at, full_at, send, recv):
        self.s, self.z = s, z
        self.own_at, self.full_at = own_at, full_at
        self.send, self.recv = send, recv

    def copy(self, way, level, c):
        sign = 1 - 2 * way
        origin = self.z - sign * level
        src = self.own_at(c) if level == 0 else self.full_at(origin, c)
        return remote(
            src,
            self.full_at(origin, c),
            self.send.at[way, level, c],
            self.recv.at[way, level, c],
            (self.s, self.z + sign),
        )

    def arrival(self, way, level, c):
        sign = 1 - 2 * way
        part = self.full_at(self.z - sign * (level + 1), c)
        return remote(
            part,
            part,
            self.send.at[way, level, c],
            self.recv.at[way, level, c],
            (self.s, self.z + sign),
        )

    def sends(self, way, level):
        if way == 0:
            return (self.z >= level) & (self.z < LINE - 1)
        return (self.z <= LINE - 1 - level) & (self.z > 0)

    def gets(self, way, level):
        return self.z >= level + 1 if way == 0 else self.z <= LINE - 2 - level

    def start(self, c):
        for way in range(2):
            pl.when(self.sends(way, 0))(lambda way=way: self.copy(way, 0, c).start())

    def forward(self, level, c):
        for way in range(2):
            pl.when(self.gets(way, level - 1))(
                lambda way=way: self.arrival(way, level - 1, c).wait_recv()
            )
            if level < LINE - 1:
                pl.when(self.sends(way, level))(
                    lambda way=way: self.copy(way, level, c).start()
                )

    def drain(self, c):
        for way in range(2):
            for level in range(LINE - 1):
                pl.when(self.sends(way, level))(
                    lambda way=way, level=level: self.copy(way, level, c).wait_send()
                )


class PlaneGather:
    def __init__(self, s, z, own, block_at, half_at, send, recv, local):
        self.s, self.z, self.own = s, z, own
        self.block_at, self.half_at = block_at, half_at
        self.send, self.recv, self.local = send, recv, local
        self.near = (flip(s, 1), flip(s, 2))
        self.diag = flip(self.near[0], 2)
        self.twin = flip(s, 0)
        self.twin_near = (flip(self.near[0], 0), flip(self.near[1], 0))
        self.twin_diag = flip(self.diag, 0)

    def plan(self, i):
        block, half = self.block_at, self.half_at
        return (
            (self.own, block(self.s), self.near[0]),
            (self.own, block(self.s), self.near[1]),
            (half(self.near[1], 0), half(self.near[1], 0), self.near[0]),
            (half(self.near[0], 1), half(self.near[0], 1), self.near[1]),
            (self.own, block(self.s), self.twin),
            (block(self.near[0]), block(self.near[0]), self.twin),
            (block(self.near[1]), block(self.near[1]), self.twin),
            (half(self.diag, 0), half(self.diag, 0), self.twin),
            (half(self.diag, 1), half(self.diag, 1), self.twin),
        )[i]

    def landing(self, i):
        block, half = self.block_at, self.half_at
        return (
            block(self.near[0]),
            block(self.near[1]),
            half(self.diag, 0),
            half(self.diag, 1),
            block(self.twin),
            block(self.twin_near[0]),
            block(self.twin_near[1]),
            half(self.twin_diag, 0),
            half(self.twin_diag, 1),
        )[i]

    def copy(self, i):
        src, dst, target = self.plan(i)
        return remote(src, dst, self.send.at[i], self.recv.at[i], (target, self.z))

    def got(self, i):
        part = self.landing(i)
        remote(part, part, self.send.at[i], self.recv.at[i], (self.twin, self.z)).wait_recv()

    def keep(self):
        return pltpu.make_async_copy(self.own, self.block_at(self.s), self.local)

    def start(self):
        for i in (0, 1, 4):
            self.copy(i).start()
        self.keep().start()

    def turn(self):
        self.got(0)
        self.copy(3).start()
        self.copy(5).start()
        self.got(1)
        self.copy(2).start()
        self.copy(6).start()

    def last(self):
        self.got(2)
        self.copy(7).start()
        self.got(3)
        self.copy(8).start()

    def arrive(self):
        for i in range(4, 9):
            self.got(i)
        self.keep().wait()

    def drain(self):
        for i in range(9):
            self.copy(i).wait_send()


class Spread:
    def __init__(self, s, z, slot_at, send, recv):
        self.s, self.z, self.slot_at, self.send, self.recv = s, z, slot_at, send, recv

    def copy(self, bits, origin):
        slot = self.slot_at(origin)
        return remote(
            slot,
            slot,
            self.send.at[bits - 1],
            self.recv.at[bits - 1],
            (flip_all(self.s, bits), self.z),
        )

    def start(self):
        for bits in range(1, PLANE):
            self.copy(bits, self.s).start()

    def finish(self):
        for bits in range(1, PLANE):
            self.copy(bits, flip_all(self.s, bits)).wait_recv()
        for bits in range(1, PLANE):
            self.copy(bits, self.s).wait_send()


def rows_of(ref, size, parts=2):
    def block(place):
        return ref.at[pl.ds(pl.multiple_of(place * size, size), size)]

    def half(place, h):
        part = size // parts
        return ref.at[pl.ds(pl.multiple_of(place * size + h * part, part), part)]

    return block, half


def columns_of(ref, size):
    height = ref.shape[0] // 2

    def block(place):
        return ref.at[:, pl.ds(pl.multiple_of(place * size, size), size)]

    def half(place, h):
        return ref.at[
            pl.ds(h * height, height), pl.ds(pl.multiple_of(place * size, size), size)
        ]

    return block, half


def chunk_rows(c):
    return pl.ds(pl.multiple_of(c * CHUNK, CHUNK), CHUNK)


def feature_columns(z, width):
    return pl.ds(pl.multiple_of(z * width, width), width)


def each_chunk(chunks, body):
    lax.fori_loop(0, chunks, lambda c, carry: (body(c), carry)[1], 0)


def dma(*shape):
    return pltpu.SemaphoreType.DMA(shape)


def struct(shape, kind):
    return jax.ShapeDtypeStruct(shape, kind)


def vm(*shape, kind=BF16):
    return pltpu.VMEM(shape, kind)


def sigmoid(values):
    return 0.5 * jnp.tanh(0.5 * values) + 0.5


ROOT = 0.7978845608028654


def gelu_of(values):
    return 0.5 * values * (1.0 + jnp.tanh(ROOT * (values + 0.044715 * values * values * values)))


def gelu_pair(values):
    squared = values * values
    bent = jnp.tanh(ROOT * values * (1.0 + 0.044715 * squared))
    half = 0.5 * (1.0 + bent)
    slope = half + 0.5 * values * (1.0 - bent * bent) * (ROOT * (1.0 + 3 * 0.044715 * squared))
    return values * half, slope


def dot(left_side, right_side):
    return jnp.dot(left_side, right_side, preferred_element_type=F32)


def dot_nt(left_side, right_side):
    return lax.dot_general(
        left_side, right_side, (((1,), (1,)), ((), ())), preferred_element_type=F32
    )


def dot_tn(left_side, right_side):
    return lax.dot_general(
        left_side, right_side, (((0,), (0,)), ((), ())), preferred_element_type=F32
    )


SUBS = 8


LANE = 128


def put(ref, at, values):
    for lane in range(ref.shape[0]):
        ref[lane, at, :] = values[:, lane * LANE : (lane + 1) * LANE]


def get(ref, at):
    return jnp.concatenate([ref[lane, at, :] for lane in range(ref.shape[0])], axis=1)


def strided(ref, step):
    at = pl.ds(step, SUBS, stride=ref.shape[1] // SUBS)
    return [ref[lane, at, :] for lane in range(ref.shape[0])]


def strided_put(ref, step, values):
    at = pl.ds(step, SUBS, stride=ref.shape[1] // SUBS)
    for lane in range(ref.shape[0]):
        ref[lane, at, :] = values[lane]


def lanes_of(values):
    return [values[:, i * LANE : (i + 1) * LANE] for i in range(values.shape[1] // LANE)]


def first_kernel(
    tok, cot, small, gains, gate_blocks, scan, gate, mix, ffn, masks,
    row_order, tile, cells, lane_order,
    normed_out, scan_rows_out, gate_rows_out, conv_out, decay_rows_out, input_rows_out, hidden_out,
    mixed_out, scan_w_out, gate_w_out, gates_w_out,
    scales, decay_sum, par, gain_own, mix_all, ffn_all, cot_all,
    normed, scan_rows, gate_rows, conv, decay_rows, input_rows, hidden, mixed, scan_w, gate_w, gates_w,
    tok_all, small_all, gains_all, blocks_all, gain_full, kept, driven, slots,
    tok_send, tok_recv, cot_send, cot_recv, gain_send, gain_recv, plane_send, plane_recv,
    small_send, small_recv, carry_send, carry_recv, halo_send, halo_recv, local, out_sem,
):
    s, z = lax.axis_index("seq"), lax.axis_index("tp")
    rows, width = tok.shape
    chunks, features, lanes = rows // CHUNK, width * LINE, gate.shape[1]
    part = gate_blocks.shape[0]

    def line_of(own, full, send, recv):
        return LineGather(
            s, z,
            lambda c: own.at[chunk_rows(c)],
            lambda o, c: full.at[chunk_rows(c), feature_columns(o, width)],
            send, recv,
        )

    toks = line_of(tok, tok_all, tok_send, tok_recv)
    cots = line_of(cot, cot_all, cot_send, cot_recv)
    gain_line = LineGather(
        s, z, lambda c: gains_all.at[z], lambda o, c: gains_all.at[o], gain_send, gain_recv
    )
    planes = []
    for i, (own, full, make) in enumerate(
        (
            (scan, scan_w, rows_of),
            (gate, gate_w, rows_of),
            (mix, mix_all, columns_of),
            (ffn, ffn_all, rows_of),
        )
    ):
        size = own.shape[1] if make is columns_of else own.shape[0]
        planes.append(
            PlaneGather(s, z, own, *make(full, size), plane_send.at[i], plane_recv.at[i], local.at[i])
        )
    spreads = [
        Spread(s, z, lambda p: gains_all.at[z, p], small_send.at[0], small_recv.at[0]),
        Spread(s, z, lambda p: small_all.at[p], small_send.at[1], small_recv.at[1]),
        Spread(
            s, z, lambda p: blocks_all.at[pl.ds(pl.multiple_of(p * part, 16), part)],
            small_send.at[2], small_recv.at[2],
        ),
    ]
    keep = pltpu.make_async_copy(cot, cot_all.at[:, feature_columns(z, width)], local.at[6])
    keep.start()
    outs = {
        name: pltpu.make_async_copy(src, dst, out_sem.at[i])
        for i, (name, src, dst) in enumerate(
            (
                ("normed", normed, normed_out), ("scan_rows", scan_rows, scan_rows_out),
                ("gate_rows", gate_rows, gate_rows_out), ("conv", conv, conv_out),
                ("decay_rows", decay_rows, decay_rows_out), ("input_rows", input_rows, input_rows_out),
                ("hidden", hidden, hidden_out), ("mixed", mixed, mixed_out),
                ("scan_w", scan_w, scan_w_out), ("gate_w", gate_w, gate_w_out),
                ("gates_w", gates_w, gates_w_out),
            )
        )
    }
    tok_all[:, feature_columns(z, width)] = tok[...]
    gains_all[z, s] = gains[...]
    small_all[s] = small[...]
    blocks_all[pl.ds(pl.multiple_of(s * part, 16), part), :] = gate_blocks[...]
    meet(s, z)
    for spread in spreads:
        spread.start()
    for c in range(chunks):
        toks.start(c)
    for plane in planes[:2]:
        plane.start()
    for spread in spreads:
        spread.finish()
    gain_line.start(0)
    for c in range(chunks):
        toks.forward(1, c)
    gain_line.forward(1, 0)
    placed = dot(
        jnp.concatenate([small_all[p] for p in range(PLANE)], axis=1), lane_order[...]
    )
    par[...] = placed
    falling = jnp.exp(-placed[7:8, :])
    par[7:8, :] = CD * jnp.log1p(falling)
    par[8:9, :] = CD * falling / (1.0 + falling)
    half = blocks_all.shape[1] // 2
    for i in range(2):
        wide = dot(blocks_all[:, i * half : (i + 1) * half], tile[...]).astype(BF16)
        gates_w[:, i * lanes : (i + 1) * lanes] = dot(row_order[...], wide).astype(BF16) * cells[...]
    planes[0].turn()
    planes[1].turn()
    planes[2].start()
    planes[3].start()
    for c in range(chunks):
        toks.forward(2, c)
    gain_line.forward(2, 0)
    planes[0].last()
    planes[1].last()
    gain_line.forward(3, 0)
    for c in range(chunks):
        cots.start(c)
    pick = lax.broadcasted_iota(jnp.int32, (LANE, LANE), 0)
    place = lax.broadcasted_iota(jnp.int32, (LANE, LANE), 1)
    cut = LANE // 2
    even = jnp.concatenate(
        [gains_all[o, p] for o in range(LINE) for p in range(0, PLANE, 2)], axis=0
    ).astype(BF16)
    odd = jnp.concatenate(
        [gains_all[o, p] for o in range(LINE) for p in range(1, PLANE, 2)], axis=0
    ).astype(BF16)
    for i in range(2):
        from_even = (pick == place + i * cut) & (place < cut)
        from_odd = (pick == place + (i - 1) * cut) & (place >= cut)
        spots = dot(even, from_even.astype(F32).astype(BF16)) + dot(
            odd, from_odd.astype(F32).astype(BF16)
        )
        for q in range(spots.shape[0] // 8):
            gain_full[i : i + 1, q * LANE : (q + 1) * LANE] = spots[8 * q : 8 * q + 1, :]
    gain_own[0:2, :] = gain_full[0:2, feature_columns(z, width)]
    planes[0].arrive()
    planes[1].arrive()
    for name in ("scan_w", "gate_w", "gates_w"):
        outs[name].start()

    def project(c):
        toks.forward(3, c)
        pl.when(c >= 2)(lambda: cots.forward(1, c - 2))
        at = chunk_rows(c)
        x = tok_all[at, :].astype(F32)
        scale = lax.rsqrt(jnp.sum(x * x, axis=1, keepdims=True) / features + EPSILON)
        scales[at, :] = jnp.broadcast_to(scale, (CHUNK, LANE))
        low = (x * scale * gain_full[0:1, :]).astype(BF16)
        normed[at, :] = low
        scan_rows[pl.ds(pl.multiple_of(c * CHUNK + 8, 8), CHUNK), :] = dot(low, scan_w[...])
        gate_rows[at, :] = dot(low, gate_w[...])

    each_chunk(chunks, project)
    halo = remote(
        scan_rows.at[pl.ds(rows, 8)], scan_rows.at[pl.ds(0, 8)], halo_send, halo_recv,
        (lax.rem(s + 1, PLANE), z),
    )
    first, final = s == 0, s == PLANE - 1
    pl.when(jnp.logical_not(final))(lambda: halo.start())

    @pl.when(first)
    def _():
        scan_rows[0:8, :] = jnp.zeros((8, lanes), F32)

    planes[2].turn()
    planes[3].turn()
    decay_sum[...] = jnp.zeros_like(decay_sum)
    pl.when(jnp.logical_not(first))(lambda: halo.wait_recv())
    for name in ("normed", "scan_rows", "gate_rows"):
        outs[name].start()

    def gates(c):
        at = chunk_rows(c)
        block = scan_rows[pl.ds(pl.multiple_of(c * CHUNK, 8), CHUNK + 8), :]
        mask = masks[at, :]
        total = par[4:5, :] + par[0:1, :] * block[8:, :]
        for lag in range(1, KW):
            total = total + mask[:, lag : lag + 1] * (
                par[lag : lag + 1, :] * block[8 - lag : 8 - lag + CHUNK, :]
            )
        low = total.astype(BF16)
        conv[at, :] = low
        rows_now = dot(low, gates_w[...])
        decays = rows_now[:, :lanes] + par[5:6, :]
        inputs = rows_now[:, lanes:] + par[6:7, :]
        decay_rows[at, :] = decays
        input_rows[at, :] = inputs
        decay = jnp.exp(-sigmoid(decays) * par[7:8, :])
        goes_on = mask[:, 0:1]
        multiplier = 1.0 + goes_on * (
            jnp.sqrt(jnp.maximum(1.0 - decay * decay, FLOOR_VALUE)) - 1.0
        )
        put(kept, at, goes_on * decay)
        put(driven, at, multiplier * sigmoid(inputs) * low.astype(F32))
        decay_sum[0:1, :] += jnp.sum(decay, axis=0, keepdims=True)
        pl.when(c < 2)(lambda: cots.forward(1, c + chunks - 2))
        pl.when(c >= 2)(lambda: cots.forward(2, c - 2))

    each_chunk(chunks, gates)
    for name in ("conv", "decay_rows", "input_rows"):
        outs[name].start()
    planes[2].last()
    planes[3].last()
    count = rows // SUBS

    def total_of(step, carry):
        keeps, drives = strided(kept, step), strided(driven, step)
        return (
            [p * k for p, k in zip(carry[0], keeps)],
            [k * v + d for k, v, d in zip(keeps, carry[1], drives)],
        )

    groups = lanes // LANE
    product, value = lax.fori_loop(
        0,
        count,
        total_of,
        ([jnp.ones((SUBS, LANE), F32)] * groups, [jnp.zeros((SUBS, LANE), F32)] * groups),
        unroll=4,
    )
    product, value = jnp.concatenate(product, axis=1), jnp.concatenate(value, axis=1)
    whole = (jnp.ones((1, lanes), F32), jnp.zeros((1, lanes), F32))
    for sub in range(SUBS):
        here = product[sub : sub + 1, :]
        whole = (whole[0] * here, here * whole[1] + value[sub : sub + 1, :])
    slots[s, 0:1, :] = whole[0]
    slots[s, 1:2, :] = whole[1]
    spread = Spread(s, z, lambda p: slots.at[p], carry_send, carry_recv)
    spread.start()
    spread.finish()
    entry = jnp.zeros((1, lanes), F32)
    for place in range(PLANE - 1):
        entry = jnp.where(
            place < s, slots[place, 0:1, :] * entry + slots[place, 1:2, :], entry
        )
    hidden[0:8, :] = jnp.broadcast_to(entry, (8, lanes))
    entries = []
    for sub in range(SUBS):
        entries.append(entry)
        entry = product[sub : sub + 1, :] * entry + value[sub : sub + 1, :]

    def step_on(step, now):
        keeps, drives = strided(kept, step), strided(driven, step)
        now = [k * v + d for k, v, d in zip(keeps, now, drives)]
        strided_put(driven, step, now)
        return now

    lax.fori_loop(0, count, step_on, lanes_of(jnp.concatenate(entries, axis=0)), unroll=4)

    def mix(c):
        at = chunk_rows(c)
        now = get(driven, at)
        hidden[pl.ds(pl.multiple_of(c * CHUNK + 8, 8), CHUNK), :] = now
        mixed[at, :] = (gelu_of(gate_rows[at, :]) * now).astype(BF16)
        pl.when(c < 2)(lambda: cots.forward(2, c + chunks - 2))

    each_chunk(chunks, mix)
    for name in ("hidden", "mixed"):
        outs[name].start()
    for c in range(chunks):
        cots.forward(3, c)
    for plane in planes[2:]:
        plane.arrive()
    for plane in planes:
        plane.drain()
    for c in range(chunks):
        toks.drain(c)
        cots.drain(c)
    gain_line.drain(0)
    pl.when(jnp.logical_not(final))(lambda: halo.wait_send())
    keep.wait()
    for copy in outs.values():
        copy.wait()


def first_half(tok, cot, small, gains, gate_blocks, scan, gate, mix, ffn, masks, consts):
    rows, width = tok.shape
    features, lanes = width * LINE, gate.shape[1]
    chunks = rows // CHUNK
    return pl.pallas_call(
        first_kernel,
        out_shape=(
            struct((rows, features), BF16),
            struct((rows + 8, lanes), F32),
            struct((rows, lanes), F32),
            struct((rows, lanes), BF16),
            struct((rows, lanes), F32),
            struct((rows, lanes), F32),
            struct((rows + 8, lanes), F32),
            struct((rows, lanes), BF16),
            struct((features, lanes), BF16),
            struct((features, lanes), BF16),
            struct((lanes, 2 * lanes), BF16),
            struct((rows, LANE), F32),
            struct((8, lanes), F32),
            struct((16, lanes), F32),
            struct((8, width), F32),
            struct((mix.shape[0], mix.shape[1] * PLANE), BF16),
            struct((ffn.shape[0] * PLANE, ffn.shape[1]), BF16),
            struct((rows, features), BF16),
        ),
        in_specs=[VM] * 14,
        out_specs=[ANY] * 11 + [VM] * 4 + [ANY] * 3,
        scratch_shapes=[
            vm(rows, features), vm(rows + 8, lanes, kind=F32), vm(rows, lanes, kind=F32),
            vm(rows, lanes), vm(rows, lanes, kind=F32), vm(rows, lanes, kind=F32),
            vm(rows + 8, lanes, kind=F32), vm(rows, lanes), vm(features, lanes), vm(features, lanes),
            vm(lanes, 2 * lanes), vm(rows, features),
            vm(PLANE, *small.shape), vm(LINE, PLANE, *gains.shape, kind=F32),
            vm(PLANE * gate_blocks.shape[0], gate_blocks.shape[1]), vm(8, features, kind=F32),
            vm(lanes // LANE, rows, LANE, kind=F32), vm(lanes // LANE, rows, LANE, kind=F32),
            vm(PLANE, 8, lanes, kind=F32),
            dma(2, LINE - 1, chunks), dma(2, LINE - 1, chunks),
            dma(2, LINE - 1, chunks), dma(2, LINE - 1, chunks),
            dma(2, LINE - 1, 1), dma(2, LINE - 1, 1),
            dma(4, 9), dma(4, 9), dma(3, 7), dma(3, 7), dma(7), dma(7),
            pltpu.SemaphoreType.DMA, pltpu.SemaphoreType.DMA, dma(7), dma(11),
        ],
        compiler_params=pltpu.CompilerParams(
            collective_id=0, has_side_effects=True, vmem_limit_bytes=60 << 20
        ),
        name="first_half",
    )(tok, cot, small, gains, gate_blocks, scan, gate, mix, ffn, masks, *consts)


class WeightGrads:
    def __init__(self, s, z, stage, land, adds, add_land, own, send, recv, load):
        self.s, self.z = s, z
        self.stage, self.land, self.adds, self.add_land = stage, land, adds, add_land
        self.own, self.send, self.recv, self.load = own, send, recv, load
        self.size = own.shape[0]
        self.near = (flip(s, 1), flip(s, 2))

    def stage_of(self, k):
        return self.stage.at[pl.ds(k * self.size, self.size)]

    def copy(self, k):
        half = self.size // 2
        if k < 2:
            src, dst = self.stage_of(k), self.land.at[k]
        else:
            src = self.stage.at[pl.ds(2 * self.size + (k - 2) * half, half)]
            dst = self.add_land.at[pl.ds((k - 2) * half, half)]
        return remote(src, dst, self.send.at[k], self.recv.at[k], (self.near[k % 2], self.z))

    def product(self, owner, left, right):
        return dot_tn(left[:, feature_columns(owner, self.size)], right[...])

    def across(self, left, right):
        self.stage_of(2)[...] = self.product(flip(self.near[0], 2), left, right).astype(BF16)
        self.copy(2).start()
        self.copy(3).start()

    def beside(self, k, left, right):
        half = self.size // 2
        value = self.product(self.near[k], left, right)
        mine, other = (pl.ds(half, half), slice(half, None)), slice(0, half)
        if k == 1:
            mine, other = (pl.ds(0, half), slice(0, half)), slice(half, None)
        self.copy(3 - k).wait_recv()
        back = pltpu.make_async_copy(
            self.add_land.at[mine[0]], self.adds.at[mine[0]], self.load.at[2 + k]
        )
        back.start()
        self.stage_of(k)[other, :] = value[other].astype(BF16)
        back.wait()
        self.stage_of(k)[mine[1], :] = (value[mine[1]] + self.adds[mine[0], :].astype(F32)).astype(BF16)
        self.copy(k).start()

    def mine(self, left, right):
        self.own[...] = self.product(self.s, left, right)

    def finish(self):
        backs = []
        for k in range(2):
            self.copy(k).wait()
            self.copy(2 + k).wait_send()
            backs.append(
                pltpu.make_async_copy(self.land.at[k], self.stage_of(k), self.load.at[k])
            )
            backs[k].start()
        for back in backs:
            back.wait()
        self.own[...] += self.stage_of(0)[...].astype(F32) + self.stage_of(1)[...].astype(F32)


class LineReduce:
    def __init__(self, s, z, part, land, send, recv):
        self.s, self.z, self.part, self.land = s, z, part, land
        self.send, self.recv = send, recv

    def copy(self, o, target, slot, c):
        return remote(
            self.part.at[c, o],
            self.land.at[c, slot],
            self.send.at[o, c],
            self.recv.at[slot, c],
            (self.s, self.z + target),
        )

    def got(self, slot, c):
        part = self.land.at[c, slot]
        remote(part, part, self.send.at[0, c], self.recv.at[slot, c], (self.s, self.z)).wait_recv()

    def start(self, c):
        self.start_ends(c)
        self.start_rest(c)

    def start_ends(self, c):
        end = LINE - 1
        pl.when(self.z == 0)(lambda: self.copy(end, 1, LINE, c).start())
        pl.when(self.z == end)(lambda: self.copy(0, -1, LINE, c).start())

    def start_rest(self, c):
        end = LINE - 1
        pl.when(self.z == 0)(lambda: self.copy(2, 2, 1, c).start())
        pl.when(self.z == end)(lambda: self.copy(1, -2, 3, c).start())
        for me in range(LINE):

            def work(me=me):
                if me < end:
                    self.copy(me + 1, 1, 0, c).start()
                if me > 0:
                    self.copy(me - 1, -1, 2, c).start()

            pl.when(self.z == me)(work)

    def forward(self, c):
        end = LINE - 1
        for me, o, step, slot in ((1, end, 2, 1), (2, 0, -2, 3)):

            def work(o=o, step=step, slot=slot):
                self.got(LINE, c)
                self.part[c, o] = (
                    self.part[c, o].astype(F32) + self.land[c, LINE].astype(F32)
                ).astype(BF16)
                self.copy(o, step, slot, c).start()

            pl.when(self.z == me)(work)

    def total(self, c, into, more=False):
        slots = ((2, 3), (0, 2, 3), (0, 1, 2), (0, 1))
        for me in range(LINE):

            def work(me=me):
                for slot in slots[me]:
                    self.got(slot, c)
                value = self.land[c, slots[me][0]].astype(F32)
                for slot in slots[me][1:]:
                    value = value + self.land[c, slot].astype(F32)
                into[...] = into[...] + value if more else value

            pl.when(self.z == me)(work)

    def drain(self, c):
        for o in range(LINE):
            part = self.part.at[c, o]
            pl.when(self.z != o)(
                lambda part=part, o=o: remote(
                    part, part, self.send.at[o, c], self.recv.at[0, c], (self.s, self.z)
                ).wait_send()
            )


class LineSpread:
    def __init__(self, s, z, slot_at, send, recv):
        self.s, self.z, self.slot_at, self.send, self.recv = s, z, slot_at, send, recv

    def copy(self, step, origin, c):
        slot = self.slot_at(origin, c)
        target = (self.s, lax.rem(self.z + step, LINE))
        return remote(slot, slot, self.send.at[step - 1, c], self.recv.at[step - 1, c], target)

    def start(self, c):
        for step in range(1, LINE):
            self.copy(step, self.z, c).start()

    def finish(self, c):
        for step in range(1, LINE):
            self.copy(step, lax.rem(self.z + LINE - step, LINE), c).wait_recv()

    def drain(self, c):
        for step in range(1, LINE):
            self.copy(step, self.z, c).wait_send()


class Halves:
    def __init__(self, s, z, src, out, own, send, recv):
        self.s, self.z, self.src, self.out = s, z, src, out
        self.own, self.send, self.recv = own, send, recv

    def keep(self, c):
        at = chunk_rows(c)
        return pltpu.make_async_copy(self.src.at[at], self.out.at[0, at], self.own.at[c])

    def give(self, c):
        at = chunk_rows(c)
        return remote(
            self.src.at[at], self.out.at[1, at], self.send.at[c], self.recv.at[c],
            (flip(self.s, 0), self.z),
        )

    def start(self, c):
        self.keep(c).start()
        self.give(c).start()

    def drain(self, c):
        self.keep(c).wait()
        self.give(c).wait()


def as_row(column):
    return jnp.transpose(jnp.broadcast_to(column, (CHUNK, LANE)))[0:8, :]


def as_columns(row):
    return jnp.transpose(jnp.broadcast_to(row[0:1, :], (LANE, CHUNK)))


def in_range(c, chunks, body):
    pl.when((c >= 0) & (c < chunks))(lambda: body(c))


CUT = 768
AHEAD = 2
THIRDS = 3
GROUP = 2 * CHUNK


def group_rows(g):
    return pl.ds(pl.multiple_of(g * GROUP, GROUP), GROUP)


def feed_kernel(
    mixed, mix_w, tok, cot, gain, up, down, gate_w, cot_all,
    resid, grad, gain_grad, down_own, lands, adds, grad_all, bo_part, low_pair, cot_pair, mid_pair, gate_pair, up_pair,
    part, land, low, low_grad, cots, mid, g_gate, g_up, bo_out, gate_v, up_v, down_v,
    acc, inner, scales, squares, inners,
    red_send, red_recv, gs_send, gs_recv, line_send, line_recv, grad_send, grad_recv,
    sq_send, sq_recv, in_send, in_recv, plane_send, plane_recv, local,
    own_sem, give_send, give_recv, out_sem, load_sem, w_send, w_recv, w_load,
):
    s, z = lax.axis_index("seq"), lax.axis_index("tp")
    rows, width = tok.shape
    chunks, features = rows // CHUNK, width * LINE
    loads = [
        pltpu.make_async_copy(gate_w, gate_v, load_sem.at[0]),
        pltpu.make_async_copy(cot_all, cots, load_sem.at[1]),
    ]
    for load in loads:
        load.start()
    meet(s, z)
    red = LineReduce(s, z, part, land, red_send, red_recv)
    red_gs = LineReduce(s, z, part, land, gs_send, gs_recv)

    def line_of(full, send, recv):
        return LineGather(
            s, z,
            lambda c: full.at[chunk_rows(c), feature_columns(z, width)],
            lambda o, c: full.at[chunk_rows(c), feature_columns(o, width)],
            send, recv,
        )

    line = line_of(low, line_send, line_recv)
    grads = line_of(low_grad, grad_send, grad_recv)
    planes = [
        PlaneGather(
            s, z, up, *rows_of(up_v, up.shape[0]), plane_send.at[0], plane_recv.at[0], local.at[0]
        ),
        PlaneGather(
            s, z, down, *columns_of(down_v, down.shape[1]), plane_send.at[1], plane_recv.at[1],
            local.at[1],
        ),
    ]
    square_spread = LineSpread(s, z, lambda o, c: squares.at[o, c], sq_send, sq_recv)
    inner_spread = LineSpread(s, z, lambda o, c: inners.at[o, c], in_send, in_recv)
    pairs = [
        Halves(s, z, src, out, own_sem.at[i], give_send.at[i], give_recv.at[i])
        for i, (src, out) in enumerate(
            ((low, low_pair), (cots, cot_pair), (mid, mid_pair), (g_gate, gate_pair), (g_up, up_pair))
        )
    ]
    gain_grad[...] = jnp.zeros_like(gain_grad)

    def bo_copy(c):
        return pltpu.make_async_copy(bo_out.at[c], bo_part.at[c], out_sem.at[0, c])

    def grad_copy(c):
        at = chunk_rows(c)
        return pltpu.make_async_copy(low_grad.at[at], grad_all.at[at], out_sem.at[1, c])

    def project(c):
        values = dot(mixed[chunk_rows(c), :], mix_w[...])
        for o in range(LINE):
            here = values[:, o * width : (o + 1) * width]
            part[c, o] = here.astype(BF16)

            @pl.when(z == o)
            def _(here=here):
                resid[chunk_rows(c), :] = here

        red.start(c)

    for c in range(AHEAD):
        project(c)
    for plane in planes:
        plane.start()

    def reduced(c):
        at = chunk_rows(c)
        red.total(c, acc)
        values = tok[at, :].astype(F32) + (resid[at, :] + acc[...])
        resid[at, :] = values
        squares[z, c] = as_row(jnp.sum(values * values, axis=1, keepdims=True))
        square_spread.start(c)

    def scaled(c):
        at = chunk_rows(c)
        square_spread.finish(c)
        sums = squares[0, c] + squares[1, c] + squares[2, c] + squares[3, c]
        scale = lax.rsqrt(as_columns(sums) / features + EPSILON)
        scales[at, :] = scale
        low[at, feature_columns(z, width)] = (resid[at, :] * scale[:, 0:1] * gain[1:2, :]).astype(
            BF16
        )
        line.start(c)

    def forward(cut, g):
        at = group_rows(g)
        cols = slice(cut * CUT, (cut + 1) * CUT)
        x = low[at, :]
        gate_pre, up_pre = dot(x, gate_v[:, cols]), dot(x, up_v[:, cols])
        act, slope = gelu_pair(gate_pre)
        here = (act * up_pre).astype(BF16)
        mid[at, cols] = here
        back = dot_nt(cots[at, :], down_v[cols, :])
        gate_grad = (back * up_pre * slope).astype(BF16)
        up_grad = (back * act).astype(BF16)
        g_gate[at, cols] = gate_grad
        g_up[at, cols] = up_grad
        products = jnp.sum(
            gate_grad.astype(F32) * gate_pre + up_grad.astype(F32) * up_pre, axis=1, keepdims=True
        )
        if cut == 0:
            inner[...] = products
        else:
            inner[...] += products

    def backward(g):
        at = group_rows(g)
        back = dot_nt(g_gate[at, :], gate_v[...]) + dot_nt(g_up[at, :], up_v[...])
        for k in range(GROUP // CHUNK):
            c = g * (GROUP // CHUNK) + k
            here = slice(k * CHUNK, (k + 1) * CHUNK)
            red.drain(c)
            for o in range(LINE):
                part[c, o] = back[here, o * width : (o + 1) * width].astype(BF16)
            red_gs.start(c)
            inners[z, c] = as_row(inner[here, :])
            inner_spread.start(c)
        block = dot(mid[at, :], down_v[...])
        for k in range(GROUP // CHUNK):
            c = g * (GROUP // CHUNK) + k
            here = slice(k * CHUNK, (k + 1) * CHUNK)
            for o in range(LINE):
                bo_out[c, o] = block[here, o * width : (o + 1) * width].astype(BF16)
            for pair in pairs:
                pair.start(c)
            bo_copy(c).start()

    def turned(c):
        at = chunk_rows(c)
        red_gs.total(c, acc)
        inner_spread.finish(c)
        sums = inners[0, c] + inners[1, c] + inners[2, c] + inners[3, c]
        scale = scales[at, :]
        coef = scale * scale * as_columns(sums) / features
        above = acc[...] + part[c, z].astype(F32)
        scale, values = scale[:, 0:1], resid[at, :]
        gain_grad[0:1, :] += jnp.sum(above * values * scale, axis=0, keepdims=True)
        total = cot[at, :].astype(F32) + scale * gain[1:2, :] * above - values * coef[:, 0:1]
        grad[at, :] = total
        low_grad[at, feature_columns(z, width)] = total.astype(BF16)
        grads.start(c)

    def twice(start, body):
        def both(t):
            pl.when((t >= start) & (lax.rem(t - start, 2) == 0) & (t < start + chunks))(
                lambda: (body(t - start), body(t - start + 1)) and None
            )

        return both

    def whole(c):
        grads.forward(3, c)
        grad_copy(c).start()

    left, right = down_v, gate_v.at[pl.ds(0, 2 * rows)]
    fills = [
        pltpu.make_async_copy(
            src.at[half], dst.at[pl.ds(half * rows, rows)], load_sem.at[2 + 2 * i + half]
        )
        for i, (src, dst) in enumerate(((cot_pair, left), (mid_pair, right)))
        for half in range(2)
    ]
    weight = WeightGrads(
        s, z, mid, lands, g_up.at[pl.ds(0, features // PLANE)], adds, down_own, w_send, w_recv, w_load
    )

    def ready_pairs(c):
        for pair in pairs:
            pair.drain(c)

    def weigh_one():
        each_chunk(chunks, ready_pairs)
        for plane in planes:
            plane.drain()
        for copy in fills:
            copy.start()
        for copy in fills:
            copy.wait()
        weight.across(left, right)
        weight.mine(left, right)

    def weigh_two():
        weight.beside(0, left, right)
        weight.beside(1, left, right)

    gs_one = twice(6, lambda c: red_gs.forward(c))
    gs_three = twice(7, turned)
    to_one = twice(8, lambda c: grads.forward(1, c))
    to_two = twice(9, lambda c: grads.forward(2, c))
    to_three = twice(10, whole)

    def turn(t, carry):
        g, odd = (t - 4) // 2, lax.rem(t, 2) == 1
        ready = (t >= 4) & (t < chunks + 4)

        @pl.when(t == 2)
        def _():
            for plane in planes:
                plane.turn()

        @pl.when(t == 4)
        def _():
            for plane in planes:
                plane.last()
            for plane in planes:
                plane.arrive()
            for load in loads:
                load.wait()

        in_range(t, chunks, lambda c: red.forward(c))
        gs_one(t)
        in_range(t - 2, chunks, lambda c: line.forward(1, c))
        in_range(t - 3, chunks, lambda c: line.forward(3, c))
        to_one(t)
        to_three(t)
        pl.when(ready & jnp.logical_not(odd))(lambda: forward(0, g))
        gs_three(t)
        pl.when(t == chunks + 5)(weigh_one)
        in_range(t - 1, chunks, reduced)
        in_range(t - 1, chunks, scaled)
        in_range(t - 2, chunks, lambda c: line.forward(2, c))
        to_two(t)
        pl.when(ready & jnp.logical_not(odd))(lambda: forward(1, g))
        in_range(t + AHEAD, chunks, project)
        pl.when(ready & odd)(lambda: backward(g))
        pl.when(t == chunks + 6)(weigh_two)
        return carry

    lax.fori_loop(0, chunks + 9, turn, 0)

    def close(c):
        red_gs.drain(c)
        line.drain(c)
        grads.drain(c)
        square_spread.drain(c)
        inner_spread.drain(c)
        bo_copy(c).wait()
        grad_copy(c).wait()

    each_chunk(chunks, close)
    weight.finish()


def feed_both(mixed, mix_w, tok, cot, gain, up, down, gate_w, cot_all):
    rows, width = tok.shape
    features, hidden = width * LINE, gate_w.shape[1]
    chunks = rows // CHUNK

    def pair(size):
        return struct((2, rows, size), BF16)

    return pl.pallas_call(
        feed_kernel,
        out_shape=(
            struct((rows, width), F32),
            struct((rows, width), F32),
            struct((8, width), F32),
            struct((features // PLANE, hidden), F32),
            struct((2, features // PLANE, hidden), BF16),
            struct((features // PLANE, hidden), BF16),
            struct((rows, features), BF16),
            struct((chunks, LINE, CHUNK, width), BF16),
            pair(features), pair(features), pair(hidden), pair(hidden), pair(hidden),
        ),
        in_specs=[VM] * 7 + [ANY] * 2,
        out_specs=[VM] * 4 + [ANY] * 9,
        scratch_shapes=[
            vm(chunks, LINE, CHUNK, width), vm(chunks, LINE + 1, CHUNK, width),
            vm(rows, features), vm(rows, features), vm(rows, features),
            vm(rows, hidden), vm(rows, hidden), vm(rows, hidden),
            vm(chunks, LINE, CHUNK, width),
            vm(features, hidden), vm(features, hidden), vm(hidden, features),
            vm(CHUNK, width, kind=F32), vm(GROUP, 1, kind=F32), vm(rows, LANE, kind=F32),
            vm(LINE, chunks, 8, LANE, kind=F32), vm(LINE, chunks, 8, LANE, kind=F32),
            dma(LINE, chunks), dma(LINE + 1, chunks), dma(LINE, chunks), dma(LINE + 1, chunks),
            dma(2, LINE - 1, chunks), dma(2, LINE - 1, chunks),
            dma(2, LINE - 1, chunks), dma(2, LINE - 1, chunks),
            dma(LINE - 1, chunks), dma(LINE - 1, chunks),
            dma(LINE - 1, chunks), dma(LINE - 1, chunks),
            dma(2, 9), dma(2, 9), dma(2),
            dma(5, chunks), dma(5, chunks), dma(5, chunks), dma(2, chunks), dma(10),
            dma(4), dma(4), dma(4),
        ],
        compiler_params=pltpu.CompilerParams(
            collective_id=2, has_side_effects=True, vmem_limit_bytes=64 << 20
        ),
        name="feed_both",
    )(mixed, mix_w, tok, cot, gain, up, down, gate_w, cot_all)


def recur_back_kernel(
    masks, par, gates_w,
    low_src, mix_w_src, gate_rows_src, hidden_src, decay_rows_src, conv_src, input_rows_src, scan_rows_src,
    scales, resid, normed_src, mixed_src, bo_part, feed_pair, feed_up_pair, feed_gate_pair,
    gates_grad, sums, coefs, out, up_own, third_own,
    normed_twin, mixed_twin, low_twin, scan_pair, gate_pair, lands, third_lands, adds, third_adds,
    kept, grads, both, conv_grad, gate_low, slots, inners,
    low, mix_w, gate_rows, hidden, decay_rows, conv, input_rows, scan_rows,
    part, land, left, right, right_third, stages, stages_third, add_v, third_add_v,
    small_send, small_recv, halo_send, halo_recv, in_send, in_recv,
    own_sem, give_send, give_recv, twin_send, twin_recv,
    bo_send, bo_recv, w_send, w_recv, w_load, load_sem,
):
    s, z = lax.axis_index("seq"), lax.axis_index("tp")
    rows, features = low.shape
    lanes = gate_rows.shape[1]
    chunks = rows // CHUNK
    wholes = [
        remote(src, out, twin_send.at[i], twin_recv.at[i], (flip(s, 0), z))
        for i, (src, out) in enumerate(
            ((normed_src, normed_twin), (mixed_src, mixed_twin), (low_src, low_twin))
        )
    ]
    pairs = [
        Halves(s, z, src, out, own_sem.at[i], give_send.at[i], give_recv.at[i])
        for i, (src, out) in enumerate(
            ((both.at[:, pl.ds(0, lanes)], scan_pair), (gate_low, gate_pair))
        )
    ]
    inner_spread = LineSpread(s, z, lambda o, c: inners.at[o, c], in_send, in_recv)
    third = right_third.shape[1]
    loads = [
        pltpu.make_async_copy(src, dst, load_sem.at[i])
        for i, (src, dst) in enumerate(
            (
                (bo_part, part), (feed_pair, left), (feed_up_pair, right),
                (feed_gate_pair.at[:, pl.ds(0, third)], right_third),
                (low_src, low), (mix_w_src, mix_w), (gate_rows_src, gate_rows),
                (hidden_src, hidden), (decay_rows_src, decay_rows), (conv_src, conv),
                (input_rows_src, input_rows), (scan_rows_src, scan_rows), (resid, out),
                (scales, coefs),
            )
        )
    ]
    for load in loads[:1] + loads[4:] + loads[1:4]:
        load.start()
    meet(s, z)
    for whole in wholes:
        whole.start()
    sums[...] = jnp.zeros_like(sums)
    red = LineReduce(s, z, part, land, bo_send, bo_recv)
    weights = [
        WeightGrads(s, z, *refs, w_send.at[i], w_recv.at[i], w_load.at[i])
        for i, refs in enumerate(
            (
                (stages, lands, add_v, adds, up_own),
                (stages_third, third_lands, third_add_v, third_adds, third_own),
            )
        )
    ]
    loads[0].wait()
    for c in range(chunks):
        red.start_ends(c)
    for c in range(chunks):
        red.start_rest(c)

    def result(c):
        at = chunk_rows(c)
        red.total(c, out.at[at], True)
        out[at, :] += part[c, z].astype(F32)

    def sum_on(t):
        in_range(t, chunks, lambda c: red.forward(c))
        in_range(t - 2, chunks, result)

    for load in loads[4:9]:
        load.wait()

    def start(g):
        at = group_rows(g)
        grad = dot_nt(low[at, :], mix_w[...])
        for k in range(GROUP // CHUNK):
            c = g * (GROUP // CHUNK) + k
            here = chunk_rows(c)
            act, slope = gelu_pair(gate_rows[here, :])
            now = hidden[pl.ds(pl.multiple_of(c * CHUNK + 8, 8), CHUNK), :]
            part = grad[k * CHUNK : (k + 1) * CHUNK, :]
            gate_low[here, :] = (part * now * slope).astype(BF16)
            put(grads, here, part * act)
            decay = jnp.exp(-sigmoid(decay_rows[here, :]) * par[7:8, :])
            put(kept, here, masks[here, 0:1] * decay)

    lax.fori_loop(0, rows // GROUP, lambda g, carry: (start(g), carry)[1], 0)
    for c in range(chunks):
        pairs[1].start(c)
    count, groups = rows // SUBS, lanes // LANE

    def total_of(step, carry):
        keeps, adds = strided(kept, count - 1 - step), strided(grads, count - 1 - step)
        return (
            [p * k for p, k in zip(carry[0], keeps)],
            [k * (v + a) for k, v, a in zip(keeps, carry[1], adds)],
        )

    product, value = lax.fori_loop(
        0,
        count,
        total_of,
        ([jnp.ones((SUBS, LANE), F32)] * groups, [jnp.zeros((SUBS, LANE), F32)] * groups),
        unroll=4,
    )
    product, value = jnp.concatenate(product, axis=1), jnp.concatenate(value, axis=1)
    whole = (jnp.ones((1, lanes), F32), jnp.zeros((1, lanes), F32))
    for sub in range(SUBS - 1, -1, -1):
        here = product[sub : sub + 1, :]
        whole = (whole[0] * here, here * whole[1] + value[sub : sub + 1, :])
    slots[s, 0:1, :] = whole[0]
    slots[s, 1:2, :] = whole[1]
    spread = Spread(s, z, lambda p: slots.at[p], small_send, small_recv)
    spread.start()
    for load in loads[1:4]:
        load.wait()
    weights[0].across(left, right)
    weights[1].across(left, right_third)
    spread.finish()
    entry = jnp.zeros((1, lanes), F32)
    for place in range(PLANE - 1, 0, -1):
        entry = jnp.where(
            place > s, slots[place, 0:1, :] * entry + slots[place, 1:2, :], entry
        )
    entries = []
    for sub in range(SUBS - 1, -1, -1):
        entries.append(entry)
        entry = product[sub : sub + 1, :] * entry + value[sub : sub + 1, :]

    def step_back(step, now):
        keeps, adds = strided(kept, count - 1 - step), strided(grads, count - 1 - step)
        now = [v + a for v, a in zip(now, adds)]
        strided_put(grads, count - 1 - step, now)
        return [k * v for k, v in zip(keeps, now)]

    lax.fori_loop(
        0, count, step_back, lanes_of(jnp.concatenate(entries[::-1], axis=0)), unroll=4
    )

    def gates(c):
        at = chunk_rows(c)
        tall = pl.ds(pl.multiple_of(c * CHUNK, 8), CHUNK + 8)
        adjoint = get(grads, at)
        before = hidden[tall, :][7 : 7 + CHUNK, :]
        mask = masks[at, :]
        goes_on = mask[:, 0:1]
        opened = sigmoid(decay_rows[at, :])
        entered = sigmoid(input_rows[at, :])
        rate = par[7:8, :]
        decay = jnp.exp(-opened * rate)
        room = 1.0 - decay * decay
        root = jnp.sqrt(jnp.maximum(room, FLOOR_VALUE))
        multiplier = 1.0 + goes_on * (root - 1.0)
        conv_f = conv[at, :].astype(F32)
        direct = adjoint * multiplier
        grad_input = (direct * conv_f * (entered * (1.0 - entered))).astype(BF16)
        through = jnp.where(
            room > FLOOR_VALUE, 1.0, jnp.where(room == FLOOR_VALUE, 0.5, 0.0)
        )
        grad_decay = goes_on * (
            adjoint * before - adjoint * entered * conv_f * (through * decay / root)
        )
        scaled = grad_decay * decay * opened
        grad_rows = (-scaled * rate * (1.0 - opened)).astype(BF16)
        joined = jnp.concatenate([grad_rows, grad_input], axis=1)
        both[at, :] = joined
        grad_conv = direct * entered + dot_nt(joined, gates_w[...])
        conv_grad[at, :] = grad_conv
        block = scan_rows[tall, :]
        sums[0:1, :] += jnp.sum(grad_conv * block[8:, :], axis=0, keepdims=True)
        for lag in range(1, KW):
            sums[lag : lag + 1, :] += jnp.sum(
                mask[:, lag : lag + 1] * (grad_conv * block[8 - lag : 8 - lag + CHUNK, :]),
                axis=0,
                keepdims=True,
            )
        sums[4:5, :] += jnp.sum(grad_conv, axis=0, keepdims=True)
        sums[5:6, :] += jnp.sum(grad_rows.astype(F32), axis=0, keepdims=True)
        sums[6:7, :] += jnp.sum(grad_input.astype(F32), axis=0, keepdims=True)
        sums[7:8, :] += jnp.sum(scaled, axis=0, keepdims=True)
        pl.when(c == 0)(lambda: weights[0].beside(0, left, right))
        pl.when(c == 1)(lambda: weights[0].beside(1, left, right))
        pl.when(c == 2)(lambda: weights[1].beside(0, left, right_third))
        pl.when(c == 3)(lambda: weights[1].beside(1, left, right_third))
        pl.when(c == 4)(lambda: weights[0].mine(left, right))
        pl.when(c == 5)(lambda: weights[1].mine(left, right_third))
        sum_on(c)

    for load in loads[9:]:
        load.wait()
    each_chunk(chunks, gates)
    halo = remote(
        conv_grad.at[pl.ds(0, 8)], conv_grad.at[pl.ds(rows, 8)], halo_send, halo_recv,
        (lax.rem(s + PLANE - 1, PLANE), z),
    )
    first, final = s == 0, s == PLANE - 1
    pl.when(jnp.logical_not(first))(lambda: halo.start())
    gates_grad[...] = dot_tn(conv[...], both[...])
    sums[7:8, :] = sums[7:8, :] * par[8:9, :]

    @pl.when(final)
    def _():
        conv_grad[rows : rows + 8, :] = jnp.zeros((8, lanes), F32)

    pl.when(jnp.logical_not(final))(lambda: halo.wait_recv())

    def finish(c):
        at = chunk_rows(c)
        tall = pl.ds(pl.multiple_of(c * CHUNK, 8), CHUNK + 8)
        block, mask = conv_grad[tall, :], masks[tall, :]
        total = par[0:1, :] * block[:CHUNK, :]
        for lag in range(1, KW):
            total = total + mask[lag : lag + CHUNK, lag : lag + 1] * (
                par[lag : lag + 1, :] * block[lag : lag + CHUNK, :]
            )
        grad = total.astype(BF16)
        both[at, 0:lanes] = grad
        pairs[0].start(c)
        products = grad.astype(F32) * scan_rows[
            pl.ds(pl.multiple_of(c * CHUNK + 8, 8), CHUNK), :
        ] + gate_low[at, :].astype(F32) * gate_rows[at, :]
        inners[z, c] = as_row(jnp.sum(products, axis=1, keepdims=True))
        inner_spread.start(c)
        sum_on(c + chunks)

    each_chunk(chunks, finish)
    for weight in weights:
        weight.finish()

    def close(c):
        at = chunk_rows(c)
        inner_spread.finish(c)
        total = inners[0, c] + inners[1, c] + inners[2, c] + inners[3, c]
        scale = coefs[at, :]
        coefs[at, :] = scale * scale * as_columns(total) / features
        inner_spread.drain(c)
        red.drain(c)
        for pair in pairs:
            pair.drain(c)

    each_chunk(chunks, close)
    for whole in wholes:
        whole.wait()
    pl.when(jnp.logical_not(first))(lambda: halo.wait_send())


def recur_back(low, mix_w, gate_rows, hidden, conv, decay_rows, input_rows, scan_rows, masks, par,
               gates_w, scales, resid, normed, mixed, bo_part, pairs):
    rows, features = low.shape
    lanes, width = gate_rows.shape[1], resid.shape[1]
    chunks, hidden_size, part = rows // CHUNK, pairs[1].shape[2], features // PLANE
    two = hidden_size // THIRDS * (THIRDS - 1)

    def pair(size):
        return struct((2, rows, size), BF16)

    return pl.pallas_call(
        recur_back_kernel,
        out_shape=(
            struct((lanes, 2 * lanes), F32),
            struct((8, lanes), F32),
            struct((rows, LANE), F32),
            struct((rows, width), F32),
            struct((part, hidden_size), F32),
            struct((part, two), F32),
            struct((rows, features), BF16), struct((rows, lanes), BF16), struct((rows, features), BF16),
            pair(lanes), pair(lanes),
            struct((2, part, hidden_size), BF16),
            struct((2, part, two), BF16),
            struct((part, hidden_size), BF16),
            struct((part, two), BF16),
        ),
        in_specs=[VM] * 3 + [ANY] * 16,
        out_specs=[VM] * 6 + [ANY] * 9,
        scratch_shapes=[
            vm(lanes // LANE, rows, LANE, kind=F32), vm(lanes // LANE, rows, LANE, kind=F32),
            vm(rows, 2 * lanes), vm(rows + 8, lanes, kind=F32), vm(rows, lanes),
            vm(PLANE, 8, lanes, kind=F32), vm(LINE, chunks, 8, LANE, kind=F32),
            vm(rows, features), vm(lanes, features), vm(rows, lanes, kind=F32),
            vm(rows + 8, lanes, kind=F32), vm(rows, lanes, kind=F32), vm(rows, lanes),
            vm(rows, lanes, kind=F32), vm(rows + 8, lanes, kind=F32),
            vm(chunks, LINE, CHUNK, width), vm(chunks, LINE + 1, CHUNK, width),
            vm(2 * rows, features), vm(2 * rows, hidden_size), vm(2 * rows, two),
            vm(3 * part, hidden_size), vm(3 * part, two),
            vm(part, hidden_size), vm(part, two),
            dma(7), dma(7), pltpu.SemaphoreType.DMA, pltpu.SemaphoreType.DMA,
            dma(LINE - 1, chunks), dma(LINE - 1, chunks),
            dma(2, chunks), dma(2, chunks), dma(2, chunks), dma(3), dma(3),
            dma(LINE, chunks), dma(LINE + 1, chunks), dma(2, 4), dma(2, 4), dma(2, 4), dma(14),
        ],
        compiler_params=pltpu.CompilerParams(
            collective_id=4, has_side_effects=True, vmem_limit_bytes=64 << 20
        ),
        name="recur_back",
    )(
        masks, par, gates_w, low, mix_w, gate_rows, hidden, decay_rows, conv, input_rows, scan_rows,
        scales, resid, normed, mixed, bo_part,
        *[pair.reshape(2 * rows, pair.shape[2]) for pair in pairs],
    )


def last_kernel(
    scan_w, gate_w, grad, tok, coefs, scales, gain, pack,
    normed, normed_twin, mixed, mixed_twin, low, low_twin, scan_pair, gate_pair,
    feed_pair, feed_gate_pair,
    tokens_grad, gain_grad, pack_sum, mix_own, scan_own, gate_own, third_own, lands, third_lands, adds, third_adds,
    part, land, acc, left, right, right_third, stages, stages_third, add_v, third_add_v, pack_land, gain_land,
    red_send, red_recv, w_send, w_recv, w_load, load_sem, pack_send, pack_recv, gain_send, gain_recv,
):
    s, z = lax.axis_index("seq"), lax.axis_index("tp")
    rows, width = tok.shape
    chunks = rows // CHUNK
    third = right_third.shape[1]
    loads = [
        pltpu.make_async_copy(src, dst, load_sem.at[i])
        for i, (src, dst) in enumerate(
            (
                (scan_pair, right.at[1]), (gate_pair, right.at[2]),
                (normed, left.at[1, :rows]), (normed_twin, left.at[1, rows:]),
                (mixed, right.at[0, :rows]), (mixed_twin, right.at[0, rows:]),
                (low, left.at[0, :rows]), (low_twin, left.at[0, rows:]), (feed_pair, left.at[2]),
                (feed_gate_pair.at[:, pl.ds(2 * third, third)], right_third),
            )
        )
    ]
    for load in loads:
        load.start()
    meet(s, z)
    packs = [
        remote(
            pack.at[flip_all(s, bits)], pack_land.at[s], pack_send.at[bits - 1],
            pack_recv.at[bits - 1], (flip_all(s, bits), z),
        )
        for bits in range(1, PLANE)
    ]
    for copy in packs:
        copy.start()
    red = LineReduce(s, z, part, land, red_send, red_recv)
    weights = [
        WeightGrads(
            s, z, stages.at[i], lands.at[i], add_v.at[i], adds.at[i], own,
            w_send.at[i], w_recv.at[i], w_load.at[i],
        )
        for i, own in enumerate((mix_own, scan_own, gate_own))
    ]
    weights.append(
        WeightGrads(
            s, z, stages_third, third_lands, third_add_v, third_adds, third_own,
            w_send.at[3], w_recv.at[3], w_load.at[3],
        )
    )
    gain_land[s] = jnp.zeros_like(gain_grad)

    def project(g):
        at = group_rows(g)
        values = dot_nt(right[1, at, :], scan_w[...]) + dot_nt(right[2, at, :], gate_w[...])
        for k in range(GROUP // CHUNK):
            c = g * (GROUP // CHUNK) + k
            here = slice(k * CHUNK, (k + 1) * CHUNK)
            for o in range(LINE):
                part[c, o] = values[here, o * width : (o + 1) * width].astype(BF16)
            red.start_ends(c)

    def reduced(c):
        at = chunk_rows(c)
        red.total(c, acc)
        up = acc[...] + part[c, z].astype(F32)
        scale, values = scales[at, 0:1], tok[at, :].astype(F32)
        gain_land[s, 0:1, :] += jnp.sum(up * values * scale, axis=0, keepdims=True)
        tokens_grad[at, :] = (
            grad[at, :] + scale * gain[0:1, :] * up - values * coefs[at, 0:1]
        )

    for load in loads[:2]:
        load.wait()
    project(0)

    for g in range(1, chunks * CHUNK // GROUP):
        project(g)
    for c in range(chunks):
        red.start_rest(c)
    for load in loads[2:]:
        load.wait()
    factors = (
        (left.at[0], right.at[0]), (left.at[1], right.at[1]), (left.at[1], right.at[2]),
        (left.at[2], right_third),
    )
    for weight, pair in zip(weights[::-1], factors[::-1]):
        weight.across(*pair)
    for weight, pair in zip(weights[::-1], factors[::-1]):
        weight.beside(0, *pair)
        weight.beside(1, *pair)

    def weigh(t):
        for i in range(4):
            pl.when(t == i)(lambda i=i: weights[i].mine(*factors[i]))
            pl.when(t == chunks - 1 + i // 2)(lambda i=i: weights[3 - i].finish())

    def turn(t, carry):
        in_range(t, chunks, lambda c: red.forward(c))
        weigh(t)
        in_range(t - 1, chunks, reduced)
        return carry

    lax.fori_loop(0, chunks + 1, turn, 0)
    gain_spread = Spread(s, z, lambda p: gain_land.at[p], gain_send, gain_recv)
    gain_spread.start()
    for bits in range(1, PLANE):
        other = pack_land.at[flip_all(s, bits)]
        remote(
            other, other, pack_send.at[bits - 1], pack_recv.at[bits - 1], (flip_all(s, bits), z)
        ).wait_recv()
    total = pack[s]
    for bits in range(1, PLANE):
        total = total + pack_land[flip_all(s, bits)]
    pack_sum[...] = total
    gain_spread.finish()
    total = gain_land[0]
    for place in range(1, PLANE):
        total = total + gain_land[place]
    gain_grad[...] = total
    for copy in packs:
        copy.wait_send()
    each_chunk(chunks, red.drain)


def last_reduce(scan_w, gate_w, grad, tok, coefs, scales, gain, pack, pairs):
    rows, width = tok.shape
    features, lanes = width * LINE, scan_w.shape[1]
    chunks, part = rows // CHUNK, features // PLANE
    return pl.pallas_call(
        last_kernel,
        out_shape=(
            struct((rows, width), F32),
            struct((8, width), F32),
            struct(pack.shape[1:], F32),
            struct((part, lanes), F32),
            struct((part, lanes), F32),
            struct((part, lanes), F32),
            struct((part, pairs[9].shape[2] // THIRDS), F32),
            struct((3, 2, part, lanes), BF16),
            struct((2, part, pairs[9].shape[2] // THIRDS), BF16),
            struct((3, part, lanes), BF16),
            struct((part, pairs[9].shape[2] // THIRDS), BF16),
        ),
        in_specs=[VM] * 8 + [ANY] * 10,
        out_specs=[VM] * 7 + [ANY] * 4,
        scratch_shapes=[
            vm(chunks, LINE, CHUNK, width), vm(chunks, LINE + 1, CHUNK, width),
            vm(CHUNK, width, kind=F32),
            vm(3, 2 * rows, features), vm(3, 2 * rows, lanes), vm(2 * rows, pairs[9].shape[2] // THIRDS),
            vm(3, 3 * part, lanes), vm(3 * part, pairs[9].shape[2] // THIRDS),
            vm(3, part, lanes), vm(part, pairs[9].shape[2] // THIRDS),
            vm(*pack.shape, kind=F32), vm(PLANE, 8, width, kind=F32),
            dma(LINE, chunks), dma(LINE + 1, chunks),
            dma(4, 4), dma(4, 4), dma(4, 4), dma(10), dma(7), dma(7), dma(7), dma(7),
        ],
        compiler_params=pltpu.CompilerParams(
            collective_id=5, has_side_effects=True, vmem_limit_bytes=63 << 20
        ),
        name="last_reduce",
    )(
        scan_w, gate_w, grad, tok, coefs, scales, gain, pack,
        *pairs[:6],
        *[pair.reshape(2 * rows, pair.shape[2]) for pair in pairs[6:]],
    )


def placements(lanes, groups, seq_devices):
    cut, part = BW // seq_devices, lanes // seq_devices
    rows = np.arange(lanes)
    source = (rows % BW) // cut * part + rows // BW * cut + rows % cut
    row_order = (source[:, None] == rows[None, :]).astype(np.float32)
    tile = (np.arange(2 * LANE)[:, None] == rows[None, :] % BW).astype(np.float32)
    cells = (rows[:, None] // BW == rows[None, :] // BW).astype(np.float32)
    spots = np.arange(seq_devices * LANE)
    lane_order = (
        (rows[None, :] // part == spots[:, None] // LANE)
        & (rows[None, :] % part == spots[:, None] % LANE)
    ).astype(np.float32)
    return tuple(jnp.asarray(m, BF16) for m in (row_order, tile, cells, lane_order))


def shards_fast(
    tokens, mix_gain, scan_branch, gate_branch, kernel_taps, kernel_bias, decay_gate, decay_bias,
    input_gate, input_bias, decay_logit, mixer_out, feed_gain, gate_weight, up_weight, down_weight,
    lengths, cotangent,
):
    row_count, width = tokens.shape
    seq_devices = lax.axis_size("seq")
    shard_index = lax.axis_index("seq")
    ext_offsets = seq_offsets(lengths, shard_index * row_count, row_count + 8)
    lag_at = jnp.array([1, 1, 2, 3, 0, 0, 0, 0], jnp.int32)
    masks = (ext_offsets[:, None] >= lag_at[None, :]).astype(F32)
    lanes = scan_branch.shape[1]
    part = lanes // seq_devices
    groups = lanes // BW
    consts = placements(lanes, groups, seq_devices)
    small = jnp.concatenate(
        [
            kernel_taps, kernel_bias[None], decay_bias[None], input_bias[None], decay_logit[None],
            jnp.zeros((8, part), BF16),
        ]
    )
    small = jnp.pad(small, ((0, 0), (0, LANE - part)))
    gains = jnp.pad(
        jnp.concatenate([mix_gain, feed_gain]).astype(F32)[None, :], ((0, 7), (0, 0))
    )
    pad = ((0, 0), (0, 2 * LANE - BW))
    gate_blocks = jnp.concatenate(
        [jnp.pad(m.reshape(part, BW), pad) for m in (decay_gate, input_gate)], 1
    )
    (
        normed_first, scan_pad, gate_rows, conv_rows, decay_rows, input_rows, hidden_state, mixed,
        scan_w, gate_w, gates_w, scale_first_rows, decay_sums, par, gain_own, mix_w, ffn_gate, cot_full,
    ) = first_half(
        tokens, cotangent, small, gains, gate_blocks, scan_branch, gate_branch, mixer_out, gate_weight,
        masks, consts,
    )
    (
        resid, grad_resid, feed_grads, down_own, _, _, grad_branch, bo_part,
        low_pair, cot_pair, mid_pair, gate_pair, up_pair,
    ) = feed_both(
        mixed, mix_w, tokens, cotangent, gain_own, up_weight, down_weight, ffn_gate, cot_full
    )
    (
        gates_grad, sums, first_coefs, block_out, up_own, third_b,
        normed_twin, mixed_twin, branch_twin, scan_pair, gaterow_pair, *_,
    ) = recur_back(
        grad_branch, mix_w, gate_rows, hidden_state, conv_rows, decay_rows, input_rows, scan_pad,
        masks, par, gates_w, scale_first_rows, resid, normed_first, mixed, bo_part,
        (low_pair, up_pair, gate_pair),
    )

    def own_parts(rows):
        return rows.reshape(rows.shape[0], seq_devices, part).transpose(1, 0, 2)

    small = own_parts(jnp.concatenate([sums, decay_sums[0:1]], 0)).reshape(seq_devices, -1)
    tiles = [
        jnp.stack(
            [
                gates_grad[g * BW : (g + 1) * BW, i * lanes + g * BW : i * lanes + (g + 1) * BW]
                for g in range(groups)
            ]
        )
        .reshape(groups, seq_devices, -1)
        .transpose(1, 0, 2)
        .reshape(seq_devices, -1)
        for i in range(2)
    ]
    feed_part = feed_grads[0].reshape(seq_devices, -1)
    flat_grads = jnp.concatenate([*tiles, small, feed_part], 1)
    grad_rows = -(-flat_grads.shape[1] // (128 * 8)) * 8
    grad_pack = jnp.pad(flat_grads, ((0, 0), (0, grad_rows * 128 - flat_grads.shape[1])))
    tokens_grad, mix_grads, pack_sum, mix_own, scan_own, gaterow_own, third_c, *_ = last_reduce(
        scan_w, gate_w, grad_resid, tokens, first_coefs, scale_first_rows,
        gain_own,
        grad_pack.reshape(seq_devices, grad_rows, 128),
        (
            normed_first, normed_twin, mixed, mixed_twin, grad_branch, branch_twin, scan_pair,
            gaterow_pair, low_pair, gate_pair,
        ),
    )
    pack_sum = pack_sum.reshape(-1)
    gate_size = part * BW
    cut_at = 2 * gate_size
    small_sum = pack_sum[cut_at : cut_at + 9 * part].reshape(9, part)
    feed_sum = pack_sum[cut_at + 9 * part : cut_at + 9 * part + mix_gain.shape[0]]
    mix_sum = lax.dynamic_slice(
        mix_grads[0], (shard_index * mix_gain.shape[0],), (mix_gain.shape[0],)
    )
    return (
        block_out,
        tokens_grad,
        mix_sum,
        scan_own,
        gaterow_own,
        small_sum[0:KW],
        small_sum[KW],
        pack_sum[:gate_size].reshape(groups, -1),
        small_sum[KW + 1],
        pack_sum[gate_size : 2 * gate_size].reshape(groups, -1),
        small_sum[KW + 2],
        small_sum[KW + 3],
        mix_own.T,
        feed_sum,
        jnp.concatenate([third_b, third_c], axis=1),
        up_own,
        down_own.T,
        small_sum[KW + 4] / (row_count * seq_devices),
    )


def solution(mesh):
    placed = (
        P("seq", "tp"),
        P(("tp", "seq")),
        P("seq", "tp"),
        P("seq", "tp"),
        P(None, ("tp", "seq")),
        P(("tp", "seq")),
        P("tp", "seq"),
        P(("tp", "seq")),
        P("tp", "seq"),
        P(("tp", "seq")),
        P(("tp", "seq")),
        P("tp", "seq"),
        P(("tp", "seq")),
        P("seq", "tp"),
        P("seq", "tp"),
        P("tp", "seq"),
        P(),
        P("seq", "tp"),
    )
    return jax.shard_map(
        shards_fast if (mesh.shape["seq"], mesh.shape["tp"]) == (PLANE, LINE) else shards_general,
        mesh=mesh,
        in_specs=placed,
        out_specs=(
            P("seq", "tp"),
            P("seq", "tp"),
            P(("tp", "seq")),
            P("seq", "tp"),
            P("seq", "tp"),
            P(None, ("tp", "seq")),
            P(("tp", "seq")),
            P("tp", "seq"),
            P(("tp", "seq")),
            P("tp", "seq"),
            P(("tp", "seq")),
            P(("tp", "seq")),
            P("tp", "seq"),
            P(("tp", "seq")),
            P("seq", "tp"),
            P("seq", "tp"),
            P("tp", "seq"),
            P(("tp", "seq")),
        ),
        check_vma=False,
    )
```

```python
import functools

import jax
import jax.numpy as jnp
import numpy as np
from jax import lax
from jax.experimental import pallas as pl
from jax.experimental.pallas import tpu as pltpu
from jax.sharding import PartitionSpec as P


D = 2048
KW = 4
CD = 8
BW = 160


EPSILON = 1e-06
FLOOR_VALUE = 0.001


def from_behind(value, axis, steps):
    count = lax.axis_size(axis)
    initial, last = (max(0, -steps), min(count, count - steps))
    return lax.ppermute(value, axis, [(source, source + steps) for source in range(initial, last)])


def entering(part, axis, combine, identity, reverse):
    count = lax.axis_size(axis)
    place = lax.axis_index(axis)
    ahead = count - 1 - place if reverse else place
    gathered = jax.tree.map(lambda a: lax.all_gather(a, axis), part)
    state = jax.tree.map(lambda a, e: jnp.zeros_like(a) + jnp.asarray(e, a.dtype), part, identity)

    def one(turn, state):
        source = count - 1 - turn if reverse else turn
        return combine(
            state, jax.tree.map(lambda a: lax.dynamic_index_in_dim(a, source, 0, False), gathered)
        )

    return lax.fori_loop(0, ahead, one, state)


def matmul(left_side, right_side):
    return jnp.dot(left_side, right_side, preferred_element_type=jnp.float32)


def matmul_tn(left_side, right_side):
    return lax.dot_general(
        left_side, right_side, (((0,), (0,)), ((), ())), preferred_element_type=jnp.float32
    )


def matmul_nt(left_side, right_side):
    return lax.dot_general(
        left_side, right_side, (((1,), (1,)), ((), ())), preferred_element_type=jnp.float32
    )


def smooth_gelu(values):
    return jax.nn.gelu(values, approximate=True)


def combine(earlier, later):
    return (earlier[0] * later[0], later[1] + later[0] * earlier[1])


def seq_offsets(lengths, first_index, row_total):
    ends_all = jnp.cumsum(lengths, dtype=jnp.int32)
    starts_all = ends_all - lengths
    position = first_index + jnp.arange(row_total, dtype=jnp.int32)
    begins = jnp.max(
        jnp.where(starts_all[None, :] <= position[:, None], starts_all[None, :], 0), axis=1
    )
    return position - begins


def recurrence_terms(decay_rows, input_rows, decay_param, conv_values, resets):
    recur_gate = jax.nn.sigmoid(decay_rows)
    input_open = jax.nn.sigmoid(input_rows)
    decay_now = jnp.exp(-CD * recur_gate * jax.nn.softplus(-decay_param))
    multiplier = jnp.where(
        resets[:, None], 1.0, jnp.sqrt(jnp.maximum(1.0 - decay_now * decay_now, FLOOR_VALUE))
    )
    kept_decay = jnp.where(resets[:, None], 0.0, decay_now)
    return (kept_decay, multiplier * input_open * conv_values, decay_now)


def row_scale(values):
    squares_sum = lax.psum(jnp.sum(values * values, axis=1), "tp")
    return lax.rsqrt(squares_sum / D + EPSILON)


def spread_rows(values):
    return lax.all_gather(values, "tp", axis=1, tiled=True)


def spread_grads(values):
    return lax.all_gather(values, "tp", axis=1, tiled=True)


def reduce_features(values):
    return lax.psum_scatter(values, "tp", scatter_dimension=1, tiled=True)


def norm_back(values, row_scales, gain_vector, upstream):
    weighted = upstream * gain_vector
    inner_sum = lax.psum(jnp.sum(weighted * values, axis=1), "tp")
    cubed = row_scales * row_scales * row_scales * inner_sum / D
    back_rows = row_scales[:, None] * weighted - values * cubed[:, None]
    return (back_rows, jnp.sum(upstream * values * row_scales[:, None], axis=0))


def block_mix(blocked, matrices):
    mixed_blocks = jnp.einsum("tnb,nbc->tnc", blocked, matrices, preferred_element_type=jnp.float32)
    return mixed_blocks.reshape(blocked.shape[0], -1)


def block_outer(blocked, gradients):
    shaped = gradients.reshape(blocked.shape)
    outer_sum = jnp.einsum("tnb,tnc->nbc", blocked, shaped, preferred_element_type=jnp.float32)
    return outer_sum.reshape(blocked.shape[1], -1)


def block_back(gradients, matrices):
    shaped = gradients.reshape(gradients.shape[0], matrices.shape[0], matrices.shape[1])
    backed = jnp.einsum("tnc,nbc->tnb", shaped, matrices, preferred_element_type=jnp.float32)
    return backed.reshape(gradients.shape[0], -1)


def shards_general(
    tokens,
    mix_gain,
    scan_branch,
    gate_branch,
    kernel_taps,
    kernel_bias,
    decay_gate,
    decay_bias,
    input_gate,
    input_bias,
    decay_logit,
    mixer_out,
    feed_gain,
    gate_weight,
    up_weight,
    down_weight,
    lengths,
    cotangent,
):
    row_count = tokens.shape[0]
    seq_devices = lax.axis_size("seq")
    shard_index = lax.axis_index("seq")
    offsets = seq_offsets(lengths, shard_index * row_count, row_count)
    resets = offsets == 0
    gathered = (
        lax.all_gather(mix_gain, "seq", axis=0, tiled=True),
        lax.all_gather(scan_branch, "seq", axis=0, tiled=True),
        lax.all_gather(gate_branch, "seq", axis=0, tiled=True),
        lax.all_gather(kernel_taps, "seq", axis=1, tiled=True),
        lax.all_gather(kernel_bias, "seq", axis=0, tiled=True),
        lax.all_gather(decay_gate, "seq", axis=1, tiled=True),
        lax.all_gather(decay_bias, "seq", axis=0, tiled=True),
        lax.all_gather(input_gate, "seq", axis=1, tiled=True),
        lax.all_gather(input_bias, "seq", axis=0, tiled=True),
        lax.all_gather(decay_logit, "seq", axis=0, tiled=True),
        lax.all_gather(mixer_out, "seq", axis=1, tiled=True),
        lax.all_gather(feed_gain, "seq", axis=0, tiled=True),
        lax.all_gather(gate_weight, "seq", axis=0, tiled=True),
        lax.all_gather(up_weight, "seq", axis=0, tiled=True),
        lax.all_gather(down_weight, "seq", axis=1, tiled=True),
    )
    mix_f = gathered[0].astype(jnp.float32)
    taps_f = gathered[3].astype(jnp.float32)
    taps_bias = gathered[4].astype(jnp.float32)
    feed_f = gathered[11].astype(jnp.float32)
    tokens_f = tokens.astype(jnp.float32)
    scale_first = row_scale(tokens_f)
    normed_first = spread_rows((tokens_f * scale_first[:, None] * mix_f).astype(jnp.bfloat16))
    scan_rows = matmul(normed_first, gathered[1])
    gate_rows = matmul(normed_first, gathered[2])
    gelu_rows, gelu_pull = jax.vjp(smooth_gelu, gate_rows)
    rim_rows = from_behind(scan_rows[row_count - (KW - 1) :], "seq", 1)
    padded_rows = jnp.concatenate([rim_rows, scan_rows], axis=0)
    conv_sum = taps_bias + taps_f[0] * scan_rows
    for lag_step in range(1, KW):
        lagged = padded_rows[KW - 1 - lag_step : KW - 1 - lag_step + row_count]
        conv_sum = conv_sum + jnp.where(
            (offsets >= lag_step)[:, None], taps_f[lag_step] * lagged, 0.0
        )
    conv_rows = conv_sum.astype(jnp.bfloat16)
    lanes = scan_rows.shape[1]
    groups = lanes // BW
    conv_blocks = conv_rows.reshape(row_count, groups, BW)
    decay_mats = gathered[5].reshape(groups, BW, BW)
    input_mats = gathered[7].reshape(groups, BW, BW)
    decay_rows = block_mix(conv_blocks, decay_mats) + gathered[6].astype(jnp.float32)
    input_rows = block_mix(conv_blocks, input_mats) + gathered[8].astype(jnp.float32)

    def local_terms(decay_in, input_in, logit_in, conv_in):
        kept_part, driven_part, decay_part = recurrence_terms(
            decay_in, input_in, logit_in, conv_in, resets
        )
        return ((kept_part, driven_part), decay_part)

    terms_out, terms_pull, decay_now = jax.vjp(
        local_terms,
        decay_rows,
        input_rows,
        gathered[9].astype(jnp.float32),
        conv_rows.astype(jnp.float32),
        has_aux=True,
    )
    kept_decay, driven = terms_out
    local_prod, local_state = lax.associative_scan(combine, (kept_decay, driven), axis=0)
    before = entering(
        (local_prod[row_count - 1], local_state[row_count - 1]),
        "seq",
        combine,
        (jnp.ones((lanes,), jnp.float32), jnp.zeros((lanes,), jnp.float32)),
        False,
    )
    state_in = before[1]
    hidden_state = local_state + local_prod * state_in[None, :]
    mixed = (gelu_rows * hidden_state).astype(jnp.bfloat16)
    resid = tokens_f + reduce_features(matmul(mixed, gathered[10]))
    scale_second = row_scale(resid)
    normed_second = spread_rows((resid * scale_second[:, None] * feed_f).astype(jnp.bfloat16))
    gate_pre = matmul(normed_second, gathered[12])
    up_pre = matmul(normed_second, gathered[13])
    gelu_mid, mid_pull = jax.vjp(smooth_gelu, gate_pre)
    hidden_mid = (gelu_mid * up_pre).astype(jnp.bfloat16)
    block_out = resid + reduce_features(matmul(hidden_mid, gathered[14]))
    cot_full = spread_grads(cotangent)
    down_grad = matmul_tn(hidden_mid, cot_full)
    grad_mid = matmul_nt(cot_full, gathered[14])
    grad_gate = mid_pull(grad_mid * up_pre)[0].astype(jnp.bfloat16)
    grad_up = (grad_mid * gelu_mid).astype(jnp.bfloat16)
    gate_grad = matmul_tn(normed_second, grad_gate)
    up_grad = matmul_tn(normed_second, grad_up)
    grad_second = reduce_features(
        matmul_nt(grad_gate, gathered[12]) + matmul_nt(grad_up, gathered[13])
    )
    back_second, feed_grad = norm_back(resid, scale_second, feed_f, grad_second)
    grad_resid = cotangent.astype(jnp.float32) + back_second
    grad_branch = spread_grads(grad_resid.astype(jnp.bfloat16))
    out_grad = matmul_tn(mixed, grad_branch)
    grad_mixed = matmul_nt(grad_branch, gathered[10])
    grad_hidden = grad_mixed * gelu_rows
    grad_gate_rows = gelu_pull(grad_mixed * hidden_state)[0].astype(jnp.bfloat16)
    next_decay = jnp.concatenate([kept_decay[1:], jnp.ones_like(kept_decay[:1])], axis=0)
    tail_prod, local_adjoint = lax.associative_scan(
        combine, (next_decay, grad_hidden), reverse=True, axis=0
    )
    after = entering(
        (local_prod[row_count - 1], kept_decay[0] * local_adjoint[0]),
        "seq",
        combine,
        (jnp.ones((lanes,), jnp.float32), jnp.zeros((lanes,), jnp.float32)),
        True,
    )
    adjoint_in = after[1]
    adjoint = local_adjoint + tail_prod * adjoint_in[None, :]
    prev_state = jnp.concatenate([state_in[None, :], hidden_state[:-1]], axis=0)
    grad_decay_rows, grad_input_rows, logit_grad, conv_direct = terms_pull(
        (adjoint * prev_state, adjoint)
    )
    decay_grad_low = grad_decay_rows.astype(jnp.bfloat16)
    input_grad_low = grad_input_rows.astype(jnp.bfloat16)
    decay_w_grad = block_outer(conv_blocks, decay_grad_low)
    input_w_grad = block_outer(conv_blocks, input_grad_low)
    decay_b_grad = jnp.sum(decay_grad_low.astype(jnp.float32), axis=0)
    input_b_grad = jnp.sum(input_grad_low.astype(jnp.float32), axis=0)
    grad_conv = (
        conv_direct
        + block_back(decay_grad_low, decay_mats)
        + block_back(input_grad_low, input_mats)
    )
    rim_back = from_behind(grad_conv[: KW - 1], "seq", -1)
    grad_extended = jnp.concatenate([grad_conv, rim_back], axis=0)
    ext_offsets = seq_offsets(lengths, shard_index * row_count, row_count + KW - 1)
    grad_scan = taps_f[0] * grad_conv
    tap_grads = [jnp.sum(grad_conv * scan_rows, axis=0)]
    for lag_step in range(1, KW):
        ahead = grad_extended[lag_step : lag_step + row_count]
        ahead_ok = (ext_offsets[lag_step : lag_step + row_count] >= lag_step)[:, None]
        grad_scan = grad_scan + jnp.where(ahead_ok, taps_f[lag_step] * ahead, 0.0)
        lagged = padded_rows[KW - 1 - lag_step : KW - 1 - lag_step + row_count]
        tap_grads.append(
            jnp.sum(jnp.where((offsets >= lag_step)[:, None], grad_conv * lagged, 0.0), axis=0)
        )
    taps_grad = jnp.stack(tap_grads, axis=0)
    taps_bias_grad = jnp.sum(grad_conv, axis=0)
    scan_grad_low = grad_scan.astype(jnp.bfloat16)
    scan_w_grad = matmul_tn(normed_first, scan_grad_low)
    gatebr_grad = matmul_tn(normed_first, grad_gate_rows)
    grad_first = reduce_features(
        matmul_nt(scan_grad_low, gathered[1]) + matmul_nt(grad_gate_rows, gathered[2])
    )
    back_first, mix_grad = norm_back(tokens_f, scale_first, mix_f, grad_first)
    tokens_grad = grad_resid + back_first
    decay_total = jnp.sum(decay_now, axis=0)
    summed = (
        lax.psum_scatter(mix_grad, "seq", scatter_dimension=0, tiled=True),
        lax.psum_scatter(scan_w_grad, "seq", scatter_dimension=0, tiled=True),
        lax.psum_scatter(gatebr_grad, "seq", scatter_dimension=0, tiled=True),
        lax.psum_scatter(taps_grad, "seq", scatter_dimension=1, tiled=True),
        lax.psum_scatter(taps_bias_grad, "seq", scatter_dimension=0, tiled=True),
        lax.psum_scatter(decay_w_grad, "seq", scatter_dimension=1, tiled=True),
        lax.psum_scatter(decay_b_grad, "seq", scatter_dimension=0, tiled=True),
        lax.psum_scatter(input_w_grad, "seq", scatter_dimension=1, tiled=True),
        lax.psum_scatter(input_b_grad, "seq", scatter_dimension=0, tiled=True),
        lax.psum_scatter(logit_grad, "seq", scatter_dimension=0, tiled=True),
        lax.psum_scatter(out_grad, "seq", scatter_dimension=1, tiled=True),
        lax.psum_scatter(feed_grad, "seq", scatter_dimension=0, tiled=True),
        lax.psum_scatter(gate_grad, "seq", scatter_dimension=0, tiled=True),
        lax.psum_scatter(up_grad, "seq", scatter_dimension=0, tiled=True),
        lax.psum_scatter(down_grad, "seq", scatter_dimension=1, tiled=True),
        lax.psum_scatter(decay_total, "seq", scatter_dimension=0, tiled=True),
    )
    mean_decay = summed[15] / (row_count * seq_devices)
    return (
        block_out,
        tokens_grad,
        summed[0],
        summed[1],
        summed[2],
        summed[3],
        summed[4],
        summed[5],
        summed[6],
        summed[7],
        summed[8],
        summed[9],
        summed[10],
        summed[11],
        summed[12],
        summed[13],
        summed[14],
        mean_decay,
    )


MESH = pl.DeviceIdType.MESH
F32 = jnp.float32
BF16 = jnp.bfloat16
LINE = 4
PLANE = 8
CHUNK = 128
ANY = pl.BlockSpec(memory_space=pl.ANY)
VM = pl.BlockSpec(memory_space=pltpu.VMEM)


def flip(place, bit):
    step = 1 << bit
    return place + step - 2 * step * lax.rem(place // step, 2)


def flip_all(place, bits):
    for bit in range(3):
        if bits & (1 << bit):
            place = flip(place, bit)
    return place


def meet(s, z):
    barrier = pltpu.get_barrier_semaphore()
    for bits in range(1, PLANE):
        pl.semaphore_signal(barrier, inc=1, device_id=(flip_all(s, bits), z), device_id_type=MESH)
    for step in range(1, LINE):
        pl.semaphore_signal(
            barrier, inc=1, device_id=(s, lax.rem(z + step, LINE)), device_id_type=MESH
        )
    pl.semaphore_wait(barrier, PLANE - 1 + LINE - 1)


def remote(src, dst, send, recv, target):
    return pltpu.make_async_remote_copy(
        src_ref=src,
        dst_ref=dst,
        send_sem=send,
        recv_sem=recv,
        device_id=target,
        device_id_type=MESH,
    )


class LineGather:
    def __init__(self, s, z, own_at, full_at, send, recv):
        self.s, self.z = s, z
        self.own_at, self.full_at = own_at, full_at
        self.send, self.recv = send, recv

    def copy(self, way, level, c):
        sign = 1 - 2 * way
        origin = self.z - sign * level
        src = self.own_at(c) if level == 0 else self.full_at(origin, c)
        return remote(
            src,
            self.full_at(origin, c),
            self.send.at[way, level, c],
            self.recv.at[way, level, c],
            (self.s, self.z + sign),
        )

    def arrival(self, way, level, c):
        sign = 1 - 2 * way
        part = self.full_at(self.z - sign * (level + 1), c)
        return remote(
            part,
            part,
            self.send.at[way, level, c],
            self.recv.at[way, level, c],
            (self.s, self.z + sign),
        )

    def sends(self, way, level):
        if way == 0:
            return (self.z >= level) & (self.z < LINE - 1)
        return (self.z <= LINE - 1 - level) & (self.z > 0)

    def gets(self, way, level):
        return self.z >= level + 1 if way == 0 else self.z <= LINE - 2 - level

    def start(self, c):
        for way in range(2):
            pl.when(self.sends(way, 0))(lambda way=way: self.copy(way, 0, c).start())

    def forward(self, level, c):
        for way in range(2):
            pl.when(self.gets(way, level - 1))(
                lambda way=way: self.arrival(way, level - 1, c).wait_recv()
            )
            if level < LINE - 1:
                pl.when(self.sends(way, level))(
                    lambda way=way: self.copy(way, level, c).start()
                )

    def drain(self, c):
        for way in range(2):
            for level in range(LINE - 1):
                pl.when(self.sends(way, level))(
                    lambda way=way, level=level: self.copy(way, level, c).wait_send()
                )


class PlaneGather:
    def __init__(self, s, z, own, block_at, half_at, send, recv, local):
        self.s, self.z, self.own = s, z, own
        self.block_at, self.half_at = block_at, half_at
        self.send, self.recv, self.local = send, recv, local
        self.near = (flip(s, 1), flip(s, 2))
        self.diag = flip(self.near[0], 2)
        self.twin = flip(s, 0)
        self.twin_near = (flip(self.near[0], 0), flip(self.near[1], 0))
        self.twin_diag = flip(self.diag, 0)

    def plan(self, i):
        block, half = self.block_at, self.half_at
        return (
            (self.own, block(self.s), self.near[0]),
            (self.own, block(self.s), self.near[1]),
            (half(self.near[1], 0), half(self.near[1], 0), self.near[0]),
            (half(self.near[0], 1), half(self.near[0], 1), self.near[1]),
            (self.own, block(self.s), self.twin),
            (block(self.near[0]), block(self.near[0]), self.twin),
            (block(self.near[1]), block(self.near[1]), self.twin),
            (half(self.diag, 0), half(self.diag, 0), self.twin),
            (half(self.diag, 1), half(self.diag, 1), self.twin),
        )[i]

    def landing(self, i):
        block, half = self.block_at, self.half_at
        return (
            block(self.near[0]),
            block(self.near[1]),
            half(self.diag, 0),
            half(self.diag, 1),
            block(self.twin),
            block(self.twin_near[0]),
            block(self.twin_near[1]),
            half(self.twin_diag, 0),
            half(self.twin_diag, 1),
        )[i]

    def copy(self, i):
        src, dst, target = self.plan(i)
        return remote(src, dst, self.send.at[i], self.recv.at[i], (target, self.z))

    def got(self, i):
        part = self.landing(i)
        remote(part, part, self.send.at[i], self.recv.at[i], (self.twin, self.z)).wait_recv()

    def keep(self):
        return pltpu.make_async_copy(self.own, self.block_at(self.s), self.local)

    def start(self):
        for i in (0, 1, 4):
            self.copy(i).start()
        self.keep().start()

    def turn(self):
        self.got(0)
        self.copy(3).start()
        self.copy(5).start()
        self.got(1)
        self.copy(2).start()
        self.copy(6).start()

    def last(self):
        self.got(2)
        self.copy(7).start()
        self.got(3)
        self.copy(8).start()

    def arrive(self):
        for i in range(4, 9):
            self.got(i)
        self.keep().wait()

    def drain(self):
        for i in range(9):
            self.copy(i).wait_send()


class Spread:
    def __init__(self, s, z, slot_at, send, recv):
        self.s, self.z, self.slot_at, self.send, self.recv = s, z, slot_at, send, recv

    def copy(self, bits, origin):
        slot = self.slot_at(origin)
        return remote(
            slot,
            slot,
            self.send.at[bits - 1],
            self.recv.at[bits - 1],
            (flip_all(self.s, bits), self.z),
        )

    def start(self):
        for bits in range(1, PLANE):
            self.copy(bits, self.s).start()

    def finish(self):
        for bits in range(1, PLANE):
            self.copy(bits, flip_all(self.s, bits)).wait_recv()
        for bits in range(1, PLANE):
            self.copy(bits, self.s).wait_send()


def rows_of(ref, size, parts=2):
    def block(place):
        return ref.at[pl.ds(pl.multiple_of(place * size, size), size)]

    def half(place, h):
        part = size // parts
        return ref.at[pl.ds(pl.multiple_of(place * size + h * part, part), part)]

    return block, half


def columns_of(ref, size):
    height = ref.shape[0] // 2

    def block(place):
        return ref.at[:, pl.ds(pl.multiple_of(place * size, size), size)]

    def half(place, h):
        return ref.at[
            pl.ds(h * height, height), pl.ds(pl.multiple_of(place * size, size), size)
        ]

    return block, half


def chunk_rows(c):
    return pl.ds(pl.multiple_of(c * CHUNK, CHUNK), CHUNK)


def feature_columns(z, width):
    return pl.ds(pl.multiple_of(z * width, width), width)


def each_chunk(chunks, body):
    lax.fori_loop(0, chunks, lambda c, carry: (body(c), carry)[1], 0)


def dma(*shape):
    return pltpu.SemaphoreType.DMA(shape)


def struct(shape, kind):
    return jax.ShapeDtypeStruct(shape, kind)


def vm(*shape, kind=BF16):
    return pltpu.VMEM(shape, kind)


def sigmoid(values):
    return 0.5 * jnp.tanh(0.5 * values) + 0.5


ROOT = 0.7978845608028654


def gelu_of(values):
    return 0.5 * values * (1.0 + jnp.tanh(ROOT * (values + 0.044715 * values * values * values)))


def gelu_pair(values):
    squared = values * values
    bent = jnp.tanh(ROOT * values * (1.0 + 0.044715 * squared))
    half = 0.5 * (1.0 + bent)
    slope = half + 0.5 * values * (1.0 - bent * bent) * (ROOT * (1.0 + 3 * 0.044715 * squared))
    return values * half, slope


def dot(left_side, right_side):
    return jnp.dot(left_side, right_side, preferred_element_type=F32)


def dot_nt(left_side, right_side):
    return lax.dot_general(
        left_side, right_side, (((1,), (1,)), ((), ())), preferred_element_type=F32
    )


def dot_tn(left_side, right_side):
    return lax.dot_general(
        left_side, right_side, (((0,), (0,)), ((), ())), preferred_element_type=F32
    )


SUBS = 8


LANE = 128


def put(ref, at, values):
    for lane in range(ref.shape[0]):
        ref[lane, at, :] = values[:, lane * LANE : (lane + 1) * LANE]


def get(ref, at):
    return jnp.concatenate([ref[lane, at, :] for lane in range(ref.shape[0])], axis=1)


def strided(ref, step):
    at = pl.ds(step, SUBS, stride=ref.shape[1] // SUBS)
    return [ref[lane, at, :] for lane in range(ref.shape[0])]


def strided_put(ref, step, values):
    at = pl.ds(step, SUBS, stride=ref.shape[1] // SUBS)
    for lane in range(ref.shape[0]):
        ref[lane, at, :] = values[lane]


def lanes_of(values):
    return [values[:, i * LANE : (i + 1) * LANE] for i in range(values.shape[1] // LANE)]


def first_kernel(
    tok, cot, small, gains, gate_blocks, scan, gate, mix, ffn, masks,
    row_order, tile, cells, lane_order,
    normed_out, scan_rows_out, gate_rows_out, conv_out, decay_rows_out, input_rows_out, hidden_out,
    mixed_out, scan_w_out, gate_w_out, gates_w_out,
    scales, decay_sum, par, gain_own, mix_all, ffn_all, cot_all,
    normed, scan_rows, gate_rows, conv, decay_rows, input_rows, hidden, mixed, scan_w, gate_w, gates_w,
    tok_all, small_all, gains_all, blocks_all, gain_full, kept, driven, slots,
    tok_send, tok_recv, cot_send, cot_recv, gain_send, gain_recv, plane_send, plane_recv,
    small_send, small_recv, carry_send, carry_recv, halo_send, halo_recv, local, out_sem,
):
    s, z = lax.axis_index("seq"), lax.axis_index("tp")
    rows, width = tok.shape
    chunks, features, lanes = rows // CHUNK, width * LINE, gate.shape[1]
    part = gate_blocks.shape[0]

    def line_of(own, full, send, recv):
        return LineGather(
            s, z,
            lambda c: own.at[chunk_rows(c)],
            lambda o, c: full.at[chunk_rows(c), feature_columns(o, width)],
            send, recv,
        )

    toks = line_of(tok, tok_all, tok_send, tok_recv)
    cots = line_of(cot, cot_all, cot_send, cot_recv)
    gain_line = LineGather(
        s, z, lambda c: gains_all.at[z], lambda o, c: gains_all.at[o], gain_send, gain_recv
    )
    planes = []
    for i, (own, full, make) in enumerate(
        (
            (scan, scan_w, rows_of),
            (gate, gate_w, rows_of),
            (mix, mix_all, columns_of),
            (ffn, ffn_all, rows_of),
        )
    ):
        size = own.shape[1] if make is columns_of else own.shape[0]
        planes.append(
            PlaneGather(s, z, own, *make(full, size), plane_send.at[i], plane_recv.at[i], local.at[i])
        )
    spreads = [
        Spread(s, z, lambda p: gains_all.at[z, p], small_send.at[0], small_recv.at[0]),
        Spread(s, z, lambda p: small_all.at[p], small_send.at[1], small_recv.at[1]),
        Spread(
            s, z, lambda p: blocks_all.at[pl.ds(pl.multiple_of(p * part, 16), part)],
            small_send.at[2], small_recv.at[2],
        ),
    ]
    keep = pltpu.make_async_copy(cot, cot_all.at[:, feature_columns(z, width)], local.at[6])
    keep.start()
    outs = {
        name: pltpu.make_async_copy(src, dst, out_sem.at[i])
        for i, (name, src, dst) in enumerate(
            (
                ("normed", normed, normed_out), ("scan_rows", scan_rows, scan_rows_out),
                ("gate_rows", gate_rows, gate_rows_out), ("conv", conv, conv_out),
                ("decay_rows", decay_rows, decay_rows_out), ("input_rows", input_rows, input_rows_out),
                ("hidden", hidden, hidden_out), ("mixed", mixed, mixed_out),
                ("scan_w", scan_w, scan_w_out), ("gate_w", gate_w, gate_w_out),
                ("gates_w", gates_w, gates_w_out),
            )
        )
    }
    tok_all[:, feature_columns(z, width)] = tok[...]
    gains_all[z, s] = gains[...]
    small_all[s] = small[...]
    blocks_all[pl.ds(pl.multiple_of(s * part, 16), part), :] = gate_blocks[...]
    meet(s, z)
    for spread in spreads:
        spread.start()
    for c in range(chunks):
        toks.start(c)
    for plane in planes[:2]:
        plane.start()
    for spread in spreads:
        spread.finish()
    gain_line.start(0)
    for c in range(chunks):
        toks.forward(1, c)
    gain_line.forward(1, 0)
    placed = dot(
        jnp.concatenate([small_all[p] for p in range(PLANE)], axis=1), lane_order[...]
    )
    par[...] = placed
    falling = jnp.exp(-placed[7:8, :])
    par[7:8, :] = CD * jnp.log1p(falling)
    par[8:9, :] = CD * falling / (1.0 + falling)
    half = blocks_all.shape[1] // 2
    for i in range(2):
        wide = dot(blocks_all[:, i * half : (i + 1) * half], tile[...]).astype(BF16)
        gates_w[:, i * lanes : (i + 1) * lanes] = dot(row_order[...], wide).astype(BF16) * cells[...]
    planes[0].turn()
    planes[1].turn()
    planes[2].start()
    planes[3].start()
    for c in range(chunks):
        toks.forward(2, c)
    gain_line.forward(2, 0)
    planes[0].last()
    planes[1].last()
    gain_line.forward(3, 0)
    for c in range(chunks):
        cots.start(c)
    pick = lax.broadcasted_iota(jnp.int32, (LANE, LANE), 0)
    place = lax.broadcasted_iota(jnp.int32, (LANE, LANE), 1)
    cut = LANE // 2
    even = jnp.concatenate(
        [gains_all[o, p] for o in range(LINE) for p in range(0, PLANE, 2)], axis=0
    ).astype(BF16)
    odd = jnp.concatenate(
        [gains_all[o, p] for o in range(LINE) for p in range(1, PLANE, 2)], axis=0
    ).astype(BF16)
    for i in range(2):
        from_even = (pick == place + i * cut) & (place < cut)
        from_odd = (pick == place + (i - 1) * cut) & (place >= cut)
        spots = dot(even, from_even.astype(F32).astype(BF16)) + dot(
            odd, from_odd.astype(F32).astype(BF16)
        )
        for q in range(spots.shape[0] // 8):
            gain_full[i : i + 1, q * LANE : (q + 1) * LANE] = spots[8 * q : 8 * q + 1, :]
    gain_own[0:2, :] = gain_full[0:2, feature_columns(z, width)]
    planes[0].arrive()
    planes[1].arrive()
    for name in ("scan_w", "gate_w", "gates_w"):
        outs[name].start()

    def project(c):
        toks.forward(3, c)
        pl.when(c >= 2)(lambda: cots.forward(1, c - 2))
        at = chunk_rows(c)
        x = tok_all[at, :].astype(F32)
        scale = lax.rsqrt(jnp.sum(x * x, axis=1, keepdims=True) / features + EPSILON)
        scales[at, :] = jnp.broadcast_to(scale, (CHUNK, LANE))
        low = (x * scale * gain_full[0:1, :]).astype(BF16)
        normed[at, :] = low
        scan_rows[pl.ds(pl.multiple_of(c * CHUNK + 8, 8), CHUNK), :] = dot(low, scan_w[...])
        gate_rows[at, :] = dot(low, gate_w[...])

    each_chunk(chunks, project)
    halo = remote(
        scan_rows.at[pl.ds(rows, 8)], scan_rows.at[pl.ds(0, 8)], halo_send, halo_recv,
        (lax.rem(s + 1, PLANE), z),
    )
    first, final = s == 0, s == PLANE - 1
    pl.when(jnp.logical_not(final))(lambda: halo.start())

    @pl.when(first)
    def _():
        scan_rows[0:8, :] = jnp.zeros((8, lanes), F32)

    planes[2].turn()
    planes[3].turn()
    decay_sum[...] = jnp.zeros_like(decay_sum)
    pl.when(jnp.logical_not(first))(lambda: halo.wait_recv())
    for name in ("normed", "scan_rows", "gate_rows"):
        outs[name].start()

    def gates(c):
        at = chunk_rows(c)
        block = scan_rows[pl.ds(pl.multiple_of(c * CHUNK, 8), CHUNK + 8), :]
        mask = masks[at, :]
        total = par[4:5, :] + par[0:1, :] * block[8:, :]
        for lag in range(1, KW):
            total = total + mask[:, lag : lag + 1] * (
                par[lag : lag + 1, :] * block[8 - lag : 8 - lag + CHUNK, :]
            )
        low = total.astype(BF16)
        conv[at, :] = low
        rows_now = dot(low, gates_w[...])
        decays = rows_now[:, :lanes] + par[5:6, :]
        inputs = rows_now[:, lanes:] + par[6:7, :]
        decay_rows[at, :] = decays
        input_rows[at, :] = inputs
        decay = jnp.exp(-sigmoid(decays) * par[7:8, :])
        goes_on = mask[:, 0:1]
        multiplier = 1.0 + goes_on * (
            jnp.sqrt(jnp.maximum(1.0 - decay * decay, FLOOR_VALUE)) - 1.0
        )
        put(kept, at, goes_on * decay)
        put(driven, at, multiplier * sigmoid(inputs) * low.astype(F32))
        decay_sum[0:1, :] += jnp.sum(decay, axis=0, keepdims=True)
        pl.when(c < 2)(lambda: cots.forward(1, c + chunks - 2))
        pl.when(c >= 2)(lambda: cots.forward(2, c - 2))

    each_chunk(chunks, gates)
    for name in ("conv", "decay_rows", "input_rows"):
        outs[name].start()
    planes[2].last()
    planes[3].last()
    count = rows // SUBS

    def total_of(step, carry):
        keeps, drives = strided(kept, step), strided(driven, step)
        return (
            [p * k for p, k in zip(carry[0], keeps)],
            [k * v + d for k, v, d in zip(keeps, carry[1], drives)],
        )

    groups = lanes // LANE
    product, value = lax.fori_loop(
        0,
        count,
        total_of,
        ([jnp.ones((SUBS, LANE), F32)] * groups, [jnp.zeros((SUBS, LANE), F32)] * groups),
        unroll=4,
    )
    product, value = jnp.concatenate(product, axis=1), jnp.concatenate(value, axis=1)
    whole = (jnp.ones((1, lanes), F32), jnp.zeros((1, lanes), F32))
    for sub in range(SUBS):
        here = product[sub : sub + 1, :]
        whole = (whole[0] * here, here * whole[1] + value[sub : sub + 1, :])
    slots[s, 0:1, :] = whole[0]
    slots[s, 1:2, :] = whole[1]
    spread = Spread(s, z, lambda p: slots.at[p], carry_send, carry_recv)
    spread.start()
    spread.finish()
    entry = jnp.zeros((1, lanes), F32)
    for place in range(PLANE - 1):
        entry = jnp.where(
            place < s, slots[place, 0:1, :] * entry + slots[place, 1:2, :], entry
        )
    hidden[0:8, :] = jnp.broadcast_to(entry, (8, lanes))
    entries = []
    for sub in range(SUBS):
        entries.append(entry)
        entry = product[sub : sub + 1, :] * entry + value[sub : sub + 1, :]

    def step_on(step, now):
        keeps, drives = strided(kept, step), strided(driven, step)
        now = [k * v + d for k, v, d in zip(keeps, now, drives)]
        strided_put(driven, step, now)
        return now

    lax.fori_loop(0, count, step_on, lanes_of(jnp.concatenate(entries, axis=0)), unroll=4)

    def mix(c):
        at = chunk_rows(c)
        now = get(driven, at)
        hidden[pl.ds(pl.multiple_of(c * CHUNK + 8, 8), CHUNK), :] = now
        mixed[at, :] = (gelu_of(gate_rows[at, :]) * now).astype(BF16)
        pl.when(c < 2)(lambda: cots.forward(2, c + chunks - 2))

    each_chunk(chunks, mix)
    for name in ("hidden", "mixed"):
        outs[name].start()
    for c in range(chunks):
        cots.forward(3, c)
    for plane in planes[2:]:
        plane.arrive()
    for plane in planes:
        plane.drain()
    for c in range(chunks):
        toks.drain(c)
        cots.drain(c)
    gain_line.drain(0)
    pl.when(jnp.logical_not(final))(lambda: halo.wait_send())
    keep.wait()
    for copy in outs.values():
        copy.wait()


def first_half(tok, cot, small, gains, gate_blocks, scan, gate, mix, ffn, masks, consts):
    rows, width = tok.shape
    features, lanes = width * LINE, gate.shape[1]
    chunks = rows // CHUNK
    return pl.pallas_call(
        first_kernel,
        out_shape=(
            struct((rows, features), BF16),
            struct((rows + 8, lanes), F32),
            struct((rows, lanes), F32),
            struct((rows, lanes), BF16),
            struct((rows, lanes), F32),
            struct((rows, lanes), F32),
            struct((rows + 8, lanes), F32),
            struct((rows, lanes), BF16),
            struct((features, lanes), BF16),
            struct((features, lanes), BF16),
            struct((lanes, 2 * lanes), BF16),
            struct((rows, LANE), F32),
            struct((8, lanes), F32),
            struct((16, lanes), F32),
            struct((8, width), F32),
            struct((mix.shape[0], mix.shape[1] * PLANE), BF16),
            struct((ffn.shape[0] * PLANE, ffn.shape[1]), BF16),
            struct((rows, features), BF16),
        ),
        in_specs=[VM] * 14,
        out_specs=[ANY] * 11 + [VM] * 4 + [ANY] * 3,
        scratch_shapes=[
            vm(rows, features), vm(rows + 8, lanes, kind=F32), vm(rows, lanes, kind=F32),
            vm(rows, lanes), vm(rows, lanes, kind=F32), vm(rows, lanes, kind=F32),
            vm(rows + 8, lanes, kind=F32), vm(rows, lanes), vm(features, lanes), vm(features, lanes),
            vm(lanes, 2 * lanes), vm(rows, features),
            vm(PLANE, *small.shape), vm(LINE, PLANE, *gains.shape, kind=F32),
            vm(PLANE * gate_blocks.shape[0], gate_blocks.shape[1]), vm(8, features, kind=F32),
            vm(lanes // LANE, rows, LANE, kind=F32), vm(lanes // LANE, rows, LANE, kind=F32),
            vm(PLANE, 8, lanes, kind=F32),
            dma(2, LINE - 1, chunks), dma(2, LINE - 1, chunks),
            dma(2, LINE - 1, chunks), dma(2, LINE - 1, chunks),
            dma(2, LINE - 1, 1), dma(2, LINE - 1, 1),
            dma(4, 9), dma(4, 9), dma(3, 7), dma(3, 7), dma(7), dma(7),
            pltpu.SemaphoreType.DMA, pltpu.SemaphoreType.DMA, dma(7), dma(11),
        ],
        compiler_params=pltpu.CompilerParams(
            collective_id=0, has_side_effects=True, vmem_limit_bytes=60 << 20
        ),
        name="first_half",
    )(tok, cot, small, gains, gate_blocks, scan, gate, mix, ffn, masks, *consts)


class WeightGrads:
    def __init__(self, s, z, stage, land, adds, add_land, own, send, recv, load):
        self.s, self.z = s, z
        self.stage, self.land, self.adds, self.add_land = stage, land, adds, add_land
        self.own, self.send, self.recv, self.load = own, send, recv, load
        self.size = own.shape[0]
        self.near = (flip(s, 1), flip(s, 2))

    def stage_of(self, k):
        return self.stage.at[pl.ds(k * self.size, self.size)]

    def copy(self, k):
        half = self.size // 2
        if k < 2:
            src, dst = self.stage_of(k), self.land.at[k]
        else:
            src = self.stage.at[pl.ds(2 * self.size + (k - 2) * half, half)]
            dst = self.add_land.at[pl.ds((k - 2) * half, half)]
        return remote(src, dst, self.send.at[k], self.recv.at[k], (self.near[k % 2], self.z))

    def product(self, owner, left, right):
        return dot_tn(left[:, feature_columns(owner, self.size)], right[...])

    def across(self, left, right):
        self.stage_of(2)[...] = self.product(flip(self.near[0], 2), left, right).astype(BF16)
        self.copy(2).start()
        self.copy(3).start()

    def beside(self, k, left, right):
        half = self.size // 2
        value = self.product(self.near[k], left, right)
        mine, other = (pl.ds(half, half), slice(half, None)), slice(0, half)
        if k == 1:
            mine, other = (pl.ds(0, half), slice(0, half)), slice(half, None)
        self.copy(3 - k).wait_recv()
        back = pltpu.make_async_copy(
            self.add_land.at[mine[0]], self.adds.at[mine[0]], self.load.at[2 + k]
        )
        back.start()
        self.stage_of(k)[other, :] = value[other].astype(BF16)
        back.wait()
        self.stage_of(k)[mine[1], :] = (value[mine[1]] + self.adds[mine[0], :].astype(F32)).astype(BF16)
        self.copy(k).start()

    def mine(self, left, right):
        self.own[...] = self.product(self.s, left, right)

    def finish(self):
        backs = []
        for k in range(2):
            self.copy(k).wait()
            self.copy(2 + k).wait_send()
            backs.append(
                pltpu.make_async_copy(self.land.at[k], self.stage_of(k), self.load.at[k])
            )
            backs[k].start()
        for back in backs:
            back.wait()
        self.own[...] += self.stage_of(0)[...].astype(F32) + self.stage_of(1)[...].astype(F32)


class LineReduce:
    def __init__(self, s, z, part, land, send, recv):
        self.s, self.z, self.part, self.land = s, z, part, land
        self.send, self.recv = send, recv

    def copy(self, o, target, slot, c):
        return remote(
            self.part.at[c, o],
            self.land.at[c, slot],
            self.send.at[o, c],
            self.recv.at[slot, c],
            (self.s, self.z + target),
        )

    def got(self, slot, c):
        part = self.land.at[c, slot]
        remote(part, part, self.send.at[0, c], self.recv.at[slot, c], (self.s, self.z)).wait_recv()

    def start(self, c):
        self.start_ends(c)
        self.start_rest(c)

    def start_ends(self, c):
        end = LINE - 1
        pl.when(self.z == 0)(lambda: self.copy(end, 1, LINE, c).start())
        pl.when(self.z == end)(lambda: self.copy(0, -1, LINE, c).start())

    def start_rest(self, c):
        end = LINE - 1
        pl.when(self.z == 0)(lambda: self.copy(2, 2, 1, c).start())
        pl.when(self.z == end)(lambda: self.copy(1, -2, 3, c).start())
        for me in range(LINE):

            def work(me=me):
                if me < end:
                    self.copy(me + 1, 1, 0, c).start()
                if me > 0:
                    self.copy(me - 1, -1, 2, c).start()

            pl.when(self.z == me)(work)

    def forward(self, c):
        end = LINE - 1
        for me, o, step, slot in ((1, end, 2, 1), (2, 0, -2, 3)):

            def work(o=o, step=step, slot=slot):
                self.got(LINE, c)
                self.part[c, o] = (
                    self.part[c, o].astype(F32) + self.land[c, LINE].astype(F32)
                ).astype(BF16)
                self.copy(o, step, slot, c).start()

            pl.when(self.z == me)(work)

    def total(self, c, into, more=False):
        slots = ((2, 3), (0, 2, 3), (0, 1, 2), (0, 1))
        for me in range(LINE):

            def work(me=me):
                for slot in slots[me]:
                    self.got(slot, c)
                value = self.land[c, slots[me][0]].astype(F32)
                for slot in slots[me][1:]:
                    value = value + self.land[c, slot].astype(F32)
                into[...] = into[...] + value if more else value

            pl.when(self.z == me)(work)

    def drain(self, c):
        for o in range(LINE):
            part = self.part.at[c, o]
            pl.when(self.z != o)(
                lambda part=part, o=o: remote(
                    part, part, self.send.at[o, c], self.recv.at[0, c], (self.s, self.z)
                ).wait_send()
            )


class LineSpread:
    def __init__(self, s, z, slot_at, send, recv):
        self.s, self.z, self.slot_at, self.send, self.recv = s, z, slot_at, send, recv

    def copy(self, step, origin, c):
        slot = self.slot_at(origin, c)
        target = (self.s, lax.rem(self.z + step, LINE))
        return remote(slot, slot, self.send.at[step - 1, c], self.recv.at[step - 1, c], target)

    def start(self, c):
        for step in range(1, LINE):
            self.copy(step, self.z, c).start()

    def finish(self, c):
        for step in range(1, LINE):
            self.copy(step, lax.rem(self.z + LINE - step, LINE), c).wait_recv()

    def drain(self, c):
        for step in range(1, LINE):
            self.copy(step, self.z, c).wait_send()


class Halves:
    def __init__(self, s, z, src, out, own, send, recv):
        self.s, self.z, self.src, self.out = s, z, src, out
        self.own, self.send, self.recv = own, send, recv

    def keep(self, c):
        at = chunk_rows(c)
        return pltpu.make_async_copy(self.src.at[at], self.out.at[0, at], self.own.at[c])

    def give(self, c):
        at = chunk_rows(c)
        return remote(
            self.src.at[at], self.out.at[1, at], self.send.at[c], self.recv.at[c],
            (flip(self.s, 0), self.z),
        )

    def start(self, c):
        self.keep(c).start()
        self.give(c).start()

    def drain(self, c):
        self.keep(c).wait()
        self.give(c).wait()


def as_row(column):
    return jnp.transpose(jnp.broadcast_to(column, (CHUNK, LANE)))[0:8, :]


def as_columns(row):
    return jnp.transpose(jnp.broadcast_to(row[0:1, :], (LANE, CHUNK)))


def in_range(c, chunks, body):
    pl.when((c >= 0) & (c < chunks))(lambda: body(c))


CUT = 768
AHEAD = 2
THIRDS = 3
GROUP = 2 * CHUNK


def group_rows(g):
    return pl.ds(pl.multiple_of(g * GROUP, GROUP), GROUP)


def feed_kernel(
    mixed, mix_w, tok, cot, gain, up, down, gate_w, cot_all,
    resid, grad, gain_grad, down_own, lands, adds, grad_all, bo_part, low_pair, cot_pair, mid_pair, gate_pair, up_pair,
    part, land, low, low_grad, cots, mid, g_gate, g_up, bo_out, gate_v, up_v, down_v,
    acc, inner, scales, squares, inners,
    red_send, red_recv, gs_send, gs_recv, line_send, line_recv, grad_send, grad_recv,
    sq_send, sq_recv, in_send, in_recv, plane_send, plane_recv, local,
    own_sem, give_send, give_recv, out_sem, load_sem, w_send, w_recv, w_load,
):
    s, z = lax.axis_index("seq"), lax.axis_index("tp")
    rows, width = tok.shape
    chunks, features = rows // CHUNK, width * LINE
    loads = [
        pltpu.make_async_copy(gate_w, gate_v, load_sem.at[0]),
        pltpu.make_async_copy(cot_all, cots, load_sem.at[1]),
    ]
    for load in loads:
        load.start()
    meet(s, z)
    red = LineReduce(s, z, part, land, red_send, red_recv)
    red_gs = LineReduce(s, z, part, land, gs_send, gs_recv)

    def line_of(full, send, recv):
        return LineGather(
            s, z,
            lambda c: full.at[chunk_rows(c), feature_columns(z, width)],
            lambda o, c: full.at[chunk_rows(c), feature_columns(o, width)],
            send, recv,
        )

    line = line_of(low, line_send, line_recv)
    grads = line_of(low_grad, grad_send, grad_recv)
    planes = [
        PlaneGather(
            s, z, up, *rows_of(up_v, up.shape[0]), plane_send.at[0], plane_recv.at[0], local.at[0]
        ),
        PlaneGather(
            s, z, down, *columns_of(down_v, down.shape[1]), plane_send.at[1], plane_recv.at[1],
            local.at[1],
        ),
    ]
    square_spread = LineSpread(s, z, lambda o, c: squares.at[o, c], sq_send, sq_recv)
    inner_spread = LineSpread(s, z, lambda o, c: inners.at[o, c], in_send, in_recv)
    pairs = [
        Halves(s, z, src, out, own_sem.at[i], give_send.at[i], give_recv.at[i])
        for i, (src, out) in enumerate(
            ((low, low_pair), (cots, cot_pair), (mid, mid_pair), (g_gate, gate_pair), (g_up, up_pair))
        )
    ]
    gain_grad[...] = jnp.zeros_like(gain_grad)

    def bo_copy(c):
        return pltpu.make_async_copy(bo_out.at[c], bo_part.at[c], out_sem.at[0, c])

    def grad_copy(c):
        at = chunk_rows(c)
        return pltpu.make_async_copy(low_grad.at[at], grad_all.at[at], out_sem.at[1, c])

    def project(c):
        values = dot(mixed[chunk_rows(c), :], mix_w[...])
        for o in range(LINE):
            here = values[:, o * width : (o + 1) * width]
            part[c, o] = here.astype(BF16)

            @pl.when(z == o)
            def _(here=here):
                resid[chunk_rows(c), :] = here

        red.start(c)

    for c in range(AHEAD):
        project(c)
    for plane in planes:
        plane.start()

    def reduced(c):
        at = chunk_rows(c)
        red.total(c, acc)
        values = tok[at, :].astype(F32) + (resid[at, :] + acc[...])
        resid[at, :] = values
        squares[z, c] = as_row(jnp.sum(values * values, axis=1, keepdims=True))
        square_spread.start(c)

    def scaled(c):
        at = chunk_rows(c)
        square_spread.finish(c)
        sums = squares[0, c] + squares[1, c] + squares[2, c] + squares[3, c]
        scale = lax.rsqrt(as_columns(sums) / features + EPSILON)
        scales[at, :] = scale
        low[at, feature_columns(z, width)] = (resid[at, :] * scale[:, 0:1] * gain[1:2, :]).astype(
            BF16
        )
        line.start(c)

    def forward(cut, g):
        at = group_rows(g)
        cols = slice(cut * CUT, (cut + 1) * CUT)
        x = low[at, :]
        gate_pre, up_pre = dot(x, gate_v[:, cols]), dot(x, up_v[:, cols])
        act, slope = gelu_pair(gate_pre)
        here = (act * up_pre).astype(BF16)
        mid[at, cols] = here
        back = dot_nt(cots[at, :], down_v[cols, :])
        gate_grad = (back * up_pre * slope).astype(BF16)
        up_grad = (back * act).astype(BF16)
        g_gate[at, cols] = gate_grad
        g_up[at, cols] = up_grad
        products = jnp.sum(
            gate_grad.astype(F32) * gate_pre + up_grad.astype(F32) * up_pre, axis=1, keepdims=True
        )
        if cut == 0:
            inner[...] = products
        else:
            inner[...] += products

    def backward(g):
        at = group_rows(g)
        back = dot_nt(g_gate[at, :], gate_v[...]) + dot_nt(g_up[at, :], up_v[...])
        for k in range(GROUP // CHUNK):
            c = g * (GROUP // CHUNK) + k
            here = slice(k * CHUNK, (k + 1) * CHUNK)
            red.drain(c)
            for o in range(LINE):
                part[c, o] = back[here, o * width : (o + 1) * width].astype(BF16)
            red_gs.start_ends(c)
        for k in range(GROUP // CHUNK):
            c = g * (GROUP // CHUNK) + k
            here = slice(k * CHUNK, (k + 1) * CHUNK)
            red_gs.start_rest(c)
            inners[z, c] = as_row(inner[here, :])
            inner_spread.start(c)
        block = dot(mid[at, :], down_v[...])
        for k in range(GROUP // CHUNK):
            c = g * (GROUP // CHUNK) + k
            here = slice(k * CHUNK, (k + 1) * CHUNK)
            for o in range(LINE):
                bo_out[c, o] = block[here, o * width : (o + 1) * width].astype(BF16)
            for pair in pairs:
                pair.start(c)
            bo_copy(c).start()

    def turned(c):
        at = chunk_rows(c)
        red_gs.total(c, acc)
        inner_spread.finish(c)
        sums = inners[0, c] + inners[1, c] + inners[2, c] + inners[3, c]
        scale = scales[at, :]
        coef = scale * scale * as_columns(sums) / features
        above = acc[...] + part[c, z].astype(F32)
        scale, values = scale[:, 0:1], resid[at, :]
        gain_grad[0:1, :] += jnp.sum(above * values * scale, axis=0, keepdims=True)
        total = cot[at, :].astype(F32) + scale * gain[1:2, :] * above - values * coef[:, 0:1]
        grad[at, :] = total
        low_grad[at, feature_columns(z, width)] = total.astype(BF16)
        grads.start(c)

    def twice(start, body):
        def both(t):
            pl.when((t >= start) & (lax.rem(t - start, 2) == 0) & (t < start + chunks))(
                lambda: (body(t - start), body(t - start + 1)) and None
            )

        return both

    def whole(c):
        grads.forward(3, c)
        grad_copy(c).start()

    left, right = down_v, gate_v.at[pl.ds(0, 2 * rows)]
    fills = [
        pltpu.make_async_copy(
            src.at[half], dst.at[pl.ds(half * rows, rows)], load_sem.at[2 + 2 * i + half]
        )
        for i, (src, dst) in enumerate(((cot_pair, left), (mid_pair, right)))
        for half in range(2)
    ]
    weight = WeightGrads(
        s, z, mid, lands, g_up.at[pl.ds(0, features // PLANE)], adds, down_own, w_send, w_recv, w_load
    )

    def ready_pairs(c):
        for pair in pairs:
            pair.drain(c)

    def weigh_one():
        each_chunk(chunks, ready_pairs)
        for plane in planes:
            plane.drain()
        for copy in fills:
            copy.start()
        for copy in fills:
            copy.wait()
        weight.across(left, right)
        weight.mine(left, right)

    def weigh_two():
        weight.beside(0, left, right)
        weight.beside(1, left, right)

    gs_one = twice(6, lambda c: red_gs.forward(c))
    gs_three = twice(7, turned)
    to_one = twice(8, lambda c: grads.forward(1, c))
    to_two = twice(9, lambda c: grads.forward(2, c))
    to_three = twice(10, whole)

    def turn(t, carry):
        g, odd = (t - 4) // 2, lax.rem(t, 2) == 1
        ready = (t >= 4) & (t < chunks + 4)

        @pl.when(t == 2)
        def _():
            for plane in planes:
                plane.turn()

        @pl.when(t == 4)
        def _():
            for plane in planes:
                plane.last()
            for plane in planes:
                plane.arrive()
            for load in loads:
                load.wait()

        in_range(t, chunks, lambda c: red.forward(c))
        gs_one(t)
        in_range(t - 2, chunks, lambda c: line.forward(1, c))
        in_range(t - 3, chunks, lambda c: line.forward(3, c))
        to_one(t)
        to_three(t)
        pl.when(ready & jnp.logical_not(odd))(lambda: forward(0, g))
        gs_three(t)
        pl.when(t == chunks + 5)(weigh_one)
        in_range(t - 1, chunks, reduced)
        in_range(t - 1, chunks, scaled)
        in_range(t - 2, chunks, lambda c: line.forward(2, c))
        to_two(t)
        pl.when(ready & jnp.logical_not(odd))(lambda: forward(1, g))
        in_range(t + AHEAD, chunks, project)
        pl.when(ready & odd)(lambda: backward(g))
        pl.when(t == chunks + 6)(weigh_two)
        return carry

    lax.fori_loop(0, chunks + 9, turn, 0)

    def close(c):
        red_gs.drain(c)
        line.drain(c)
        grads.drain(c)
        square_spread.drain(c)
        inner_spread.drain(c)
        bo_copy(c).wait()
        grad_copy(c).wait()

    each_chunk(chunks, close)
    weight.finish()


def feed_both(mixed, mix_w, tok, cot, gain, up, down, gate_w, cot_all):
    rows, width = tok.shape
    features, hidden = width * LINE, gate_w.shape[1]
    chunks = rows // CHUNK

    def pair(size):
        return struct((2, rows, size), BF16)

    return pl.pallas_call(
        feed_kernel,
        out_shape=(
            struct((rows, width), F32),
            struct((rows, width), F32),
            struct((8, width), F32),
            struct((features // PLANE, hidden), F32),
            struct((2, features // PLANE, hidden), BF16),
            struct((features // PLANE, hidden), BF16),
            struct((rows, features), BF16),
            struct((chunks, LINE, CHUNK, width), BF16),
            pair(features), pair(features), pair(hidden), pair(hidden), pair(hidden),
        ),
        in_specs=[VM] * 7 + [ANY] * 2,
        out_specs=[VM] * 4 + [ANY] * 9,
        scratch_shapes=[
            vm(chunks, LINE, CHUNK, width), vm(chunks, LINE + 1, CHUNK, width),
            vm(rows, features), vm(rows, features), vm(rows, features),
            vm(rows, hidden), vm(rows, hidden), vm(rows, hidden),
            vm(chunks, LINE, CHUNK, width),
            vm(features, hidden), vm(features, hidden), vm(hidden, features),
            vm(CHUNK, width, kind=F32), vm(GROUP, 1, kind=F32), vm(rows, LANE, kind=F32),
            vm(LINE, chunks, 8, LANE, kind=F32), vm(LINE, chunks, 8, LANE, kind=F32),
            dma(LINE, chunks), dma(LINE + 1, chunks), dma(LINE, chunks), dma(LINE + 1, chunks),
            dma(2, LINE - 1, chunks), dma(2, LINE - 1, chunks),
            dma(2, LINE - 1, chunks), dma(2, LINE - 1, chunks),
            dma(LINE - 1, chunks), dma(LINE - 1, chunks),
            dma(LINE - 1, chunks), dma(LINE - 1, chunks),
            dma(2, 9), dma(2, 9), dma(2),
            dma(5, chunks), dma(5, chunks), dma(5, chunks), dma(2, chunks), dma(10),
            dma(4), dma(4), dma(4),
        ],
        compiler_params=pltpu.CompilerParams(
            collective_id=2, has_side_effects=True, vmem_limit_bytes=64 << 20
        ),
        name="feed_both",
    )(mixed, mix_w, tok, cot, gain, up, down, gate_w, cot_all)


def recur_back_kernel(
    masks, par, gates_w,
    low_src, mix_w_src, gate_rows_src, hidden_src, decay_rows_src, conv_src, input_rows_src, scan_rows_src,
    scales, resid, normed_src, mixed_src, bo_part, feed_pair, feed_up_pair, feed_gate_pair,
    gates_grad, sums, coefs, out, up_own, third_own,
    normed_twin, mixed_twin, low_twin, scan_pair, gate_pair, lands, third_lands, adds, third_adds,
    kept, grads, both, conv_grad, gate_low, slots, inners,
    low, mix_w, gate_rows, hidden, decay_rows, conv, input_rows, scan_rows,
    part, land, left, right, right_third, stages, stages_third, add_v, third_add_v,
    small_send, small_recv, halo_send, halo_recv, in_send, in_recv,
    own_sem, give_send, give_recv, twin_send, twin_recv,
    bo_send, bo_recv, w_send, w_recv, w_load, load_sem,
):
    s, z = lax.axis_index("seq"), lax.axis_index("tp")
    rows, features = low.shape
    lanes = gate_rows.shape[1]
    chunks = rows // CHUNK
    wholes = [
        remote(src, out, twin_send.at[i], twin_recv.at[i], (flip(s, 0), z))
        for i, (src, out) in enumerate(
            ((normed_src, normed_twin), (mixed_src, mixed_twin), (low_src, low_twin))
        )
    ]
    pairs = [
        Halves(s, z, src, out, own_sem.at[i], give_send.at[i], give_recv.at[i])
        for i, (src, out) in enumerate(
            ((both.at[:, pl.ds(0, lanes)], scan_pair), (gate_low, gate_pair))
        )
    ]
    inner_spread = LineSpread(s, z, lambda o, c: inners.at[o, c], in_send, in_recv)
    third = right_third.shape[1]
    loads = [
        pltpu.make_async_copy(src, dst, load_sem.at[i])
        for i, (src, dst) in enumerate(
            (
                (bo_part, part), (feed_pair, left), (feed_up_pair, right),
                (feed_gate_pair.at[:, pl.ds(0, third)], right_third),
                (low_src, low), (mix_w_src, mix_w), (gate_rows_src, gate_rows),
                (hidden_src, hidden), (decay_rows_src, decay_rows), (conv_src, conv),
                (input_rows_src, input_rows), (scan_rows_src, scan_rows), (resid, out),
                (scales, coefs),
            )
        )
    ]
    for load in loads[:1] + loads[4:] + loads[1:4]:
        load.start()
    meet(s, z)
    for whole in wholes:
        whole.start()
    sums[...] = jnp.zeros_like(sums)
    red = LineReduce(s, z, part, land, bo_send, bo_recv)
    weights = [
        WeightGrads(s, z, *refs, w_send.at[i], w_recv.at[i], w_load.at[i])
        for i, refs in enumerate(
            (
                (stages, lands, add_v, adds, up_own),
                (stages_third, third_lands, third_add_v, third_adds, third_own),
            )
        )
    ]
    loads[0].wait()
    for c in range(chunks):
        red.start_ends(c)
    for c in range(chunks):
        red.start_rest(c)

    def result(c):
        at = chunk_rows(c)
        red.total(c, out.at[at], True)
        out[at, :] += part[c, z].astype(F32)

    def sum_on(t):
        in_range(t, chunks, lambda c: red.forward(c))
        in_range(t - 2, chunks, result)

    for load in loads[4:9]:
        load.wait()

    def start(g):
        at = group_rows(g)
        grad = dot_nt(low[at, :], mix_w[...])
        for k in range(GROUP // CHUNK):
            c = g * (GROUP // CHUNK) + k
            here = chunk_rows(c)
            act, slope = gelu_pair(gate_rows[here, :])
            now = hidden[pl.ds(pl.multiple_of(c * CHUNK + 8, 8), CHUNK), :]
            part = grad[k * CHUNK : (k + 1) * CHUNK, :]
            gate_low[here, :] = (part * now * slope).astype(BF16)
            put(grads, here, part * act)
            decay = jnp.exp(-sigmoid(decay_rows[here, :]) * par[7:8, :])
            put(kept, here, masks[here, 0:1] * decay)

    lax.fori_loop(0, rows // GROUP, lambda g, carry: (start(g), carry)[1], 0)
    for c in range(chunks):
        pairs[1].start(c)
    count, groups = rows // SUBS, lanes // LANE

    def total_of(step, carry):
        keeps, adds = strided(kept, count - 1 - step), strided(grads, count - 1 - step)
        return (
            [p * k for p, k in zip(carry[0], keeps)],
            [k * (v + a) for k, v, a in zip(keeps, carry[1], adds)],
        )

    product, value = lax.fori_loop(
        0,
        count,
        total_of,
        ([jnp.ones((SUBS, LANE), F32)] * groups, [jnp.zeros((SUBS, LANE), F32)] * groups),
        unroll=4,
    )
    product, value = jnp.concatenate(product, axis=1), jnp.concatenate(value, axis=1)
    whole = (jnp.ones((1, lanes), F32), jnp.zeros((1, lanes), F32))
    for sub in range(SUBS - 1, -1, -1):
        here = product[sub : sub + 1, :]
        whole = (whole[0] * here, here * whole[1] + value[sub : sub + 1, :])
    slots[s, 0:1, :] = whole[0]
    slots[s, 1:2, :] = whole[1]
    spread = Spread(s, z, lambda p: slots.at[p], small_send, small_recv)
    spread.start()
    for load in loads[1:4]:
        load.wait()
    weights[0].across(left, right)
    weights[1].across(left, right_third)
    spread.finish()
    entry = jnp.zeros((1, lanes), F32)
    for place in range(PLANE - 1, 0, -1):
        entry = jnp.where(
            place > s, slots[place, 0:1, :] * entry + slots[place, 1:2, :], entry
        )
    entries = []
    for sub in range(SUBS - 1, -1, -1):
        entries.append(entry)
        entry = product[sub : sub + 1, :] * entry + value[sub : sub + 1, :]

    def step_back(step, now):
        keeps, adds = strided(kept, count - 1 - step), strided(grads, count - 1 - step)
        now = [v + a for v, a in zip(now, adds)]
        strided_put(grads, count - 1 - step, now)
        return [k * v for k, v in zip(keeps, now)]

    lax.fori_loop(
        0, count, step_back, lanes_of(jnp.concatenate(entries[::-1], axis=0)), unroll=4
    )

    def gates(c):
        at = chunk_rows(c)
        tall = pl.ds(pl.multiple_of(c * CHUNK, 8), CHUNK + 8)
        adjoint = get(grads, at)
        before = hidden[tall, :][7 : 7 + CHUNK, :]
        mask = masks[at, :]
        goes_on = mask[:, 0:1]
        opened = sigmoid(decay_rows[at, :])
        entered = sigmoid(input_rows[at, :])
        rate = par[7:8, :]
        decay = jnp.exp(-opened * rate)
        room = 1.0 - decay * decay
        root = jnp.sqrt(jnp.maximum(room, FLOOR_VALUE))
        multiplier = 1.0 + goes_on * (root - 1.0)
        conv_f = conv[at, :].astype(F32)
        direct = adjoint * multiplier
        grad_input = (direct * conv_f * (entered * (1.0 - entered))).astype(BF16)
        through = jnp.where(
            room > FLOOR_VALUE, 1.0, jnp.where(room == FLOOR_VALUE, 0.5, 0.0)
        )
        grad_decay = goes_on * (
            adjoint * before - adjoint * entered * conv_f * (through * decay / root)
        )
        scaled = grad_decay * decay * opened
        grad_rows = (-scaled * rate * (1.0 - opened)).astype(BF16)
        joined = jnp.concatenate([grad_rows, grad_input], axis=1)
        both[at, :] = joined
        grad_conv = direct * entered + dot_nt(joined, gates_w[...])
        conv_grad[at, :] = grad_conv
        block = scan_rows[tall, :]
        sums[0:1, :] += jnp.sum(grad_conv * block[8:, :], axis=0, keepdims=True)
        for lag in range(1, KW):
            sums[lag : lag + 1, :] += jnp.sum(
                mask[:, lag : lag + 1] * (grad_conv * block[8 - lag : 8 - lag + CHUNK, :]),
                axis=0,
                keepdims=True,
            )
        sums[4:5, :] += jnp.sum(grad_conv, axis=0, keepdims=True)
        sums[5:6, :] += jnp.sum(grad_rows.astype(F32), axis=0, keepdims=True)
        sums[6:7, :] += jnp.sum(grad_input.astype(F32), axis=0, keepdims=True)
        sums[7:8, :] += jnp.sum(scaled, axis=0, keepdims=True)
        pl.when(c == 0)(lambda: weights[0].beside(0, left, right))
        pl.when(c == 1)(lambda: weights[0].beside(1, left, right))
        pl.when(c == 2)(lambda: weights[1].beside(0, left, right_third))
        pl.when(c == 3)(lambda: weights[1].beside(1, left, right_third))
        pl.when(c == 4)(lambda: weights[0].mine(left, right))
        pl.when(c == 5)(lambda: weights[1].mine(left, right_third))
        sum_on(c)

    for load in loads[9:]:
        load.wait()
    each_chunk(chunks, gates)
    halo = remote(
        conv_grad.at[pl.ds(0, 8)], conv_grad.at[pl.ds(rows, 8)], halo_send, halo_recv,
        (lax.rem(s + PLANE - 1, PLANE), z),
    )
    first, final = s == 0, s == PLANE - 1
    pl.when(jnp.logical_not(first))(lambda: halo.start())
    gates_grad[...] = dot_tn(conv[...], both[...])
    sums[7:8, :] = sums[7:8, :] * par[8:9, :]

    @pl.when(final)
    def _():
        conv_grad[rows : rows + 8, :] = jnp.zeros((8, lanes), F32)

    pl.when(jnp.logical_not(final))(lambda: halo.wait_recv())

    def finish(c):
        at = chunk_rows(c)
        tall = pl.ds(pl.multiple_of(c * CHUNK, 8), CHUNK + 8)
        block, mask = conv_grad[tall, :], masks[tall, :]
        total = par[0:1, :] * block[:CHUNK, :]
        for lag in range(1, KW):
            total = total + mask[lag : lag + CHUNK, lag : lag + 1] * (
                par[lag : lag + 1, :] * block[lag : lag + CHUNK, :]
            )
        grad = total.astype(BF16)
        both[at, 0:lanes] = grad
        pairs[0].start(c)
        products = grad.astype(F32) * scan_rows[
            pl.ds(pl.multiple_of(c * CHUNK + 8, 8), CHUNK), :
        ] + gate_low[at, :].astype(F32) * gate_rows[at, :]
        inners[z, c] = as_row(jnp.sum(products, axis=1, keepdims=True))
        inner_spread.start(c)
        sum_on(c + chunks)

    each_chunk(chunks, finish)
    for weight in weights:
        weight.finish()

    def close(c):
        at = chunk_rows(c)
        inner_spread.finish(c)
        total = inners[0, c] + inners[1, c] + inners[2, c] + inners[3, c]
        scale = coefs[at, :]
        coefs[at, :] = scale * scale * as_columns(total) / features
        inner_spread.drain(c)
        red.drain(c)
        for pair in pairs:
            pair.drain(c)

    each_chunk(chunks, close)
    for whole in wholes:
        whole.wait()
    pl.when(jnp.logical_not(first))(lambda: halo.wait_send())


def recur_back(low, mix_w, gate_rows, hidden, conv, decay_rows, input_rows, scan_rows, masks, par,
               gates_w, scales, resid, normed, mixed, bo_part, pairs):
    rows, features = low.shape
    lanes, width = gate_rows.shape[1], resid.shape[1]
    chunks, hidden_size, part = rows // CHUNK, pairs[1].shape[2], features // PLANE
    two = hidden_size // THIRDS * (THIRDS - 1)

    def pair(size):
        return struct((2, rows, size), BF16)

    return pl.pallas_call(
        recur_back_kernel,
        out_shape=(
            struct((lanes, 2 * lanes), F32),
            struct((8, lanes), F32),
            struct((rows, LANE), F32),
            struct((rows, width), F32),
            struct((part, hidden_size), F32),
            struct((part, two), F32),
            struct((rows, features), BF16), struct((rows, lanes), BF16), struct((rows, features), BF16),
            pair(lanes), pair(lanes),
            struct((2, part, hidden_size), BF16),
            struct((2, part, two), BF16),
            struct((part, hidden_size), BF16),
            struct((part, two), BF16),
        ),
        in_specs=[VM] * 3 + [ANY] * 16,
        out_specs=[VM] * 6 + [ANY] * 9,
        scratch_shapes=[
            vm(lanes // LANE, rows, LANE, kind=F32), vm(lanes // LANE, rows, LANE, kind=F32),
            vm(rows, 2 * lanes), vm(rows + 8, lanes, kind=F32), vm(rows, lanes),
            vm(PLANE, 8, lanes, kind=F32), vm(LINE, chunks, 8, LANE, kind=F32),
            vm(rows, features), vm(lanes, features), vm(rows, lanes, kind=F32),
            vm(rows + 8, lanes, kind=F32), vm(rows, lanes, kind=F32), vm(rows, lanes),
            vm(rows, lanes, kind=F32), vm(rows + 8, lanes, kind=F32),
            vm(chunks, LINE, CHUNK, width), vm(chunks, LINE + 1, CHUNK, width),
            vm(2 * rows, features), vm(2 * rows, hidden_size), vm(2 * rows, two),
            vm(3 * part, hidden_size), vm(3 * part, two),
            vm(part, hidden_size), vm(part, two),
            dma(7), dma(7), pltpu.SemaphoreType.DMA, pltpu.SemaphoreType.DMA,
            dma(LINE - 1, chunks), dma(LINE - 1, chunks),
            dma(2, chunks), dma(2, chunks), dma(2, chunks), dma(3), dma(3),
            dma(LINE, chunks), dma(LINE + 1, chunks), dma(2, 4), dma(2, 4), dma(2, 4), dma(14),
        ],
        compiler_params=pltpu.CompilerParams(
            collective_id=4, has_side_effects=True, vmem_limit_bytes=64 << 20
        ),
        name="recur_back",
    )(
        masks, par, gates_w, low, mix_w, gate_rows, hidden, decay_rows, conv, input_rows, scan_rows,
        scales, resid, normed, mixed, bo_part,
        *[pair.reshape(2 * rows, pair.shape[2]) for pair in pairs],
    )


def last_kernel(
    scan_w, gate_w, grad, tok, coefs, scales, gain, pack,
    normed, normed_twin, mixed, mixed_twin, low, low_twin, scan_pair, gate_pair,
    feed_pair, feed_gate_pair,
    tokens_grad, gain_grad, pack_sum, mix_own, scan_own, gate_own, third_own, lands, third_lands, adds, third_adds,
    part, land, acc, left, right, right_third, stages, stages_third, add_v, third_add_v, pack_land, gain_land,
    red_send, red_recv, w_send, w_recv, w_load, load_sem, pack_send, pack_recv, gain_send, gain_recv,
):
    s, z = lax.axis_index("seq"), lax.axis_index("tp")
    rows, width = tok.shape
    chunks = rows // CHUNK
    third = right_third.shape[1]
    loads = [
        pltpu.make_async_copy(src, dst, load_sem.at[i])
        for i, (src, dst) in enumerate(
            (
                (scan_pair, right.at[1]), (gate_pair, right.at[2]),
                (normed, left.at[1, :rows]), (normed_twin, left.at[1, rows:]),
                (mixed, right.at[0, :rows]), (mixed_twin, right.at[0, rows:]),
                (low, left.at[0, :rows]), (low_twin, left.at[0, rows:]), (feed_pair, left.at[2]),
                (feed_gate_pair.at[:, pl.ds(2 * third, third)], right_third),
            )
        )
    ]
    for load in loads:
        load.start()
    meet(s, z)
    packs = [
        remote(
            pack.at[flip_all(s, bits)], pack_land.at[s], pack_send.at[bits - 1],
            pack_recv.at[bits - 1], (flip_all(s, bits), z),
        )
        for bits in range(1, PLANE)
    ]
    for copy in packs:
        copy.start()
    red = LineReduce(s, z, part, land, red_send, red_recv)
    weights = [
        WeightGrads(
            s, z, stages.at[i], lands.at[i], add_v.at[i], adds.at[i], own,
            w_send.at[i], w_recv.at[i], w_load.at[i],
        )
        for i, own in enumerate((mix_own, scan_own, gate_own))
    ]
    weights.append(
        WeightGrads(
            s, z, stages_third, third_lands, third_add_v, third_adds, third_own,
            w_send.at[3], w_recv.at[3], w_load.at[3],
        )
    )
    gain_land[s] = jnp.zeros_like(gain_grad)

    def project(g):
        at = group_rows(g)
        values = dot_nt(right[1, at, :], scan_w[...]) + dot_nt(right[2, at, :], gate_w[...])
        for k in range(GROUP // CHUNK):
            c = g * (GROUP // CHUNK) + k
            here = slice(k * CHUNK, (k + 1) * CHUNK)
            for o in range(LINE):
                part[c, o] = values[here, o * width : (o + 1) * width].astype(BF16)
            red.start_ends(c)

    def reduced(c):
        at = chunk_rows(c)
        red.total(c, acc)
        up = acc[...] + part[c, z].astype(F32)
        scale, values = scales[at, 0:1], tok[at, :].astype(F32)
        gain_land[s, 0:1, :] += jnp.sum(up * values * scale, axis=0, keepdims=True)
        tokens_grad[at, :] = (
            grad[at, :] + scale * gain[0:1, :] * up - values * coefs[at, 0:1]
        )

    for load in loads[:2]:
        load.wait()
    project(0)

    for g in range(1, chunks * CHUNK // GROUP):
        project(g)
    for c in range(chunks):
        red.start_rest(c)
    for load in loads[2:]:
        load.wait()
    factors = (
        (left.at[0], right.at[0]), (left.at[1], right.at[1]), (left.at[1], right.at[2]),
        (left.at[2], right_third),
    )
    for weight, pair in zip(weights[::-1], factors[::-1]):
        weight.across(*pair)
    for weight, pair in zip(weights[::-1], factors[::-1]):
        weight.beside(0, *pair)
        weight.beside(1, *pair)

    def weigh(t):
        for i in range(4):
            pl.when(t == i)(lambda i=i: weights[i].mine(*factors[i]))
            pl.when(t == chunks - 1 + i // 2)(lambda i=i: weights[3 - i].finish())

    def turn(t, carry):
        in_range(t, chunks, lambda c: red.forward(c))
        weigh(t)
        in_range(t - 1, chunks, reduced)
        return carry

    lax.fori_loop(0, chunks + 1, turn, 0)
    gain_spread = Spread(s, z, lambda p: gain_land.at[p], gain_send, gain_recv)
    gain_spread.start()
    for bits in range(1, PLANE):
        other = pack_land.at[flip_all(s, bits)]
        remote(
            other, other, pack_send.at[bits - 1], pack_recv.at[bits - 1], (flip_all(s, bits), z)
        ).wait_recv()
    total = pack[s]
    for bits in range(1, PLANE):
        total = total + pack_land[flip_all(s, bits)]
    pack_sum[...] = total
    gain_spread.finish()
    total = gain_land[0]
    for place in range(1, PLANE):
        total = total + gain_land[place]
    gain_grad[...] = total
    for copy in packs:
        copy.wait_send()
    each_chunk(chunks, red.drain)


def last_reduce(scan_w, gate_w, grad, tok, coefs, scales, gain, pack, pairs):
    rows, width = tok.shape
    features, lanes = width * LINE, scan_w.shape[1]
    chunks, part = rows // CHUNK, features // PLANE
    return pl.pallas_call(
        last_kernel,
        out_shape=(
            struct((rows, width), F32),
            struct((8, width), F32),
            struct(pack.shape[1:], F32),
            struct((part, lanes), F32),
            struct((part, lanes), F32),
            struct((part, lanes), F32),
            struct((part, pairs[9].shape[2] // THIRDS), F32),
            struct((3, 2, part, lanes), BF16),
            struct((2, part, pairs[9].shape[2] // THIRDS), BF16),
            struct((3, part, lanes), BF16),
            struct((part, pairs[9].shape[2] // THIRDS), BF16),
        ),
        in_specs=[VM] * 8 + [ANY] * 10,
        out_specs=[VM] * 7 + [ANY] * 4,
        scratch_shapes=[
            vm(chunks, LINE, CHUNK, width), vm(chunks, LINE + 1, CHUNK, width),
            vm(CHUNK, width, kind=F32),
            vm(3, 2 * rows, features), vm(3, 2 * rows, lanes), vm(2 * rows, pairs[9].shape[2] // THIRDS),
            vm(3, 3 * part, lanes), vm(3 * part, pairs[9].shape[2] // THIRDS),
            vm(3, part, lanes), vm(part, pairs[9].shape[2] // THIRDS),
            vm(*pack.shape, kind=F32), vm(PLANE, 8, width, kind=F32),
            dma(LINE, chunks), dma(LINE + 1, chunks),
            dma(4, 4), dma(4, 4), dma(4, 4), dma(10), dma(7), dma(7), dma(7), dma(7),
        ],
        compiler_params=pltpu.CompilerParams(
            collective_id=5, has_side_effects=True, vmem_limit_bytes=63 << 20
        ),
        name="last_reduce",
    )(
        scan_w, gate_w, grad, tok, coefs, scales, gain, pack,
        *pairs[:6],
        *[pair.reshape(2 * rows, pair.shape[2]) for pair in pairs[6:]],
    )


def placements(lanes, groups, seq_devices):
    cut, part = BW // seq_devices, lanes // seq_devices
    rows = np.arange(lanes)
    source = (rows % BW) // cut * part + rows // BW * cut + rows % cut
    row_order = (source[:, None] == rows[None, :]).astype(np.float32)
    tile = (np.arange(2 * LANE)[:, None] == rows[None, :] % BW).astype(np.float32)
    cells = (rows[:, None] // BW == rows[None, :] // BW).astype(np.float32)
    spots = np.arange(seq_devices * LANE)
    lane_order = (
        (rows[None, :] // part == spots[:, None] // LANE)
        & (rows[None, :] % part == spots[:, None] % LANE)
    ).astype(np.float32)
    return tuple(jnp.asarray(m, BF16) for m in (row_order, tile, cells, lane_order))


def shards_fast(
    tokens, mix_gain, scan_branch, gate_branch, kernel_taps, kernel_bias, decay_gate, decay_bias,
    input_gate, input_bias, decay_logit, mixer_out, feed_gain, gate_weight, up_weight, down_weight,
    lengths, cotangent,
):
    row_count, width = tokens.shape
    seq_devices = lax.axis_size("seq")
    shard_index = lax.axis_index("seq")
    ext_offsets = seq_offsets(lengths, shard_index * row_count, row_count + 8)
    lag_at = jnp.array([1, 1, 2, 3, 0, 0, 0, 0], jnp.int32)
    masks = (ext_offsets[:, None] >= lag_at[None, :]).astype(F32)
    lanes = scan_branch.shape[1]
    part = lanes // seq_devices
    groups = lanes // BW
    consts = placements(lanes, groups, seq_devices)
    small = jnp.concatenate(
        [
            kernel_taps, kernel_bias[None], decay_bias[None], input_bias[None], decay_logit[None],
            jnp.zeros((8, part), BF16),
        ]
    )
    small = jnp.pad(small, ((0, 0), (0, LANE - part)))
    gains = jnp.pad(
        jnp.concatenate([mix_gain, feed_gain]).astype(F32)[None, :], ((0, 7), (0, 0))
    )
    pad = ((0, 0), (0, 2 * LANE - BW))
    gate_blocks = jnp.concatenate(
        [jnp.pad(m.reshape(part, BW), pad) for m in (decay_gate, input_gate)], 1
    )
    (
        normed_first, scan_pad, gate_rows, conv_rows, decay_rows, input_rows, hidden_state, mixed,
        scan_w, gate_w, gates_w, scale_first_rows, decay_sums, par, gain_own, mix_w, ffn_gate, cot_full,
    ) = first_half(
        tokens, cotangent, small, gains, gate_blocks, scan_branch, gate_branch, mixer_out, gate_weight,
        masks, consts,
    )
    (
        resid, grad_resid, feed_grads, down_own, _, _, grad_branch, bo_part,
        low_pair, cot_pair, mid_pair, gate_pair, up_pair,
    ) = feed_both(
        mixed, mix_w, tokens, cotangent, gain_own, up_weight, down_weight, ffn_gate, cot_full
    )
    (
        gates_grad, sums, first_coefs, block_out, up_own, third_b,
        normed_twin, mixed_twin, branch_twin, scan_pair, gaterow_pair, *_,
    ) = recur_back(
        grad_branch, mix_w, gate_rows, hidden_state, conv_rows, decay_rows, input_rows, scan_pad,
        masks, par, gates_w, scale_first_rows, resid, normed_first, mixed, bo_part,
        (low_pair, up_pair, gate_pair),
    )

    def own_parts(rows):
        return rows.reshape(rows.shape[0], seq_devices, part).transpose(1, 0, 2)

    small = own_parts(jnp.concatenate([sums, decay_sums[0:1]], 0)).reshape(seq_devices, -1)
    tiles = [
        jnp.stack(
            [
                gates_grad[g * BW : (g + 1) * BW, i * lanes + g * BW : i * lanes + (g + 1) * BW]
                for g in range(groups)
            ]
        )
        .reshape(groups, seq_devices, -1)
        .transpose(1, 0, 2)
        .reshape(seq_devices, -1)
        for i in range(2)
    ]
    feed_part = feed_grads[0].reshape(seq_devices, -1)
    flat_grads = jnp.concatenate([*tiles, small, feed_part], 1)
    grad_rows = -(-flat_grads.shape[1] // (128 * 8)) * 8
    grad_pack = jnp.pad(flat_grads, ((0, 0), (0, grad_rows * 128 - flat_grads.shape[1])))
    tokens_grad, mix_grads, pack_sum, mix_own, scan_own, gaterow_own, third_c, *_ = last_reduce(
        scan_w, gate_w, grad_resid, tokens, first_coefs, scale_first_rows,
        gain_own,
        grad_pack.reshape(seq_devices, grad_rows, 128),
        (
            normed_first, normed_twin, mixed, mixed_twin, grad_branch, branch_twin, scan_pair,
            gaterow_pair, low_pair, gate_pair,
        ),
    )
    pack_sum = pack_sum.reshape(-1)
    gate_size = part * BW
    cut_at = 2 * gate_size
    small_sum = pack_sum[cut_at : cut_at + 9 * part].reshape(9, part)
    feed_sum = pack_sum[cut_at + 9 * part : cut_at + 9 * part + mix_gain.shape[0]]
    mix_sum = lax.dynamic_slice(
        mix_grads[0], (shard_index * mix_gain.shape[0],), (mix_gain.shape[0],)
    )
    return (
        block_out,
        tokens_grad,
        mix_sum,
        scan_own,
        gaterow_own,
        small_sum[0:KW],
        small_sum[KW],
        pack_sum[:gate_size].reshape(groups, -1),
        small_sum[KW + 1],
        pack_sum[gate_size : 2 * gate_size].reshape(groups, -1),
        small_sum[KW + 2],
        small_sum[KW + 3],
        mix_own.T,
        feed_sum,
        jnp.concatenate([third_b, third_c], axis=1),
        up_own,
        down_own.T,
        small_sum[KW + 4] / (row_count * seq_devices),
    )


def solution(mesh):
    placed = (
        P("seq", "tp"),
        P(("tp", "seq")),
        P("seq", "tp"),
        P("seq", "tp"),
        P(None, ("tp", "seq")),
        P(("tp", "seq")),
        P("tp", "seq"),
        P(("tp", "seq")),
        P("tp", "seq"),
        P(("tp", "seq")),
        P(("tp", "seq")),
        P("tp", "seq"),
        P(("tp", "seq")),
        P("seq", "tp"),
        P("seq", "tp"),
        P("tp", "seq"),
        P(),
        P("seq", "tp"),
    )
    return jax.shard_map(
        shards_fast if (mesh.shape["seq"], mesh.shape["tp"]) == (PLANE, LINE) else shards_general,
        mesh=mesh,
        in_specs=placed,
        out_specs=(
            P("seq", "tp"),
            P("seq", "tp"),
            P(("tp", "seq")),
            P("seq", "tp"),
            P("seq", "tp"),
            P(None, ("tp", "seq")),
            P(("tp", "seq")),
            P("tp", "seq"),
            P(("tp", "seq")),
            P("tp", "seq"),
            P(("tp", "seq")),
            P(("tp", "seq")),
            P("tp", "seq"),
            P(("tp", "seq")),
            P("seq", "tp"),
            P("seq", "tp"),
            P("tp", "seq"),
            P(("tp", "seq")),
        ),
        check_vma=False,
    )
```
